32 devices in a mesh: dp: 2 (over x), blk: 16 (over z, y, core).
Axes of the slice: x: 2, y: 2, z: 4, core: 2. Of those that a mesh axis runs over, the one named last changes fastest.
Arguments:
- decoder_rows: bfloat16 [32768, 768], P(('dp', 'blk')), may hold values from -6 to 6
- encoder_rows: bfloat16 [2048, 768], P(('dp', 'blk')), may hold values from -6 to 6
- target_lengths: int32 [32, 4], P(('dp', 'blk')), may hold values from 1 to 512, 1024 in all within a row
- target_question: int32 [32, 4], P(('dp', 'blk')), may hold values from 0 to 3, each once within a row
- passage_question: int32 [32], P('dp'), may hold values from 0 to 3, as said below
- self_gain: float32 [768], replicated, may hold values from 0.1 to 1.9
- self_query: bfloat16 [768, 768], replicated, may hold values from -0.4375 to 0.4375
- self_key: bfloat16 [768, 768], replicated, may hold values from -0.21875 to 0.21875
- self_value: bfloat16 [768, 768], replicated, may hold values from -0.21875 to 0.21875
- self_output: bfloat16 [768, 768], replicated, may hold values from -0.875 to 0.875
- position_bias_matrix: bfloat16 [32, 12], replicated, may hold values from -4 to 4
- cross_gain: float32 [768], replicated, may hold values from 0.1 to 1.9
- cross_query: bfloat16 [768, 768], replicated, may hold values from -0.4375 to 0.4375
- cross_key: bfloat16 [768, 768], replicated, may hold values from -0.21875 to 0.21875
- cross_value: bfloat16 [768, 768], replicated, may hold values from -0.21875 to 0.21875
- cross_output: bfloat16 [768, 768], replicated, may hold values from -0.875 to 0.875
- feed_gain: float32 [768], replicated, may hold values from 0.1 to 1.9
- feed_input_weight: bfloat16 [768, 3072], replicated, may hold values from -0.21875 to 0.21875
- feed_out: bfloat16 [3072, 768], replicated, may hold values from -0.109375 to 0.109375
- cotangent: bfloat16 [32768, 768], P(('dp', 'blk')), may hold values from -6 to 6
Outputs:
- block_out: bfloat16 [32768, 768], P(('dp', 'blk'))
- grad_decoder: float32 [32768, 768], P(('dp', 'blk'))
- grad_encoder: float32 [2048, 768], P(('dp', 'blk'))
- grad_self_gain: float32 [768], replicated
- grad_self_query: float32 [768, 768], P('blk')
- grad_self_key: float32 [768, 768], P('blk')
- grad_self_value: float32 [768, 768], P('blk')
- grad_self_output: float32 [768, 768], P('blk')
- grad_bias_table: float32 [32, 12], replicated
- grad_cross_gain: float32 [768], replicated
- grad_cross_query: float32 [768, 768], P('blk')
- grad_cross_key: float32 [768, 768], P('blk')
- grad_cross_value: float32 [768, 768], P('blk')
- grad_cross_output: float32 [768, 768], P('blk')
- grad_feed_gain: float32 [768], replicated
- grad_feed_in: float32 [768, 3072], P('blk')
- grad_feed_out: float32 [3072, 768], P('blk')
The draws below stay inside these ranges and needn't reach their ends.
Inputs may be any that keep to these rules, and one draw needn't show every extreme that they name: `target_lengths`: the 4 lengths of a sequence sum to 1024; in every sequence the largest is exactly 512. `target_question`: each row is a permutation of the 4 questions. `passage_question`: within the 16 passages of one dp index, each of the 4 questions owns exactly 4 passages.
All inputs are finite; a program needn't handle non-finite values.
Results may differ from the reference program's by a relative error of at most 0.029.
The reference program's roundings to bfloat16 on the way count: a program that leaves them out, or rounds other values in their place, can miss the bound.
Values may be sent and summed in bfloat16 or wider, within the bound.
A program may use at most 576 MiB of HBM per device.

```python
import math
import jax
import jax.numpy as jnp
import numpy as np
from jax import lax

D = 768
H = 12
HD = 64
FF = 3072
BUCKETS = 32
LEN = 1024
TARGETS = 4
SEQ_DEV = 1
ENC_DEV = 64
SEQS = 32
TOKENS = 32768
ENC_ROWS = 2048
N_DP = 2
N_BLK = 16


def draw_passage_question(key, part):
    key = jax.random.fold_in(key, 7)
    subkeys = jax.random.split(key, N_DP)
    orders = jax.vmap(lambda subkey: jax.random.permutation(subkey, N_BLK))(subkeys)
    return (orders % TARGETS).astype(jnp.int32).reshape(-1)


def block_scale(own_key, dims, cuts, smallest, largest):
    def one(position, parts):
        heights = jax.random.uniform(jax.random.fold_in(jax.random.fold_in(own_key, 6), position), (parts,), jnp.float32, smallest / len(cuts), largest / len(cuts))
        return jnp.repeat(jnp.exp(heights), dims[position] // parts).reshape((-1,) + (1,) * (len(dims) - position - 1))

    level = one(*cuts[0])
    for cut in cuts[1:]:
        level = level * one(*cut)
    return level


def length_profile(amount, total, reach, skew):
    portions = [(1 << 20) // math.isqrt(grade ** skew) + 1 for grade in range(2, amount + 1)]
    surplus, counts = total - reach - (amount - 1), [1] * (amount - 1)
    while surplus > 0:
        free = [i for i in range(amount - 1) if counts[i] < reach]
        whole, budget = sum([portions[i] for i in free]), surplus
        for i in free:
            more = min(reach - counts[i], max(1, budget * portions[i] // whole), surplus)
            counts[i] = counts[i] + more
            surplus = surplus - more
    return np.array([reach] + counts)


def uneven_parts(key, count, total, bound, lean):
    if count == 2:
        one = jax.random.randint(key, (), max(1, total - bound), min(bound, total - 1) + 1)
        return jnp.stack([one, total - one])
    tallies = jnp.asarray(length_profile(count, total, bound, lean), jnp.int32)
    couples = (count - 1) // 2
    source_of, receiver = tallies[1:1 + 2 * couples:2], tallies[2:2 + 2 * couples:2]
    slack = jnp.minimum(source_of - 1, bound - receiver)
    moved = jax.random.randint(jax.random.fold_in(key, 1), (couples,), 0, 1 << 20) % (slack + 1)
    tallies = tallies.at[1:1 + 2 * couples:2].set(source_of - moved).at[2:2 + 2 * couples:2].set(receiver + moved)
    return tallies[jax.random.permutation(jax.random.fold_in(key, 2), count)]


def gaussian(rng, dims, spread, limit, shards=(), kind=jnp.bfloat16):
    result = jax.random.normal(rng, dims, jnp.float32) * spread
    if len(shards) > 0:
        result = block_scale(rng, dims, shards, -0.22, 0.18) * result
    return jnp.clip(result, min=-limit, max=limit).astype(kind)


def setup_inputs(seed: int = 0) -> dict:
    arg_keys = jax.random.split(jax.random.key(seed), 21)
    decoder_rows = gaussian(arg_keys[0], (TOKENS, D), 1.0, 6.0, ((0, 32),))
    encoder_rows = gaussian(arg_keys[1], (ENC_ROWS, D), 1.0, 6.0, ((0, 32),))
    target_lengths = jax.vmap(lambda own: uneven_parts(own, TARGETS, LEN, LEN // 2, 2))(jax.random.split(arg_keys[2], SEQS)).reshape((SEQS, TARGETS)).astype(jnp.int32)
    target_question = jax.vmap(lambda own: jax.random.permutation(own, TARGETS))(jax.random.split(arg_keys[3], SEQS)).reshape((SEQS, TARGETS)).astype(jnp.int32)
    passage_question = draw_passage_question(jax.random.fold_in(arg_keys[20], 71), 0)
    self_gain = jnp.clip(1.0 + 0.18 * jax.random.normal(arg_keys[5], (D,), jnp.float32), 0.1, 1.9)
    self_query = gaussian(arg_keys[6], (D, D), (D // 4) ** -0.5, 0.4375)
    self_key = gaussian(arg_keys[7], (D, D), D ** -0.5, 0.21875)
    self_value = gaussian(arg_keys[8], (D, D), D ** -0.5, 0.21875)
    self_output = gaussian(arg_keys[9], (D, D), (D // 16) ** -0.5, 0.875)
    position_bias_matrix = gaussian(arg_keys[10], (BUCKETS, H), 1.0, 4.0)
    cross_gain = jnp.clip(1.0 + 0.18 * jax.random.normal(arg_keys[11], (D,), jnp.float32), 0.1, 1.9)
    cross_query = gaussian(arg_keys[12], (D, D), (D // 4) ** -0.5, 0.4375)
    cross_key = gaussian(arg_keys[13], (D, D), D ** -0.5, 0.21875)
    cross_value = gaussian(arg_keys[14], (D, D), D ** -0.5, 0.21875)
    cross_output = gaussian(arg_keys[15], (D, D), (D // 16) ** -0.5, 0.875)
    feed_gain = jnp.clip(1.0 + 0.18 * jax.random.normal(arg_keys[16], (D,), jnp.float32), 0.1, 1.9)
    feed_input_weight = gaussian(arg_keys[17], (D, FF), D ** -0.5, 0.21875)
    feed_out = gaussian(arg_keys[18], (FF, D), FF ** -0.5, 0.109375)
    cotangent = gaussian(arg_keys[19], (TOKENS, D), 1.0, 6.0, ((0, 32),))
    return {"decoder_rows": decoder_rows, "encoder_rows": encoder_rows, "target_lengths": target_lengths, "target_question": target_question, "passage_question": passage_question, "self_gain": self_gain, "self_query": self_query, "self_key": self_key, "self_value": self_value, "self_output": self_output, "position_bias_matrix": position_bias_matrix, "cross_gain": cross_gain, "cross_query": cross_query, "cross_key": cross_key, "cross_value": cross_value, "cross_output": cross_output, "feed_gain": feed_gain, "feed_input_weight": feed_input_weight, "feed_out": feed_out, "cotangent": cotangent}


@jax.custom_vjp
def low(v):
    return lax.optimization_barrier(v.astype(jnp.bfloat16)).astype(jnp.float32)

@jax.custom_vjp
def low_back(v):
    return v

def low_keep(v):
    return (low(v), None)

def low_pass(kept, grad):
    return (grad,)

def back_keep(v):
    return (v, None)

def back_low(kept, grad):
    return (low(grad),)
low.defvjp(low_keep, low_pass)
low_back.defvjp(back_keep, back_low)
eps_norm = 1e-06
bucket_edges = (19, 21, 24, 27, 31, 35, 40, 46, 52, 59, 67, 77, 87, 99, 113)
highest = lax.Precision.HIGHEST

def matmul(left_side, right_side):
    return jnp.dot(left_side, right_side, precision=highest, preferred_element_type=jnp.float32)

def norm_rows(values, gain):
    inverse = lax.rsqrt(lax.optimization_barrier(jnp.mean(values * values, axis=-1, keepdims=True)) + eps_norm)
    return values * inverse * gain

def bucket_index(offsets):
    upper_part = 16 + sum(((offsets >= edge_at).astype(jnp.int32) for edge_at in bucket_edges))
    return jnp.where(offsets < 16, offsets, upper_part).astype(jnp.int32)

def target_layout(target_lengths, target_question):
    positions = jnp.arange(LEN, dtype=jnp.int32)
    seg_ends = jnp.cumsum(target_lengths, axis=1).astype(jnp.int32)
    segment = lax.optimization_barrier(jnp.sum((positions[None, :, None] >= seg_ends[:, None, :TARGETS - 1]).astype(jnp.int32), axis=-1)).astype(jnp.int32)
    chosen = segment[:, :, None] == jnp.arange(TARGETS, dtype=jnp.int32)
    question_tokens = lax.optimization_barrier(jnp.sum(jnp.where(chosen, target_question[:, None, :], 0), axis=-1)).astype(jnp.int32)
    return (segment, question_tokens)

def attention(queries, keys, values, score_bias, allowed):
    query_count = queries.shape[0]
    key_count = keys.shape[0]
    query_heads = queries.reshape(query_count, H, HD)
    key_heads = keys.reshape(key_count, H, HD)
    value_heads = values.reshape(key_count, H, HD)
    raw_scores = jnp.einsum('qhd,khd->hqk', query_heads, key_heads, precision=highest) * HD ** (-0.5)
    if score_bias is not None:
        raw_scores = raw_scores + score_bias
    scores = jnp.where(allowed[None], low_back(raw_scores), -1e+30)
    attention_probabilities = jax.nn.softmax(scores, axis=-1)
    mixed_out = jnp.einsum('hqk,khd->qhd', low(attention_probabilities), value_heads, precision=highest)
    return low(low_back(mixed_out.reshape(query_count, D)))

def layer_sequence(weights, seq_input, seg_ids, row_quest, key_group, value_group, quest_group, bias_full):
    self_gain, self_query, self_key, self_value, self_output, cross_gain, cross_query, cross_output, feed_gain, feed_input_weight, feed_out = weights
    positions = jnp.arange(LEN, dtype=jnp.int32)
    act_self = low(norm_rows(seq_input, self_gain))
    query_self = low(low_back(matmul(act_self, self_query)))
    key_self = low(low_back(matmul(act_self, self_key)))
    value_self = low(low_back(matmul(act_self, self_value)))
    allowed_self = (positions[None, :] <= positions[:, None]) & (seg_ids[:, None] == seg_ids[None, :])
    attn_self = attention(query_self, key_self, value_self, bias_full, allowed_self)
    resid_self = seq_input + low_back(matmul(attn_self, self_output))
    act_cross = low(norm_rows(resid_self, cross_gain))
    query_cross = low(low_back(matmul(act_cross, cross_query)))
    allowed_cross = row_quest[:, None] == quest_group[None, :]
    attn_cross = attention(query_cross, key_group, value_group, None, allowed_cross)
    resid_cross = resid_self + low_back(matmul(attn_cross, cross_output))
    act_feed = low(norm_rows(resid_cross, feed_gain))
    pre_feed = low_back(matmul(act_feed, feed_input_weight))
    hidden = low(jax.nn.gelu(pre_feed, approximate=False))
    return resid_cross + low_back(matmul(hidden, feed_out))

def forward(decoder_f, encoder_f, self_gain, self_query, self_key, self_value, self_output, position_bias_matrix, cross_gain, cross_query, cross_key, cross_value, cross_output, feed_gain, feed_input_weight, feed_out, segment, question_tokens, key_question):
    positions = jnp.arange(LEN, dtype=jnp.int32)
    buckets = bucket_index(jnp.maximum(positions[:, None] - positions[None, :], 0))
    bias_full = jnp.transpose(position_bias_matrix[buckets], (2, 0, 1))
    group_rows = encoder_f.reshape(N_DP, N_BLK * ENC_DEV, D)
    key_all = low(low_back(jnp.einsum('gkd,de->gke', group_rows, cross_key, precision=highest)))
    value_all = low(low_back(jnp.einsum('gkd,de->gke', group_rows, cross_value, precision=highest)))
    weights = (self_gain, self_query, self_key, self_value, self_output, cross_gain, cross_query, cross_output, feed_gain, feed_input_weight, feed_out)
    seq_inputs = decoder_f.reshape(SEQS, LEN, D)
    group_ids = (jnp.arange(SEQS, dtype=jnp.int32) // (SEQ_DEV * N_BLK)).astype(jnp.int32)
    checked = jax.checkpoint(layer_sequence)

    def seq_step(running, seq_items):
        seq_input, seg_ids, row_quest, group_idx = seq_items
        block_result = checked(weights, seq_input, seg_ids, row_quest, key_all[group_idx], value_all[group_idx], key_question[group_idx], bias_full)
        return (running, block_result)
    unused, outputs = lax.scan(seq_step, None, (seq_inputs, segment, question_tokens, group_ids))
    return outputs.reshape(TOKENS, D)

def reference(decoder_rows, encoder_rows, target_lengths, target_question, passage_question, self_gain, self_query, self_key, self_value, self_output, position_bias_matrix, cross_gain, cross_query, cross_key, cross_value, cross_output, feed_gain, feed_input_weight, feed_out, cotangent):
    segment, question_tokens = target_layout(target_lengths, target_question)
    key_question = jnp.repeat(passage_question, ENC_DEV).reshape(N_DP, N_BLK * ENC_DEV).astype(jnp.int32)
    float_args = tuple((item.astype(jnp.float32) for item in (decoder_rows, encoder_rows, self_gain, self_query, self_key, self_value, self_output, position_bias_matrix, cross_gain, cross_query, cross_key, cross_value, cross_output, feed_gain, feed_input_weight, feed_out)))

    def closed(*params):
        return forward(*params, segment, question_tokens, key_question)
    block_result, pullback = jax.vjp(closed, *float_args)
    grads = pullback(cotangent.astype(jnp.float32))
    return (block_result.astype(jnp.bfloat16), grads[0], grads[1], grads[2], grads[3], grads[4], grads[5], grads[6], grads[7], grads[8], grads[9], grads[10], grads[11], grads[12], grads[13], grads[14], grads[15])
```

```python
import functools
from functools import partial

import jax
import jax.numpy as jnp
from jax import lax
from jax.experimental import pallas as pl
from jax.experimental.pallas import tpu as pltpu
from jax.sharding import PartitionSpec as P

D = 768
H = 12
HD = 64
BUCKETS = 32
LEN = 1024
TARGETS = 4
PAIRS = H // 2
LANES = 2 * HD
TILE = 256
SCALE = HD ** -0.5
NEG = -1e30
VMEM_LIMIT = 60 * 1024 * 1024

eps_norm = 1e-06
bucket_edges = (19, 21, 24, 27, 31, 35, 40, 46, 52, 59, 67, 77, 87, 99, 113)


def dot_nn(a, b):
    return jnp.dot(a, b, preferred_element_type=jnp.float32)


def dot_nt(a, b):
    return lax.dot_general(a, b, (((1,), (1,)), ((), ())), preferred_element_type=jnp.float32)


def dot_tn(a, b):
    return lax.dot_general(a, b, (((0,), (0,)), ((), ())), preferred_element_type=jnp.float32)


def lane_ids(rows):
    return lax.broadcasted_iota(jnp.int32, (rows, LANES), 1)


def in_half(rows, head):
    lane = lane_ids(rows)
    return lane < HD if head == 0 else lane >= HD


def split3(value):
    high = value.astype(jnp.bfloat16).astype(jnp.float32)
    rest = value - high
    mid = rest.astype(jnp.bfloat16).astype(jnp.float32)
    return high, mid, rest - mid


def triple_lanes(first, second, rows):
    lane = lane_ids(rows)
    out = jnp.zeros((rows, LANES), jnp.float32)
    for base, value in ((HD, first), (0, second)):
        for place, part in enumerate(split3(value)):
            out = jnp.where(lane == base + place, part, out)
    return out


def bucket_vector(table_t, offsets):
    upper = jnp.full(offsets.shape, 16, jnp.int32)
    for edge in bucket_edges:
        upper = upper + (offsets >= edge).astype(jnp.int32)
    bucket = jnp.where(offsets < 16, offsets, upper)
    rows = lax.broadcasted_iota(jnp.int32, (BUCKETS, offsets.shape[1]), 0)
    chosen = (rows == bucket).astype(jnp.float32).astype(jnp.bfloat16)
    return chosen


WIN = 3 * TILE


def self_forward_kernel(q_ref, k_ref, v_ref, aq_ref, ak_ref, table_ref, o_ref, aug_ref, bias_ref):
    lane768 = lax.broadcasted_iota(jnp.int32, (1, WIN), 1)
    offsets = 2 * TILE - lane768
    chosen = bucket_vector(None, jnp.maximum(offsets, 0))
    line = dot_nn(table_ref[0], chosen)
    line = jnp.where(offsets >= 0, line, NEG)
    far = table_ref[0][:, BUCKETS - 1 :].astype(jnp.float32)
    for head in range(2):
        spread = jnp.broadcast_to(line[head : head + 1], (TILE, WIN))
        bias_ref[head] = pltpu.roll(spread, 0, 1, stride=1, stride_axis=0)[:, TILE:]
    aq, ak = aq_ref[...], ak_ref[...]
    outs = {}
    logs = {}
    for head in range(2):
        half = in_half(LEN, head)
        q = jnp.where(half, q_ref[...] * jnp.bfloat16(SCALE), aq)
        k = jnp.where(half, k_ref[...], ak)
        v = jnp.where(half, v_ref[...], jnp.zeros((), jnp.bfloat16))
        for i in range(LEN // TILE):
            lo = max(0, i - 2) * TILE
            hi = (i + 1) * TILE
            scores = dot_nt(q[i * TILE : hi], k[lo:hi])
            near = min(2 * TILE, hi - lo)
            parts = []
            if hi - lo > near:
                parts.append(scores[:, : hi - lo - near] + far[head : head + 1])
            parts.append(scores[:, hi - lo - near :] + bias_ref[head][:, 2 * TILE - near :])
            scores = parts[0] if len(parts) == 1 else jnp.concatenate(parts, axis=1)
            top = jnp.max(scores, axis=1, keepdims=True)
            expo = jnp.exp(scores - top)
            total = jnp.sum(expo, axis=1, keepdims=True)
            mixed = dot_nn(expo.astype(jnp.bfloat16), v[lo:hi]) / total
            logs[i, head] = top + jnp.log(total)
            outs[i, head] = mixed
            if head == 1:
                o_ref[i * TILE : hi] = (outs[i, 0] + outs[i, 1]).astype(jnp.bfloat16)
                aug = triple_lanes(logs[i, 0], logs[i, 1], TILE)
                lane = lane_ids(TILE)
                place = lane & (HD - 1)
                aug_ref[i * TILE : hi] = jnp.where(
                    place < 3, aug, aq_ref[i * TILE : hi].astype(jnp.float32)
                ).astype(jnp.bfloat16)


def pair_spec(offset=0):
    return pl.BlockSpec((LEN, LANES), lambda p: (0, p + offset))


def whole(shape):
    return pl.BlockSpec(shape, lambda p: (0,) * len(shape))


def self_forward(q, k, v, aq, ak, table_pairs):
    return pl.pallas_call(
        self_forward_kernel,
        grid=(PAIRS,),
        in_specs=[pair_spec()] * 3 + [whole((LEN, LANES))] * 2
        + [pl.BlockSpec((1, 2, BUCKETS), lambda p: (p, 0, 0))],
        out_specs=[pair_spec(), pair_spec()],
        out_shape=[jax.ShapeDtypeStruct((LEN, D), jnp.bfloat16)] * 2,
        scratch_shapes=[pltpu.VMEM((2, TILE, 2 * TILE), jnp.float32)],
        compiler_params=pltpu.CompilerParams(vmem_limit_bytes=VMEM_LIMIT),
        cost_estimate=pl.CostEstimate(flops=4 * H * LEN * LEN * HD, bytes_accessed=10 * LEN * D, transcendentals=0),
    )(q, k, v, aq, ak, table_pairs)


def self_backward_kernel(q_ref, k_ref, v_ref, do_ref, o_ref, aug_ref, ak_ref, av_ref, table_ref,
                         dq_ref, dk_ref, dv_ref, gt_ref, bias_ref, g_ref, gfar_ref, dqt_ref):
    lane768 = lax.broadcasted_iota(jnp.int32, (1, WIN), 1)
    offsets = lane768 - TILE
    chosen = bucket_vector(None, jnp.maximum(offsets, 0))
    line = dot_nn(table_ref[0], chosen)
    line = jnp.where(offsets >= 0, line, NEG)
    far = table_ref[0][:, BUCKETS - 1 :].astype(jnp.float32)
    for head in range(2):
        spread = jnp.broadcast_to(line[head : head + 1], (TILE, WIN))
        bias_ref[head] = pltpu.roll(spread, 0, 1, stride=1, stride_axis=0)[:, TILE:]
    g_ref[...] = jnp.zeros_like(g_ref)
    gfar_ref[...] = jnp.zeros_like(gfar_ref)
    dqt_ref[...] = jnp.zeros_like(dqt_ref)
    product = do_ref[...].astype(jnp.float32) * o_ref[...].astype(jnp.float32)
    deltas = []
    for head in range(2):
        half = in_half(LEN, head)
        deltas.append(jnp.sum(jnp.where(half, product, 0.0), axis=1, keepdims=True))
    aug_do = (-triple_lanes(deltas[0], deltas[1], LEN)).astype(jnp.bfloat16)
    q_scaled = q_ref[...] * jnp.bfloat16(SCALE)
    k_t = k_ref[...].T
    accs = {}
    for head in range(2):
        half = in_half(LEN, head)
        q = jnp.where(half, q_scaled, aug_ref[...])
        k = jnp.where(half, k_ref[...], ak_ref[...])
        v = jnp.where(half, v_ref[...], av_ref[...])
        do = jnp.where(half, do_ref[...], aug_do)
        for j in range(LEN // TILE):
            lo = j * TILE
            hi = min(LEN, (j + 3) * TILE)
            width = hi - lo
            near = min(2 * TILE, width)
            scores = dot_nt(k[lo : lo + TILE], q[lo:hi])
            parts = [scores[:, :near] + bias_ref[head][:, :near]]
            if width > near:
                parts.append(scores[:, near:] + far[head : head + 1])
            scores = parts[0] if len(parts) == 1 else jnp.concatenate(parts, axis=1)
            probs = jnp.exp(scores)
            grad_probs = dot_nt(v[lo : lo + TILE], do[lo:hi])
            grad_scores = probs * grad_probs
            g_ref[head, :, :near] += grad_scores[:, :near]
            if width > near:
                gfar_ref[head] += grad_scores[:, near:]
            ds = grad_scores.astype(jnp.bfloat16)
            accs[j, head] = (dot_nn(ds, q[lo:hi]), dot_nn(probs.astype(jnp.bfloat16), do[lo:hi]))
            dqt_ref[head * HD : (head + 1) * HD, lo:hi] += dot_nn(
                k_t[head * HD : (head + 1) * HD, lo : lo + TILE], ds
            )
            if head == 1:
                lower = in_half(TILE, 0)
                dk_ref[lo : lo + TILE] = jnp.where(lower, accs[j, 0][0], accs[j, 1][0]).astype(jnp.bfloat16)
                dv_ref[lo : lo + TILE] = jnp.where(lower, accs[j, 0][1], accs[j, 1][1]).astype(jnp.bfloat16)
    dq_ref[...] = (dqt_ref[...] * SCALE).T.astype(jnp.bfloat16)
    rows = []
    for head in range(2):
        total = jnp.zeros((8, WIN), jnp.float32)
        pad = jnp.zeros((8, TILE), jnp.float32)
        for a in range(TILE // 8):
            strip = jnp.concatenate([pad, g_ref[head, 8 * a : 8 * a + 8, :]], axis=1)
            if a:
                strip = pltpu.roll(strip, WIN - 8 * a, 1)
            total = total + strip
        line_sum = jnp.zeros((1, WIN), jnp.float32)
        for s in range(8):
            one = total[s : s + 1]
            line_sum = line_sum + (pltpu.roll(one, WIN - s, 1) if s else one)
        rows.append(line_sum)
    lines = jnp.concatenate(rows, axis=0)
    lines = jnp.where(offsets >= 0, lines, 0.0)
    high, mid, low = split3(lines)
    sums = sum(dot_nt(part.astype(jnp.bfloat16), chosen) for part in (high, mid, low))
    for head in range(2):
        far_sum = jnp.sum(gfar_ref[head])
        lane32 = lax.broadcasted_iota(jnp.int32, (1, BUCKETS), 1)
        gt_ref[0, head : head + 1, :] = sums[head : head + 1] + jnp.where(lane32 == BUCKETS - 1, far_sum, 0.0)


def self_backward(q, k, v, do, o, aug, ak, av, table_pairs):
    return pl.pallas_call(
        self_backward_kernel,
        grid=(PAIRS,),
        in_specs=[pair_spec()] * 6 + [whole((LEN, LANES))] * 2
        + [pl.BlockSpec((1, 2, BUCKETS), lambda p: (p, 0, 0))],
        out_specs=[pair_spec()] * 3 + [pl.BlockSpec((1, 2, BUCKETS), lambda p: (p, 0, 0))],
        out_shape=[jax.ShapeDtypeStruct((LEN, D), jnp.bfloat16)] * 3
        + [jax.ShapeDtypeStruct((PAIRS, 2, BUCKETS), jnp.float32)],
        scratch_shapes=[
            pltpu.VMEM((2, TILE, 2 * TILE), jnp.float32),
            pltpu.VMEM((2, TILE, 2 * TILE), jnp.float32),
            pltpu.VMEM((2, TILE, TILE), jnp.float32),
            pltpu.VMEM((LANES, LEN), jnp.float32),
        ],
        compiler_params=pltpu.CompilerParams(vmem_limit_bytes=VMEM_LIMIT),
        cost_estimate=pl.CostEstimate(flops=10 * H * LEN * LEN * HD, bytes_accessed=18 * LEN * D, transcendentals=0),
    )(q, k, v, do, o, aug, ak, av, table_pairs)


CT = 256


def cross_forward_kernel(order_ref, item_ref, q_ref, kv_ref, o_ref, aug_ref, ks_ref, vs_ref, passage):
    slots = order_ref.shape[0]
    per_q = slots // TARGETS
    keys_q = per_q * passage
    lower = lax.broadcasted_iota(jnp.int32, (passage, D), 1) % LANES < HD
    zero = jnp.zeros((), jnp.bfloat16)

    @pl.loop(0, slots)
    def _(s):
        src = pl.multiple_of(order_ref[s] * passage, passage)
        dst = pl.multiple_of(s * passage, passage)
        keys = kv_ref[pl.ds(src, passage), :D]
        values = kv_ref[pl.ds(src, passage), D:]
        ks_ref[0, pl.ds(dst, passage)] = jnp.where(lower, keys, zero)
        ks_ref[1, pl.ds(dst, passage)] = jnp.where(lower, zero, keys)
        vs_ref[0, pl.ds(dst, passage)] = jnp.where(lower, values, zero)
        vs_ref[1, pl.ds(dst, passage)] = jnp.where(lower, zero, values)

    o_ref[...] = jnp.zeros_like(o_ref)
    aug_ref[...] = jnp.zeros_like(aug_ref)

    @pl.loop(0, item_ref[4, 0])
    def _(n):
        row0 = pl.multiple_of(item_ref[0, n] * CT, CT)
        key0 = pl.multiple_of(item_ref[1, n] * keys_q, keys_q)
        rows = lax.broadcasted_iota(jnp.int32, (CT, 1), 0)
        valid = (rows >= item_ref[2, n]) & (rows < item_ref[3, n])
        for pair in range(PAIRS):
            cols = slice(pair * LANES, (pair + 1) * LANES)
            q = q_ref[pl.ds(row0, CT), cols] * jnp.bfloat16(SCALE)
            outs, logs = [], []
            for head in range(2):
                scores = dot_nt(q, ks_ref[head, pl.ds(key0, keys_q), cols])
                top = jnp.max(scores, axis=1, keepdims=True)
                expo = jnp.exp(scores - top)
                total = jnp.sum(expo, axis=1, keepdims=True)
                outs.append(dot_nn(expo.astype(jnp.bfloat16), vs_ref[head, pl.ds(key0, keys_q), cols]) / total)
                logs.append(top + jnp.log(total))
            mixed = (outs[0] + outs[1]).astype(jnp.bfloat16)
            aug = triple_lanes(logs[0], logs[1], CT).astype(jnp.bfloat16)
            o_ref[pl.ds(row0, CT), cols] = jnp.where(valid, mixed, o_ref[pl.ds(row0, CT), cols])
            aug_ref[pl.ds(row0, CT), cols] = jnp.where(valid, aug, aug_ref[pl.ds(row0, CT), cols])


def smem_spec():
    return pl.BlockSpec(memory_space=pltpu.SMEM)


def vmem_spec():
    return pl.BlockSpec(memory_space=pltpu.VMEM)


def cross_forward(order, items, q, kv, passage):
    keys = kv.shape[0]
    return pl.pallas_call(
        partial(cross_forward_kernel, passage=passage),
        in_specs=[smem_spec(), smem_spec(), vmem_spec(), vmem_spec()],
        out_specs=[vmem_spec(), vmem_spec()],
        out_shape=[jax.ShapeDtypeStruct((LEN, D), jnp.bfloat16)] * 2,
        scratch_shapes=[pltpu.VMEM((2, keys, D), jnp.bfloat16)] * 2,
        compiler_params=pltpu.CompilerParams(vmem_limit_bytes=VMEM_LIMIT),
        cost_estimate=pl.CostEstimate(flops=2 * H * LEN * LEN * HD, bytes_accessed=10 * LEN * D, transcendentals=0),
    )(order, items, q, kv)


def cross_backward_kernel(order_ref, item_ref, q_ref, kv_ref, do_ref, o_ref, aug_ref,
                          dq_ref, dkv_ref, ks_ref, vs_ref, kt_ref, dk_ref, dv_ref, dqt_ref, passage):
    slots = order_ref.shape[0]
    per_q = slots // TARGETS
    keys_q = per_q * passage
    lane = lax.broadcasted_iota(jnp.int32, (passage, D), 1) % LANES
    lower = lane < HD
    ones = jnp.where((lane & (HD - 1)) < 3, 1.0, 0.0).astype(jnp.bfloat16)
    minus = -ones

    @pl.loop(0, slots)
    def _(s):
        src = pl.multiple_of(order_ref[s] * passage, passage)
        dst = pl.multiple_of(s * passage, passage)
        keys = kv_ref[pl.ds(src, passage), :D]
        values = kv_ref[pl.ds(src, passage), D:]
        ks_ref[0, pl.ds(dst, passage)] = jnp.where(lower, keys, minus)
        ks_ref[1, pl.ds(dst, passage)] = jnp.where(lower, minus, keys)
        vs_ref[0, pl.ds(dst, passage)] = jnp.where(lower, values, ones)
        vs_ref[1, pl.ds(dst, passage)] = jnp.where(lower, ones, values)

    lower_k = lax.broadcasted_iota(jnp.int32, (keys_q, LANES), 1) < HD
    for s in range(TARGETS):
        for pair in range(PAIRS):
            rows = slice(s * keys_q, (s + 1) * keys_q)
            cols = slice(pair * LANES, (pair + 1) * LANES)
            both = jnp.where(lower_k, ks_ref[0, rows, cols], ks_ref[1, rows, cols])
            kt_ref[cols, rows] = both.T
    dk_ref[...] = jnp.zeros_like(dk_ref)
    dv_ref[...] = jnp.zeros_like(dv_ref)
    dqt_ref[...] = jnp.zeros_like(dqt_ref)

    @pl.loop(0, item_ref[4, 0])
    def _(n):
        row0 = pl.multiple_of(item_ref[0, n] * CT, CT)
        key0 = pl.multiple_of(item_ref[1, n] * keys_q, keys_q)
        rows = lax.broadcasted_iota(jnp.int32, (CT, 1), 0)
        valid = (rows >= item_ref[2, n]) & (rows < item_ref[3, n])
        here = pl.ds(row0, CT)
        there = pl.ds(key0, keys_q)
        for pair in range(PAIRS):
            cols = slice(pair * LANES, (pair + 1) * LANES)
            q_scaled = q_ref[here, cols] * jnp.bfloat16(SCALE)
            do_pair = jnp.where(valid, do_ref[here, cols], jnp.zeros((), jnp.bfloat16))
            product = do_pair.astype(jnp.float32) * o_ref[here, cols].astype(jnp.float32)
            deltas = []
            for head in range(2):
                deltas.append(jnp.sum(jnp.where(in_half(CT, head), product, 0.0), axis=1, keepdims=True))
            aug_do = (-triple_lanes(deltas[0], deltas[1], CT)).astype(jnp.bfloat16)
            aug = jnp.where(valid, aug_ref[here, cols], jnp.bfloat16(1e30))
            parts = []
            for head in range(2):
                half = in_half(CT, head)
                q = jnp.where(half, q_scaled, aug)
                do = jnp.where(half, do_pair, aug_do)
                probs = jnp.exp(dot_nt(ks_ref[head, there, cols], q))
                grad_scores = probs * dot_nt(vs_ref[head, there, cols], do)
                ds = grad_scores.astype(jnp.bfloat16)
                parts.append((dot_nn(ds, q), dot_nn(probs.astype(jnp.bfloat16), do)))
                hrow = pair * LANES + head * HD
                dqt_ref[hrow : hrow + HD, here] += dot_nn(kt_ref[hrow : hrow + HD, there], ds)
            dk_ref[there, cols] += jnp.where(lower_k, parts[0][0], parts[1][0])
            dv_ref[there, cols] += jnp.where(lower_k, parts[0][1], parts[1][1])

    for pair in range(PAIRS):
        cols = slice(pair * LANES, (pair + 1) * LANES)
        dq_ref[:, cols] = (dqt_ref[cols, :] * SCALE).T.astype(jnp.bfloat16)

    @pl.loop(0, slots)
    def _(s):
        src = pl.multiple_of(s * passage, passage)
        dst = pl.multiple_of(order_ref[s] * passage, passage)
        dkv_ref[pl.ds(dst, passage), :D] = dk_ref[pl.ds(src, passage)].astype(jnp.bfloat16)
        dkv_ref[pl.ds(dst, passage), D:] = dv_ref[pl.ds(src, passage)].astype(jnp.bfloat16)


def cross_backward(order, items, q, kv, do, o, aug, passage):
    keys = kv.shape[0]
    return pl.pallas_call(
        partial(cross_backward_kernel, passage=passage),
        in_specs=[smem_spec(), smem_spec()] + [vmem_spec()] * 5,
        out_specs=[vmem_spec(), vmem_spec()],
        out_shape=[
            jax.ShapeDtypeStruct((LEN, D), jnp.bfloat16),
            jax.ShapeDtypeStruct((keys, 2 * D), jnp.bfloat16),
        ],
        scratch_shapes=[pltpu.VMEM((2, keys, D), jnp.bfloat16)] * 2
        + [
            pltpu.VMEM((D, keys), jnp.bfloat16),
            pltpu.VMEM((keys, D), jnp.float32),
            pltpu.VMEM((keys, D), jnp.float32),
            pltpu.VMEM((D, LEN), jnp.float32),
        ],
        compiler_params=pltpu.CompilerParams(vmem_limit_bytes=VMEM_LIMIT),
        cost_estimate=pl.CostEstimate(flops=5 * H * LEN * LEN * HD, bytes_accessed=18 * LEN * D, transcendentals=0),
    )(order, items, q, kv, do, o, aug)


def cross_items(lengths, questions):
    ends = jnp.cumsum(lengths)
    starts = ends - lengths
    tiles = LEN // CT
    slots = tiles + TARGETS - 1
    first = starts // CT
    last = (ends - 1) // CT
    count = last - first + 1
    done = jnp.cumsum(count)
    number = jnp.arange(slots, dtype=jnp.int32)
    seg = jnp.sum((number[:, None] >= done[None, :]).astype(jnp.int32), axis=1)
    pick = (jnp.minimum(seg, TARGETS - 1)[:, None] == jnp.arange(TARGETS, dtype=jnp.int32)[None, :]).astype(jnp.int32)
    take = lambda a: jnp.sum(pick * a[None, :], axis=1)
    tile = jnp.clip(take(first) + number - take(done - count), 0, tiles - 1)
    lo = jnp.clip(take(starts) - tile * CT, 0, CT)
    hi = jnp.clip(take(ends) - tile * CT, 0, CT)
    total = jnp.broadcast_to(jnp.sum(count), (slots,))
    return jnp.stack([tile, take(questions), lo, hi, total]).astype(jnp.int32)


def passage_order(passage_question):
    count = passage_question.shape[0]
    ids = jnp.arange(count, dtype=jnp.int32)
    before = (passage_question[None, :] < passage_question[:, None]) | (
        (passage_question[None, :] == passage_question[:, None]) & (ids[None, :] < ids[:, None])
    )
    rank = jnp.sum(before.astype(jnp.int32), axis=1)
    return jnp.sum(jnp.where(rank[:, None] == ids[None, :], ids[:, None], 0), axis=0).astype(jnp.int32)


def segment_aug(segment):
    place = jnp.arange(LANES, dtype=jnp.int32)[None, :] & (HD - 1)
    seg = segment[:, None]
    mark = (place >= 3) & (place < 3 + TARGETS)
    same = place - 3 == seg
    aq = jnp.where(mark & same, 1.0, 0.0).astype(jnp.bfloat16)
    ak = jnp.where(place < 3, -1.0, jnp.where(mark & ~same, NEG, 0.0)).astype(jnp.bfloat16)
    av = jnp.broadcast_to(jnp.where(place < 3, 1.0, 0.0), (LEN, LANES)).astype(jnp.bfloat16)
    return aq, ak, av

FF_STEPS = 4
ROWS = 256


def normal_cdf_pair(u):
    x = jnp.abs(u) * 0.7071067811865476
    gauss = jnp.exp(-0.5 * u * u)
    t = 1.0 / (1.0 + 0.3275911 * x)
    poly = ((((1.061405429 * t - 1.453152027) * t + 1.421413741) * t - 0.284496736) * t + 0.254829592) * t
    tail = 0.5 * poly * gauss
    return jnp.where(u >= 0, 1.0 - tail, tail), gauss * 0.3989422804014327


def norm_parts(values):
    return lax.rsqrt(jnp.mean(values * values, axis=1, keepdims=True) + eps_norm)


def norm_back(values, inverse, gain, grad):
    scaled = grad * gain
    inner = jnp.mean(scaled * values, axis=1, keepdims=True)
    return inverse * scaled - values * (inverse * inverse * inverse * inner)


def feed_kernel(y1_ref, oc_ref, wco_ref, gain_ref, g_ref, w1_ref, w2_ref,
                out_ref, dw1_ref, dw2_ref, dy2_ref, doc_ref, dwco_ref, dgain_ref,
                y2_ref, act_ref, acc_ref, da_ref, hid_ref, du_ref):
    step = pl.program_id(0)

    @pl.when(step == 0)
    def _():
        for r in range(0, LEN, ROWS):
            rows = slice(r, r + ROWS)
            y2 = y1_ref[rows] + dot_nn(oc_ref[rows], wco_ref[...])
            y2_ref[rows] = y2
            act_ref[rows] = (y2 * norm_parts(y2) * gain_ref[...]).astype(jnp.bfloat16)
        acc_ref[...] = y2_ref[...]
        da_ref[...] = jnp.zeros_like(da_ref)

    for r in range(0, LEN, ROWS):
        rows = slice(r, r + ROWS)
        u = dot_nn(act_ref[rows], w1_ref[...])
        dh = dot_nt(g_ref[rows], w2_ref[...])
        cdf, density = normal_cdf_pair(u)
        hid = (u * cdf).astype(jnp.bfloat16)
        du = (dh * (cdf + u * density)).astype(jnp.bfloat16)
        hid_ref[rows] = hid
        du_ref[rows] = du
        acc_ref[rows] += dot_nn(hid, w2_ref[...])
        da_ref[rows] += dot_nt(du, w1_ref[...])
    dw2_ref[...] = dot_tn(hid_ref[...], g_ref[...]).astype(jnp.bfloat16)
    dw1_ref[...] = dot_tn(act_ref[...], du_ref[...]).astype(jnp.bfloat16)

    @pl.when(step == FF_STEPS - 1)
    def _():
        gain_sum = jnp.zeros((1, D), jnp.float32)
        for r in range(0, LEN, ROWS):
            rows = slice(r, r + ROWS)
            out_ref[rows] = acc_ref[rows].astype(jnp.bfloat16)
            y2 = y2_ref[rows]
            inverse = norm_parts(y2)
            da = da_ref[rows]
            gain_sum = gain_sum + jnp.sum(da * y2 * inverse, axis=0, keepdims=True)
            dy2 = g_ref[rows].astype(jnp.float32) + norm_back(y2, inverse, gain_ref[...], da)
            dy2_ref[rows] = dy2
            e2 = dy2.astype(jnp.bfloat16)
            du_ref[rows] = e2
            doc_ref[rows] = dot_nt(e2, wco_ref[...]).astype(jnp.bfloat16)
        dgain_ref[...] = gain_sum
        dwco_ref[...] = dot_tn(oc_ref[...], du_ref[...]).astype(jnp.bfloat16)


def feed_block(y1, oc, wco, gain, g, w1, w2):
    ff = w1.shape[1]
    cols = ff // FF_STEPS
    fixed = lambda shape: pl.BlockSpec(shape, lambda c: (0, 0))
    return pl.pallas_call(
        feed_kernel,
        grid=(FF_STEPS,),
        in_specs=[
            fixed((LEN, D)), fixed((LEN, D)), fixed((D, D)), fixed((1, D)), fixed((LEN, D)),
            pl.BlockSpec((D, cols), lambda c: (0, c)),
            pl.BlockSpec((cols, D), lambda c: (c, 0)),
        ],
        out_specs=[
            fixed((LEN, D)),
            pl.BlockSpec((D, cols), lambda c: (0, c)),
            pl.BlockSpec((cols, D), lambda c: (c, 0)),
            fixed((LEN, D)), fixed((LEN, D)), fixed((D, D)), fixed((1, D)),
        ],
        out_shape=[
            jax.ShapeDtypeStruct((LEN, D), jnp.bfloat16),
            jax.ShapeDtypeStruct((D, ff), jnp.bfloat16),
            jax.ShapeDtypeStruct((ff, D), jnp.bfloat16),
            jax.ShapeDtypeStruct((LEN, D), jnp.float32),
            jax.ShapeDtypeStruct((LEN, D), jnp.bfloat16),
            jax.ShapeDtypeStruct((D, D), jnp.bfloat16),
            jax.ShapeDtypeStruct((1, D), jnp.float32),
        ],
        scratch_shapes=[
            pltpu.VMEM((LEN, D), jnp.float32),
            pltpu.VMEM((LEN, D), jnp.bfloat16),
            pltpu.VMEM((LEN, D), jnp.float32),
            pltpu.VMEM((LEN, D), jnp.float32),
            pltpu.VMEM((LEN, cols), jnp.bfloat16),
            pltpu.VMEM((LEN, cols), jnp.bfloat16),
        ],
        compiler_params=pltpu.CompilerParams(vmem_limit_bytes=VMEM_LIMIT),
        cost_estimate=pl.CostEstimate(flops=12 * LEN * D * ff, bytes_accessed=40 * LEN * D, transcendentals=0),
    )(y1, oc, wco, gain, g, w1, w2)


def bits_of(count):
    return count.bit_length() - 1


def swap(value, axis, bit, size):
    return lax.ppermute(value, axis, [(i, i ^ (1 << bit)) for i in range(size)])


def total_of(terms):
    out = terms[0].astype(jnp.float32)
    for term in terms[1:]:
        out = out + term.astype(jnp.float32)
    return out


def gather_rows(rows, n_blk):
    out = rows
    for bit in range(bits_of(n_blk)):
        out = jnp.concatenate([out, swap(out, "blk", bit, n_blk)], axis=0)
    return out


def scatter_slots(value, n_blk):
    terms = [value]
    for bit in reversed(range(bits_of(n_blk))):
        half = 1 << bit
        send = total_of([t[half:] for t in terms]).astype(jnp.bfloat16)
        kept = total_of([t[:half] for t in terms]).astype(jnp.bfloat16)
        terms = [kept, swap(send, "blk", bit, n_blk)]
    return total_of(terms)[0]


def scatter_sum(grad, n_blk, n_dp, order):
    bits = bits_of(n_blk)
    me = lax.axis_index("blk")
    terms = [grad.reshape((2,) * bits + (grad.shape[0] // n_blk, grad.shape[1]))]
    left = list(reversed(range(bits)))
    for bit in order:
        axis = left.index(bit)
        mine = (me >> bit) & 1
        pick = lambda t, which: lax.dynamic_index_in_dim(t, which, axis, keepdims=False)
        send = total_of([pick(t, 1 - mine) for t in terms]).astype(jnp.bfloat16)
        kept = total_of([pick(t, mine) for t in terms]).astype(jnp.bfloat16)
        terms = [kept, swap(send, "blk", bit, n_blk)]
        left.remove(bit)
    for bit in range(bits_of(n_dp)):
        own = total_of(terms).astype(jnp.bfloat16)
        terms = [own, swap(own, "dp", bit, n_dp)]
    return total_of(terms)


def per_device(
    decoder_rows,
    encoder_rows,
    target_lengths,
    target_question,
    passage_question,
    self_gain,
    self_query,
    self_key,
    self_value,
    self_output,
    position_bias_matrix,
    cross_gain,
    cross_query,
    cross_key,
    cross_value,
    cross_output,
    feed_gain,
    feed_input_weight,
    feed_out,
    cotangent,
    n_dp,
    n_blk,
):
    passage = encoder_rows.shape[0]
    orders = [list(range(bits_of(n_blk)))] * 10
    me = lax.axis_index("blk")
    encoder_all = gather_rows(encoder_rows, n_blk)
    slot_device = me ^ jnp.arange(n_blk, dtype=jnp.int32)
    slot_pick = slot_device[:, None] == jnp.arange(n_blk, dtype=jnp.int32)[None, :]
    slot_question = jnp.sum(jnp.where(slot_pick, passage_question[None, :], 0), axis=1)
    order = passage_order(slot_question)
    items = cross_items(target_lengths[0], target_question[0])
    positions = jnp.arange(LEN, dtype=jnp.int32)
    seg_ends = jnp.cumsum(target_lengths[0])
    segment = jnp.sum((positions[:, None] >= seg_ends[None, : TARGETS - 1]).astype(jnp.int32), axis=-1)
    aq, ak, av = segment_aug(segment)
    table_pairs = position_bias_matrix.T.reshape(PAIRS, 2, BUCKETS)
    self_gain2, cross_gain2, feed_gain2 = self_gain[None], cross_gain[None], feed_gain[None]

    inputs = decoder_rows.astype(jnp.float32)
    inv_self = norm_parts(inputs)
    act_self = (inputs * inv_self * self_gain2).astype(jnp.bfloat16)
    query_self = dot_nn(act_self, self_query).astype(jnp.bfloat16)
    key_self = dot_nn(act_self, self_key).astype(jnp.bfloat16)
    value_self = dot_nn(act_self, self_value).astype(jnp.bfloat16)
    attn_self, aug_self = self_forward(query_self, key_self, value_self, aq, ak, table_pairs)
    resid_self = inputs + dot_nn(attn_self, self_output)
    inv_cross = norm_parts(resid_self)
    act_cross = (resid_self * inv_cross * cross_gain2).astype(jnp.bfloat16)
    query_cross = dot_nn(act_cross, cross_query).astype(jnp.bfloat16)
    pair_weight = jnp.concatenate([cross_key, cross_value], axis=1)
    pair_all = dot_nn(encoder_all, pair_weight).astype(jnp.bfloat16)
    attn_cross, aug_cross = cross_forward(order, items, query_cross, pair_all, passage)

    block_out, grad_feed_in, grad_feed_out, grad_resid_cross, grad_attn_cross, grad_cross_output, gain_feed = feed_block(
        resid_self, attn_cross, cross_output, feed_gain2, cotangent, feed_input_weight, feed_out
    )
    sum_feed_out = scatter_sum(grad_feed_out, n_blk, n_dp, orders[9])
    sum_feed_in = scatter_sum(grad_feed_in, n_blk, n_dp, orders[8])
    sum_cross_output = scatter_sum(grad_cross_output, n_blk, n_dp, orders[7])

    dqc, dkv = cross_backward(
        order, items, query_cross, pair_all, grad_attn_cross, attn_cross, aug_cross, passage
    )
    grad_pair = dot_tn(encoder_all, dkv).astype(jnp.bfloat16)
    sum_cross_key = scatter_sum(grad_pair[:, :D], n_blk, n_dp, orders[5])
    sum_cross_value = scatter_sum(grad_pair[:, D:], n_blk, n_dp, orders[6])
    encoder_part = dot_nt(dkv, pair_weight).astype(jnp.bfloat16)
    grad_encoder = scatter_slots(encoder_part.reshape(n_blk, passage, D), n_blk)
    sum_cross_query = scatter_sum(dot_tn(act_cross, dqc).astype(jnp.bfloat16), n_blk, n_dp, orders[4])

    da_cross = dot_nt(dqc, cross_query)
    gain_cross = jnp.sum(da_cross * resid_self * inv_cross, axis=0)
    grad_resid_self = grad_resid_cross + norm_back(resid_self, inv_cross, cross_gain2, da_cross)
    round_self = grad_resid_self.astype(jnp.bfloat16)
    sum_self_output = scatter_sum(dot_tn(attn_self, round_self).astype(jnp.bfloat16), n_blk, n_dp, orders[3])
    grad_attn_self = dot_nt(round_self, self_output).astype(jnp.bfloat16)
    dq, dk, dv, table_parts = self_backward(
        query_self, key_self, value_self, grad_attn_self, attn_self, aug_self, ak, av, table_pairs
    )
    sum_self_query = scatter_sum(dot_tn(act_self, dq).astype(jnp.bfloat16), n_blk, n_dp, orders[0])
    sum_self_key = scatter_sum(dot_tn(act_self, dk).astype(jnp.bfloat16), n_blk, n_dp, orders[1])
    sum_self_value = scatter_sum(dot_tn(act_self, dv).astype(jnp.bfloat16), n_blk, n_dp, orders[2])
    da_self = dot_nt(dq, self_query) + dot_nt(dk, self_key) + dot_nt(dv, self_value)
    gain_self = jnp.sum(da_self * inputs * inv_self, axis=0)
    grad_decoder = grad_resid_self + norm_back(inputs, inv_self, self_gain2, da_self)
    grad_table = table_parts.reshape(H, BUCKETS).T
    gain_self, gain_cross, gain_feed, table_sum = lax.psum(
        (gain_self, gain_cross, gain_feed[0], grad_table), ("dp", "blk")
    )
    return (
        block_out,
        grad_decoder,
        grad_encoder,
        gain_self,
        sum_self_query,
        sum_self_key,
        sum_self_value,
        sum_self_output,
        table_sum,
        gain_cross,
        sum_cross_query,
        sum_cross_key,
        sum_cross_value,
        sum_cross_output,
        gain_feed,
        sum_feed_in,
        sum_feed_out,
    )


def solution(mesh):
    split, copied, owned = P(("dp", "blk"), None), P(), P("blk", None)
    return jax.shard_map(
        partial(per_device, n_dp=mesh.shape["dp"], n_blk=mesh.shape["blk"]),
        mesh=mesh,
        in_specs=(split,) * 4 + (P("dp"),) + (copied,) * 14 + (split,),
        out_specs=(split,) * 3 + (copied,) + (owned,) * 4 + (copied,) * 2 + (owned,) * 4 + (copied,) + (owned,) * 2,
        check_vma=False,
    )
```

```python
import functools
from functools import partial

import jax
import jax.numpy as jnp
from jax import lax
from jax.experimental import pallas as pl
from jax.experimental.pallas import tpu as pltpu
from jax.sharding import PartitionSpec as P

D = 768
H = 12
HD = 64
BUCKETS = 32
LEN = 1024
TARGETS = 4
PAIRS = H // 2
LANES = 2 * HD
TILE = 256
SCALE = HD ** -0.5
NEG = -1e30
VMEM_LIMIT = 60 * 1024 * 1024

eps_norm = 1e-06
bucket_edges = (19, 21, 24, 27, 31, 35, 40, 46, 52, 59, 67, 77, 87, 99, 113)


def dot_nn(a, b):
    return jnp.dot(a, b, preferred_element_type=jnp.float32)


def dot_nt(a, b):
    return lax.dot_general(a, b, (((1,), (1,)), ((), ())), preferred_element_type=jnp.float32)


def dot_tn(a, b):
    return lax.dot_general(a, b, (((0,), (0,)), ((), ())), preferred_element_type=jnp.float32)


def lane_ids(rows):
    return lax.broadcasted_iota(jnp.int32, (rows, LANES), 1)


def in_half(rows, head):
    lane = lane_ids(rows)
    return lane < HD if head == 0 else lane >= HD


def split3(value):
    high = value.astype(jnp.bfloat16).astype(jnp.float32)
    rest = value - high
    mid = rest.astype(jnp.bfloat16).astype(jnp.float32)
    return high, mid, rest - mid


def triple_lanes(first, second, rows):
    lane = lane_ids(rows)
    out = jnp.zeros((rows, LANES), jnp.float32)
    for base, value in ((HD, first), (0, second)):
        for place, part in enumerate(split3(value)):
            out = jnp.where(lane == base + place, part, out)
    return out


def bucket_vector(table_t, offsets):
    upper = jnp.full(offsets.shape, 16, jnp.int32)
    for edge in bucket_edges:
        upper = upper + (offsets >= edge).astype(jnp.int32)
    bucket = jnp.where(offsets < 16, offsets, upper)
    rows = lax.broadcasted_iota(jnp.int32, (BUCKETS, offsets.shape[1]), 0)
    chosen = (rows == bucket).astype(jnp.float32).astype(jnp.bfloat16)
    return chosen


WIN = 3 * TILE


def self_forward_kernel(q_ref, k_ref, v_ref, aq_ref, ak_ref, table_ref, o_ref, aug_ref, bias_ref):
    lane768 = lax.broadcasted_iota(jnp.int32, (1, WIN), 1)
    offsets = 2 * TILE - lane768
    chosen = bucket_vector(None, jnp.maximum(offsets, 0))
    line = dot_nn(table_ref[0], chosen)
    line = jnp.where(offsets >= 0, line, NEG)
    far = table_ref[0][:, BUCKETS - 1 :].astype(jnp.float32)
    for head in range(2):
        spread = jnp.broadcast_to(line[head : head + 1], (TILE, WIN))
        bias_ref[head] = pltpu.roll(spread, 0, 1, stride=1, stride_axis=0)[:, TILE:]
    aq, ak = aq_ref[...], ak_ref[...]
    outs = {}
    logs = {}
    for head in range(2):
        half = in_half(LEN, head)
        q = jnp.where(half, q_ref[...] * jnp.bfloat16(SCALE), aq)
        k = jnp.where(half, k_ref[...], ak)
        v = jnp.where(half, v_ref[...], jnp.zeros((), jnp.bfloat16))
        for i in range(LEN // TILE):
            lo = max(0, i - 2) * TILE
            hi = (i + 1) * TILE
            scores = dot_nt(q[i * TILE : hi], k[lo:hi])
            near = min(2 * TILE, hi - lo)
            parts = []
            if hi - lo > near:
                parts.append(scores[:, : hi - lo - near] + far[head : head + 1])
            parts.append(scores[:, hi - lo - near :] + bias_ref[head][:, 2 * TILE - near :])
            scores = parts[0] if len(parts) == 1 else jnp.concatenate(parts, axis=1)
            top = jnp.max(scores, axis=1, keepdims=True)
            expo = jnp.exp(scores - top)
            total = jnp.sum(expo, axis=1, keepdims=True)
            mixed = dot_nn(expo.astype(jnp.bfloat16), v[lo:hi]) / total
            logs[i, head] = top + jnp.log(total)
            outs[i, head] = mixed
            if head == 1:
                o_ref[i * TILE : hi] = (outs[i, 0] + outs[i, 1]).astype(jnp.bfloat16)
                aug = triple_lanes(logs[i, 0], logs[i, 1], TILE)
                lane = lane_ids(TILE)
                place = lane & (HD - 1)
                aug_ref[i * TILE : hi] = jnp.where(
                    place < 3, aug, aq_ref[i * TILE : hi].astype(jnp.float32)
                ).astype(jnp.bfloat16)


def pair_spec(offset=0):
    return pl.BlockSpec((LEN, LANES), lambda p: (0, p + offset))


def whole(shape):
    return pl.BlockSpec(shape, lambda p: (0,) * len(shape))


def self_forward(q, k, v, aq, ak, table_pairs):
    return pl.pallas_call(
        self_forward_kernel,
        grid=(PAIRS,),
        in_specs=[pair_spec()] * 3 + [whole((LEN, LANES))] * 2
        + [pl.BlockSpec((1, 2, BUCKETS), lambda p: (p, 0, 0))],
        out_specs=[pair_spec(), pair_spec()],
        out_shape=[jax.ShapeDtypeStruct((LEN, D), jnp.bfloat16)] * 2,
        scratch_shapes=[pltpu.VMEM((2, TILE, 2 * TILE), jnp.float32)],
        compiler_params=pltpu.CompilerParams(vmem_limit_bytes=VMEM_LIMIT),
        cost_estimate=pl.CostEstimate(flops=4 * H * LEN * LEN * HD, bytes_accessed=10 * LEN * D, transcendentals=0),
    )(q, k, v, aq, ak, table_pairs)


def self_backward_kernel(q_ref, k_ref, v_ref, do_ref, o_ref, aug_ref, ak_ref, av_ref, table_ref,
                         dq_ref, dk_ref, dv_ref, gt_ref, bias_ref, g_ref, gfar_ref, dqt_ref):
    lane768 = lax.broadcasted_iota(jnp.int32, (1, WIN), 1)
    offsets = lane768 - TILE
    chosen = bucket_vector(None, jnp.maximum(offsets, 0))
    line = dot_nn(table_ref[0], chosen)
    line = jnp.where(offsets >= 0, line, NEG)
    far = table_ref[0][:, BUCKETS - 1 :].astype(jnp.float32)
    for head in range(2):
        spread = jnp.broadcast_to(line[head : head + 1], (TILE, WIN))
        bias_ref[head] = pltpu.roll(spread, 0, 1, stride=1, stride_axis=0)[:, TILE:]
    g_ref[...] = jnp.zeros_like(g_ref)
    gfar_ref[...] = jnp.zeros_like(gfar_ref)
    dqt_ref[...] = jnp.zeros_like(dqt_ref)
    product = do_ref[...].astype(jnp.float32) * o_ref[...].astype(jnp.float32)
    deltas = []
    for head in range(2):
        half = in_half(LEN, head)
        deltas.append(jnp.sum(jnp.where(half, product, 0.0), axis=1, keepdims=True))
    aug_do = (-triple_lanes(deltas[0], deltas[1], LEN)).astype(jnp.bfloat16)
    q_scaled = q_ref[...] * jnp.bfloat16(SCALE)
    k_t = k_ref[...].T
    accs = {}
    for head in range(2):
        half = in_half(LEN, head)
        q = jnp.where(half, q_scaled, aug_ref[...])
        k = jnp.where(half, k_ref[...], ak_ref[...])
        v = jnp.where(half, v_ref[...], av_ref[...])
        do = jnp.where(half, do_ref[...], aug_do)
        for j in range(LEN // TILE):
            lo = j * TILE
            hi = min(LEN, (j + 3) * TILE)
            width = hi - lo
            near = min(2 * TILE, width)
            scores = dot_nt(k[lo : lo + TILE], q[lo:hi])
            parts = [scores[:, :near] + bias_ref[head][:, :near]]
            if width > near:
                parts.append(scores[:, near:] + far[head : head + 1])
            scores = parts[0] if len(parts) == 1 else jnp.concatenate(parts, axis=1)
            probs = jnp.exp(scores)
            grad_probs = dot_nt(v[lo : lo + TILE], do[lo:hi])
            grad_scores = probs * grad_probs
            g_ref[head, :, :near] += grad_scores[:, :near]
            if width > near:
                gfar_ref[head] += grad_scores[:, near:]
            ds = grad_scores.astype(jnp.bfloat16)
            accs[j, head] = (dot_nn(ds, q[lo:hi]), dot_nn(probs.astype(jnp.bfloat16), do[lo:hi]))
            dqt_ref[head * HD : (head + 1) * HD, lo:hi] += dot_nn(
                k_t[head * HD : (head + 1) * HD, lo : lo + TILE], ds
            )
            if head == 1:
                lower = in_half(TILE, 0)
                dk_ref[lo : lo + TILE] = jnp.where(lower, accs[j, 0][0], accs[j, 1][0]).astype(jnp.bfloat16)
                dv_ref[lo : lo + TILE] = jnp.where(lower, accs[j, 0][1], accs[j, 1][1]).astype(jnp.bfloat16)
    dq_ref[...] = (dqt_ref[...] * SCALE).T.astype(jnp.bfloat16)
    rows = []
    for head in range(2):
        total = jnp.zeros((8, WIN), jnp.float32)
        pad = jnp.zeros((8, TILE), jnp.float32)
        for a in range(TILE // 8):
            strip = jnp.concatenate([pad, g_ref[head, 8 * a : 8 * a + 8, :]], axis=1)
            if a:
                strip = pltpu.roll(strip, WIN - 8 * a, 1)
            total = total + strip
        line_sum = jnp.zeros((1, WIN), jnp.float32)
        for s in range(8):
            one = total[s : s + 1]
            line_sum = line_sum + (pltpu.roll(one, WIN - s, 1) if s else one)
        rows.append(line_sum)
    lines = jnp.concatenate(rows, axis=0)
    lines = jnp.where(offsets >= 0, lines, 0.0)
    high, mid, low = split3(lines)
    sums = sum(dot_nt(part.astype(jnp.bfloat16), chosen) for part in (high, mid, low))
    for head in range(2):
        far_sum = jnp.sum(gfar_ref[head])
        lane32 = lax.broadcasted_iota(jnp.int32, (1, BUCKETS), 1)
        gt_ref[0, head : head + 1, :] = sums[head : head + 1] + jnp.where(lane32 == BUCKETS - 1, far_sum, 0.0)


def self_backward(q, k, v, do, o, aug, ak, av, table_pairs):
    return pl.pallas_call(
        self_backward_kernel,
        grid=(PAIRS,),
        in_specs=[pair_spec()] * 6 + [whole((LEN, LANES))] * 2
        + [pl.BlockSpec((1, 2, BUCKETS), lambda p: (p, 0, 0))],
        out_specs=[pair_spec()] * 3 + [pl.BlockSpec((1, 2, BUCKETS), lambda p: (p, 0, 0))],
        out_shape=[jax.ShapeDtypeStruct((LEN, D), jnp.bfloat16)] * 3
        + [jax.ShapeDtypeStruct((PAIRS, 2, BUCKETS), jnp.float32)],
        scratch_shapes=[
            pltpu.VMEM((2, TILE, 2 * TILE), jnp.float32),
            pltpu.VMEM((2, TILE, 2 * TILE), jnp.float32),
            pltpu.VMEM((2, TILE, TILE), jnp.float32),
            pltpu.VMEM((LANES, LEN), jnp.float32),
        ],
        compiler_params=pltpu.CompilerParams(vmem_limit_bytes=VMEM_LIMIT),
        cost_estimate=pl.CostEstimate(flops=10 * H * LEN * LEN * HD, bytes_accessed=18 * LEN * D, transcendentals=0),
    )(q, k, v, do, o, aug, ak, av, table_pairs)


CT = 256


def cross_forward_kernel(order_ref, item_ref, q_ref, kv_ref, o_ref, aug_ref, ks_ref, vs_ref, passage):
    slots = order_ref.shape[0]
    per_q = slots // TARGETS
    keys_q = per_q * passage
    lower = lax.broadcasted_iota(jnp.int32, (passage, D), 1) % LANES < HD
    zero = jnp.zeros((), jnp.bfloat16)

    @pl.loop(0, slots)
    def _(s):
        src = pl.multiple_of(order_ref[s] * passage, passage)
        dst = pl.multiple_of(s * passage, passage)
        keys = kv_ref[pl.ds(src, passage), :D]
        values = kv_ref[pl.ds(src, passage), D:]
        ks_ref[0, pl.ds(dst, passage)] = jnp.where(lower, keys, zero)
        ks_ref[1, pl.ds(dst, passage)] = jnp.where(lower, zero, keys)
        vs_ref[0, pl.ds(dst, passage)] = jnp.where(lower, values, zero)
        vs_ref[1, pl.ds(dst, passage)] = jnp.where(lower, zero, values)

    o_ref[...] = jnp.zeros_like(o_ref)
    aug_ref[...] = jnp.zeros_like(aug_ref)

    @pl.loop(0, item_ref[4, 0])
    def _(n):
        row0 = pl.multiple_of(item_ref[0, n] * CT, CT)
        key0 = pl.multiple_of(item_ref[1, n] * keys_q, keys_q)
        rows = lax.broadcasted_iota(jnp.int32, (CT, 1), 0)
        valid = (rows >= item_ref[2, n]) & (rows < item_ref[3, n])
        for pair in range(PAIRS):
            cols = slice(pair * LANES, (pair + 1) * LANES)
            q = q_ref[pl.ds(row0, CT), cols] * jnp.bfloat16(SCALE)
            outs, logs = [], []
            for head in range(2):
                scores = dot_nt(q, ks_ref[head, pl.ds(key0, keys_q), cols])
                top = jnp.max(scores, axis=1, keepdims=True)
                expo = jnp.exp(scores - top)
                total = jnp.sum(expo, axis=1, keepdims=True)
                outs.append(dot_nn(expo.astype(jnp.bfloat16), vs_ref[head, pl.ds(key0, keys_q), cols]) / total)
                logs.append(top + jnp.log(total))
            mixed = (outs[0] + outs[1]).astype(jnp.bfloat16)
            aug = triple_lanes(logs[0], logs[1], CT).astype(jnp.bfloat16)
            o_ref[pl.ds(row0, CT), cols] = jnp.where(valid, mixed, o_ref[pl.ds(row0, CT), cols])
            aug_ref[pl.ds(row0, CT), cols] = jnp.where(valid, aug, aug_ref[pl.ds(row0, CT), cols])


def smem_spec():
    return pl.BlockSpec(memory_space=pltpu.SMEM)


def vmem_spec():
    return pl.BlockSpec(memory_space=pltpu.VMEM)


def cross_forward(order, items, q, kv, passage):
    keys = kv.shape[0]
    return pl.pallas_call(
        partial(cross_forward_kernel, passage=passage),
        in_specs=[smem_spec(), smem_spec(), vmem_spec(), vmem_spec()],
        out_specs=[vmem_spec(), vmem_spec()],
        out_shape=[jax.ShapeDtypeStruct((LEN, D), jnp.bfloat16)] * 2,
        scratch_shapes=[pltpu.VMEM((2, keys, D), jnp.bfloat16)] * 2,
        compiler_params=pltpu.CompilerParams(vmem_limit_bytes=VMEM_LIMIT),
        cost_estimate=pl.CostEstimate(flops=2 * H * LEN * LEN * HD, bytes_accessed=10 * LEN * D, transcendentals=0),
    )(order, items, q, kv)


def cross_backward_kernel(order_ref, item_ref, q_ref, kv_ref, do_ref, o_ref, aug_ref,
                          dq_ref, dkv_ref, ks_ref, vs_ref, kt_ref, dk_ref, dv_ref, dqt_ref, passage):
    slots = order_ref.shape[0]
    per_q = slots // TARGETS
    keys_q = per_q * passage
    lane = lax.broadcasted_iota(jnp.int32, (passage, D), 1) % LANES
    lower = lane < HD
    ones = jnp.where((lane & (HD - 1)) < 3, 1.0, 0.0).astype(jnp.bfloat16)
    minus = -ones

    @pl.loop(0, slots)
    def _(s):
        src = pl.multiple_of(order_ref[s] * passage, passage)
        dst = pl.multiple_of(s * passage, passage)
        keys = kv_ref[pl.ds(src, passage), :D]
        values = kv_ref[pl.ds(src, passage), D:]
        ks_ref[0, pl.ds(dst, passage)] = jnp.where(lower, keys, minus)
        ks_ref[1, pl.ds(dst, passage)] = jnp.where(lower, minus, keys)
        vs_ref[0, pl.ds(dst, passage)] = jnp.where(lower, values, ones)
        vs_ref[1, pl.ds(dst, passage)] = jnp.where(lower, ones, values)

    lower_k = lax.broadcasted_iota(jnp.int32, (keys_q, LANES), 1) < HD
    for s in range(TARGETS):
        for pair in range(PAIRS):
            rows = slice(s * keys_q, (s + 1) * keys_q)
            cols = slice(pair * LANES, (pair + 1) * LANES)
            both = jnp.where(lower_k, ks_ref[0, rows, cols], ks_ref[1, rows, cols])
            kt_ref[cols, rows] = both.T
    dk_ref[...] = jnp.zeros_like(dk_ref)
    dv_ref[...] = jnp.zeros_like(dv_ref)
    dqt_ref[...] = jnp.zeros_like(dqt_ref)

    @pl.loop(0, item_ref[4, 0])
    def _(n):
        row0 = pl.multiple_of(item_ref[0, n] * CT, CT)
        key0 = pl.multiple_of(item_ref[1, n] * keys_q, keys_q)
        rows = lax.broadcasted_iota(jnp.int32, (CT, 1), 0)
        valid = (rows >= item_ref[2, n]) & (rows < item_ref[3, n])
        here = pl.ds(row0, CT)
        there = pl.ds(key0, keys_q)
        for pair in range(PAIRS):
            cols = slice(pair * LANES, (pair + 1) * LANES)
            q_scaled = q_ref[here, cols] * jnp.bfloat16(SCALE)
            do_pair = jnp.where(valid, do_ref[here, cols], jnp.zeros((), jnp.bfloat16))
            product = do_pair.astype(jnp.float32) * o_ref[here, cols].astype(jnp.float32)
            deltas = []
            for head in range(2):
                deltas.append(jnp.sum(jnp.where(in_half(CT, head), product, 0.0), axis=1, keepdims=True))
            aug_do = (-triple_lanes(deltas[0], deltas[1], CT)).astype(jnp.bfloat16)
            aug = jnp.where(valid, aug_ref[here, cols], jnp.bfloat16(1e30))
            parts = []
            for head in range(2):
                half = in_half(CT, head)
                q = jnp.where(half, q_scaled, aug)
                do = jnp.where(half, do_pair, aug_do)
                probs = jnp.exp(dot_nt(ks_ref[head, there, cols], q))
                grad_scores = probs * dot_nt(vs_ref[head, there, cols], do)
                ds = grad_scores.astype(jnp.bfloat16)
                parts.append((dot_nn(ds, q), dot_nn(probs.astype(jnp.bfloat16), do)))
                hrow = pair * LANES + head * HD
                dqt_ref[hrow : hrow + HD, here] += dot_nn(kt_ref[hrow : hrow + HD, there], ds)
            dk_ref[there, cols] += jnp.where(lower_k, parts[0][0], parts[1][0])
            dv_ref[there, cols] += jnp.where(lower_k, parts[0][1], parts[1][1])

    for pair in range(PAIRS):
        cols = slice(pair * LANES, (pair + 1) * LANES)
        dq_ref[:, cols] = (dqt_ref[cols, :] * SCALE).T.astype(jnp.bfloat16)

    @pl.loop(0, slots)
    def _(s):
        src = pl.multiple_of(s * passage, passage)
        dst = pl.multiple_of(order_ref[s] * passage, passage)
        dkv_ref[pl.ds(dst, passage), :D] = dk_ref[pl.ds(src, passage)].astype(jnp.bfloat16)
        dkv_ref[pl.ds(dst, passage), D:] = dv_ref[pl.ds(src, passage)].astype(jnp.bfloat16)


def cross_backward(order, items, q, kv, do, o, aug, passage):
    keys = kv.shape[0]
    return pl.pallas_call(
        partial(cross_backward_kernel, passage=passage),
        in_specs=[smem_spec(), smem_spec()] + [vmem_spec()] * 5,
        out_specs=[vmem_spec(), vmem_spec()],
        out_shape=[
            jax.ShapeDtypeStruct((LEN, D), jnp.bfloat16),
            jax.ShapeDtypeStruct((keys, 2 * D), jnp.bfloat16),
        ],
        scratch_shapes=[pltpu.VMEM((2, keys, D), jnp.bfloat16)] * 2
        + [
            pltpu.VMEM((D, keys), jnp.bfloat16),
            pltpu.VMEM((keys, D), jnp.float32),
            pltpu.VMEM((keys, D), jnp.float32),
            pltpu.VMEM((D, LEN), jnp.float32),
        ],
        compiler_params=pltpu.CompilerParams(vmem_limit_bytes=VMEM_LIMIT),
        cost_estimate=pl.CostEstimate(flops=5 * H * LEN * LEN * HD, bytes_accessed=18 * LEN * D, transcendentals=0),
    )(order, items, q, kv, do, o, aug)


def cross_items(lengths, questions):
    ends = jnp.cumsum(lengths)
    starts = ends - lengths
    tiles = LEN // CT
    slots = tiles + TARGETS - 1
    first = starts // CT
    last = (ends - 1) // CT
    count = last - first + 1
    done = jnp.cumsum(count)
    number = jnp.arange(slots, dtype=jnp.int32)
    seg = jnp.sum((number[:, None] >= done[None, :]).astype(jnp.int32), axis=1)
    pick = (jnp.minimum(seg, TARGETS - 1)[:, None] == jnp.arange(TARGETS, dtype=jnp.int32)[None, :]).astype(jnp.int32)
    take = lambda a: jnp.sum(pick * a[None, :], axis=1)
    tile = jnp.clip(take(first) + number - take(done - count), 0, tiles - 1)
    lo = jnp.clip(take(starts) - tile * CT, 0, CT)
    hi = jnp.clip(take(ends) - tile * CT, 0, CT)
    total = jnp.broadcast_to(jnp.sum(count), (slots,))
    return jnp.stack([tile, take(questions), lo, hi, total]).astype(jnp.int32)


def passage_order(passage_question):
    count = passage_question.shape[0]
    ids = jnp.arange(count, dtype=jnp.int32)
    before = (passage_question[None, :] < passage_question[:, None]) | (
        (passage_question[None, :] == passage_question[:, None]) & (ids[None, :] < ids[:, None])
    )
    rank = jnp.sum(before.astype(jnp.int32), axis=1)
    return jnp.sum(jnp.where(rank[:, None] == ids[None, :], ids[:, None], 0), axis=0).astype(jnp.int32)


def segment_aug(segment):
    place = jnp.arange(LANES, dtype=jnp.int32)[None, :] & (HD - 1)
    seg = segment[:, None]
    mark = (place >= 3) & (place < 3 + TARGETS)
    same = place - 3 == seg
    aq = jnp.where(mark & same, 1.0, 0.0).astype(jnp.bfloat16)
    ak = jnp.where(place < 3, -1.0, jnp.where(mark & ~same, NEG, 0.0)).astype(jnp.bfloat16)
    av = jnp.broadcast_to(jnp.where(place < 3, 1.0, 0.0), (LEN, LANES)).astype(jnp.bfloat16)
    return aq, ak, av


ROWS = 256


def norm_parts(values):
    return lax.rsqrt(jnp.mean(values * values, axis=1, keepdims=True) + eps_norm)


def norm_back(values, inverse, gain, grad):
    scaled = grad * gain
    inner = jnp.mean(scaled * values, axis=1, keepdims=True)
    return inverse * scaled - values * (inverse * inverse * inverse * inner)


def bits_of(count):
    return count.bit_length() - 1


def place_bits(n_blk, n_dp, kind):
    blk = [("blk", bit) for bit in range(bits_of(n_blk))]
    dp = [("dp", bit) for bit in range(bits_of(n_dp))]
    if kind == "x":
        return blk[:1] + dp + blk[1:]
    if kind == "z":
        return blk[:1] + blk[2:] + blk[1:2]
    return blk


def position(owner, piece, order):
    slot = 0
    for axis, bit in order:
        mine = (lax.axis_index(axis) // (1 << bit)) % 2
        static = ((owner if axis == "blk" else piece) >> bit) & 1
        slot = 2 * slot + (1 - mine if static else mine)
    return slot


def partner(axis, bit):
    me = lax.axis_index(axis)
    mine = (me // (1 << bit)) % 2
    return {axis: me + (1 - 2 * mine) * (1 << bit)}


class Exchange:
    def __init__(self, count, n_blk, n_dp, kind):
        if kind == "x" and count % n_dp:
            kind = "y"
        self.n_blk, self.n_dp, self.count, self.kind = n_blk, n_dp, count, kind
        self.order = place_bits(n_blk, n_dp, kind)
        self.pieces = n_dp if kind == "x" else 1
        self.slots = n_blk * self.pieces
        self.mats = count // self.pieces
        self.last = [("dp", bit) for bit in range(bits_of(n_dp))]
        self.steps = len(self.order) + len(self.last)
        self.rows = D // n_blk
        self.offsets = []
        at = 0
        for k in range(len(self.order)):
            size = self.slots >> (k + 1)
            self.offsets.append((at, size))
            at += size
        for j in range(len(self.last)):
            size = (1 << j) if kind == "x" else 1
            self.offsets.append((at, size))
            at += size
        self.received = at

    def scratch(self):
        shape = (self.mats, self.rows, D)
        return [
            pltpu.VMEM((self.slots,) + shape, jnp.bfloat16),
            pltpu.VMEM((self.received,) + shape, jnp.bfloat16),
            pltpu.SemaphoreType.DMA((self.steps,)),
            pltpu.SemaphoreType.DMA((self.steps,)),
        ]

    def bind(self, refs, out_ref):
        self.buf, self.recv, self.send_sem, self.recv_sem = refs
        self.out = out_ref

    def put(self, index, value):
        piece, inner = index // self.mats, index % self.mats
        for owner in range(self.n_blk):
            slot = position(owner, piece, self.order)
            self.buf[slot, inner] = value[owner * self.rows : (owner + 1) * self.rows].astype(jnp.bfloat16)

    def copy(self, k):
        at, size = self.offsets[k]
        if k < len(self.order):
            axis, bit = self.order[k]
            src = self.buf.at[pl.ds(size, size)]
        else:
            axis, bit = self.last[k - len(self.order)]
            src = self.buf.at[pl.ds(0, size)]
        return pltpu.make_async_remote_copy(
            src_ref=src,
            dst_ref=self.recv.at[pl.ds(at, size)],
            send_sem=self.send_sem.at[k],
            recv_sem=self.recv_sem.at[k],
            device_id=partner(axis, bit),
            device_id_type=pl.DeviceIdType.MESH,
        )

    def start(self, k):
        self.copy(k).start()

    def finish(self, k):
        self.copy(k).wait()
        at, size = self.offsets[k]
        final = k == self.steps - 1
        if k < len(self.order) or self.kind != "x":
            for s in range(size):
                for m in range(self.mats):
                    total = self.buf[s, m].astype(jnp.float32) + self.recv[at + s, m].astype(jnp.float32)
                    if final:
                        self.out[m] = total
                    else:
                        self.buf[s, m] = total.astype(jnp.bfloat16)
            return
        for s in range(size):
            for m in range(self.mats):
                self.buf[size + s, m] = self.recv[at + s, m]
        if final:
            for s in range(self.pieces):
                spot = position(0, s, self.last[::-1])
                for m in range(self.mats):
                    self.out[spot * self.mats + m] = self.buf[s, m].astype(jnp.float32)

    def advance(self, k):
        self.finish(k)
        if k + 1 < self.steps:
            self.start(k + 1)


def enter_barrier(n_blk, n_dp):
    barrier = pltpu.get_barrier_semaphore()
    links = [("blk", bit) for bit in range(bits_of(n_blk))] + [("dp", bit) for bit in range(bits_of(n_dp))]
    for axis, bit in links:
        pl.semaphore_signal(barrier, inc=1, device_id=partner(axis, bit), device_id_type=pl.DeviceIdType.MESH)
    pl.semaphore_wait(barrier, len(links))


def tail_kernel(n_blk, n_dp, plans, *refs):
    (x_ref, gain_ref, dy1_ref, act_ref, dq_ref, dk_ref, dv_ref, wq_ref, wk_ref, wv_ref,
     actc_ref, dqc_ref, enc_ref, dkv_ref, o_ref, oc_ref, e2_ref, small_ref) = refs[:18]
    outs = refs[18 : 18 + len(plans)]
    dx_ref, sums_ref = refs[18 + len(plans) : 20 + len(plans)]
    scratch = refs[20 + len(plans) :]
    for i, plan in enumerate(plans):
        plan.bind(scratch[4 * i : 4 * i + 4], outs[i])
    tot_ref, got_ref, tsend, trecv = scratch[4 * len(plans) :]
    enter_barrier(n_blk, n_dp)
    crossx, crossy, selfx, selfy = plans

    crossx.put(0, dot_tn(actc_ref[...], dqc_ref[...]))
    crossx.put(1, dot_tn(enc_ref[...], dkv_ref[:, :D]))
    crossx.start(0)
    crossy.put(0, dot_tn(enc_ref[...], dkv_ref[:, D:]))
    crossy.put(1, dot_tn(oc_ref[...], e2_ref[...]))
    crossy.put(2, dot_tn(o_ref[...], dy1_ref[...].astype(jnp.bfloat16)))
    crossy.start(0)
    crossx.advance(0)
    selfx.put(0, dot_tn(act_ref[...], dq_ref[...]))
    selfx.put(1, dot_tn(act_ref[...], dk_ref[...]))
    selfx.start(0)
    crossy.advance(0)
    selfy.put(0, dot_tn(act_ref[...], dv_ref[...]))
    selfy.start(0)
    selfx.advance(0)
    gain_sum = jnp.zeros((1, D), jnp.float32)
    for i, r in enumerate(range(0, LEN, ROWS)):
        rows = slice(r, r + ROWS)
        da = dot_nt(dq_ref[rows], wq_ref[...]) + dot_nt(dk_ref[rows], wk_ref[...]) + dot_nt(dv_ref[rows], wv_ref[...])
        x = x_ref[rows].astype(jnp.float32)
        inverse = norm_parts(x)
        gain_sum = gain_sum + jnp.sum(da * x * inverse, axis=0, keepdims=True)
        dx_ref[rows] = dy1_ref[rows] + norm_back(x, inverse, gain_ref[...], da)
        if i == 0:
            selfy.advance(0)
        if i == 1:
            crossx.advance(1)
        if i == 2:
            crossy.advance(1)
    tot_ref[...] = small_ref[...]
    tot_ref[0:1] = gain_sum
    links = [("blk", bit) for bit in range(bits_of(n_blk))] + [("dp", bit) for bit in range(bits_of(n_dp))]

    def small_copy(j):
        axis, bit = links[j]
        return pltpu.make_async_remote_copy(
            src_ref=tot_ref,
            dst_ref=got_ref.at[j],
            send_sem=tsend.at[j],
            recv_sem=trecv.at[j],
            device_id=partner(axis, bit),
            device_id_type=pl.DeviceIdType.MESH,
        )

    small_copy(0).start()
    longest = max(plan.steps for plan in plans)
    for k in range(1, longest):
        for plan in (selfx, selfy, crossx, crossy):
            step = k if plan in (selfx, selfy) else k + 1
            if step < plan.steps:
                plan.advance(step)
        if k - 1 < len(links):
            small_copy(k - 1).wait()
            tot_ref[...] = tot_ref[...] + got_ref[k - 1]
            if k < len(links):
                small_copy(k).start()
    for j in range(longest - 1, len(links)):
        small_copy(j).wait()
        tot_ref[...] = tot_ref[...] + got_ref[j]
        if j + 1 < len(links):
            small_copy(j + 1).start()
    sums_ref[...] = tot_ref[...]


def tail_block(n_blk, n_dp, *args):
    plans = [
        Exchange(2, n_blk, n_dp, "x"),
        Exchange(3, n_blk, n_dp, "y"),
        Exchange(2, n_blk, n_dp, "x"),
        Exchange(1, n_blk, n_dp, "y"),
    ]
    links = bits_of(n_blk) + bits_of(n_dp)
    scratch = [item for plan in plans for item in plan.scratch()]
    scratch += [
        pltpu.VMEM((8, D), jnp.float32),
        pltpu.VMEM((links, 8, D), jnp.float32),
        pltpu.SemaphoreType.DMA((links,)),
        pltpu.SemaphoreType.DMA((links,)),
    ]
    return pl.pallas_call(
        partial(tail_kernel, n_blk, n_dp, plans),
        in_specs=[vmem_spec()] * len(args),
        out_specs=[vmem_spec()] * (len(plans) + 2),
        out_shape=[jax.ShapeDtypeStruct((plan.count, plan.rows, D), jnp.float32) for plan in plans]
        + [jax.ShapeDtypeStruct((LEN, D), jnp.float32), jax.ShapeDtypeStruct((8, D), jnp.float32)],
        scratch_shapes=scratch,
        compiler_params=pltpu.CompilerParams(
            vmem_limit_bytes=VMEM_LIMIT, collective_id=1, has_side_effects=True
        ),
        cost_estimate=pl.CostEstimate(flops=22 * LEN * D * D, bytes_accessed=80 * LEN * D, transcendentals=0),
    )(*args)


FF_STEPS = 4


def normal_cdf_pair(u):
    x = jnp.abs(u) * 0.7071067811865476
    gauss = jnp.exp(-0.5 * u * u)
    t = 1.0 / (1.0 + 0.3275911 * x)
    poly = ((((1.061405429 * t - 1.453152027) * t + 1.421413741) * t - 0.284496736) * t + 0.254829592) * t
    tail = 0.5 * poly * gauss
    return jnp.where(u >= 0, 1.0 - tail, tail), gauss * 0.3989422804014327


def rest_slot(owner, piece, order):
    slot = 0
    for axis, bit in order[1:]:
        mine = (lax.axis_index(axis) // (1 << bit)) % 2
        its = ((owner if axis == "blk" else piece) // (1 << bit)) % 2
        slot = 2 * slot + (its + mine) % 2
    return slot


def feed_kernel(plan_in, plan_out, y1_ref, oc_ref, wco_ref, gain_ref, g_ref, w1_ref, w2_ref,
                out_ref, isend_ref, ikeep_ref, osend_ref, okeep_ref, dy2_ref, e2_ref, doc_ref, dgain_ref,
                y2_ref, act_ref, acc_ref, da_ref, hid_ref, du_ref):
    step = pl.program_id(0)
    even_core = lax.axis_index("blk") % 2 == 0

    @pl.when(step == 0)
    def _():
        for r in range(0, LEN, ROWS):
            rows = slice(r, r + ROWS)
            y2 = y1_ref[rows] + dot_nn(oc_ref[rows], wco_ref[...])
            y2_ref[rows] = y2
            act_ref[rows] = (y2 * norm_parts(y2) * gain_ref[...]).astype(jnp.bfloat16)
        acc_ref[...] = y2_ref[...]
        da_ref[...] = jnp.zeros_like(da_ref)

    for r in range(0, LEN, ROWS):
        rows = slice(r, r + ROWS)
        u = dot_nn(act_ref[rows], w1_ref[...])
        dh = dot_nt(g_ref[rows], w2_ref[...])
        cdf, density = normal_cdf_pair(u)
        hid = (u * cdf).astype(jnp.bfloat16)
        du = (dh * (cdf + u * density)).astype(jnp.bfloat16)
        hid_ref[rows] = hid
        du_ref[rows] = du
        acc_ref[rows] += dot_nn(hid, w2_ref[...])
        da_ref[rows] += dot_nt(du, w1_ref[...])

    dw2 = dot_tn(hid_ref[...], g_ref[...])
    own_rows = plan_out.rows * plan_out.count
    group = dw2.shape[0] // own_rows
    for t in range(0, group, 2):
        for m in range(plan_out.count):
            piece, inner = m // plan_out.mats, m % plan_out.mats
            even = dw2[t * own_rows + m * plan_out.rows : t * own_rows + (m + 1) * plan_out.rows]
            odd = dw2[(t + 1) * own_rows + m * plan_out.rows : (t + 1) * own_rows + (m + 1) * plan_out.rows]
            slot = rest_slot(step * group + t, piece, plan_out.order)
            osend_ref[slot, inner] = jnp.where(even_core, odd, even).astype(jnp.bfloat16)
            okeep_ref[slot, inner] = jnp.where(even_core, even, odd).astype(jnp.bfloat16)
    dw1 = dot_tn(act_ref[...], du_ref[...])
    for t in range(0, plan_in.n_blk, 2):
        even = dw1[t * plan_in.rows : (t + 1) * plan_in.rows]
        odd = dw1[(t + 1) * plan_in.rows : (t + 2) * plan_in.rows]
        slot = rest_slot(t, 0, plan_in.order)
        isend_ref[slot, 0] = jnp.where(even_core, odd, even).astype(jnp.bfloat16)
        ikeep_ref[slot, 0] = jnp.where(even_core, even, odd).astype(jnp.bfloat16)

    @pl.when(step == FF_STEPS - 1)
    def _():
        gain_sum = jnp.zeros((1, D), jnp.float32)
        for r in range(0, LEN, ROWS):
            rows = slice(r, r + ROWS)
            out_ref[rows] = acc_ref[rows].astype(jnp.bfloat16)
            y2 = y2_ref[rows]
            inverse = norm_parts(y2)
            da = da_ref[rows]
            gain_sum = gain_sum + jnp.sum(da * y2 * inverse, axis=0, keepdims=True)
            dy2 = g_ref[rows].astype(jnp.float32) + norm_back(y2, inverse, gain_ref[...], da)
            dy2_ref[rows] = dy2
            e2 = dy2.astype(jnp.bfloat16)
            e2_ref[rows] = e2
            doc_ref[rows] = dot_nt(e2, wco_ref[...]).astype(jnp.bfloat16)
        dgain_ref[...] = gain_sum


def feed_block(y1, oc, wco, gain, g, w1, w2, plan_in, plan_out):
    ff = w1.shape[1]
    cols = ff // FF_STEPS
    fixed = lambda shape: pl.BlockSpec(shape, lambda c: (0,) * len(shape))
    half_in = (plan_in.slots // 2, plan_in.mats, plan_in.rows, D)
    half_out = (plan_out.slots // 2, plan_out.mats, plan_out.rows, D)
    in_spec = pl.BlockSpec((half_in[0], 1) + half_in[2:], lambda c: (0, c, 0, 0))
    like = jax.ShapeDtypeStruct
    return pl.pallas_call(
        partial(feed_kernel, plan_in, plan_out),
        grid=(FF_STEPS,),
        in_specs=[
            fixed((LEN, D)), fixed((LEN, D)), fixed((D, D)), fixed((1, D)), fixed((LEN, D)),
            pl.BlockSpec((D, cols), lambda c: (0, c)),
            pl.BlockSpec((cols, D), lambda c: (c, 0)),
        ],
        out_specs=[
            fixed((LEN, D)), in_spec, in_spec, fixed(half_out), fixed(half_out),
            fixed((LEN, D)), fixed((LEN, D)), fixed((LEN, D)), fixed((1, D)),
        ],
        out_shape=[
            like((LEN, D), jnp.bfloat16),
            like(half_in, jnp.bfloat16),
            like(half_in, jnp.bfloat16),
            like(half_out, jnp.bfloat16),
            like(half_out, jnp.bfloat16),
            like((LEN, D), jnp.float32),
            like((LEN, D), jnp.bfloat16),
            like((LEN, D), jnp.bfloat16),
            like((1, D), jnp.float32),
        ],
        scratch_shapes=[
            pltpu.VMEM((LEN, D), jnp.float32),
            pltpu.VMEM((LEN, D), jnp.bfloat16),
            pltpu.VMEM((LEN, D), jnp.float32),
            pltpu.VMEM((LEN, D), jnp.float32),
            pltpu.VMEM((LEN, cols), jnp.bfloat16),
            pltpu.VMEM((LEN, cols), jnp.bfloat16),
        ],
        compiler_params=pltpu.CompilerParams(vmem_limit_bytes=VMEM_LIMIT),
        cost_estimate=pl.CostEstimate(flops=12 * LEN * D * ff, bytes_accessed=40 * LEN * D, transcendentals=0),
    )(y1, oc, wco, gain, g, w1, w2)


def swap(value, axis, bit, size):
    return lax.ppermute(value, axis, [(i, i ^ (1 << bit)) for i in range(size)])


def total_of(terms):
    out = terms[0].astype(jnp.float32)
    for term in terms[1:]:
        out = out + term.astype(jnp.float32)
    return out


def gather_rows(rows, n_blk):
    out = rows
    masks = [0]
    for bit in reversed(range(bits_of(n_blk))):
        out = jnp.concatenate([out, swap(out, "blk", bit, n_blk)], axis=0)
        masks = masks + [mask | (1 << bit) for mask in masks]
    return out, masks


def scatter_slots(value, n_blk):
    terms = [value]
    for bit in range(bits_of(n_blk)):
        half = terms[0].shape[0] // 2
        send = total_of([t[half:] for t in terms]).astype(jnp.bfloat16)
        kept = total_of([t[:half] for t in terms]).astype(jnp.bfloat16)
        terms = [kept, swap(send, "blk", bit, n_blk)]
    return total_of(terms)[0]


def scatter_step(terms, axis, bit, n):
    half = terms[0].shape[0] // 2
    send = total_of([t[half:] for t in terms]).astype(jnp.bfloat16)
    kept = total_of([t[:half] for t in terms]).astype(jnp.bfloat16)
    return [kept, swap(send, axis, bit, n)]


def per_device(
    decoder_rows,
    encoder_rows,
    target_lengths,
    target_question,
    passage_question,
    self_gain,
    self_query,
    self_key,
    self_value,
    self_output,
    position_bias_matrix,
    cross_gain,
    cross_query,
    cross_key,
    cross_value,
    cross_output,
    feed_gain,
    feed_input_weight,
    feed_out,
    cotangent,
    n_dp,
    n_blk,
):
    passage = encoder_rows.shape[0]
    sizes = {"blk": n_blk, "dp": n_dp}
    me = lax.axis_index("blk")
    encoder_all, masks = gather_rows(encoder_rows, n_blk)
    slot_device = me ^ jnp.array(masks, dtype=jnp.int32)
    slot_pick = slot_device[:, None] == jnp.arange(n_blk, dtype=jnp.int32)[None, :]
    slot_question = jnp.sum(jnp.where(slot_pick, passage_question[None, :], 0), axis=1)
    order = passage_order(slot_question)
    items = cross_items(target_lengths[0], target_question[0])
    positions = jnp.arange(LEN, dtype=jnp.int32)
    seg_ends = jnp.cumsum(target_lengths[0])
    segment = jnp.sum((positions[:, None] >= seg_ends[None, : TARGETS - 1]).astype(jnp.int32), axis=-1)
    aq, ak, av = segment_aug(segment)
    table_pairs = position_bias_matrix.T.reshape(PAIRS, 2, BUCKETS)
    self_gain2, cross_gain2, feed_gain2 = self_gain[None], cross_gain[None], feed_gain[None]

    inputs = decoder_rows.astype(jnp.float32)
    act_self = (inputs * norm_parts(inputs) * self_gain2).astype(jnp.bfloat16)
    query_self = dot_nn(act_self, self_query).astype(jnp.bfloat16)
    key_self = dot_nn(act_self, self_key).astype(jnp.bfloat16)
    value_self = dot_nn(act_self, self_value).astype(jnp.bfloat16)
    attn_self, aug_self = self_forward(query_self, key_self, value_self, aq, ak, table_pairs)
    attn_self, encoder_all = lax.optimization_barrier((attn_self, encoder_all))
    resid_self = inputs + dot_nn(attn_self, self_output)
    inv_cross = norm_parts(resid_self)
    act_cross = (resid_self * inv_cross * cross_gain2).astype(jnp.bfloat16)
    query_cross = dot_nn(act_cross, cross_query).astype(jnp.bfloat16)
    pair_weight = jnp.concatenate([cross_key, cross_value], axis=1)
    pair_all = dot_nn(encoder_all, pair_weight).astype(jnp.bfloat16)
    attn_cross, aug_cross = cross_forward(order, items, query_cross, pair_all, passage)

    plan_in = Exchange(4, n_blk, n_dp, "y")
    plan_out = Exchange(4, n_blk, n_dp, "x")
    (block_out, in_send, in_keep, out_send, out_keep, grad_resid_cross, round_cross, grad_attn_cross, gain_feed) = feed_block(
        resid_self, attn_cross, cross_output, feed_gain2, cotangent, feed_input_weight, feed_out, plan_in, plan_out
    )
    first_in, first_out = plan_in.order[0], plan_out.order[0]
    terms_in = [in_keep, swap(in_send, *first_in, sizes[first_in[0]])]
    terms_out = [out_keep, swap(out_send, *first_out, sizes[first_out[0]])]
    (terms_in, terms_out), grad_attn_cross = lax.optimization_barrier(((terms_in, terms_out), grad_attn_cross))
    step = lambda plan, terms, k: scatter_step(terms, *plan.order[k], sizes[plan.order[k][0]])
    next_in, next_out = step(plan_in, terms_in, 1), step(plan_out, terms_out, 1)
    dqc, dkv = cross_backward(
        order, items, query_cross, pair_all, grad_attn_cross, attn_cross, aug_cross, passage
    )
    (terms_in, terms_out), dqc, dkv = lax.optimization_barrier(((next_in, next_out), dqc, dkv))
    next_in, next_out = step(plan_in, terms_in, 2), step(plan_out, terms_out, 2)
    encoder_part = dot_nt(dkv, pair_weight).astype(jnp.bfloat16)
    da_cross = dot_nt(dqc, cross_query)
    gain_cross = jnp.sum(da_cross * resid_self * inv_cross, axis=0)
    grad_resid_self = grad_resid_cross + norm_back(resid_self, inv_cross, cross_gain2, da_cross)
    round_self = grad_resid_self.astype(jnp.bfloat16)
    grad_attn_self = dot_nt(round_self, self_output).astype(jnp.bfloat16)
    (terms_in, terms_out), grad_attn_self, encoder_part = lax.optimization_barrier(
        ((next_in, next_out), grad_attn_self, encoder_part)
    )
    for k in range(3, len(plan_in.order)):
        terms_in = step(plan_in, terms_in, k)
    for k in range(3, len(plan_out.order)):
        terms_out = step(plan_out, terms_out, k)
    total_in = total_of(terms_in)[0]
    for bit in range(bits_of(n_dp)):
        own = total_in.astype(jnp.bfloat16)
        total_in = total_of([own, swap(own, "dp", bit, n_dp)])
    sum_feed_in = jnp.swapaxes(total_in, 0, 1).reshape(D // n_blk, -1)
    total_out = total_of(terms_out)[0]
    if plan_out.kind == "x":
        for bit in range(bits_of(n_dp)):
            own = total_out.astype(jnp.bfloat16)
            other = swap(own, "dp", bit, n_dp)
            low = (lax.axis_index("dp") >> bit) & 1 == 0
            total_out = jnp.concatenate([jnp.where(low, own, other), jnp.where(low, other, own)], axis=0)
        total_out = total_out.astype(jnp.float32)
    else:
        for bit in range(bits_of(n_dp)):
            own = total_out.astype(jnp.bfloat16)
            total_out = total_of([own, swap(own, "dp", bit, n_dp)])
    sum_feed_out = total_out.reshape(-1, D)
    grad_encoder = scatter_slots(encoder_part.reshape(n_blk, passage, D), n_blk)
    dq, dk, dv, table_parts = self_backward(
        query_self, key_self, value_self, grad_attn_self, attn_self, aug_self, ak, av, table_pairs
    )
    sum_feed_in, sum_feed_out, grad_encoder, dq, dk, dv = lax.optimization_barrier(
        (sum_feed_in, sum_feed_out, grad_encoder, dq, dk, dv)
    )
    small = jnp.concatenate(
        [
            jnp.zeros((1, D), jnp.float32),
            gain_cross[None],
            gain_feed,
            jnp.pad(table_parts.reshape(1, H * BUCKETS), ((0, 0), (0, D - H * BUCKETS))),
            jnp.zeros((4, D), jnp.float32),
        ],
        axis=0,
    )
    crossx, crossy, selfx, selfy, grad_decoder, sums = tail_block(
        n_blk, n_dp,
        decoder_rows, self_gain2, grad_resid_self, act_self, dq, dk, dv, self_query, self_key, self_value,
        act_cross, dqc, encoder_all, dkv, attn_self, attn_cross, round_cross, small,
    )
    return (
        block_out,
        grad_decoder,
        grad_encoder,
        sums[0],
        selfx[0],
        selfx[1],
        selfy[0],
        crossy[2],
        sums[3, : H * BUCKETS].reshape(H, BUCKETS).T,
        sums[1],
        crossx[0],
        crossx[1],
        crossy[0],
        crossy[1],
        sums[2],
        sum_feed_in,
        sum_feed_out,
    )


def solution(mesh):
    split, copied, owned = P(("dp", "blk"), None), P(), P("blk", None)
    return jax.shard_map(
        partial(per_device, n_dp=mesh.shape["dp"], n_blk=mesh.shape["blk"]),
        mesh=mesh,
        in_specs=(split,) * 4 + (P("dp"),) + (copied,) * 14 + (split,),
        out_specs=(split,) * 3 + (copied,) + (owned,) * 4 + (copied,) * 2 + (owned,) * 4 + (copied,) + (owned,) * 2,
        check_vma=False,
    )
```

```python
import functools
from functools import partial

import jax
import jax.numpy as jnp
from jax import lax
from jax.experimental import pallas as pl
from jax.experimental.pallas import tpu as pltpu
from jax.sharding import PartitionSpec as P

D = 768
H = 12
HD = 64
BUCKETS = 32
LEN = 1024
TARGETS = 4
PAIRS = H // 2
LANES = 2 * HD
TILE = 256
SCALE = HD ** -0.5
NEG = -1e30
VMEM_LIMIT = 60 * 1024 * 1024

eps_norm = 1e-06
bucket_edges = (19, 21, 24, 27, 31, 35, 40, 46, 52, 59, 67, 77, 87, 99, 113)


def dot_nn(a, b):
    return jnp.dot(a, b, preferred_element_type=jnp.float32)


def dot_nt(a, b):
    return lax.dot_general(a, b, (((1,), (1,)), ((), ())), preferred_element_type=jnp.float32)


def dot_tn(a, b):
    return lax.dot_general(a, b, (((0,), (0,)), ((), ())), preferred_element_type=jnp.float32)


def lane_ids(rows):
    return lax.broadcasted_iota(jnp.int32, (rows, LANES), 1)


def in_half(rows, head):
    lane = lane_ids(rows)
    return lane < HD if head == 0 else lane >= HD


def split3(value):
    high = value.astype(jnp.bfloat16).astype(jnp.float32)
    rest = value - high
    mid = rest.astype(jnp.bfloat16).astype(jnp.float32)
    return high, mid, rest - mid


def triple_lanes(first, second, rows):
    lane = lane_ids(rows)
    out = jnp.zeros((rows, LANES), jnp.float32)
    for base, value in ((HD, first), (0, second)):
        for place, part in enumerate(split3(value)):
            out = jnp.where(lane == base + place, part, out)
    return out


def bucket_vector(table_t, offsets):
    upper = jnp.full(offsets.shape, 16, jnp.int32)
    for edge in bucket_edges:
        upper = upper + (offsets >= edge).astype(jnp.int32)
    bucket = jnp.where(offsets < 16, offsets, upper)
    rows = lax.broadcasted_iota(jnp.int32, (BUCKETS, offsets.shape[1]), 0)
    chosen = (rows == bucket).astype(jnp.float32).astype(jnp.bfloat16)
    return chosen


WIN = 3 * TILE


def self_forward_kernel(q_ref, k_ref, v_ref, aq_ref, ak_ref, table_ref, o_ref, aug_ref, bias_ref):
    lane768 = lax.broadcasted_iota(jnp.int32, (1, WIN), 1)
    offsets = 2 * TILE - lane768
    chosen = bucket_vector(None, jnp.maximum(offsets, 0))
    line = dot_nn(table_ref[0], chosen)
    line = jnp.where(offsets >= 0, line, NEG)
    far = table_ref[0][:, BUCKETS - 1 :].astype(jnp.float32)
    for head in range(2):
        spread = jnp.broadcast_to(line[head : head + 1], (TILE, WIN))
        bias_ref[head] = pltpu.roll(spread, 0, 1, stride=1, stride_axis=0)[:, TILE:]
    aq, ak = aq_ref[...], ak_ref[...]
    outs = {}
    logs = {}
    for head in range(2):
        half = in_half(LEN, head)
        q = jnp.where(half, q_ref[...] * jnp.bfloat16(SCALE), aq)
        k = jnp.where(half, k_ref[...], ak)
        v = jnp.where(half, v_ref[...], jnp.zeros((), jnp.bfloat16))
        for i in range(LEN // TILE):
            lo = max(0, i - 2) * TILE
            hi = (i + 1) * TILE
            scores = dot_nt(q[i * TILE : hi], k[lo:hi])
            near = min(2 * TILE, hi - lo)
            parts = []
            if hi - lo > near:
                parts.append(scores[:, : hi - lo - near] + far[head : head + 1])
            parts.append(scores[:, hi - lo - near :] + bias_ref[head][:, 2 * TILE - near :])
            scores = parts[0] if len(parts) == 1 else jnp.concatenate(parts, axis=1)
            top = jnp.max(scores, axis=1, keepdims=True)
            expo = jnp.exp(scores - top)
            total = jnp.sum(expo, axis=1, keepdims=True)
            mixed = dot_nn(expo.astype(jnp.bfloat16), v[lo:hi]) / total
            logs[i, head] = top + jnp.log(total)
            outs[i, head] = mixed
            if head == 1:
                o_ref[i * TILE : hi] = (outs[i, 0] + outs[i, 1]).astype(jnp.bfloat16)
                aug = triple_lanes(logs[i, 0], logs[i, 1], TILE)
                lane = lane_ids(TILE)
                place = lane & (HD - 1)
                aug_ref[i * TILE : hi] = jnp.where(
                    place < 3, aug, aq_ref[i * TILE : hi].astype(jnp.float32)
                ).astype(jnp.bfloat16)


def pair_spec(offset=0):
    return pl.BlockSpec((LEN, LANES), lambda p: (0, p + offset))


def whole(shape):
    return pl.BlockSpec(shape, lambda p: (0,) * len(shape))


def self_forward(q, k, v, aq, ak, table_pairs):
    return pl.pallas_call(
        self_forward_kernel,
        grid=(PAIRS,),
        in_specs=[pair_spec()] * 3 + [whole((LEN, LANES))] * 2
        + [pl.BlockSpec((1, 2, BUCKETS), lambda p: (p, 0, 0))],
        out_specs=[pair_spec(), pair_spec()],
        out_shape=[jax.ShapeDtypeStruct((LEN, D), jnp.bfloat16)] * 2,
        scratch_shapes=[pltpu.VMEM((2, TILE, 2 * TILE), jnp.float32)],
        compiler_params=pltpu.CompilerParams(vmem_limit_bytes=VMEM_LIMIT),
        cost_estimate=pl.CostEstimate(flops=4 * H * LEN * LEN * HD, bytes_accessed=10 * LEN * D, transcendentals=0),
    )(q, k, v, aq, ak, table_pairs)


def self_backward_kernel(q_ref, k_ref, v_ref, do_ref, o_ref, aug_ref, ak_ref, av_ref, table_ref,
                         dq_ref, dk_ref, dv_ref, gt_ref, bias_ref, g_ref, gfar_ref, dqt_ref):
    lane768 = lax.broadcasted_iota(jnp.int32, (1, WIN), 1)
    offsets = lane768 - TILE
    chosen = bucket_vector(None, jnp.maximum(offsets, 0))
    line = dot_nn(table_ref[0], chosen)
    line = jnp.where(offsets >= 0, line, NEG)
    far = table_ref[0][:, BUCKETS - 1 :].astype(jnp.float32)
    for head in range(2):
        spread = jnp.broadcast_to(line[head : head + 1], (TILE, WIN))
        bias_ref[head] = pltpu.roll(spread, 0, 1, stride=1, stride_axis=0)[:, TILE:]
    g_ref[...] = jnp.zeros_like(g_ref)
    gfar_ref[...] = jnp.zeros_like(gfar_ref)
    dqt_ref[...] = jnp.zeros_like(dqt_ref)
    product = do_ref[...].astype(jnp.float32) * o_ref[...].astype(jnp.float32)
    deltas = []
    for head in range(2):
        half = in_half(LEN, head)
        deltas.append(jnp.sum(jnp.where(half, product, 0.0), axis=1, keepdims=True))
    aug_do = (-triple_lanes(deltas[0], deltas[1], LEN)).astype(jnp.bfloat16)
    q_scaled = q_ref[...] * jnp.bfloat16(SCALE)
    k_t = k_ref[...].T
    accs = {}
    for head in range(2):
        half = in_half(LEN, head)
        q = jnp.where(half, q_scaled, aug_ref[...])
        k = jnp.where(half, k_ref[...], ak_ref[...])
        v = jnp.where(half, v_ref[...], av_ref[...])
        do = jnp.where(half, do_ref[...], aug_do)
        for j in range(LEN // TILE):
            lo = j * TILE
            hi = min(LEN, (j + 3) * TILE)
            width = hi - lo
            near = min(2 * TILE, width)
            scores = dot_nt(k[lo : lo + TILE], q[lo:hi])
            parts = [scores[:, :near] + bias_ref[head][:, :near]]
            if width > near:
                parts.append(scores[:, near:] + far[head : head + 1])
            scores = parts[0] if len(parts) == 1 else jnp.concatenate(parts, axis=1)
            probs = jnp.exp(scores)
            grad_probs = dot_nt(v[lo : lo + TILE], do[lo:hi])
            grad_scores = probs * grad_probs
            g_ref[head, :, :near] += grad_scores[:, :near]
            if width > near:
                gfar_ref[head] += grad_scores[:, near:]
            ds = grad_scores.astype(jnp.bfloat16)
            accs[j, head] = (dot_nn(ds, q[lo:hi]), dot_nn(probs.astype(jnp.bfloat16), do[lo:hi]))
            dqt_ref[head * HD : (head + 1) * HD, lo:hi] += dot_nn(
                k_t[head * HD : (head + 1) * HD, lo : lo + TILE], ds
            )
            if head == 1:
                lower = in_half(TILE, 0)
                dk_ref[lo : lo + TILE] = jnp.where(lower, accs[j, 0][0], accs[j, 1][0]).astype(jnp.bfloat16)
                dv_ref[lo : lo + TILE] = jnp.where(lower, accs[j, 0][1], accs[j, 1][1]).astype(jnp.bfloat16)
    dq_ref[...] = (dqt_ref[...] * SCALE).T.astype(jnp.bfloat16)
    rows = []
    for head in range(2):
        total = jnp.zeros((8, WIN), jnp.float32)
        pad = jnp.zeros((8, TILE), jnp.float32)
        for a in range(TILE // 8):
            strip = jnp.concatenate([pad, g_ref[head, 8 * a : 8 * a + 8, :]], axis=1)
            if a:
                strip = pltpu.roll(strip, WIN - 8 * a, 1)
            total = total + strip
        line_sum = jnp.zeros((1, WIN), jnp.float32)
        for s in range(8):
            one = total[s : s + 1]
            line_sum = line_sum + (pltpu.roll(one, WIN - s, 1) if s else one)
        rows.append(line_sum)
    lines = jnp.concatenate(rows, axis=0)
    lines = jnp.where(offsets >= 0, lines, 0.0)
    high, mid, low = split3(lines)
    sums = sum(dot_nt(part.astype(jnp.bfloat16), chosen) for part in (high, mid, low))
    for head in range(2):
        far_sum = jnp.sum(gfar_ref[head])
        lane32 = lax.broadcasted_iota(jnp.int32, (1, BUCKETS), 1)
        gt_ref[0, head : head + 1, :] = sums[head : head + 1] + jnp.where(lane32 == BUCKETS - 1, far_sum, 0.0)


def self_backward(q, k, v, do, o, aug, ak, av, table_pairs):
    return pl.pallas_call(
        self_backward_kernel,
        grid=(PAIRS,),
        in_specs=[pair_spec()] * 6 + [whole((LEN, LANES))] * 2
        + [pl.BlockSpec((1, 2, BUCKETS), lambda p: (p, 0, 0))],
        out_specs=[pair_spec()] * 3 + [pl.BlockSpec((1, 2, BUCKETS), lambda p: (p, 0, 0))],
        out_shape=[jax.ShapeDtypeStruct((LEN, D), jnp.bfloat16)] * 3
        + [jax.ShapeDtypeStruct((PAIRS, 2, BUCKETS), jnp.float32)],
        scratch_shapes=[
            pltpu.VMEM((2, TILE, 2 * TILE), jnp.float32),
            pltpu.VMEM((2, TILE, 2 * TILE), jnp.float32),
            pltpu.VMEM((2, TILE, TILE), jnp.float32),
            pltpu.VMEM((LANES, LEN), jnp.float32),
        ],
        compiler_params=pltpu.CompilerParams(vmem_limit_bytes=VMEM_LIMIT),
        cost_estimate=pl.CostEstimate(flops=10 * H * LEN * LEN * HD, bytes_accessed=18 * LEN * D, transcendentals=0),
    )(q, k, v, do, o, aug, ak, av, table_pairs)


CT = 256


def cross_forward_kernel(order_ref, item_ref, q_ref, kv_ref, o_ref, aug_ref, ks_ref, vs_ref, passage):
    slots = order_ref.shape[0]
    per_q = slots // TARGETS
    keys_q = per_q * passage
    lower = lax.broadcasted_iota(jnp.int32, (passage, D), 1) % LANES < HD
    zero = jnp.zeros((), jnp.bfloat16)

    @pl.loop(0, slots)
    def _(s):
        src = pl.multiple_of(order_ref[s] * passage, passage)
        dst = pl.multiple_of(s * passage, passage)
        keys = kv_ref[pl.ds(src, passage), :D]
        values = kv_ref[pl.ds(src, passage), D:]
        ks_ref[0, pl.ds(dst, passage)] = jnp.where(lower, keys, zero)
        ks_ref[1, pl.ds(dst, passage)] = jnp.where(lower, zero, keys)
        vs_ref[0, pl.ds(dst, passage)] = jnp.where(lower, values, zero)
        vs_ref[1, pl.ds(dst, passage)] = jnp.where(lower, zero, values)

    o_ref[...] = jnp.zeros_like(o_ref)
    aug_ref[...] = jnp.zeros_like(aug_ref)

    @pl.loop(0, item_ref[4, 0])
    def _(n):
        row0 = pl.multiple_of(item_ref[0, n] * CT, CT)
        key0 = pl.multiple_of(item_ref[1, n] * keys_q, keys_q)
        rows = lax.broadcasted_iota(jnp.int32, (CT, 1), 0)
        valid = (rows >= item_ref[2, n]) & (rows < item_ref[3, n])
        for pair in range(PAIRS):
            cols = slice(pair * LANES, (pair + 1) * LANES)
            q = q_ref[pl.ds(row0, CT), cols] * jnp.bfloat16(SCALE)
            outs, logs = [], []
            for head in range(2):
                scores = dot_nt(q, ks_ref[head, pl.ds(key0, keys_q), cols])
                top = jnp.max(scores, axis=1, keepdims=True)
                expo = jnp.exp(scores - top)
                total = jnp.sum(expo, axis=1, keepdims=True)
                outs.append(dot_nn(expo.astype(jnp.bfloat16), vs_ref[head, pl.ds(key0, keys_q), cols]) / total)
                logs.append(top + jnp.log(total))
            mixed = (outs[0] + outs[1]).astype(jnp.bfloat16)
            aug = triple_lanes(logs[0], logs[1], CT).astype(jnp.bfloat16)
            o_ref[pl.ds(row0, CT), cols] = jnp.where(valid, mixed, o_ref[pl.ds(row0, CT), cols])
            aug_ref[pl.ds(row0, CT), cols] = jnp.where(valid, aug, aug_ref[pl.ds(row0, CT), cols])


def smem_spec():
    return pl.BlockSpec(memory_space=pltpu.SMEM)


def vmem_spec():
    return pl.BlockSpec(memory_space=pltpu.VMEM)


def cross_forward(order, items, q, kv, passage):
    keys = kv.shape[0]
    return pl.pallas_call(
        partial(cross_forward_kernel, passage=passage),
        in_specs=[smem_spec(), smem_spec(), vmem_spec(), vmem_spec()],
        out_specs=[vmem_spec(), vmem_spec()],
        out_shape=[jax.ShapeDtypeStruct((LEN, D), jnp.bfloat16)] * 2,
        scratch_shapes=[pltpu.VMEM((2, keys, D), jnp.bfloat16)] * 2,
        compiler_params=pltpu.CompilerParams(vmem_limit_bytes=VMEM_LIMIT),
        cost_estimate=pl.CostEstimate(flops=2 * H * LEN * LEN * HD, bytes_accessed=10 * LEN * D, transcendentals=0),
    )(order, items, q, kv)


def cross_backward_kernel(order_ref, item_ref, q_ref, kv_ref, do_ref, o_ref, aug_ref,
                          dq_ref, dkv_ref, ks_ref, vs_ref, kt_ref, dk_ref, dv_ref, dqt_ref, passage):
    slots = order_ref.shape[0]
    per_q = slots // TARGETS
    keys_q = per_q * passage
    lane = lax.broadcasted_iota(jnp.int32, (passage, D), 1) % LANES
    lower = lane < HD
    ones = jnp.where((lane & (HD - 1)) < 3, 1.0, 0.0).astype(jnp.bfloat16)
    minus = -ones

    @pl.loop(0, slots)
    def _(s):
        src = pl.multiple_of(order_ref[s] * passage, passage)
        dst = pl.multiple_of(s * passage, passage)
        keys = kv_ref[pl.ds(src, passage), :D]
        values = kv_ref[pl.ds(src, passage), D:]
        ks_ref[0, pl.ds(dst, passage)] = jnp.where(lower, keys, minus)
        ks_ref[1, pl.ds(dst, passage)] = jnp.where(lower, minus, keys)
        vs_ref[0, pl.ds(dst, passage)] = jnp.where(lower, values, ones)
        vs_ref[1, pl.ds(dst, passage)] = jnp.where(lower, ones, values)

    lower_k = lax.broadcasted_iota(jnp.int32, (keys_q, LANES), 1) < HD
    for s in range(TARGETS):
        for pair in range(PAIRS):
            rows = slice(s * keys_q, (s + 1) * keys_q)
            cols = slice(pair * LANES, (pair + 1) * LANES)
            both = jnp.where(lower_k, ks_ref[0, rows, cols], ks_ref[1, rows, cols])
            kt_ref[cols, rows] = both.T
    dk_ref[...] = jnp.zeros_like(dk_ref)
    dv_ref[...] = jnp.zeros_like(dv_ref)
    dqt_ref[...] = jnp.zeros_like(dqt_ref)

    @pl.loop(0, item_ref[4, 0])
    def _(n):
        row0 = pl.multiple_of(item_ref[0, n] * CT, CT)
        key0 = pl.multiple_of(item_ref[1, n] * keys_q, keys_q)
        rows = lax.broadcasted_iota(jnp.int32, (CT, 1), 0)
        valid = (rows >= item_ref[2, n]) & (rows < item_ref[3, n])
        here = pl.ds(row0, CT)
        there = pl.ds(key0, keys_q)
        for pair in range(PAIRS):
            cols = slice(pair * LANES, (pair + 1) * LANES)
            q_scaled = q_ref[here, cols] * jnp.bfloat16(SCALE)
            do_pair = jnp.where(valid, do_ref[here, cols], jnp.zeros((), jnp.bfloat16))
            product = do_pair.astype(jnp.float32) * o_ref[here, cols].astype(jnp.float32)
            deltas = []
            for head in range(2):
                deltas.append(jnp.sum(jnp.where(in_half(CT, head), product, 0.0), axis=1, keepdims=True))
            aug_do = (-triple_lanes(deltas[0], deltas[1], CT)).astype(jnp.bfloat16)
            aug = jnp.where(valid, aug_ref[here, cols], jnp.bfloat16(1e30))
            parts = []
            for head in range(2):
                half = in_half(CT, head)
                q = jnp.where(half, q_scaled, aug)
                do = jnp.where(half, do_pair, aug_do)
                probs = jnp.exp(dot_nt(ks_ref[head, there, cols], q))
                grad_scores = probs * dot_nt(vs_ref[head, there, cols], do)
                ds = grad_scores.astype(jnp.bfloat16)
                parts.append((dot_nn(ds, q), dot_nn(probs.astype(jnp.bfloat16), do)))
                hrow = pair * LANES + head * HD
                dqt_ref[hrow : hrow + HD, here] += dot_nn(kt_ref[hrow : hrow + HD, there], ds)
            dk_ref[there, cols] += jnp.where(lower_k, parts[0][0], parts[1][0])
            dv_ref[there, cols] += jnp.where(lower_k, parts[0][1], parts[1][1])

    for pair in range(PAIRS):
        cols = slice(pair * LANES, (pair + 1) * LANES)
        dq_ref[:, cols] = (dqt_ref[cols, :] * SCALE).T.astype(jnp.bfloat16)

    @pl.loop(0, slots)
    def _(s):
        src = pl.multiple_of(s * passage, passage)
        dst = pl.multiple_of(order_ref[s] * passage, passage)
        dkv_ref[pl.ds(dst, passage), :D] = dk_ref[pl.ds(src, passage)].astype(jnp.bfloat16)
        dkv_ref[pl.ds(dst, passage), D:] = dv_ref[pl.ds(src, passage)].astype(jnp.bfloat16)


def cross_backward(order, items, q, kv, do, o, aug, passage):
    keys = kv.shape[0]
    return pl.pallas_call(
        partial(cross_backward_kernel, passage=passage),
        in_specs=[smem_spec(), smem_spec()] + [vmem_spec()] * 5,
        out_specs=[vmem_spec(), vmem_spec()],
        out_shape=[
            jax.ShapeDtypeStruct((LEN, D), jnp.bfloat16),
            jax.ShapeDtypeStruct((keys, 2 * D), jnp.bfloat16),
        ],
        scratch_shapes=[pltpu.VMEM((2, keys, D), jnp.bfloat16)] * 2
        + [
            pltpu.VMEM((D, keys), jnp.bfloat16),
            pltpu.VMEM((keys, D), jnp.float32),
            pltpu.VMEM((keys, D), jnp.float32),
            pltpu.VMEM((D, LEN), jnp.float32),
        ],
        compiler_params=pltpu.CompilerParams(vmem_limit_bytes=VMEM_LIMIT),
        cost_estimate=pl.CostEstimate(flops=5 * H * LEN * LEN * HD, bytes_accessed=18 * LEN * D, transcendentals=0),
    )(order, items, q, kv, do, o, aug)


def cross_items(lengths, questions):
    ends = jnp.cumsum(lengths)
    starts = ends - lengths
    tiles = LEN // CT
    slots = tiles + TARGETS - 1
    first = starts // CT
    last = (ends - 1) // CT
    count = last - first + 1
    done = jnp.cumsum(count)
    number = jnp.arange(slots, dtype=jnp.int32)
    seg = jnp.sum((number[:, None] >= done[None, :]).astype(jnp.int32), axis=1)
    pick = (jnp.minimum(seg, TARGETS - 1)[:, None] == jnp.arange(TARGETS, dtype=jnp.int32)[None, :]).astype(jnp.int32)
    take = lambda a: jnp.sum(pick * a[None, :], axis=1)
    tile = jnp.clip(take(first) + number - take(done - count), 0, tiles - 1)
    lo = jnp.clip(take(starts) - tile * CT, 0, CT)
    hi = jnp.clip(take(ends) - tile * CT, 0, CT)
    total = jnp.broadcast_to(jnp.sum(count), (slots,))
    return jnp.stack([tile, take(questions), lo, hi, total]).astype(jnp.int32)


def passage_order(passage_question):
    count = passage_question.shape[0]
    ids = jnp.arange(count, dtype=jnp.int32)
    before = (passage_question[None, :] < passage_question[:, None]) | (
        (passage_question[None, :] == passage_question[:, None]) & (ids[None, :] < ids[:, None])
    )
    rank = jnp.sum(before.astype(jnp.int32), axis=1)
    return jnp.sum(jnp.where(rank[:, None] == ids[None, :], ids[:, None], 0), axis=0).astype(jnp.int32)


def segment_aug(segment):
    place = jnp.arange(LANES, dtype=jnp.int32)[None, :] & (HD - 1)
    seg = segment[:, None]
    mark = (place >= 3) & (place < 3 + TARGETS)
    same = place - 3 == seg
    aq = jnp.where(mark & same, 1.0, 0.0).astype(jnp.bfloat16)
    ak = jnp.where(place < 3, -1.0, jnp.where(mark & ~same, NEG, 0.0)).astype(jnp.bfloat16)
    av = jnp.broadcast_to(jnp.where(place < 3, 1.0, 0.0), (LEN, LANES)).astype(jnp.bfloat16)
    return aq, ak, av


ROWS = 256


def norm_parts(values):
    return lax.rsqrt(jnp.mean(values * values, axis=1, keepdims=True) + eps_norm)


def norm_back(values, inverse, gain, grad):
    scaled = grad * gain
    inner = jnp.mean(scaled * values, axis=1, keepdims=True)
    return inverse * scaled - values * (inverse * inverse * inverse * inner)


def bits_of(count):
    return count.bit_length() - 1


def place_bits(n_blk, n_dp, kind):
    blk = [("blk", bit) for bit in range(bits_of(n_blk))]
    dp = [("dp", bit) for bit in range(bits_of(n_dp))]
    if kind == "x":
        return blk[:1] + dp + blk[1:]
    if kind == "y":
        return blk[:2] + dp + blk[2:]
    return blk


def position(owner, piece, order):
    slot = 0
    for axis, bit in order:
        mine = (lax.axis_index(axis) // (1 << bit)) % 2
        static = ((owner if axis == "blk" else piece) >> bit) & 1
        slot = 2 * slot + (1 - mine if static else mine)
    return slot


def partner(axis, bit):
    me = lax.axis_index(axis)
    mine = (me // (1 << bit)) % 2
    return {axis: me + (1 - 2 * mine) * (1 << bit)}


class Exchange:
    def __init__(self, count, rows, cols, n_blk, n_dp, kind, first=0):
        if kind in "xy" and count % n_dp:
            kind = "plain"
        self.n_blk, self.n_dp, self.count, self.kind, self.first = n_blk, n_dp, count, kind, first
        self.rows, self.cols = rows, cols
        self.order = place_bits(n_blk, n_dp, kind)
        self.pieces = n_dp if kind in "xy" else 1
        self.slots = n_blk * self.pieces
        self.mats = count // self.pieces
        self.last = [("dp", bit) for bit in range(bits_of(n_dp))] if kind != "near" else []
        self.steps = len(self.order) + len(self.last)
        self.held = self.slots >> first
        self.offsets = {}
        at = self.held if first else 0
        for k in range(first, len(self.order)):
            size = self.slots >> (k + 1)
            self.offsets[k] = (at, size)
            at += size
        for j in range(len(self.last)):
            size = (1 << j) if self.pieces > 1 else 1
            self.offsets[len(self.order) + j] = (at, size)
            at += size
        self.received = at

    def scratch(self):
        shape = (self.mats, self.rows, self.cols)
        return [
            pltpu.VMEM((max(self.held, self.pieces),) + shape, jnp.bfloat16),
            pltpu.VMEM((self.received,) + shape, jnp.bfloat16),
            pltpu.SemaphoreType.DMA((self.steps,)),
            pltpu.SemaphoreType.DMA((self.steps,)),
        ]

    def out_shape(self):
        return jax.ShapeDtypeStruct((self.count, self.rows, self.cols), jnp.float32)

    def bind(self, refs, out_ref):
        self.buf, self.recv, self.send_sem, self.recv_sem = refs
        self.out = out_ref

    def put(self, index, value):
        piece, inner = index // self.mats, index % self.mats
        for owner in range(self.n_blk):
            slot = position(owner, piece, self.order)
            self.buf[slot, inner] = value[owner * self.rows : (owner + 1) * self.rows].astype(jnp.bfloat16)

    def copy(self, k):
        at, size = self.offsets[k]
        if k < len(self.order):
            axis, bit = self.order[k]
            src = self.buf.at[pl.ds(size, size)]
        else:
            axis, bit = self.last[k - len(self.order)]
            src = self.buf.at[pl.ds(0, size)]
        return pltpu.make_async_remote_copy(
            src_ref=src,
            dst_ref=self.recv.at[pl.ds(at, size)],
            send_sem=self.send_sem.at[k],
            recv_sem=self.recv_sem.at[k],
            device_id=partner(axis, bit),
            device_id_type=pl.DeviceIdType.MESH,
        )

    def start(self, k):
        self.copy(k).start()

    def add(self, at, size, final):
        for s in range(size):
            for m in range(self.mats):
                total = self.buf[s, m].astype(jnp.float32) + self.recv[at + s, m].astype(jnp.float32)
                if final:
                    self.out[m] = total
                else:
                    self.buf[s, m] = total.astype(jnp.bfloat16)

    def finish(self, k):
        self.copy(k).wait()
        at, size = self.offsets[k]
        final = k == self.steps - 1
        if k < len(self.order) or self.pieces == 1:
            self.add(at, size, final)
            return
        for s in range(size):
            for m in range(self.mats):
                self.buf[size + s, m] = self.recv[at + s, m]
        if final:
            for s in range(self.pieces):
                spot = position(0, s, self.last[::-1])
                for m in range(self.mats):
                    self.out[spot * self.mats + m] = self.buf[s, m].astype(jnp.float32)

    def advance(self, k):
        if k < self.first or k >= self.steps:
            return
        self.finish(k)
        if k + 1 < self.steps:
            self.start(k + 1)


def all_links(n_blk, n_dp):
    return [("blk", bit) for bit in range(bits_of(n_blk))] + [("dp", bit) for bit in range(bits_of(n_dp))]


def enter_barrier(n_blk, n_dp):
    barrier = pltpu.get_barrier_semaphore()
    links = all_links(n_blk, n_dp)
    for axis, bit in links:
        pl.semaphore_signal(barrier, inc=1, device_id=partner(axis, bit), device_id_type=pl.DeviceIdType.MESH)
    pl.semaphore_wait(barrier, len(links))


BLOCKS = 3
BLOCK = D // BLOCKS


def last_plans(n_blk, n_dp):
    rows = D // n_blk
    halves = 2
    feed_in, feed_out = feed_plans(n_blk, n_dp, 2)
    plans = [
        feed_in,
        feed_out,
        Exchange(3 * halves, rows, D // halves, n_blk, n_dp, "x"),
        Exchange(2 * halves, rows, D // halves, n_blk, n_dp, "y"),
    ]
    for block in range(BLOCKS):
        plans.append(Exchange(3 * halves, rows, BLOCK // halves, n_blk, n_dp, "xyx"[block]))
    return plans


def feed_plans(n_blk, n_dp, first=0):
    rows = D // n_blk
    return (
        Exchange(4, rows, D, n_blk, n_dp, "y", first),
        Exchange(4, rows, D, n_blk, n_dp, "x", first),
    )


POOL = 11
(S_ACTC, S_DQC, S_OC, S_E2, S_Q, S_K, S_V, S_DO, S_O, S_AUG, S_X) = range(POOL)
S_DQ, S_DK, S_DV, S_ACT = S_ACTC, S_DQC, S_OC, S_E2


def last_kernel(n_blk, n_dp, plans, enc_plan, *refs):
    (x_hbm, dy1_hbm, act_hbm, wq_hbm, wk_hbm, wv_hbm, actc_hbm, dqc_hbm, enc_hbm, dkv_hbm, oc_hbm, e2_hbm,
     q_hbm, k_hbm, v_hbm, do_hbm, o_hbm, aug_hbm, inkeep_hbm, inrecv_hbm, outkeep_hbm, outrecv_hbm, part_hbm,
     gain_ref, ak_ref, av_ref, table_ref, small_ref) = refs[:28]
    every = list(plans) + [enc_plan]
    outs = refs[28 : 28 + len(every)]
    dx_hbm, sums_ref = refs[28 + len(every) : 30 + len(every)]
    scratch = refs[30 + len(every) :]
    for i, plan in enumerate(every):
        plan.bind(scratch[4 * i : 4 * i + 4], outs[i])
    (pool, dy1_ref, act_t, bias_ref, g_ref, gfar_ref, dqt_ref,
     tot_ref, got_ref, tsend, trecv, load_sem, store_sem) = scratch[4 * len(every) :]
    feed_in, feed_out, crossx, crossy, self0, self1, self2 = plans
    selfs = (self0, self1, self2)

    loads = {}

    def load(name, src, dst):
        loads[name] = pltpu.make_async_copy(src, dst, load_sem.at[len(loads)])
        loads[name].start()

    def slot(index):
        return pool.at[index]

    load("actc", actc_hbm, slot(S_ACTC))
    load("dqc", dqc_hbm, slot(S_DQC))
    for plan, keep, got, name in (
        (feed_out, outkeep_hbm, outrecv_hbm, "out"),
        (feed_in, inkeep_hbm, inrecv_hbm, "in"),
    ):
        load(name + "keep", keep, plan.buf.at[pl.ds(0, plan.held)])
        load(name + "recv", got, plan.recv.at[pl.ds(0, plan.held)])
    spans = enc_hbm.shape[0] // LEN
    spare = (S_Q, S_K, S_V, S_DO, S_AUG, S_X)
    for n in range(spans):
        rows = pl.ds(n * LEN, LEN)
        load(("enc", n), enc_hbm.at[rows], slot(spare[3 * n]))
        load(("dk", n), dkv_hbm.at[rows, pl.ds(0, D)], slot(spare[3 * n + 1]))
        load(("dv", n), dkv_hbm.at[rows, pl.ds(D, D)], slot(spare[3 * n + 2]))
    load("part", part_hbm, enc_plan.buf)
    load("oc", oc_hbm, slot(S_OC))
    load("e2", e2_hbm, slot(S_E2))
    load("o", o_hbm, slot(S_O))
    load("dy1", dy1_hbm, dy1_ref)
    enter_barrier(n_blk, n_dp)

    def begin_feed(plan, name):
        loads[name + "keep"].wait()
        loads[name + "recv"].wait()
        plan.add(0, plan.held, False)
        plan.start(plan.first)

    def put_halves(plan, index, value):
        half = plan.cols
        for c in range(2):
            plan.put(2 * index + c, value[:, c * half : (c + 1) * half])

    begin_feed(feed_out, "out")
    begin_feed(feed_in, "in")
    loads["actc"].wait()
    loads["dqc"].wait()
    put_halves(crossx, 0, dot_tn(pool[S_ACTC], pool[S_DQC]))
    for w, name in ((1, "dk"), (2, "dv")):
        total = None
        for n in range(spans):
            if w == 1:
                loads["enc", n].wait()
            loads[name, n].wait()
            part = dot_tn(pool[spare[3 * n]], pool[spare[3 * n + w]])
            total = part if total is None else total + part
        put_halves(crossx, w, total)
    crossx.start(0)
    for name, src, index in (
        ("q", q_hbm, S_Q), ("k", k_hbm, S_K), ("v", v_hbm, S_V), ("do", do_hbm, S_DO), ("aug", aug_hbm, S_AUG), ("x", x_hbm, S_X),
    ):
        load(name, src, slot(index))
    loads["part"].wait()
    enc_plan.start(0)
    loads["oc"].wait()
    loads["e2"].wait()
    put_halves(crossy, 0, dot_tn(pool[S_OC], pool[S_E2]))
    loads["o"].wait()
    loads["dy1"].wait()
    put_halves(crossy, 1, dot_tn(pool[S_O], dy1_ref[...].astype(jnp.bfloat16)))
    crossy.start(0)
    load("act", act_hbm, slot(S_ACT))
    crossx.advance(0)
    for name in ("q", "k", "v", "do", "aug"):
        loads[name].wait()
    loads["act"].wait()
    act_t[...] = pool[S_ACT].T
    crossy.advance(0)
    enc_plan.advance(0)

    offsets = lax.broadcasted_iota(jnp.int32, (1, WIN), 1) - TILE
    chosen = bucket_vector(None, jnp.maximum(offsets, 0))

    def pair_body(p):
        lanes = pl.ds(pl.multiple_of(p * LANES, LANES), LANES)
        dq, dk, dv, sums = self_pair_backward(
            pool[S_Q, :, lanes], pool[S_K, :, lanes], pool[S_V, :, lanes], pool[S_DO, :, lanes], pool[S_O, :, lanes],
            pool[S_AUG, :, lanes], ak_ref[...], av_ref[...], table_ref[p], offsets, chosen,
            bias_ref, g_ref, gfar_ref, dqt_ref,
            lambda rows, value: pool.__setitem__((S_DK, rows, lanes), value),
            lambda rows, value: pool.__setitem__((S_DV, rows, lanes), value),
        )
        pool[S_DQ, :, lanes] = dq
        for head in range(2):
            tot_ref[3 + 2 * p + head] = jnp.concatenate(
                [sums[head], jnp.zeros((1, D - BUCKETS), jnp.float32)], axis=1
            )

    tot_ref[0:3] = small_ref[...]
    rounds = {
        0: [],
        1: [(feed_out, 2), (feed_in, 2)],
        2: [(crossy, 1)],
        3: [(crossx, 1), (feed_out, 3), (feed_in, 3), (enc_plan, 1)],
        4: [(crossy, 2), (self0, 0)],
        5: [(feed_out, 4), (feed_in, 4), (enc_plan, 2)],
    }
    per_block = PAIRS // BLOCKS
    for block in range(BLOCKS):
        for inner in range(per_block):
            p = block * per_block + inner
            for plan, k in rounds[p]:
                plan.advance(k)
            pair_body(p)
        cols = slice(block * BLOCK, (block + 1) * BLOCK)
        for w, index in enumerate((S_DQ, S_DK, S_DV)):
            put_halves(selfs[block], w, dot_nn(act_t[...], pool[index, :, cols]))
        selfs[block].start(0)
    wq, wk, wv = slot(S_Q), slot(S_K), slot(S_V)
    for name, src, index in (("wq", wq_hbm, S_Q), ("wk", wk_hbm, S_K), ("wv", wv_hbm, S_V)):
        load(name, src, pool.at[index, pl.ds(0, D)])
    crossx.advance(2)
    self1.advance(0)
    for name in ("wq", "wk", "wv", "x"):
        loads[name].wait()
    pending = [
        [(crossy, 3), (self0, 1), (enc_plan, 3), (self2, 0)],
        [(crossx, 3), (feed_out, 5), (feed_in, 5)],
        [(self1, 1), (crossy, 4), (self0, 2)],
        [(crossx, 4), (self2, 1)],
    ]
    gain_sum = jnp.zeros((1, D), jnp.float32)
    stores = []
    for i, r in enumerate(range(0, LEN, ROWS)):
        rows = slice(r, r + ROWS)
        da = (
            dot_nt(pool[S_DQ, rows], pool[S_Q, :D])
            + dot_nt(pool[S_DK, rows], pool[S_K, :D])
            + dot_nt(pool[S_DV, rows], pool[S_V, :D])
        )
        x = pool[S_X, rows].astype(jnp.float32)
        inverse = norm_parts(x)
        gain_sum = gain_sum + jnp.sum(da * x * inverse, axis=0, keepdims=True)
        dy1_ref[rows] = dy1_ref[rows] + norm_back(x, inverse, gain_ref[...], da)
        stores.append(pltpu.make_async_copy(dy1_ref.at[rows], dx_hbm.at[rows], store_sem.at[i]))
        stores[-1].start()
        for plan, k in pending[i]:
            plan.advance(k)
    tot_ref[0] = gain_sum
    links = all_links(n_blk, n_dp)

    def small_copy(j):
        axis, bit = links[j]
        return pltpu.make_async_remote_copy(
            src_ref=tot_ref,
            dst_ref=got_ref.at[j],
            send_sem=tsend.at[j],
            recv_sem=trecv.at[j],
            device_id=partner(axis, bit),
            device_id_type=pl.DeviceIdType.MESH,
        )

    small_copy(0).start()
    done = {feed_in: 5, feed_out: 5, crossx: 4, crossy: 4, enc_plan: 3, self0: 2, self1: 1, self2: 1}
    longest = max(plan.steps for plan in every)
    j = 0
    while True:
        for plan in (self2, self1, self0, crossx, crossy, feed_out, feed_in, enc_plan):
            done[plan] += 1
            plan.advance(done[plan])
        if j < len(links):
            small_copy(j).wait()
            tot_ref[...] = tot_ref[...] + got_ref[j]
            j += 1
            if j < len(links):
                small_copy(j).start()
        if j == len(links) and all(done[plan] >= plan.steps - 1 for plan in every):
            break
    sums_ref[...] = tot_ref[...]
    for store in stores:
        store.wait()


def self_pair_backward(q_raw, k_raw, v_raw, do_raw, o_raw, aug, ak, av, table, offsets, chosen,
                       bias_ref, g_ref, gfar_ref, dqt_ref, put_dk, put_dv):
    line = dot_nn(table, chosen)
    line = jnp.where(offsets >= 0, line, NEG)
    far = table[:, BUCKETS - 1 :].astype(jnp.float32)
    for head in range(2):
        spread = jnp.broadcast_to(line[head : head + 1], (TILE, WIN))
        bias_ref[head] = pltpu.roll(spread, 0, 1, stride=1, stride_axis=0)[:, TILE:]
    g_ref[...] = jnp.zeros_like(g_ref)
    gfar_ref[...] = jnp.zeros_like(gfar_ref)
    dqt_ref[...] = jnp.zeros_like(dqt_ref)
    product = do_raw.astype(jnp.float32) * o_raw.astype(jnp.float32)
    deltas = []
    for head in range(2):
        half = in_half(LEN, head)
        deltas.append(jnp.sum(jnp.where(half, product, 0.0), axis=1, keepdims=True))
    aug_do = (-triple_lanes(deltas[0], deltas[1], LEN)).astype(jnp.bfloat16)
    q_scaled = q_raw * jnp.bfloat16(SCALE)
    k_t = k_raw.T
    accs = {}
    for head in range(2):
        half = in_half(LEN, head)
        q = jnp.where(half, q_scaled, aug)
        k = jnp.where(half, k_raw, ak)
        v = jnp.where(half, v_raw, av)
        do = jnp.where(half, do_raw, aug_do)
        for j in range(LEN // TILE):
            lo = j * TILE
            hi = min(LEN, (j + 3) * TILE)
            width = hi - lo
            near = min(2 * TILE, width)
            scores = dot_nt(k[lo : lo + TILE], q[lo:hi])
            parts = [scores[:, :near] + bias_ref[head][:, :near]]
            if width > near:
                parts.append(scores[:, near:] + far[head : head + 1])
            scores = parts[0] if len(parts) == 1 else jnp.concatenate(parts, axis=1)
            probs = jnp.exp(scores)
            grad_probs = dot_nt(v[lo : lo + TILE], do[lo:hi])
            grad_scores = probs * grad_probs
            g_ref[head, :, :near] += grad_scores[:, :near]
            if width > near:
                gfar_ref[head] += jnp.sum(grad_scores[:, near:].reshape(TILE // 8, 8, TILE), axis=0)
            ds = grad_scores.astype(jnp.bfloat16)
            accs[j, head] = (dot_nn(ds, q[lo:hi]), dot_nn(probs.astype(jnp.bfloat16), do[lo:hi]))
            dqt_ref[head * HD : (head + 1) * HD, lo:hi] += dot_nn(
                k_t[head * HD : (head + 1) * HD, lo : lo + TILE], ds
            )
            if head == 1:
                lower = in_half(TILE, 0)
                rows = slice(lo, lo + TILE)
                put_dk(rows, jnp.where(lower, accs[j, 0][0], accs[j, 1][0]).astype(jnp.bfloat16))
                put_dv(rows, jnp.where(lower, accs[j, 0][1], accs[j, 1][1]).astype(jnp.bfloat16))
    dq = (dqt_ref[...] * SCALE).T.astype(jnp.bfloat16)
    rows = []
    for head in range(2):
        total = jnp.zeros((8, WIN), jnp.float32)
        pad = jnp.zeros((8, TILE), jnp.float32)
        for a in range(TILE // 8):
            strip = jnp.concatenate([pad, g_ref[head, 8 * a : 8 * a + 8, :]], axis=1)
            if a:
                strip = pltpu.roll(strip, WIN - 8 * a, 1)
            total = total + strip
        line_sum = jnp.zeros((1, WIN), jnp.float32)
        for s in range(8):
            one = total[s : s + 1]
            line_sum = line_sum + (pltpu.roll(one, WIN - s, 1) if s else one)
        rows.append(line_sum)
    lines = jnp.concatenate(rows, axis=0)
    lines = jnp.where(offsets >= 0, lines, 0.0)
    high, mid, low = split3(lines)
    sums = sum(dot_nt(part.astype(jnp.bfloat16), chosen) for part in (high, mid, low))
    lane32 = lax.broadcasted_iota(jnp.int32, (1, BUCKETS), 1)
    tables = []
    for head in range(2):
        far_sum = jnp.sum(gfar_ref[head])
        tables.append(sums[head : head + 1] + jnp.where(lane32 == BUCKETS - 1, far_sum, 0.0))
    return dq, None, None, tables


def any_spec():
    return pl.BlockSpec(memory_space=pl.ANY)


def last_block(n_blk, n_dp, plans, enc_plan, big, little, keys):
    every = list(plans) + [enc_plan]
    links = len(all_links(n_blk, n_dp))
    scratch = [item for plan in every for item in plan.scratch()]
    scratch += [
        pltpu.VMEM((POOL, LEN, D), jnp.bfloat16),
        pltpu.VMEM((LEN, D), jnp.float32),
        pltpu.VMEM((D, LEN), jnp.bfloat16),
        pltpu.VMEM((2, TILE, 2 * TILE), jnp.float32),
        pltpu.VMEM((2, TILE, 2 * TILE), jnp.float32),
        pltpu.VMEM((2, 8, TILE), jnp.float32),
        pltpu.VMEM((LANES, LEN), jnp.float32),
        pltpu.VMEM((3 + H, 1, D), jnp.float32),
        pltpu.VMEM((links, 3 + H, 1, D), jnp.float32),
        pltpu.SemaphoreType.DMA((links,)),
        pltpu.SemaphoreType.DMA((links,)),
        pltpu.SemaphoreType.DMA((len(big) + 3 * (keys // LEN) - 2 + 1,)),
        pltpu.SemaphoreType.DMA((LEN // ROWS,)),
    ]
    return pl.pallas_call(
        partial(last_kernel, n_blk, n_dp, plans, enc_plan),
        in_specs=[any_spec()] * len(big) + [vmem_spec()] * len(little),
        out_specs=[vmem_spec()] * len(every) + [any_spec(), vmem_spec()],
        out_shape=[plan.out_shape() for plan in every]
        + [jax.ShapeDtypeStruct((LEN, D), jnp.float32), jax.ShapeDtypeStruct((3 + H, 1, D), jnp.float32)],
        scratch_shapes=scratch,
        compiler_params=pltpu.CompilerParams(
            vmem_limit_bytes=VMEM_LIMIT, collective_id=1, has_side_effects=True
        ),
        cost_estimate=pl.CostEstimate(flops=40 * LEN * D * D, bytes_accessed=80 * LEN * D, transcendentals=0),
    )(*big, *little)


FF_STEPS = 4


def normal_cdf_pair(u):
    x = jnp.abs(u) * 0.7071067811865476
    gauss = jnp.exp(-0.5 * u * u)
    t = 1.0 / (1.0 + 0.3275911 * x)
    poly = ((((1.061405429 * t - 1.453152027) * t + 1.421413741) * t - 0.284496736) * t + 0.254829592) * t
    tail = 0.5 * poly * gauss
    return jnp.where(u >= 0, 1.0 - tail, tail), gauss * 0.3989422804014327


def rest_slot(owner, piece, order):
    slot = 0
    for axis, bit in order[1:]:
        mine = (lax.axis_index(axis) // (1 << bit)) % 2
        its = ((owner if axis == "blk" else piece) // (1 << bit)) % 2
        slot = 2 * slot + (its + mine) % 2
    return slot


def feed_kernel(plan_in, plan_out, y1_ref, oc_ref, wco_ref, gain_ref, g_ref, w1_ref, w2_ref,
                out_ref, isend_ref, ikeep_ref, osend_ref, okeep_ref, dy2_ref, e2_ref, doc_ref, dgain_ref,
                y2_ref, act_ref, acc_ref, da_ref, hid_ref, du_ref):
    step = pl.program_id(0)
    even_core = lax.axis_index("blk") % 2 == 0

    @pl.when(step == 0)
    def _():
        for r in range(0, LEN, ROWS):
            rows = slice(r, r + ROWS)
            y2 = y1_ref[rows] + dot_nn(oc_ref[rows], wco_ref[...])
            y2_ref[rows] = y2
            act_ref[rows] = (y2 * norm_parts(y2) * gain_ref[...]).astype(jnp.bfloat16)
        acc_ref[...] = y2_ref[...]
        da_ref[...] = jnp.zeros_like(da_ref)

    for r in range(0, LEN, ROWS):
        rows = slice(r, r + ROWS)
        u = dot_nn(act_ref[rows], w1_ref[...])
        dh = dot_nt(g_ref[rows], w2_ref[...])
        cdf, density = normal_cdf_pair(u)
        hid = (u * cdf).astype(jnp.bfloat16)
        du = (dh * (cdf + u * density)).astype(jnp.bfloat16)
        hid_ref[rows] = hid
        du_ref[rows] = du
        acc_ref[rows] += dot_nn(hid, w2_ref[...])
        da_ref[rows] += dot_nt(du, w1_ref[...])

    dw2 = dot_tn(hid_ref[...], g_ref[...])
    own_rows = plan_out.rows * plan_out.count
    group = dw2.shape[0] // own_rows
    for t in range(0, group, 2):
        for m in range(plan_out.count):
            piece, inner = m // plan_out.mats, m % plan_out.mats
            even = dw2[t * own_rows + m * plan_out.rows : t * own_rows + (m + 1) * plan_out.rows]
            odd = dw2[(t + 1) * own_rows + m * plan_out.rows : (t + 1) * own_rows + (m + 1) * plan_out.rows]
            slot = rest_slot(step * group + t, piece, plan_out.order)
            osend_ref[slot, inner] = jnp.where(even_core, odd, even).astype(jnp.bfloat16)
            okeep_ref[slot, inner] = jnp.where(even_core, even, odd).astype(jnp.bfloat16)
    dw1 = dot_tn(act_ref[...], du_ref[...])
    for t in range(0, plan_in.n_blk, 2):
        even = dw1[t * plan_in.rows : (t + 1) * plan_in.rows]
        odd = dw1[(t + 1) * plan_in.rows : (t + 2) * plan_in.rows]
        slot = rest_slot(t, step // plan_in.mats, plan_in.order)
        inner = step % plan_in.mats
        isend_ref[slot, inner] = jnp.where(even_core, odd, even).astype(jnp.bfloat16)
        ikeep_ref[slot, inner] = jnp.where(even_core, even, odd).astype(jnp.bfloat16)

    @pl.when(step == FF_STEPS - 1)
    def _():
        gain_sum = jnp.zeros((1, D), jnp.float32)
        for r in range(0, LEN, ROWS):
            rows = slice(r, r + ROWS)
            out_ref[rows] = acc_ref[rows].astype(jnp.bfloat16)
            y2 = y2_ref[rows]
            inverse = norm_parts(y2)
            da = da_ref[rows]
            gain_sum = gain_sum + jnp.sum(da * y2 * inverse, axis=0, keepdims=True)
            dy2 = g_ref[rows].astype(jnp.float32) + norm_back(y2, inverse, gain_ref[...], da)
            dy2_ref[rows] = dy2
            e2 = dy2.astype(jnp.bfloat16)
            e2_ref[rows] = e2
            doc_ref[rows] = dot_nt(e2, wco_ref[...]).astype(jnp.bfloat16)
        dgain_ref[...] = gain_sum


def feed_block(y1, oc, wco, gain, g, w1, w2, plan_in, plan_out):
    ff = w1.shape[1]
    cols = ff // FF_STEPS
    fixed = lambda shape: pl.BlockSpec(memory_space=pltpu.VMEM)
    half_in = (plan_in.slots // 2, plan_in.mats, plan_in.rows, D)
    half_out = (plan_out.slots // 2, plan_out.mats, plan_out.rows, D)
    like = jax.ShapeDtypeStruct
    return pl.pallas_call(
        partial(feed_kernel, plan_in, plan_out),
        grid=(FF_STEPS,),
        in_specs=[
            fixed((LEN, D)), fixed((LEN, D)), fixed((D, D)), fixed((1, D)), fixed((LEN, D)),
            pl.BlockSpec((D, cols), lambda c: (0, c)),
            pl.BlockSpec((cols, D), lambda c: (c, 0)),
        ],
        out_specs=[
            fixed((LEN, D)), fixed(half_in), fixed(half_in), fixed(half_out), fixed(half_out),
            fixed((LEN, D)), fixed((LEN, D)), fixed((LEN, D)), fixed((1, D)),
        ],
        out_shape=[
            like((LEN, D), jnp.bfloat16),
            like(half_in, jnp.bfloat16),
            like(half_in, jnp.bfloat16),
            like(half_out, jnp.bfloat16),
            like(half_out, jnp.bfloat16),
            like((LEN, D), jnp.float32),
            like((LEN, D), jnp.bfloat16),
            like((LEN, D), jnp.bfloat16),
            like((1, D), jnp.float32),
        ],
        scratch_shapes=[
            pltpu.VMEM((LEN, D), jnp.float32),
            pltpu.VMEM((LEN, D), jnp.bfloat16),
            pltpu.VMEM((LEN, D), jnp.float32),
            pltpu.VMEM((LEN, D), jnp.float32),
            pltpu.VMEM((LEN, cols), jnp.bfloat16),
            pltpu.VMEM((LEN, cols), jnp.bfloat16),
        ],
        compiler_params=pltpu.CompilerParams(vmem_limit_bytes=VMEM_LIMIT),
        cost_estimate=pl.CostEstimate(flops=12 * LEN * D * ff, bytes_accessed=40 * LEN * D, transcendentals=0),
    )(y1, oc, wco, gain, g, w1, w2)


def swap(value, axis, bit, size):
    return lax.ppermute(value, axis, [(i, i ^ (1 << bit)) for i in range(size)])


def total_of(terms):
    out = terms[0].astype(jnp.float32)
    for term in terms[1:]:
        out = out + term.astype(jnp.float32)
    return out


def gather_rows(rows, n_blk):
    out = rows
    masks = [0]
    for bit in reversed(range(bits_of(n_blk))):
        out = jnp.concatenate([out, swap(out, "blk", bit, n_blk)], axis=0)
        masks = masks + [mask | (1 << bit) for mask in masks]
    return out, masks


def scatter_step(terms, axis, bit, n):
    half = terms[0].shape[0] // 2
    send = total_of([t[half:] for t in terms]).astype(jnp.bfloat16)
    kept = total_of([t[:half] for t in terms]).astype(jnp.bfloat16)
    return [kept, swap(send, axis, bit, n)]


def per_device(
    decoder_rows,
    encoder_rows,
    target_lengths,
    target_question,
    passage_question,
    self_gain,
    self_query,
    self_key,
    self_value,
    self_output,
    position_bias_matrix,
    cross_gain,
    cross_query,
    cross_key,
    cross_value,
    cross_output,
    feed_gain,
    feed_input_weight,
    feed_out,
    cotangent,
    n_dp,
    n_blk,
):
    passage = encoder_rows.shape[0]
    sizes = {"blk": n_blk, "dp": n_dp}
    me = lax.axis_index("blk")
    encoder_all, masks = gather_rows(encoder_rows, n_blk)
    slot_device = me ^ jnp.array(masks, dtype=jnp.int32)
    slot_pick = slot_device[:, None] == jnp.arange(n_blk, dtype=jnp.int32)[None, :]
    slot_question = jnp.sum(jnp.where(slot_pick, passage_question[None, :], 0), axis=1)
    order = passage_order(slot_question)
    items = cross_items(target_lengths[0], target_question[0])
    positions = jnp.arange(LEN, dtype=jnp.int32)
    seg_ends = jnp.cumsum(target_lengths[0])
    segment = jnp.sum((positions[:, None] >= seg_ends[None, : TARGETS - 1]).astype(jnp.int32), axis=-1)
    aq, ak, av = segment_aug(segment)
    table_pairs = position_bias_matrix.T.reshape(PAIRS, 2, BUCKETS)
    self_gain2, cross_gain2, feed_gain2 = self_gain[None], cross_gain[None], feed_gain[None]

    inputs = decoder_rows.astype(jnp.float32)
    act_self = (inputs * norm_parts(inputs) * self_gain2).astype(jnp.bfloat16)
    query_self = dot_nn(act_self, self_query).astype(jnp.bfloat16)
    key_self = dot_nn(act_self, self_key).astype(jnp.bfloat16)
    value_self = dot_nn(act_self, self_value).astype(jnp.bfloat16)
    attn_self, aug_self = self_forward(query_self, key_self, value_self, aq, ak, table_pairs)
    attn_self, encoder_all = lax.optimization_barrier((attn_self, encoder_all))
    resid_self = inputs + dot_nn(attn_self, self_output)
    inv_cross = norm_parts(resid_self)
    act_cross = (resid_self * inv_cross * cross_gain2).astype(jnp.bfloat16)
    query_cross = dot_nn(act_cross, cross_query).astype(jnp.bfloat16)
    pair_weight = jnp.concatenate([cross_key, cross_value], axis=1)
    pair_all = dot_nn(encoder_all, pair_weight).astype(jnp.bfloat16)
    attn_cross, aug_cross = cross_forward(order, items, query_cross, pair_all, passage)

    plan_in, plan_out = feed_plans(n_blk, n_dp)
    (block_out, in_send, in_keep, out_send, out_keep, grad_resid_cross, round_cross, grad_attn_cross, gain_feed) = feed_block(
        resid_self, attn_cross, cross_output, feed_gain2, cotangent, feed_input_weight, feed_out, plan_in, plan_out
    )
    first_in, first_out = plan_in.order[0], plan_out.order[0]
    terms_in = [in_keep, swap(in_send, *first_in, sizes[first_in[0]])]
    terms_out = [out_keep, swap(out_send, *first_out, sizes[first_out[0]])]
    (terms_in, terms_out), grad_attn_cross = lax.optimization_barrier(((terms_in, terms_out), grad_attn_cross))
    step = lambda plan, terms, k: scatter_step(terms, *plan.order[k], sizes[plan.order[k][0]])
    next_in, next_out = step(plan_in, terms_in, 1), step(plan_out, terms_out, 1)
    dqc, dkv = cross_backward(
        order, items, query_cross, pair_all, grad_attn_cross, attn_cross, aug_cross, passage
    )
    (terms_in, terms_out), dqc, dkv = lax.optimization_barrier(((next_in, next_out), dqc, dkv))
    encoder_part = dot_nt(dkv, pair_weight).astype(jnp.bfloat16)
    da_cross = dot_nt(dqc, cross_query)
    gain_cross = jnp.sum(da_cross * resid_self * inv_cross, axis=0)
    grad_resid_self = grad_resid_cross + norm_back(resid_self, inv_cross, cross_gain2, da_cross)
    round_self = grad_resid_self.astype(jnp.bfloat16)
    grad_attn_self = dot_nt(round_self, self_output).astype(jnp.bfloat16)
    small = jnp.stack([jnp.zeros((1, D), jnp.float32), gain_cross[None], gain_feed])
    enc_plan = Exchange(1, passage, D, n_blk, n_dp, "near")
    big = (
        decoder_rows, grad_resid_self, act_self, self_query, self_key, self_value, act_cross, dqc, encoder_all, dkv,
        attn_cross, round_cross, query_self, key_self, value_self, grad_attn_self, attn_self, aug_self,
        terms_in[0], terms_in[1], terms_out[0], terms_out[1], encoder_part.reshape(n_blk, 1, passage, D),
    )
    feed_in, feed_out_sum, crossx, crossy, self0, self1, self2, grad_encoder, grad_decoder, sums = last_block(
        n_blk, n_dp, last_plans(n_blk, n_dp), enc_plan, big, (self_gain2, ak, av, table_pairs, small), encoder_all.shape[0]
    )
    rows = D // n_blk
    wide = lambda units: jnp.concatenate(units, axis=1)
    self_w = [wide([part[2 * w + c] for part in (self0, self1, self2) for c in range(2)]) for w in range(3)]
    cross_w = [wide([crossx[2 * w], crossx[2 * w + 1]]) for w in range(3)]
    out_w = [wide([crossy[2 * w], crossy[2 * w + 1]]) for w in range(2)]
    return (
        block_out,
        grad_decoder,
        grad_encoder[0],
        sums[0, 0],
        self_w[0],
        self_w[1],
        self_w[2],
        out_w[1],
        sums[3:, 0, :BUCKETS].T,
        sums[1, 0],
        cross_w[0],
        cross_w[1],
        cross_w[2],
        out_w[0],
        sums[2, 0],
        wide([feed_in[m] for m in range(4)]),
        feed_out_sum.reshape(-1, D),
    )


def solution(mesh):
    split, copied, owned = P(("dp", "blk"), None), P(), P("blk", None)
    return jax.shard_map(
        partial(per_device, n_dp=mesh.shape["dp"], n_blk=mesh.shape["blk"]),
        mesh=mesh,
        in_specs=(split,) * 4 + (P("dp"),) + (copied,) * 14 + (split,),
        out_specs=(split,) * 3 + (copied,) + (owned,) * 4 + (copied,) * 2 + (owned,) * 4 + (copied,) + (owned,) * 2,
        check_vma=False,
    )
```

```python
import functools
from functools import partial

import jax
import jax.numpy as jnp
from jax import lax
from jax.experimental import pallas as pl
from jax.experimental.pallas import tpu as pltpu
from jax.sharding import PartitionSpec as P

D = 768
H = 12
HD = 64
BUCKETS = 32
LEN = 1024
TARGETS = 4
PAIRS = H // 2
LANES = 2 * HD
TILE = 256
SCALE = HD ** -0.5
NEG = -1e30
VMEM_LIMIT = 60 * 1024 * 1024

eps_norm = 1e-06
bucket_edges = (19, 21, 24, 27, 31, 35, 40, 46, 52, 59, 67, 77, 87, 99, 113)


def dot_nn(a, b):
    return jnp.dot(a, b, preferred_element_type=jnp.float32)


def dot_nt(a, b):
    return lax.dot_general(a, b, (((1,), (1,)), ((), ())), preferred_element_type=jnp.float32)


def dot_tn(a, b):
    return lax.dot_general(a, b, (((0,), (0,)), ((), ())), preferred_element_type=jnp.float32)


def lane_ids(rows):
    return lax.broadcasted_iota(jnp.int32, (rows, LANES), 1)


def in_half(rows, head):
    lane = lane_ids(rows)
    return lane < HD if head == 0 else lane >= HD


def split3(value):
    high = value.astype(jnp.bfloat16).astype(jnp.float32)
    rest = value - high
    mid = rest.astype(jnp.bfloat16).astype(jnp.float32)
    return high, mid, rest - mid


def triple_lanes(first, second, rows):
    lane = lane_ids(rows)
    out = jnp.zeros((rows, LANES), jnp.float32)
    for base, value in ((HD, first), (0, second)):
        for place, part in enumerate(split3(value)):
            out = jnp.where(lane == base + place, part, out)
    return out


def bucket_vector(table_t, offsets):
    upper = jnp.full(offsets.shape, 16, jnp.int32)
    for edge in bucket_edges:
        upper = upper + (offsets >= edge).astype(jnp.int32)
    bucket = jnp.where(offsets < 16, offsets, upper)
    rows = lax.broadcasted_iota(jnp.int32, (BUCKETS, offsets.shape[1]), 0)
    chosen = (rows == bucket).astype(jnp.float32).astype(jnp.bfloat16)
    return chosen


WIN = 3 * TILE


ROWS = 256


def norm_parts(values):
    return lax.rsqrt(jnp.mean(values * values, axis=1, keepdims=True) + eps_norm)


def norm_back(values, inverse, gain, grad):
    scaled = grad * gain
    inner = jnp.mean(scaled * values, axis=1, keepdims=True)
    return inverse * scaled - values * (inverse * inverse * inverse * inner)


CT = 256


def cross_layout(n_blk, lengths_ref, question_ref, passage_ref, order_ref, item_ref, count_ref):
    per_q = n_blk // TARGETS
    bits = bits_of(n_blk)
    me = lax.axis_index("blk")
    for t in range(TARGETS + 1):
        count_ref[t] = 0
    for s in range(n_blk):
        device = 0
        for b in range(bits):
            mine = (me // (1 << b)) % 2
            flip = (s >> (bits - 1 - b)) & 1
            device = device + (1 - mine if flip else mine) * (1 << b)
        question = passage_ref[device]
        order_ref[question * per_q + count_ref[question]] = s
        count_ref[question] = count_ref[question] + 1
    end = 0
    for t in range(TARGETS):
        start, end = end, end + lengths_ref[0, t]
        question = question_ref[0, t]

        @pl.loop(start // CT, (end + CT - 1) // CT)
        def _(tile, start=start, end=end, question=question):
            n = count_ref[TARGETS]
            item_ref[0, n] = tile
            item_ref[1, n] = question
            item_ref[2, n] = start - tile * CT
            item_ref[3, n] = end - tile * CT
            count_ref[TARGETS] = n + 1


def layout_scratch(n_blk):
    return [
        pltpu.SMEM((n_blk,), jnp.int32),
        pltpu.SMEM((4, LEN // CT + TARGETS), jnp.int32),
        pltpu.SMEM((TARGETS + 1,), jnp.int32),
    ]


def cross_forward_kernel(n_blk, passage, lengths_ref, question_ref, passage_ref, q_ref, kv_ref, o_ref, aug_ref,
                         ks_ref, vs_ref, order_ref, item_ref, count_ref):
    keys_q = n_blk // TARGETS * passage
    lower = lax.broadcasted_iota(jnp.int32, (passage, D), 1) % LANES < HD
    zero = jnp.zeros((), jnp.bfloat16)
    cross_layout(n_blk, lengths_ref, question_ref, passage_ref, order_ref, item_ref, count_ref)

    @pl.loop(0, n_blk)
    def _(s):
        src = pl.multiple_of(order_ref[s] * passage, passage)
        dst = pl.multiple_of(s * passage, passage)
        keys = kv_ref[pl.ds(src, passage), :D]
        values = kv_ref[pl.ds(src, passage), D:]
        ks_ref[0, pl.ds(dst, passage)] = jnp.where(lower, keys, zero)
        ks_ref[1, pl.ds(dst, passage)] = jnp.where(lower, zero, keys)
        vs_ref[0, pl.ds(dst, passage)] = jnp.where(lower, values, zero)
        vs_ref[1, pl.ds(dst, passage)] = jnp.where(lower, zero, values)

    o_ref[...] = jnp.zeros_like(o_ref)
    aug_ref[...] = jnp.zeros_like(aug_ref)

    @pl.loop(0, count_ref[TARGETS])
    def _(n):
        row0 = pl.multiple_of(item_ref[0, n] * CT, CT)
        key0 = pl.multiple_of(item_ref[1, n] * keys_q, keys_q)
        rows = lax.broadcasted_iota(jnp.int32, (CT, 1), 0)
        valid = (rows >= item_ref[2, n]) & (rows < item_ref[3, n])
        for pair in range(PAIRS):
            cols = slice(pair * LANES, (pair + 1) * LANES)
            q = q_ref[pl.ds(row0, CT), cols] * jnp.bfloat16(SCALE)
            outs, logs = [], []
            for head in range(2):
                scores = dot_nt(q, ks_ref[head, pl.ds(key0, keys_q), cols])
                top = jnp.max(scores, axis=1, keepdims=True)
                expo = jnp.exp(scores - top)
                total = jnp.sum(expo, axis=1, keepdims=True)
                outs.append(dot_nn(expo.astype(jnp.bfloat16), vs_ref[head, pl.ds(key0, keys_q), cols]) / total)
                logs.append(top + jnp.log(total))
            mixed = (outs[0] + outs[1]).astype(jnp.bfloat16)
            aug = triple_lanes(logs[0], logs[1], CT).astype(jnp.bfloat16)
            o_ref[pl.ds(row0, CT), cols] = jnp.where(valid, mixed, o_ref[pl.ds(row0, CT), cols])
            aug_ref[pl.ds(row0, CT), cols] = jnp.where(valid, aug, aug_ref[pl.ds(row0, CT), cols])


def smem_spec():
    return pl.BlockSpec(memory_space=pltpu.SMEM)


def vmem_spec():
    return pl.BlockSpec(memory_space=pltpu.VMEM)


def any_spec():
    return pl.BlockSpec(memory_space=pl.ANY)


def cross_forward(n_blk, passage, lengths, questions, passages, q, kv):
    keys = kv.shape[0]
    return pl.pallas_call(
        partial(cross_forward_kernel, n_blk, passage),
        in_specs=[smem_spec()] * 3 + [vmem_spec()] * 2,
        out_specs=[vmem_spec(), vmem_spec()],
        out_shape=[jax.ShapeDtypeStruct((LEN, D), jnp.bfloat16)] * 2,
        scratch_shapes=[pltpu.VMEM((2, keys, D), jnp.bfloat16)] * 2 + layout_scratch(n_blk),
        compiler_params=pltpu.CompilerParams(vmem_limit_bytes=VMEM_LIMIT),
        cost_estimate=pl.CostEstimate(flops=2 * H * LEN * LEN * HD, bytes_accessed=10 * LEN * D, transcendentals=0),
    )(lengths, questions, passages, q, kv)


def cross_backward_kernel(n_blk, passage, lengths_ref, question_ref, passage_ref, q_ref, do_ref, o_ref, aug_ref,
                          kv_hbm, y1_hbm, dy2_hbm, wcq_hbm, wck_hbm, wcv_hbm, wo_hbm, gain_ref,
                          dq_ref, dkv_ref, dy1_ref, dos_ref, part_ref, dgain_ref,
                          ks_ref, vs_ref, kt_ref, dk_ref, dv_ref, dqt_ref, y1_ref, load_sem,
                          order_ref, item_ref, count_ref):
    loads = []
    for n, (src, dst) in enumerate(
        [(kv_hbm, dkv_ref), (y1_hbm, y1_ref), (dy2_hbm, dy1_ref)]
    ):
        loads.append(pltpu.make_async_copy(src, dst, load_sem.at[n]))
        loads[-1].start()
    keys_q = n_blk // TARGETS * passage
    lane = lax.broadcasted_iota(jnp.int32, (passage, D), 1) % LANES
    lower = lane < HD
    ones = jnp.where((lane & (HD - 1)) < 3, 1.0, 0.0).astype(jnp.bfloat16)
    minus = -ones
    cross_layout(n_blk, lengths_ref, question_ref, passage_ref, order_ref, item_ref, count_ref)

    loads[0].wait()

    @pl.loop(0, n_blk)
    def _(s):
        src = pl.multiple_of(order_ref[s] * passage, passage)
        dst = pl.multiple_of(s * passage, passage)
        keys = dkv_ref[pl.ds(src, passage), :D]
        values = dkv_ref[pl.ds(src, passage), D:]
        ks_ref[0, pl.ds(dst, passage)] = jnp.where(lower, keys, minus)
        ks_ref[1, pl.ds(dst, passage)] = jnp.where(lower, minus, keys)
        vs_ref[0, pl.ds(dst, passage)] = jnp.where(lower, values, ones)
        vs_ref[1, pl.ds(dst, passage)] = jnp.where(lower, ones, values)

    lower_k = lax.broadcasted_iota(jnp.int32, (keys_q, LANES), 1) < HD
    for s in range(TARGETS):
        for pair in range(PAIRS):
            rows = slice(s * keys_q, (s + 1) * keys_q)
            cols = slice(pair * LANES, (pair + 1) * LANES)
            both = jnp.where(lower_k, ks_ref[0, rows, cols], ks_ref[1, rows, cols])
            kt_ref[cols, rows] = both.T
    dk_ref[...] = jnp.zeros_like(dk_ref)
    dv_ref[...] = jnp.zeros_like(dv_ref)
    dqt_ref[...] = jnp.zeros_like(dqt_ref)

    @pl.loop(0, count_ref[TARGETS])
    def _(n):
        row0 = pl.multiple_of(item_ref[0, n] * CT, CT)
        key0 = pl.multiple_of(item_ref[1, n] * keys_q, keys_q)
        rows = lax.broadcasted_iota(jnp.int32, (CT, 1), 0)
        valid = (rows >= item_ref[2, n]) & (rows < item_ref[3, n])
        here = pl.ds(row0, CT)
        there = pl.ds(key0, keys_q)
        for pair in range(PAIRS):
            cols = slice(pair * LANES, (pair + 1) * LANES)
            q_scaled = q_ref[here, cols] * jnp.bfloat16(SCALE)
            do_pair = jnp.where(valid, do_ref[here, cols], jnp.zeros((), jnp.bfloat16))
            product = do_pair.astype(jnp.float32) * o_ref[here, cols].astype(jnp.float32)
            deltas = []
            for head in range(2):
                deltas.append(jnp.sum(jnp.where(in_half(CT, head), product, 0.0), axis=1, keepdims=True))
            aug_do = (-triple_lanes(deltas[0], deltas[1], CT)).astype(jnp.bfloat16)
            aug = jnp.where(valid, aug_ref[here, cols], jnp.bfloat16(-NEG))
            parts = []
            for head in range(2):
                half = in_half(CT, head)
                q = jnp.where(half, q_scaled, aug)
                do = jnp.where(half, do_pair, aug_do)
                probs = jnp.exp(dot_nt(ks_ref[head, there, cols], q))
                grad_scores = probs * dot_nt(vs_ref[head, there, cols], do)
                ds = grad_scores.astype(jnp.bfloat16)
                parts.append((dot_nn(ds, q), dot_nn(probs.astype(jnp.bfloat16), do)))
                hrow = pair * LANES + head * HD
                dqt_ref[hrow : hrow + HD, here] += dot_nn(kt_ref[hrow : hrow + HD, there], ds)
            dk_ref[there, cols] += jnp.where(lower_k, parts[0][0], parts[1][0])
            dv_ref[there, cols] += jnp.where(lower_k, parts[0][1], parts[1][1])

    spots = (ks_ref.at[0], ks_ref.at[1], vs_ref.at[0], vs_ref.at[1])
    for n, w in enumerate((wcq_hbm, wck_hbm, wcv_hbm, wo_hbm)):
        loads.append(pltpu.make_async_copy(w, spots[n].at[pl.ds(0, D)], load_sem.at[3 + n]))
        loads[-1].start()
    for pair in range(PAIRS):
        cols = slice(pair * LANES, (pair + 1) * LANES)
        dq_ref[:, cols] = (dqt_ref[cols, :] * SCALE).T.astype(jnp.bfloat16)

    for copy in loads[1:]:
        copy.wait()

    @pl.loop(0, n_blk)
    def _(s):
        src = pl.multiple_of(s * passage, passage)
        spot = order_ref[s]
        dst = pl.multiple_of(spot * passage, passage)
        dk = dk_ref[pl.ds(src, passage)].astype(jnp.bfloat16)
        dv = dv_ref[pl.ds(src, passage)].astype(jnp.bfloat16)
        dkv_ref[pl.ds(dst, passage), :D] = dk
        dkv_ref[pl.ds(dst, passage), D:] = dv

    group = ROWS // passage
    for s in range(0, n_blk, group):
        rows = slice(s * passage, (s + group) * passage)
        part = dot_nt(dkv_ref[rows, :D], ks_ref[1, :D]) + dot_nt(dkv_ref[rows, D:], vs_ref[0, :D])
        part_ref[s : s + group, 0] = part.astype(jnp.bfloat16).reshape(group, passage, D)
    gain_sum = jnp.zeros((1, D), jnp.float32)
    for r in range(0, LEN, ROWS):
        rows = slice(r, r + ROWS)
        da = dot_nt(dq_ref[rows], ks_ref[0, :D])
        y1 = y1_ref[rows]
        inverse = norm_parts(y1)
        gain_sum = gain_sum + jnp.sum(da * y1 * inverse, axis=0, keepdims=True)
        dy1 = dy1_ref[rows] + norm_back(y1, inverse, gain_ref[...], da)
        dy1_ref[rows] = dy1
        dos_ref[rows] = dot_nt(dy1.astype(jnp.bfloat16), vs_ref[1, :D]).astype(jnp.bfloat16)
    dgain_ref[...] = gain_sum


def cross_backward(n_blk, passage, lengths, questions, passages, q, kv, do, o, aug, y1, dy2, wcq, wck, wcv, wo, gain):
    keys = kv.shape[0]
    like = jax.ShapeDtypeStruct
    return pl.pallas_call(
        partial(cross_backward_kernel, n_blk, passage),
        in_specs=[smem_spec()] * 3 + [vmem_spec()] * 4 + [any_spec()] * 7 + [vmem_spec()],
        out_specs=[vmem_spec()] * 6,
        out_shape=[
            like((LEN, D), jnp.bfloat16),
            like((keys, 2 * D), jnp.bfloat16),
            like((LEN, D), jnp.float32),
            like((LEN, D), jnp.bfloat16),
            like((n_blk, 1, passage, D), jnp.bfloat16),
            like((1, D), jnp.float32),
        ],
        scratch_shapes=[pltpu.VMEM((2, keys, D), jnp.bfloat16)] * 2
        + [
            pltpu.VMEM((D, keys), jnp.bfloat16),
            pltpu.VMEM((keys, D), jnp.float32),
            pltpu.VMEM((keys, D), jnp.float32),
            pltpu.VMEM((D, LEN), jnp.float32),
            pltpu.VMEM((LEN, D), jnp.float32),
            pltpu.SemaphoreType.DMA((7,)),
        ]
        + layout_scratch(n_blk),
        compiler_params=pltpu.CompilerParams(vmem_limit_bytes=VMEM_LIMIT),
        cost_estimate=pl.CostEstimate(flops=5 * H * LEN * LEN * HD, bytes_accessed=18 * LEN * D, transcendentals=0),
    )(lengths, questions, passages, q, do, o, aug, kv, y1, dy2, wcq, wck, wcv, wo, gain)


def bits_of(count):
    return count.bit_length() - 1


def place_bits(n_blk, n_dp, kind):
    blk = [("blk", bit) for bit in range(bits_of(n_blk))]
    dp = [("dp", bit) for bit in range(bits_of(n_dp))]
    if kind == "x":
        return blk[:1] + dp + blk[1:]
    if kind == "y":
        return blk[:2] + dp + blk[2:]
    return blk


def position(owner, piece, order):
    slot = 0
    for axis, bit in order:
        mine = (lax.axis_index(axis) // (1 << bit)) % 2
        static = ((owner if axis == "blk" else piece) >> bit) & 1
        slot = 2 * slot + (1 - mine if static else mine)
    return slot


def partner(axis, bit):
    me = lax.axis_index(axis)
    mine = (me // (1 << bit)) % 2
    return {axis: me + (1 - 2 * mine) * (1 << bit)}


class Exchange:
    def __init__(self, count, rows, cols, n_blk, n_dp, kind, first=0):
        if kind in "xy" and count % n_dp:
            kind = "plain"
        self.n_blk, self.n_dp, self.count, self.kind, self.first = n_blk, n_dp, count, kind, first
        self.rows, self.cols = rows, cols
        self.order = place_bits(n_blk, n_dp, kind)
        self.pieces = n_dp if kind in "xy" else 1
        self.slots = n_blk * self.pieces
        self.mats = count // self.pieces
        self.last = [("dp", bit) for bit in range(bits_of(n_dp))] if kind != "near" else []
        self.steps = len(self.order) + len(self.last)
        self.held = self.slots >> first
        self.offsets = {}
        at = self.held if first else 0
        for k in range(first, len(self.order)):
            size = self.slots >> (k + 1)
            self.offsets[k] = (at, size)
            at += size
        for j in range(len(self.last)):
            size = (1 << j) if self.pieces > 1 else 1
            self.offsets[len(self.order) + j] = (at, size)
            at += size
        self.received = at

    def scratch(self):
        shape = (self.mats, self.rows, self.cols)
        return [
            pltpu.VMEM((max(self.held, self.pieces),) + shape, jnp.bfloat16),
            pltpu.VMEM((self.received,) + shape, jnp.bfloat16),
            pltpu.SemaphoreType.DMA((self.steps,)),
            pltpu.SemaphoreType.DMA((self.steps,)),
        ]

    def out_shape(self):
        return jax.ShapeDtypeStruct((self.count, self.rows, self.cols), jnp.float32)

    def bind(self, refs, out_ref):
        self.buf, self.recv, self.send_sem, self.recv_sem = refs
        self.out = out_ref

    def put(self, index, value):
        piece, inner = index // self.mats, index % self.mats
        for owner in range(self.n_blk):
            slot = position(owner, piece, self.order)
            self.buf[slot, inner] = value[owner * self.rows : (owner + 1) * self.rows].astype(jnp.bfloat16)

    def copy(self, k):
        at, size = self.offsets[k]
        if k < len(self.order):
            axis, bit = self.order[k]
            src = self.buf.at[pl.ds(size, size)]
        else:
            axis, bit = self.last[k - len(self.order)]
            src = self.buf.at[pl.ds(0, size)]
        return pltpu.make_async_remote_copy(
            src_ref=src,
            dst_ref=self.recv.at[pl.ds(at, size)],
            send_sem=self.send_sem.at[k],
            recv_sem=self.recv_sem.at[k],
            device_id=partner(axis, bit),
            device_id_type=pl.DeviceIdType.MESH,
        )

    def start(self, k):
        self.copy(k).start()

    def add(self, at, size, final):
        for s in range(size):
            for m in range(self.mats):
                total = self.buf[s, m].astype(jnp.float32) + self.recv[at + s, m].astype(jnp.float32)
                if final:
                    self.out[m] = total
                else:
                    self.buf[s, m] = total.astype(jnp.bfloat16)

    def finish(self, k):
        self.copy(k).wait()
        at, size = self.offsets[k]
        final = k == self.steps - 1
        if k < len(self.order) or self.pieces == 1:
            self.add(at, size, final)
            return
        for s in range(size):
            for m in range(self.mats):
                self.buf[size + s, m] = self.recv[at + s, m]
        if final:
            for s in range(self.pieces):
                spot = position(0, s, self.last[::-1])
                for m in range(self.mats):
                    self.out[spot * self.mats + m] = self.buf[s, m].astype(jnp.float32)

    def advance(self, k):
        if k < self.first or k >= self.steps:
            return
        self.finish(k)
        if k + 1 < self.steps:
            self.start(k + 1)


def all_links(n_blk, n_dp):
    return [("blk", bit) for bit in range(bits_of(n_blk))] + [("dp", bit) for bit in range(bits_of(n_dp))]


def enter_barrier(n_blk, n_dp):
    barrier = pltpu.get_barrier_semaphore()
    links = all_links(n_blk, n_dp)
    for axis, bit in links:
        pl.semaphore_signal(barrier, inc=1, device_id=partner(axis, bit), device_id_type=pl.DeviceIdType.MESH)
    pl.semaphore_wait(barrier, len(links))


BLOCKS = 3
BLOCK = D // BLOCKS


def last_plans(n_blk, n_dp):
    rows = D // n_blk
    halves = 2
    feed_in, feed_out = feed_plans(n_blk, n_dp, 2)
    plans = [
        feed_in,
        feed_out,
        Exchange(3 * halves, rows, D // halves, n_blk, n_dp, "x"),
        Exchange(2 * halves, rows, D // halves, n_blk, n_dp, "y"),
    ]
    for block in range(BLOCKS):
        plans.append(Exchange(3 * halves, rows, BLOCK // halves, n_blk, n_dp, "xyx"[block]))
    return plans


def feed_plans(n_blk, n_dp, first=0):
    rows = D // n_blk
    return (
        Exchange(4, rows, D, n_blk, n_dp, "y", first),
        Exchange(4, rows, D, n_blk, n_dp, "x", first),
    )


POOL = 11
(S_ACTC, S_DQC, S_OC, S_E2, S_Q, S_K, S_V, S_DO, S_O, S_AUG, S_X) = range(POOL)
S_DQ, S_DK, S_DV, S_ACT = S_ACTC, S_DQC, S_OC, S_E2


def last_kernel(n_blk, n_dp, plans, enc_plan, *refs):
    (x_hbm, dy1_hbm, act_hbm, wq_hbm, wk_hbm, wv_hbm, actc_hbm, dqc_hbm, enc_hbm, dkv_hbm, oc_hbm, e2_hbm,
     q_hbm, k_hbm, v_hbm, do_hbm, o_hbm, aug_hbm, inkeep_hbm, inrecv_hbm, outkeep_hbm, outrecv_hbm, part_hbm,
     lengths_ref, gain_ref, table_ref, gainc_ref, gainf_ref) = refs[:28]
    every = list(plans) + [enc_plan]
    outs = refs[28 : 28 + len(every)]
    dx_hbm, sums_ref = refs[28 + len(every) : 30 + len(every)]
    scratch = refs[30 + len(every) :]
    for i, plan in enumerate(every):
        plan.bind(scratch[4 * i : 4 * i + 4], outs[i])
    (pool, dy1_ref, act_t, bias_ref, g_ref, gfar_ref, dqt_ref,
     tot_ref, got_ref, tsend, trecv, load_sem, store_sem) = scratch[4 * len(every) :]
    feed_in, feed_out, crossx, crossy, self0, self1, self2 = plans
    selfs = (self0, self1, self2)

    loads = {}

    def load(name, src, dst):
        loads[name] = pltpu.make_async_copy(src, dst, load_sem.at[len(loads)])
        loads[name].start()

    def slot(index):
        return pool.at[index]

    load("actc", actc_hbm, slot(S_ACTC))
    load("dqc", dqc_hbm, slot(S_DQC))
    for plan, keep, got, name in (
        (feed_out, outkeep_hbm, outrecv_hbm, "out"),
        (feed_in, inkeep_hbm, inrecv_hbm, "in"),
    ):
        load(name + "keep", keep, plan.buf.at[pl.ds(0, plan.held)])
        load(name + "recv", got, plan.recv.at[pl.ds(0, plan.held)])
    spans = enc_hbm.shape[0] // LEN
    spare = (S_Q, S_K, S_V, S_DO, S_AUG, S_X)
    for n in range(spans):
        rows = pl.ds(n * LEN, LEN)
        load(("enc", n), enc_hbm.at[rows], slot(spare[3 * n]))
        load(("dk", n), dkv_hbm.at[rows, pl.ds(0, D)], slot(spare[3 * n + 1]))
        load(("dv", n), dkv_hbm.at[rows, pl.ds(D, D)], slot(spare[3 * n + 2]))
    load("part", part_hbm, enc_plan.buf)
    load("oc", oc_hbm, slot(S_OC))
    load("e2", e2_hbm, slot(S_E2))
    load("o", o_hbm, slot(S_O))
    load("dy1", dy1_hbm, dy1_ref)
    enter_barrier(n_blk, n_dp)

    def begin_feed(plan, name):
        loads[name + "keep"].wait()
        loads[name + "recv"].wait()
        plan.add(0, plan.held, False)
        plan.start(plan.first)

    def put_halves(plan, index, value):
        half = plan.cols
        for c in range(2):
            plan.put(2 * index + c, value[:, c * half : (c + 1) * half])

    begin_feed(feed_out, "out")
    begin_feed(feed_in, "in")
    loads["actc"].wait()
    loads["dqc"].wait()
    put_halves(crossx, 0, dot_tn(pool[S_ACTC], pool[S_DQC]))
    for w, name in ((1, "dk"), (2, "dv")):
        total = None
        for n in range(spans):
            if w == 1:
                loads["enc", n].wait()
            loads[name, n].wait()
            part = dot_tn(pool[spare[3 * n]], pool[spare[3 * n + w]])
            total = part if total is None else total + part
        put_halves(crossx, w, total)
    crossx.start(0)
    for name, src, index in (
        ("q", q_hbm, S_Q), ("k", k_hbm, S_K), ("v", v_hbm, S_V), ("do", do_hbm, S_DO), ("aug", aug_hbm, S_AUG), ("x", x_hbm, S_X),
    ):
        load(name, src, slot(index))
    loads["part"].wait()
    enc_plan.start(0)
    loads["oc"].wait()
    loads["e2"].wait()
    put_halves(crossy, 0, dot_tn(pool[S_OC], pool[S_E2]))
    loads["o"].wait()
    loads["dy1"].wait()
    put_halves(crossy, 1, dot_tn(pool[S_O], dy1_ref[...].astype(jnp.bfloat16)))
    crossy.start(0)
    load("act", act_hbm, slot(S_ACT))
    crossx.advance(0)
    for name in ("q", "k", "v", "do", "aug"):
        loads[name].wait()
    loads["act"].wait()
    act_t[...] = pool[S_ACT].T
    crossy.advance(0)
    enc_plan.advance(0)

    offsets = lax.broadcasted_iota(jnp.int32, (1, WIN), 1) - TILE
    chosen = bucket_vector(None, jnp.maximum(offsets, 0))

    def pair_body(p):
        lanes = pl.ds(pl.multiple_of(p * LANES, LANES), LANES)
        dq, dk, dv, sums = self_pair_backward(
            pool[S_Q, :, lanes], pool[S_K, :, lanes], pool[S_V, :, lanes], pool[S_DO, :, lanes], pool[S_O, :, lanes],
            pool[S_AUG, :, lanes], ak, av, table_ref[p], offsets, chosen,
            bias_ref, g_ref, gfar_ref, dqt_ref,
            lambda rows, value: pool.__setitem__((S_DK, rows, lanes), value),
            lambda rows, value: pool.__setitem__((S_DV, rows, lanes), value),
        )
        pool[S_DQ, :, lanes] = dq
        for head in range(2):
            tot_ref[3 + 2 * p + head] = jnp.concatenate(
                [sums[head], jnp.zeros((1, D - BUCKETS), jnp.float32)], axis=1
            )

    tot_ref[1] = gainc_ref[...]
    tot_ref[2] = gainf_ref[...]
    ak, av = key_marks(segment_rows(lengths_ref)), value_marks(LEN)
    rounds = {
        0: [],
        1: [(feed_out, 2), (feed_in, 2)],
        2: [(crossy, 1)],
        3: [(crossx, 1), (feed_out, 3), (feed_in, 3), (enc_plan, 1)],
        4: [(crossy, 2), (self0, 0)],
        5: [(feed_out, 4), (feed_in, 4), (enc_plan, 2)],
    }
    per_block = PAIRS // BLOCKS
    for block in range(BLOCKS):
        for inner in range(per_block):
            p = block * per_block + inner
            for plan, k in rounds[p]:
                plan.advance(k)
            pair_body(p)
        cols = slice(block * BLOCK, (block + 1) * BLOCK)
        for w, index in enumerate((S_DQ, S_DK, S_DV)):
            put_halves(selfs[block], w, dot_nn(act_t[...], pool[index, :, cols]))
        selfs[block].start(0)
    wq, wk, wv = slot(S_Q), slot(S_K), slot(S_V)
    for name, src, index in (("wq", wq_hbm, S_Q), ("wk", wk_hbm, S_K), ("wv", wv_hbm, S_V)):
        load(name, src, pool.at[index, pl.ds(0, D)])
    crossx.advance(2)
    self1.advance(0)
    for name in ("wq", "wk", "wv", "x"):
        loads[name].wait()
    pending = [
        [(crossy, 3), (self0, 1), (enc_plan, 3), (self2, 0)],
        [(crossx, 3), (feed_out, 5), (feed_in, 5)],
        [(self1, 1), (crossy, 4), (self0, 2)],
        [(crossx, 4), (self2, 1)],
    ]
    gain_sum = jnp.zeros((1, D), jnp.float32)
    stores = []
    for i, r in enumerate(range(0, LEN, ROWS)):
        rows = slice(r, r + ROWS)
        da = (
            dot_nt(pool[S_DQ, rows], pool[S_Q, :D])
            + dot_nt(pool[S_DK, rows], pool[S_K, :D])
            + dot_nt(pool[S_DV, rows], pool[S_V, :D])
        )
        x = pool[S_X, rows].astype(jnp.float32)
        inverse = norm_parts(x)
        gain_sum = gain_sum + jnp.sum(da * x * inverse, axis=0, keepdims=True)
        dy1_ref[rows] = dy1_ref[rows] + norm_back(x, inverse, gain_ref[...], da)
        stores.append(pltpu.make_async_copy(dy1_ref.at[rows], dx_hbm.at[rows], store_sem.at[i]))
        stores[-1].start()
        for plan, k in pending[i]:
            plan.advance(k)
    tot_ref[0] = gain_sum
    links = all_links(n_blk, n_dp)

    def small_copy(j):
        axis, bit = links[j]
        return pltpu.make_async_remote_copy(
            src_ref=tot_ref,
            dst_ref=got_ref.at[j],
            send_sem=tsend.at[j],
            recv_sem=trecv.at[j],
            device_id=partner(axis, bit),
            device_id_type=pl.DeviceIdType.MESH,
        )

    small_copy(0).start()
    done = {feed_in: 5, feed_out: 5, crossx: 4, crossy: 4, enc_plan: 3, self0: 2, self1: 1, self2: 1}
    longest = max(plan.steps for plan in every)
    j = 0
    while True:
        for plan in (self2, self1, self0, crossx, crossy, feed_out, feed_in, enc_plan):
            done[plan] += 1
            plan.advance(done[plan])
        if j < len(links):
            small_copy(j).wait()
            tot_ref[...] = tot_ref[...] + got_ref[j]
            j += 1
            if j < len(links):
                small_copy(j).start()
        if j == len(links) and all(done[plan] >= plan.steps - 1 for plan in every):
            break
    sums_ref[...] = tot_ref[...]
    for store in stores:
        store.wait()


def self_pair_backward(q_raw, k_raw, v_raw, do_raw, o_raw, aug, ak, av, table, offsets, chosen,
                       bias_ref, g_ref, gfar_ref, dqt_ref, put_dk, put_dv):
    line = dot_nn(table, chosen)
    line = jnp.where(offsets >= 0, line, NEG)
    far = table[:, BUCKETS - 1 :].astype(jnp.float32)
    for head in range(2):
        spread = jnp.broadcast_to(line[head : head + 1], (TILE, WIN))
        bias_ref[head] = pltpu.roll(spread, 0, 1, stride=1, stride_axis=0)[:, TILE:]
    g_ref[...] = jnp.zeros_like(g_ref)
    gfar_ref[...] = jnp.zeros_like(gfar_ref)
    dqt_ref[...] = jnp.zeros_like(dqt_ref)
    product = do_raw.astype(jnp.float32) * o_raw.astype(jnp.float32)
    deltas = []
    for head in range(2):
        half = in_half(LEN, head)
        deltas.append(jnp.sum(jnp.where(half, product, 0.0), axis=1, keepdims=True))
    aug_do = (-triple_lanes(deltas[0], deltas[1], LEN)).astype(jnp.bfloat16)
    q_scaled = q_raw * jnp.bfloat16(SCALE)
    k_t = k_raw.T
    accs = {}
    for head in range(2):
        half = in_half(LEN, head)
        q = jnp.where(half, q_scaled, aug)
        k = jnp.where(half, k_raw, ak)
        v = jnp.where(half, v_raw, av)
        do = jnp.where(half, do_raw, aug_do)
        for j in range(LEN // TILE):
            lo = j * TILE
            hi = min(LEN, (j + 3) * TILE)
            width = hi - lo
            near = min(2 * TILE, width)
            scores = dot_nt(k[lo : lo + TILE], q[lo:hi])
            parts = [scores[:, :near] + bias_ref[head][:, :near]]
            if width > near:
                parts.append(scores[:, near:] + far[head : head + 1])
            scores = parts[0] if len(parts) == 1 else jnp.concatenate(parts, axis=1)
            probs = jnp.exp(scores)
            grad_probs = dot_nt(v[lo : lo + TILE], do[lo:hi])
            grad_scores = probs * grad_probs
            g_ref[head, :, :near] += grad_scores[:, :near]
            if width > near:
                gfar_ref[head] += jnp.sum(grad_scores[:, near:].reshape(TILE // 8, 8, TILE), axis=0)
            ds = grad_scores.astype(jnp.bfloat16)
            accs[j, head] = (dot_nn(ds, q[lo:hi]), dot_nn(probs.astype(jnp.bfloat16), do[lo:hi]))
            dqt_ref[head * HD : (head + 1) * HD, lo:hi] += dot_nn(
                k_t[head * HD : (head + 1) * HD, lo : lo + TILE], ds
            )
            if head == 1:
                lower = in_half(TILE, 0)
                rows = slice(lo, lo + TILE)
                put_dk(rows, jnp.where(lower, accs[j, 0][0], accs[j, 1][0]).astype(jnp.bfloat16))
                put_dv(rows, jnp.where(lower, accs[j, 0][1], accs[j, 1][1]).astype(jnp.bfloat16))
    dq = (dqt_ref[...] * SCALE).T.astype(jnp.bfloat16)
    rows = []
    for head in range(2):
        total = jnp.zeros((8, WIN), jnp.float32)
        pad = jnp.zeros((8, TILE), jnp.float32)
        for a in range(TILE // 8):
            strip = jnp.concatenate([pad, g_ref[head, 8 * a : 8 * a + 8, :]], axis=1)
            if a:
                strip = pltpu.roll(strip, WIN - 8 * a, 1)
            total = total + strip
        line_sum = jnp.zeros((1, WIN), jnp.float32)
        for s in range(8):
            one = total[s : s + 1]
            line_sum = line_sum + (pltpu.roll(one, WIN - s, 1) if s else one)
        rows.append(line_sum)
    lines = jnp.concatenate(rows, axis=0)
    lines = jnp.where(offsets >= 0, lines, 0.0)
    high, mid, low = split3(lines)
    sums = sum(dot_nt(part.astype(jnp.bfloat16), chosen) for part in (high, mid, low))
    lane32 = lax.broadcasted_iota(jnp.int32, (1, BUCKETS), 1)
    tables = []
    for head in range(2):
        far_sum = jnp.sum(gfar_ref[head])
        tables.append(sums[head : head + 1] + jnp.where(lane32 == BUCKETS - 1, far_sum, 0.0))
    return dq, None, None, tables


def last_block(n_blk, n_dp, plans, enc_plan, big, little, keys):
    every = list(plans) + [enc_plan]
    links = len(all_links(n_blk, n_dp))
    scratch = [item for plan in every for item in plan.scratch()]
    scratch += [
        pltpu.VMEM((POOL, LEN, D), jnp.bfloat16),
        pltpu.VMEM((LEN, D), jnp.float32),
        pltpu.VMEM((D, LEN), jnp.bfloat16),
        pltpu.VMEM((2, TILE, 2 * TILE), jnp.float32),
        pltpu.VMEM((2, TILE, 2 * TILE), jnp.float32),
        pltpu.VMEM((2, 8, TILE), jnp.float32),
        pltpu.VMEM((LANES, LEN), jnp.float32),
        pltpu.VMEM((3 + H, 1, D), jnp.float32),
        pltpu.VMEM((links, 3 + H, 1, D), jnp.float32),
        pltpu.SemaphoreType.DMA((links,)),
        pltpu.SemaphoreType.DMA((links,)),
        pltpu.SemaphoreType.DMA((len(big) + 3 * (keys // LEN) - 2 + 1,)),
        pltpu.SemaphoreType.DMA((LEN // ROWS,)),
    ]
    return pl.pallas_call(
        partial(last_kernel, n_blk, n_dp, plans, enc_plan),
        in_specs=[any_spec()] * len(big) + [vmem_spec()] * len(little),
        out_specs=[vmem_spec()] * len(every) + [any_spec(), vmem_spec()],
        out_shape=[plan.out_shape() for plan in every]
        + [jax.ShapeDtypeStruct((LEN, D), jnp.float32), jax.ShapeDtypeStruct((3 + H, 1, D), jnp.float32)],
        scratch_shapes=scratch,
        compiler_params=pltpu.CompilerParams(
            vmem_limit_bytes=VMEM_LIMIT, collective_id=1, has_side_effects=True
        ),
        cost_estimate=pl.CostEstimate(flops=40 * LEN * D * D, bytes_accessed=80 * LEN * D, transcendentals=0),
    )(*big, *little)


def segment_rows(lengths_ref):
    rows = lax.broadcasted_iota(jnp.int32, (LEN, LANES), 0)
    end = jnp.zeros((1, 1), jnp.int32)
    seg = jnp.zeros((LEN, LANES), jnp.int32)
    for t in range(TARGETS - 1):
        end = end + lengths_ref[:, t : t + 1]
        seg = seg + (rows >= end).astype(jnp.int32)
    return seg


def query_marks(seg):
    place = lane_ids(LEN) & (HD - 1)
    return jnp.where((place >= 3) & (place - 3 == seg), 1.0, 0.0).astype(jnp.bfloat16)


def key_marks(seg):
    place = lane_ids(LEN) & (HD - 1)
    other = (place >= 3) & (place < 3 + TARGETS) & (place - 3 != seg)
    return jnp.where(place < 3, -1.0, jnp.where(other, NEG, 0.0)).astype(jnp.bfloat16)


def value_marks(rows):
    place = lane_ids(rows) & (HD - 1)
    return jnp.where(place < 3, 1.0, 0.0).astype(jnp.bfloat16)


def front_kernel(n_blk, n_dp, x_hbm, enc_hbm, wq_hbm, wk_hbm, wv_hbm, wo_hbm, wcq_hbm, wck_hbm, wcv_hbm,
                 lengths_ref, gain_ref, gainc_ref, table_ref,
                 q_hbm, k_hbm, v_hbm, o_hbm, aug_hbm, act_hbm, y1_hbm, actc_hbm, qc_hbm, kv_hbm, encall_hbm,
                 x_ref, w_ref, act_ref, q_ref, k_ref, v_ref, o_ref, aug_ref, y1_ref, kv_ref, enc_ref, bias_ref,
                 send_sem, recv_sem, load_sem, store_sem):
    passage = enc_hbm.shape[0]
    loads = []
    for n, (src, dst) in enumerate(
        [(enc_hbm, enc_ref.at[0]), (x_hbm, x_ref)]
        + [(w, w_ref.at[i]) for i, w in enumerate((wq_hbm, wk_hbm, wv_hbm, wo_hbm, wcq_hbm, wck_hbm, wcv_hbm))]
    ):
        loads.append(pltpu.make_async_copy(src, dst, load_sem.at[n]))
        loads[-1].start()
    stores = []

    def store(src, dst):
        stores.append(pltpu.make_async_copy(src, dst, store_sem.at[len(stores)]))
        stores[-1].start()

    bits = bits_of(n_blk)

    def gather(k):
        size = 1 << k
        return pltpu.make_async_remote_copy(
            src_ref=enc_ref.at[pl.ds(0, size)],
            dst_ref=enc_ref.at[pl.ds(size, size)],
            send_sem=send_sem.at[k],
            recv_sem=recv_sem.at[k],
            device_id=partner("blk", bits - 1 - k),
            device_id_type=pl.DeviceIdType.MESH,
        )

    barrier = pltpu.get_barrier_semaphore()
    for bit in range(bits):
        pl.semaphore_signal(barrier, inc=1, device_id=partner("blk", bit), device_id_type=pl.DeviceIdType.MESH)
    pl.semaphore_wait(barrier, bits)
    loads[0].wait()
    gather(0).start()
    loads[1].wait()
    for r in range(0, LEN, ROWS):
        rows = slice(r, r + ROWS)
        x = x_ref[rows].astype(jnp.float32)
        act_ref[rows] = (x * norm_parts(x) * gain_ref[...]).astype(jnp.bfloat16)
    for i, (ref, out) in enumerate(((q_ref, q_hbm), (k_ref, k_hbm), (v_ref, v_hbm))):
        loads[2 + i].wait()
        for r in range(0, LEN, ROWS):
            rows = slice(r, r + ROWS)
            ref[rows] = dot_nn(act_ref[rows], w_ref[i]).astype(jnp.bfloat16)
        store(ref, out)
    store(act_ref, act_hbm)
    seg = segment_rows(lengths_ref)
    aq, ak = query_marks(seg), key_marks(seg)
    offsets = 2 * TILE - lax.broadcasted_iota(jnp.int32, (1, WIN), 1)
    chosen = bucket_vector(None, jnp.maximum(offsets, 0))
    for p in range(PAIRS):
        lanes = slice(p * LANES, (p + 1) * LANES)
        if p < bits:
            gather(p).wait()
            if p + 1 < bits:
                gather(p + 1).start()
        self_pair_forward(q_ref[:, lanes], k_ref[:, lanes], v_ref[:, lanes], aq, ak, table_ref[p], offsets, chosen,
                          bias_ref, o_ref, aug_ref, lanes)
    store(o_ref, o_hbm)
    store(aug_ref, aug_hbm)
    for n in range(5, 9):
        loads[n].wait()
    for s in range(0, n_blk):
        store(enc_ref.at[s], encall_hbm.at[pl.ds(s * passage, passage)])
    for r in range(0, LEN, ROWS):
        rows = slice(r, r + ROWS)
        y1 = x_ref[rows].astype(jnp.float32) + dot_nn(o_ref[rows], w_ref[3])
        y1_ref[rows] = y1
        store(y1_ref.at[pl.ds(r, ROWS)], y1_hbm.at[pl.ds(r, ROWS)])
        actc = (y1 * norm_parts(y1) * gainc_ref[...]).astype(jnp.bfloat16)
        x_ref[rows] = actc
        store(x_ref.at[pl.ds(r, ROWS)], actc_hbm.at[pl.ds(r, ROWS)])
    group = ROWS // passage
    for s in range(0, n_blk, group):
        encs = enc_ref[s : s + group].reshape(group * passage, D)
        rows = slice(s * passage, (s + group) * passage)
        kv_ref[rows, :D] = dot_nn(encs, w_ref[5]).astype(jnp.bfloat16)
        kv_ref[rows, D:] = dot_nn(encs, w_ref[6]).astype(jnp.bfloat16)
    store(kv_ref, kv_hbm)
    stores[0].wait()
    for r in range(0, LEN, ROWS):
        rows = slice(r, r + ROWS)
        q_ref[rows] = dot_nn(x_ref[rows], w_ref[4]).astype(jnp.bfloat16)
        store(q_ref.at[pl.ds(r, ROWS)], qc_hbm.at[pl.ds(r, ROWS)])
    for copy in stores[1:]:
        copy.wait()


def self_pair_forward(q_raw, k_raw, v_raw, aq, ak, table, offsets, chosen, bias_ref, o_ref, aug_ref, lanes):
    line = dot_nn(table, chosen)
    line = jnp.where(offsets >= 0, line, NEG)
    far = table[:, BUCKETS - 1 :].astype(jnp.float32)
    for head in range(2):
        spread = jnp.broadcast_to(line[head : head + 1], (TILE, WIN))
        bias_ref[head] = pltpu.roll(spread, 0, 1, stride=1, stride_axis=0)[:, TILE:]
    first = {}
    for head in range(2):
        half = in_half(LEN, head)
        q = jnp.where(half, q_raw * jnp.bfloat16(SCALE), aq)
        k = jnp.where(half, k_raw, ak)
        v = jnp.where(half, v_raw, jnp.zeros((), jnp.bfloat16))
        for i in range(LEN // TILE):
            lo = max(0, i - 2) * TILE
            hi = (i + 1) * TILE
            scores = dot_nt(q[i * TILE : hi], k[lo:hi])
            near = min(2 * TILE, hi - lo)
            parts = []
            if hi - lo > near:
                parts.append(scores[:, : hi - lo - near] + far[head : head + 1])
            parts.append(scores[:, hi - lo - near :] + bias_ref[head][:, 2 * TILE - near :])
            scores = parts[0] if len(parts) == 1 else jnp.concatenate(parts, axis=1)
            top = jnp.max(scores, axis=1, keepdims=True)
            expo = jnp.exp(scores - top)
            total = jnp.sum(expo, axis=1, keepdims=True)
            mixed = dot_nn(expo.astype(jnp.bfloat16), v[lo:hi]) / total
            logsum = top + jnp.log(total)
            if head == 0:
                first[i] = (mixed, logsum)
                continue
            rows = slice(i * TILE, hi)
            o_ref[rows, lanes] = (first[i][0] + mixed).astype(jnp.bfloat16)
            aug = triple_lanes(first[i][1], logsum, TILE)
            place = lane_ids(TILE) & (HD - 1)
            aug_ref[rows, lanes] = jnp.where(place < 3, aug, aq[rows].astype(jnp.float32)).astype(jnp.bfloat16)


def front_block(n_blk, n_dp, big, little, keys, passage):
    wide = jax.ShapeDtypeStruct((LEN, D), jnp.bfloat16)
    n_store = 6 + n_blk + 3 * (LEN // ROWS) + 1
    return pl.pallas_call(
        partial(front_kernel, n_blk, n_dp),
        in_specs=[any_spec()] * len(big) + [vmem_spec()] * len(little),
        out_specs=[any_spec()] * 11,
        out_shape=[wide] * 6
        + [
            jax.ShapeDtypeStruct((LEN, D), jnp.float32),
            wide,
            wide,
            jax.ShapeDtypeStruct((keys, 2 * D), jnp.bfloat16),
            jax.ShapeDtypeStruct((keys, D), jnp.bfloat16),
        ],
        scratch_shapes=[
            pltpu.VMEM((LEN, D), jnp.bfloat16),
            pltpu.VMEM((7, D, D), jnp.bfloat16),
            pltpu.VMEM((LEN, D), jnp.bfloat16),
            pltpu.VMEM((LEN, D), jnp.bfloat16),
            pltpu.VMEM((LEN, D), jnp.bfloat16),
            pltpu.VMEM((LEN, D), jnp.bfloat16),
            pltpu.VMEM((LEN, D), jnp.bfloat16),
            pltpu.VMEM((LEN, D), jnp.bfloat16),
            pltpu.VMEM((LEN, D), jnp.float32),
            pltpu.VMEM((keys, 2 * D), jnp.bfloat16),
            pltpu.VMEM((n_blk, passage, D), jnp.bfloat16),
            pltpu.VMEM((2, TILE, 2 * TILE), jnp.float32),
            pltpu.SemaphoreType.DMA((bits_of(n_blk),)),
            pltpu.SemaphoreType.DMA((bits_of(n_blk),)),
            pltpu.SemaphoreType.DMA((len(big),)),
            pltpu.SemaphoreType.DMA((n_store,)),
        ],
        compiler_params=pltpu.CompilerParams(
            vmem_limit_bytes=VMEM_LIMIT, collective_id=2, has_side_effects=True
        ),
        cost_estimate=pl.CostEstimate(flops=20 * LEN * D * D, bytes_accessed=40 * LEN * D, transcendentals=0),
    )(*big, *little)


FF_STEPS = 4


def normal_cdf_pair(u):
    x = jnp.abs(u) * 0.7071067811865476
    gauss = jnp.exp(-0.5 * u * u)
    t = 1.0 / (1.0 + 0.3275911 * x)
    poly = ((((1.061405429 * t - 1.453152027) * t + 1.421413741) * t - 0.284496736) * t + 0.254829592) * t
    tail = 0.5 * poly * gauss
    return jnp.where(u >= 0, 1.0 - tail, tail), gauss * 0.3989422804014327


def rest_slot(owner, piece, order):
    slot = 0
    for axis, bit in order[2:]:
        mine = (lax.axis_index(axis) // (1 << bit)) % 2
        its = ((owner if axis == "blk" else piece) // (1 << bit)) % 2
        slot = 2 * slot + (its + mine) % 2
    return slot


class FeedParts:
    def __init__(self, plan, owners, units):
        self.plan, self.owners, self.units = plan, owners, units
        self.count = owners // 2 * len(units)

    def split(self, grad, even_core, put_send, put_keep):
        n = 0
        for t in range(0, self.owners, 2):
            for u in self.units:
                even, odd = grad(t, u), grad(t + 1, u)
                put_send(n, jnp.where(even_core, odd, even).astype(jnp.bfloat16))
                put_keep(n, jnp.where(even_core, even, odd).astype(jnp.bfloat16))
                n += 1

    def index(self, t, u):
        return t // 2 * len(self.units) + self.units.index(u)


def feed_kernel(n_blk, n_dp, plan_in, plan_out, y1_ref, oc_ref, wco_ref, gain_ref, g_ref, w1_ref, w2_ref,
                out_ref, isend_ref, ikeep_ref, osend_ref, okeep_ref, dy2_ref, e2_ref, doc_ref, dgain_ref,
                y2_ref, act_ref, acc_ref, da_ref, hid_ref, du_ref, away_ref, stay_ref, got_ref, send_sem, recv_sem):
    step = pl.program_id(0)
    even_core = lax.axis_index("blk") % 2 == 0
    group = n_blk // FF_STEPS
    parts_out = FeedParts(plan_out, group, list(range(plan_out.count)))
    parts_in = FeedParts(plan_in, n_blk, [0])

    def exchange(s):
        return pltpu.make_async_remote_copy(
            src_ref=away_ref.at[s],
            dst_ref=got_ref.at[s],
            send_sem=send_sem.at[s],
            recv_sem=recv_sem.at[s],
            device_id=partner("blk", 0),
            device_id_type=pl.DeviceIdType.MESH,
        )

    def settle(s):
        exchange(s).wait()

        def total(n):
            return (stay_ref[s % 2, n].astype(jnp.float32) + got_ref[s, n].astype(jnp.float32)).astype(jnp.bfloat16)

        def place(plan, first, second, owner, piece, inner, send_ref, keep_ref):
            axis, bit = plan.order[1]
            low = (lax.axis_index(axis) // (1 << bit)) % 2 == 0
            a, b = total(first), total(second)
            slot = rest_slot(owner, piece, plan.order)
            send_ref[slot, inner] = jnp.where(low, b, a)
            keep_ref[slot, inner] = jnp.where(low, a, b)

        for t in range(0, group, 2):
            for u in parts_out.units:
                n = parts_out.index(t, u)
                owner = s * group + t
                if plan_out.order[1][0] == "dp":
                    if u // plan_out.mats == 0:
                        twin = parts_out.index(t, u + plan_out.mats)
                        place(plan_out, n, twin, owner, 0, u % plan_out.mats, osend_ref, okeep_ref)
                elif (t >> 1) & 1 == 0:
                    place(plan_out, n, parts_out.index(t + 2, u), owner, 0, u, osend_ref, okeep_ref)
        for t in range(0, n_blk, 2):
            if (t >> 1) & 1 == 0:
                n = parts_out.count + parts_in.index(t, 0)
                twin = parts_out.count + parts_in.index(t + 2, 0)
                place(plan_in, n, twin, t, s // plan_in.mats, s % plan_in.mats, isend_ref, ikeep_ref)

    @pl.when(step == 0)
    def _():
        barrier = pltpu.get_barrier_semaphore()
        pl.semaphore_signal(
            barrier, inc=1, device_id=partner("blk", 0), device_id_type=pl.DeviceIdType.MESH
        )
        pl.semaphore_wait(barrier, 1)
        for r in range(0, LEN, ROWS):
            rows = slice(r, r + ROWS)
            y2 = y1_ref[rows] + dot_nn(oc_ref[rows], wco_ref[...])
            y2_ref[rows] = y2
            act_ref[rows] = (y2 * norm_parts(y2) * gain_ref[...]).astype(jnp.bfloat16)
        acc_ref[...] = y2_ref[...]
        da_ref[...] = jnp.zeros_like(da_ref)

    for r in range(0, LEN, ROWS):
        rows = slice(r, r + ROWS)
        u = dot_nn(act_ref[rows], w1_ref[...])
        dh = dot_nt(g_ref[rows], w2_ref[...])
        cdf, density = normal_cdf_pair(u)
        hid = (u * cdf).astype(jnp.bfloat16)
        du = (dh * (cdf + u * density)).astype(jnp.bfloat16)
        hid_ref[rows] = hid
        du_ref[rows] = du
        acc_ref[rows] += dot_nn(hid, w2_ref[...])
        da_ref[rows] += dot_nt(du, w1_ref[...])

    def put(n, value, base, ref):
        ref[base + n] = value

    dw2 = dot_tn(hid_ref[...], g_ref[...])
    own_rows = plan_out.rows * plan_out.count
    parts_out.split(
        lambda t, m: dw2[t * own_rows + m * plan_out.rows : t * own_rows + (m + 1) * plan_out.rows],
        even_core,
        lambda n, value: away_ref.__setitem__((step, n), value),
        lambda n, value: stay_ref.__setitem__((step % 2, n), value),
    )
    dw1 = dot_tn(act_ref[...], du_ref[...])
    parts_in.split(
        lambda t, m: dw1[t * plan_in.rows : (t + 1) * plan_in.rows],
        even_core,
        lambda n, value: away_ref.__setitem__((step, parts_out.count + n), value),
        lambda n, value: stay_ref.__setitem__((step % 2, parts_out.count + n), value),
    )
    exchange(step).start()

    @pl.when(step > 0)
    def _():
        settle(step - 1)

    @pl.when(step == FF_STEPS - 1)
    def _():
        gain_sum = jnp.zeros((1, D), jnp.float32)
        for r in range(0, LEN, ROWS):
            rows = slice(r, r + ROWS)
            out_ref[rows] = acc_ref[rows].astype(jnp.bfloat16)
            y2 = y2_ref[rows]
            inverse = norm_parts(y2)
            da = da_ref[rows]
            gain_sum = gain_sum + jnp.sum(da * y2 * inverse, axis=0, keepdims=True)
            dy2 = g_ref[rows].astype(jnp.float32) + norm_back(y2, inverse, gain_ref[...], da)
            dy2_ref[rows] = dy2
            e2 = dy2.astype(jnp.bfloat16)
            e2_ref[rows] = e2
            doc_ref[rows] = dot_nt(e2, wco_ref[...]).astype(jnp.bfloat16)
        dgain_ref[...] = gain_sum
        settle(step)


def feed_block(n_blk, n_dp, y1, oc, wco, gain, g, w1, w2, plan_in, plan_out):
    ff = w1.shape[1]
    cols = ff // FF_STEPS
    fixed = vmem_spec()
    quarter = lambda plan: (plan.slots // 4, plan.mats, plan.rows, D)
    like = jax.ShapeDtypeStruct
    units = n_blk // FF_STEPS // 2 * plan_out.count + n_blk // 2
    packet = (units, D // n_blk, D)
    return pl.pallas_call(
        partial(feed_kernel, n_blk, n_dp, plan_in, plan_out),
        grid=(FF_STEPS,),
        in_specs=[fixed] * 5
        + [
            pl.BlockSpec((D, cols), lambda c: (0, c)),
            pl.BlockSpec((cols, D), lambda c: (c, 0)),
        ],
        out_specs=[fixed] * 9,
        out_shape=[
            like((LEN, D), jnp.bfloat16),
            like(quarter(plan_in), jnp.bfloat16),
            like(quarter(plan_in), jnp.bfloat16),
            like(quarter(plan_out), jnp.bfloat16),
            like(quarter(plan_out), jnp.bfloat16),
            like((LEN, D), jnp.float32),
            like((LEN, D), jnp.bfloat16),
            like((LEN, D), jnp.bfloat16),
            like((1, D), jnp.float32),
        ],
        scratch_shapes=[
            pltpu.VMEM((LEN, D), jnp.float32),
            pltpu.VMEM((LEN, D), jnp.bfloat16),
            pltpu.VMEM((LEN, D), jnp.float32),
            pltpu.VMEM((LEN, D), jnp.float32),
            pltpu.VMEM((LEN, cols), jnp.bfloat16),
            pltpu.VMEM((LEN, cols), jnp.bfloat16),
            pltpu.VMEM((FF_STEPS,) + packet, jnp.bfloat16),
            pltpu.VMEM((2,) + packet, jnp.bfloat16),
            pltpu.VMEM((FF_STEPS,) + packet, jnp.bfloat16),
            pltpu.SemaphoreType.DMA((FF_STEPS,)),
            pltpu.SemaphoreType.DMA((FF_STEPS,)),
        ],
        compiler_params=pltpu.CompilerParams(
            vmem_limit_bytes=VMEM_LIMIT, collective_id=3, has_side_effects=True
        ),
        cost_estimate=pl.CostEstimate(flops=12 * LEN * D * ff, bytes_accessed=40 * LEN * D, transcendentals=0),
    )(y1, oc, wco, gain, g, w1, w2)


def unpack_kernel(in_ref, out_ref, crossx, crossy, self0, self1, self2, enc_ref, sums_ref, *outs):
    (gq, gk, gv, go, gcq, gck, gcv, gco, gin, gout, genc, gain0, gain1, gain2, table) = outs
    blocks = (self0, self1, self2)
    for w, ref in enumerate((gq, gk, gv)):
        for b, part in enumerate(blocks):
            for c in range(2):
                at = b * BLOCK + c * (BLOCK // 2)
                ref[:, at : at + BLOCK // 2] = part[2 * w + c]
    half = D // 2
    for ref, part, w in ((gcq, crossx, 0), (gck, crossx, 1), (gcv, crossx, 2), (gco, crossy, 0), (go, crossy, 1)):
        for c in range(2):
            ref[:, c * half : (c + 1) * half] = part[2 * w + c]
    rows = gq.shape[0]
    for m in range(4):
        gin[:, m * D : (m + 1) * D] = in_ref[m]
        gout[m * rows : (m + 1) * rows] = out_ref[m]
    genc[...] = enc_ref[0]
    for n, ref in enumerate((gain0, gain1, gain2)):
        ref[...] = sums_ref[n]
    tables = jnp.concatenate([sums_ref[3 + h][:, :LANES] for h in range(H)] + [jnp.zeros((4, LANES), jnp.float32)], axis=0)
    table[...] = tables.T[:BUCKETS, :H]


def unpack(n_blk, passage, parts):
    rows = D // n_blk
    like = lambda *shape: jax.ShapeDtypeStruct(shape, jnp.float32)
    return pl.pallas_call(
        unpack_kernel,
        in_specs=[vmem_spec()] * len(parts),
        out_specs=[vmem_spec()] * 15,
        out_shape=[like(rows, D)] * 8
        + [like(rows, 4 * D), like(4 * rows, D), like(passage, D)]
        + [like(1, D)] * 3
        + [like(BUCKETS, H)],
        compiler_params=pltpu.CompilerParams(vmem_limit_bytes=VMEM_LIMIT),
    )(*parts)


def swap(value, axis, bit, size):
    return lax.ppermute(value, axis, [(i, i ^ (1 << bit)) for i in range(size)])


def per_device(
    decoder_rows,
    encoder_rows,
    target_lengths,
    target_question,
    passage_question,
    self_gain,
    self_query,
    self_key,
    self_value,
    self_output,
    position_bias_matrix,
    cross_gain,
    cross_query,
    cross_key,
    cross_value,
    cross_output,
    feed_gain,
    feed_input_weight,
    feed_out,
    cotangent,
    n_dp,
    n_blk,
):
    passage = encoder_rows.shape[0]
    keys = passage * n_blk
    sizes = {"blk": n_blk, "dp": n_dp}
    table_pairs = position_bias_matrix.T.reshape(PAIRS, 2, BUCKETS)
    self_gain2, cross_gain2, feed_gain2 = self_gain[None], cross_gain[None], feed_gain[None]
    (query_self, key_self, value_self, attn_self, aug_self, act_self, resid_self, act_cross, query_cross, pair_all,
     encoder_all) = front_block(
        n_blk, n_dp,
        (decoder_rows, encoder_rows, self_query, self_key, self_value, self_output, cross_query, cross_key, cross_value),
        (target_lengths, self_gain2, cross_gain2, table_pairs), keys, passage,
    )
    layout = (target_lengths, target_question, passage_question)
    attn_cross, aug_cross = cross_forward(n_blk, passage, *layout, query_cross, pair_all)
    plan_in, plan_out = feed_plans(n_blk, n_dp)
    (block_out, in_send, in_keep, out_send, out_keep, grad_resid_cross, round_cross, grad_attn_cross, gain_feed) = feed_block(
        n_blk, n_dp, resid_self, attn_cross, cross_output, feed_gain2, cotangent, feed_input_weight, feed_out,
        plan_in, plan_out,
    )
    in_got = swap(in_send, *plan_in.order[1], sizes[plan_in.order[1][0]])
    out_got = swap(out_send, *plan_out.order[1], sizes[plan_out.order[1][0]])
    dqc, dkv, grad_resid_self, grad_attn_self, encoder_part, gain_cross = cross_backward(
        n_blk, passage, *layout, query_cross, pair_all, grad_attn_cross, attn_cross, aug_cross,
        resid_self, grad_resid_cross, cross_query, cross_key, cross_value, self_output, cross_gain2,
    )
    enc_plan = Exchange(1, passage, D, n_blk, n_dp, "near")
    big = (
        decoder_rows, grad_resid_self, act_self, self_query, self_key, self_value, act_cross, dqc, encoder_all, dkv,
        attn_cross, round_cross, query_self, key_self, value_self, grad_attn_self, attn_self, aug_self,
        in_keep, in_got, out_keep, out_got, encoder_part,
    )
    last = last_block(
        n_blk, n_dp, last_plans(n_blk, n_dp), enc_plan, big,
        (target_lengths, self_gain2, table_pairs, gain_cross, gain_feed), keys,
    )
    grad_decoder = last[8]
    (gq, gk, gv, go, gcq, gck, gcv, gco, gin, gout, genc, gain_self, gain_cross, gain_feed, table) = unpack(
        n_blk, passage, last[:8] + last[9:]
    )
    return (
        block_out, grad_decoder, genc, gain_self[0], gq, gk, gv, go, table, gain_cross[0], gcq, gck, gcv, gco,
        gain_feed[0], gin, gout,
    )


def solution(mesh):
    split, copied, owned = P(("dp", "blk"), None), P(), P("blk", None)
    return jax.shard_map(
        partial(per_device, n_dp=mesh.shape["dp"], n_blk=mesh.shape["blk"]),
        mesh=mesh,
        in_specs=(split,) * 4 + (P("dp"),) + (copied,) * 14 + (split,),
        out_specs=(split,) * 3 + (copied,) + (owned,) * 4 + (copied,) * 2 + (owned,) * 4 + (copied,) + (owned,) * 2,
        check_vma=False,
    )
```

```python
import functools
from functools import partial

import jax
import jax.numpy as jnp
from jax import lax
from jax.experimental import pallas as pl
from jax.experimental.pallas import tpu as pltpu
from jax.sharding import PartitionSpec as P

D = 768
H = 12
HD = 64
BUCKETS = 32
LEN = 1024
TARGETS = 4
PAIRS = H // 2
LANES = 2 * HD
TILE = 256
SCALE = HD ** -0.5
NEG = -1e30
VMEM_LIMIT = 60 * 1024 * 1024

eps_norm = 1e-06
bucket_edges = (19, 21, 24, 27, 31, 35, 40, 46, 52, 59, 67, 77, 87, 99, 113)


def dot_nn(a, b):
    return jnp.dot(a, b, preferred_element_type=jnp.float32)


def dot_nt(a, b):
    return lax.dot_general(a, b, (((1,), (1,)), ((), ())), preferred_element_type=jnp.float32)


def dot_tn(a, b):
    return lax.dot_general(a, b, (((0,), (0,)), ((), ())), preferred_element_type=jnp.float32)


def lane_ids(rows):
    return lax.broadcasted_iota(jnp.int32, (rows, LANES), 1)


def in_half(rows, head):
    lane = lane_ids(rows)
    return lane < HD if head == 0 else lane >= HD


def split3(value):
    high = value.astype(jnp.bfloat16).astype(jnp.float32)
    rest = value - high
    mid = rest.astype(jnp.bfloat16).astype(jnp.float32)
    return high, mid, rest - mid


def triple_lanes(first, second, rows):
    lane = lane_ids(rows)
    out = jnp.zeros((rows, LANES), jnp.float32)
    for base, value in ((HD, first), (0, second)):
        for place, part in enumerate(split3(value)):
            out = jnp.where(lane == base + place, part, out)
    return out


def bucket_vector(table_t, offsets):
    upper = jnp.full(offsets.shape, 16, jnp.int32)
    for edge in bucket_edges:
        upper = upper + (offsets >= edge).astype(jnp.int32)
    bucket = jnp.where(offsets < 16, offsets, upper)
    rows = lax.broadcasted_iota(jnp.int32, (BUCKETS, offsets.shape[1]), 0)
    chosen = (rows == bucket).astype(jnp.float32).astype(jnp.bfloat16)
    return chosen


WIN = 3 * TILE


ROWS = 256


def norm_parts(values):
    return lax.rsqrt(jnp.mean(values * values, axis=1, keepdims=True) + eps_norm)


def norm_back(values, inverse, gain, grad):
    scaled = grad * gain
    inner = jnp.mean(scaled * values, axis=1, keepdims=True)
    return inverse * scaled - values * (inverse * inverse * inverse * inner)


CT = 256


def cross_layout(n_blk, lengths_ref, question_ref, passage_ref, order_ref, item_ref, count_ref):
    per_q = n_blk // TARGETS
    bits = bits_of(n_blk)
    me = lax.axis_index("blk")
    for t in range(TARGETS + 1):
        count_ref[t] = 0
    for s in range(n_blk):
        device = 0
        for b in range(bits):
            mine = (me // (1 << b)) % 2
            flip = (s >> (bits - 1 - b)) & 1
            device = device + (1 - mine if flip else mine) * (1 << b)
        question = passage_ref[device]
        order_ref[question * per_q + count_ref[question]] = s
        count_ref[question] = count_ref[question] + 1
    end = 0
    for t in range(TARGETS):
        start, end = end, end + lengths_ref[0, t]
        question = question_ref[0, t]

        @pl.loop(start // CT, (end + CT - 1) // CT)
        def _(tile, start=start, end=end, question=question):
            n = count_ref[TARGETS]
            item_ref[0, n] = tile
            item_ref[1, n] = question
            item_ref[2, n] = start - tile * CT
            item_ref[3, n] = end - tile * CT
            count_ref[TARGETS] = n + 1


def layout_scratch(n_blk):
    return [
        pltpu.SMEM((n_blk,), jnp.int32),
        pltpu.SMEM((4, LEN // CT + TARGETS), jnp.int32),
        pltpu.SMEM((TARGETS + 1,), jnp.int32),
    ]


def cross_forward_kernel(n_blk, passage, lengths_ref, question_ref, passage_ref, q_ref, kv_ref, o_ref, aug_ref,
                         ks_ref, vs_ref, order_ref, item_ref, count_ref):
    keys_q = n_blk // TARGETS * passage
    lower = lax.broadcasted_iota(jnp.int32, (passage, D), 1) % LANES < HD
    zero = jnp.zeros((), jnp.bfloat16)
    cross_layout(n_blk, lengths_ref, question_ref, passage_ref, order_ref, item_ref, count_ref)

    @pl.loop(0, n_blk)
    def _(s):
        src = pl.multiple_of(order_ref[s] * passage, passage)
        dst = pl.multiple_of(s * passage, passage)
        keys = kv_ref[pl.ds(src, passage), :D]
        values = kv_ref[pl.ds(src, passage), D:]
        ks_ref[0, pl.ds(dst, passage)] = jnp.where(lower, keys, zero)
        ks_ref[1, pl.ds(dst, passage)] = jnp.where(lower, zero, keys)
        vs_ref[0, pl.ds(dst, passage)] = jnp.where(lower, values, zero)
        vs_ref[1, pl.ds(dst, passage)] = jnp.where(lower, zero, values)

    o_ref[...] = jnp.zeros_like(o_ref)
    aug_ref[...] = jnp.zeros_like(aug_ref)

    @pl.loop(0, count_ref[TARGETS])
    def _(n):
        row0 = pl.multiple_of(item_ref[0, n] * CT, CT)
        key0 = pl.multiple_of(item_ref[1, n] * keys_q, keys_q)
        rows = lax.broadcasted_iota(jnp.int32, (CT, 1), 0)
        valid = (rows >= item_ref[2, n]) & (rows < item_ref[3, n])
        for pair in range(PAIRS):
            cols = slice(pair * LANES, (pair + 1) * LANES)
            q = q_ref[pl.ds(row0, CT), cols] * jnp.bfloat16(SCALE)
            outs, logs = [], []
            for head in range(2):
                scores = dot_nt(q, ks_ref[head, pl.ds(key0, keys_q), cols])
                top = jnp.max(scores, axis=1, keepdims=True)
                expo = jnp.exp(scores - top)
                total = jnp.sum(expo, axis=1, keepdims=True)
                outs.append(dot_nn(expo.astype(jnp.bfloat16), vs_ref[head, pl.ds(key0, keys_q), cols]) / total)
                logs.append(top + jnp.log(total))
            mixed = (outs[0] + outs[1]).astype(jnp.bfloat16)
            aug = triple_lanes(logs[0], logs[1], CT).astype(jnp.bfloat16)
            o_ref[pl.ds(row0, CT), cols] = jnp.where(valid, mixed, o_ref[pl.ds(row0, CT), cols])
            aug_ref[pl.ds(row0, CT), cols] = jnp.where(valid, aug, aug_ref[pl.ds(row0, CT), cols])


def smem_spec():
    return pl.BlockSpec(memory_space=pltpu.SMEM)


def vmem_spec():
    return pl.BlockSpec(memory_space=pltpu.VMEM)


def any_spec():
    return pl.BlockSpec(memory_space=pl.ANY)


def cross_forward(n_blk, passage, lengths, questions, passages, q, kv):
    keys = kv.shape[0]
    return pl.pallas_call(
        partial(cross_forward_kernel, n_blk, passage),
        in_specs=[smem_spec()] * 3 + [vmem_spec()] * 2,
        out_specs=[vmem_spec(), vmem_spec()],
        out_shape=[jax.ShapeDtypeStruct((LEN, D), jnp.bfloat16)] * 2,
        scratch_shapes=[pltpu.VMEM((2, keys, D), jnp.bfloat16)] * 2 + layout_scratch(n_blk),
        compiler_params=pltpu.CompilerParams(vmem_limit_bytes=VMEM_LIMIT),
        cost_estimate=pl.CostEstimate(flops=2 * H * LEN * LEN * HD, bytes_accessed=10 * LEN * D, transcendentals=0),
    )(lengths, questions, passages, q, kv)


def cross_backward_kernel(n_blk, passage, lengths_ref, question_ref, passage_ref, q_ref, do_ref, o_ref, aug_ref,
                          kv_hbm, y1_hbm, dy2_hbm, wcq_hbm, wck_hbm, wcv_hbm, wo_hbm, gain_ref,
                          dq_ref, dkv_ref, dy1_ref, dos_ref, part_ref, dgain_ref,
                          ks_ref, vs_ref, kt_ref, dk_ref, dv_ref, dqt_ref, y1_ref, load_sem,
                          order_ref, item_ref, count_ref):
    loads = []
    for n, (src, dst) in enumerate(
        [(kv_hbm, dkv_ref), (y1_hbm, y1_ref), (dy2_hbm, dy1_ref)]
    ):
        loads.append(pltpu.make_async_copy(src, dst, load_sem.at[n]))
        loads[-1].start()
    keys_q = n_blk // TARGETS * passage
    lane = lax.broadcasted_iota(jnp.int32, (passage, D), 1) % LANES
    lower = lane < HD
    ones = jnp.where((lane & (HD - 1)) < 3, 1.0, 0.0).astype(jnp.bfloat16)
    minus = -ones
    cross_layout(n_blk, lengths_ref, question_ref, passage_ref, order_ref, item_ref, count_ref)

    loads[0].wait()

    @pl.loop(0, n_blk)
    def _(s):
        src = pl.multiple_of(order_ref[s] * passage, passage)
        dst = pl.multiple_of(s * passage, passage)
        keys = dkv_ref[pl.ds(src, passage), :D]
        values = dkv_ref[pl.ds(src, passage), D:]
        ks_ref[0, pl.ds(dst, passage)] = jnp.where(lower, keys, minus)
        ks_ref[1, pl.ds(dst, passage)] = jnp.where(lower, minus, keys)
        vs_ref[0, pl.ds(dst, passage)] = jnp.where(lower, values, ones)
        vs_ref[1, pl.ds(dst, passage)] = jnp.where(lower, ones, values)

    lower_k = lax.broadcasted_iota(jnp.int32, (keys_q, LANES), 1) < HD
    for s in range(TARGETS):
        for pair in range(PAIRS):
            rows = slice(s * keys_q, (s + 1) * keys_q)
            cols = slice(pair * LANES, (pair + 1) * LANES)
            both = jnp.where(lower_k, ks_ref[0, rows, cols], ks_ref[1, rows, cols])
            kt_ref[cols, rows] = both.T
    dk_ref[...] = jnp.zeros_like(dk_ref)
    dv_ref[...] = jnp.zeros_like(dv_ref)
    dqt_ref[...] = jnp.zeros_like(dqt_ref)

    @pl.loop(0, count_ref[TARGETS])
    def _(n):
        row0 = pl.multiple_of(item_ref[0, n] * CT, CT)
        key0 = pl.multiple_of(item_ref[1, n] * keys_q, keys_q)
        rows = lax.broadcasted_iota(jnp.int32, (CT, 1), 0)
        valid = (rows >= item_ref[2, n]) & (rows < item_ref[3, n])
        here = pl.ds(row0, CT)
        there = pl.ds(key0, keys_q)
        for pair in range(PAIRS):
            cols = slice(pair * LANES, (pair + 1) * LANES)
            q_scaled = q_ref[here, cols] * jnp.bfloat16(SCALE)
            do_pair = jnp.where(valid, do_ref[here, cols], jnp.zeros((), jnp.bfloat16))
            product = do_pair.astype(jnp.float32) * o_ref[here, cols].astype(jnp.float32)
            deltas = []
            for head in range(2):
                deltas.append(jnp.sum(jnp.where(in_half(CT, head), product, 0.0), axis=1, keepdims=True))
            aug_do = (-triple_lanes(deltas[0], deltas[1], CT)).astype(jnp.bfloat16)
            aug = jnp.where(valid, aug_ref[here, cols], jnp.bfloat16(-NEG))
            parts = []
            for head in range(2):
                half = in_half(CT, head)
                q = jnp.where(half, q_scaled, aug)
                do = jnp.where(half, do_pair, aug_do)
                probs = jnp.exp(dot_nt(ks_ref[head, there, cols], q))
                grad_scores = probs * dot_nt(vs_ref[head, there, cols], do)
                ds = grad_scores.astype(jnp.bfloat16)
                parts.append((dot_nn(ds, q), dot_nn(probs.astype(jnp.bfloat16), do)))
                hrow = pair * LANES + head * HD
                dqt_ref[hrow : hrow + HD, here] += dot_nn(kt_ref[hrow : hrow + HD, there], ds)
            dk_ref[there, cols] += jnp.where(lower_k, parts[0][0], parts[1][0])
            dv_ref[there, cols] += jnp.where(lower_k, parts[0][1], parts[1][1])

    spots = (ks_ref.at[0], ks_ref.at[1], vs_ref.at[0], vs_ref.at[1])
    for n, w in enumerate((wcq_hbm, wck_hbm, wcv_hbm, wo_hbm)):
        loads.append(pltpu.make_async_copy(w, spots[n].at[pl.ds(0, D)], load_sem.at[3 + n]))
        loads[-1].start()
    for pair in range(PAIRS):
        cols = slice(pair * LANES, (pair + 1) * LANES)
        dq_ref[:, cols] = (dqt_ref[cols, :] * SCALE).T.astype(jnp.bfloat16)

    for copy in loads[1:]:
        copy.wait()

    @pl.loop(0, n_blk)
    def _(s):
        src = pl.multiple_of(s * passage, passage)
        spot = order_ref[s]
        dst = pl.multiple_of(spot * passage, passage)
        dk = dk_ref[pl.ds(src, passage)].astype(jnp.bfloat16)
        dv = dv_ref[pl.ds(src, passage)].astype(jnp.bfloat16)
        dkv_ref[pl.ds(dst, passage), :D] = dk
        dkv_ref[pl.ds(dst, passage), D:] = dv

    group = ROWS // passage
    for s in range(0, n_blk, group):
        rows = slice(s * passage, (s + group) * passage)
        part = dot_nt(dkv_ref[rows, :D], ks_ref[1, :D]) + dot_nt(dkv_ref[rows, D:], vs_ref[0, :D])
        part_ref[s : s + group, 0] = part.astype(jnp.bfloat16).reshape(group, passage, D)
    gain_sum = jnp.zeros((1, D), jnp.float32)
    for r in range(0, LEN, ROWS):
        rows = slice(r, r + ROWS)
        da = dot_nt(dq_ref[rows], ks_ref[0, :D])
        y1 = y1_ref[rows]
        inverse = norm_parts(y1)
        gain_sum = gain_sum + jnp.sum(da * y1 * inverse, axis=0, keepdims=True)
        dy1 = dy1_ref[rows] + norm_back(y1, inverse, gain_ref[...].reshape(1, D), da)
        dy1_ref[rows] = dy1
        dos_ref[rows] = dot_nt(dy1.astype(jnp.bfloat16), vs_ref[1, :D]).astype(jnp.bfloat16)
    dgain_ref[...] = gain_sum


def cross_backward(n_blk, passage, lengths, questions, passages, q, kv, do, o, aug, y1, dy2, wcq, wck, wcv, wo, gain):
    keys = kv.shape[0]
    like = jax.ShapeDtypeStruct
    return pl.pallas_call(
        partial(cross_backward_kernel, n_blk, passage),
        in_specs=[smem_spec()] * 3 + [vmem_spec()] * 4 + [any_spec()] * 7 + [vmem_spec()],
        out_specs=[vmem_spec()] * 6,
        out_shape=[
            like((LEN, D), jnp.bfloat16),
            like((keys, 2 * D), jnp.bfloat16),
            like((LEN, D), jnp.float32),
            like((LEN, D), jnp.bfloat16),
            like((n_blk, 1, passage, D), jnp.bfloat16),
            like((1, D), jnp.float32),
        ],
        scratch_shapes=[pltpu.VMEM((2, keys, D), jnp.bfloat16)] * 2
        + [
            pltpu.VMEM((D, keys), jnp.bfloat16),
            pltpu.VMEM((keys, D), jnp.float32),
            pltpu.VMEM((keys, D), jnp.float32),
            pltpu.VMEM((D, LEN), jnp.float32),
            pltpu.VMEM((LEN, D), jnp.float32),
            pltpu.SemaphoreType.DMA((7,)),
        ]
        + layout_scratch(n_blk),
        compiler_params=pltpu.CompilerParams(vmem_limit_bytes=VMEM_LIMIT),
        cost_estimate=pl.CostEstimate(flops=5 * H * LEN * LEN * HD, bytes_accessed=18 * LEN * D, transcendentals=0),
    )(lengths, questions, passages, q, do, o, aug, kv, y1, dy2, wcq, wck, wcv, wo, gain)


def bits_of(count):
    return count.bit_length() - 1


def place_bits(n_blk, n_dp, kind):
    blk = [("blk", bit) for bit in range(bits_of(n_blk))]
    dp = [("dp", bit) for bit in range(bits_of(n_dp))]
    if kind == "x":
        return blk[:1] + dp + blk[1:]
    if kind == "y":
        return blk[:2] + dp + blk[2:]
    if kind == "feed_x":
        return blk[:1] + dp + blk[2:3] + blk[1:2] + blk[3:]
    if kind == "feed_y":
        return blk[:3] + dp + blk[3:]
    return blk


def position(owner, piece, order):
    slot = 0
    for axis, bit in order:
        mine = (lax.axis_index(axis) // (1 << bit)) % 2
        static = ((owner if axis == "blk" else piece) >> bit) & 1
        slot = 2 * slot + (1 - mine if static else mine)
    return slot


def partner(axis, bit):
    me = lax.axis_index(axis)
    mine = (me // (1 << bit)) % 2
    return {axis: me + (1 - 2 * mine) * (1 << bit)}


class Exchange:
    def __init__(self, count, rows, cols, n_blk, n_dp, kind, first=0):
        split = kind in ("x", "y", "feed_x", "feed_y")
        if split and count % n_dp:
            kind, split = "plain", False
        self.n_blk, self.n_dp, self.count, self.kind, self.first = n_blk, n_dp, count, kind, first
        self.rows, self.cols = rows, cols
        self.order = place_bits(n_blk, n_dp, kind)
        self.pieces = n_dp if split else 1
        self.slots = n_blk * self.pieces
        self.mats = count // self.pieces
        self.last = [("dp", bit) for bit in range(bits_of(n_dp))] if kind != "near" else []
        self.steps = len(self.order) + len(self.last)
        self.held = self.slots >> first
        self.offsets = {}
        at = self.held if first else 0
        for k in range(first, len(self.order)):
            size = self.slots >> (k + 1)
            self.offsets[k] = (at, size)
            at += size
        for j in range(len(self.last)):
            size = (1 << j) if self.pieces > 1 else 1
            self.offsets[len(self.order) + j] = (at, size)
            at += size
        self.received = at

    def scratch(self):
        shape = (self.mats, self.rows, self.cols)
        return [
            pltpu.VMEM((max(self.held, self.pieces),) + shape, jnp.bfloat16),
            pltpu.VMEM((self.received,) + shape, jnp.bfloat16),
            pltpu.SemaphoreType.DMA((self.steps,)),
            pltpu.SemaphoreType.DMA((self.steps,)),
        ]

    def out_shape(self):
        return jax.ShapeDtypeStruct((self.count, self.rows, self.cols), jnp.float32)

    def bind(self, refs, out_ref):
        self.buf, self.recv, self.send_sem, self.recv_sem = refs
        self.out = out_ref

    def put(self, index, value):
        piece, inner = index // self.mats, index % self.mats
        for owner in range(self.n_blk):
            slot = position(owner, piece, self.order)
            self.buf[slot, inner] = value[owner * self.rows : (owner + 1) * self.rows].astype(jnp.bfloat16)

    def copy(self, k):
        at, size = self.offsets[k]
        if k < len(self.order):
            axis, bit = self.order[k]
            src = self.buf.at[pl.ds(size, size)]
        else:
            axis, bit = self.last[k - len(self.order)]
            src = self.buf.at[pl.ds(0, size)]
        return pltpu.make_async_remote_copy(
            src_ref=src,
            dst_ref=self.recv.at[pl.ds(at, size)],
            send_sem=self.send_sem.at[k],
            recv_sem=self.recv_sem.at[k],
            device_id=partner(axis, bit),
            device_id_type=pl.DeviceIdType.MESH,
        )

    def start(self, k):
        self.copy(k).start()

    def add(self, at, size, final):
        for s in range(size):
            for m in range(self.mats):
                total = self.buf[s, m].astype(jnp.float32) + self.recv[at + s, m].astype(jnp.float32)
                if final:
                    self.out[m] = total
                else:
                    self.buf[s, m] = total.astype(jnp.bfloat16)

    def finish(self, k):
        self.copy(k).wait()
        at, size = self.offsets[k]
        final = k == self.steps - 1
        if k < len(self.order) or self.pieces == 1:
            self.add(at, size, final)
            return
        for s in range(size):
            for m in range(self.mats):
                self.buf[size + s, m] = self.recv[at + s, m]
        if final:
            for s in range(self.pieces):
                spot = position(0, s, self.last[::-1])
                for m in range(self.mats):
                    self.out[spot * self.mats + m] = self.buf[s, m].astype(jnp.float32)

    def advance(self, k):
        if k < self.first or k >= self.steps:
            return
        self.finish(k)
        if k + 1 < self.steps:
            self.start(k + 1)


def all_links(n_blk, n_dp):
    return [("blk", bit) for bit in range(bits_of(n_blk))] + [("dp", bit) for bit in range(bits_of(n_dp))]


def enter_barrier(n_blk, n_dp):
    barrier = pltpu.get_barrier_semaphore()
    links = all_links(n_blk, n_dp)
    for axis, bit in links:
        pl.semaphore_signal(barrier, inc=1, device_id=partner(axis, bit), device_id_type=pl.DeviceIdType.MESH)
    pl.semaphore_wait(barrier, len(links))


BLOCK_PAIRS = (2, 2, 1, 1)
BLOCK_KINDS = ("x", "y", "plain", "plain")
FEED_DONE = 3


def last_plans(n_blk, n_dp):
    rows = D // n_blk
    halves = 2
    feed_in, feed_out = feed_plans(n_blk, n_dp, FEED_DONE)
    plans = [
        feed_in,
        feed_out,
        Exchange(3 * halves, rows, D // halves, n_blk, n_dp, "x"),
        Exchange(2 * halves, rows, D // halves, n_blk, n_dp, "y"),
    ]
    for pairs, kind in zip(BLOCK_PAIRS, BLOCK_KINDS):
        plans.append(Exchange(3 * pairs, rows, LANES, n_blk, n_dp, kind))
    return plans


def feed_plans(n_blk, n_dp, first=0):
    rows = D // n_blk
    return (
        Exchange(4, rows, D, n_blk, n_dp, "feed_y", first),
        Exchange(4, rows, D, n_blk, n_dp, "feed_x", first),
    )


POOL = 11
(S_ACTC, S_DQC, S_OC, S_E2, S_Q, S_K, S_V, S_DO, S_O, S_AUG, S_X) = range(POOL)
S_DQ, S_DK, S_DV, S_ACT = S_ACTC, S_DQC, S_OC, S_E2


def last_kernel(n_blk, n_dp, plans, enc_plan, *refs):
    (x_hbm, dy1_hbm, act_hbm, wq_hbm, wk_hbm, wv_hbm, actc_hbm, dqc_hbm, enc_hbm, dkv_hbm, oc_hbm, e2_hbm,
     q_hbm, k_hbm, v_hbm, do_hbm, o_hbm, aug_hbm, inkeep_hbm, inrecv_hbm, outkeep_hbm, outrecv_hbm, part_hbm,
     lengths_ref, gain_ref, table_ref, gainc_ref, gainf_ref) = refs[:28]
    every = list(plans) + [enc_plan]
    outs = refs[28 : 28 + len(every)]
    dx_hbm, sums_ref = refs[28 + len(every) : 30 + len(every)]
    scratch = refs[30 + len(every) :]
    for i, plan in enumerate(every):
        plan.bind(scratch[4 * i : 4 * i + 4], outs[i])
    (pool, dy1_ref, act_t, bias_ref, g_ref, gfar_ref, dqt_ref,
     tot_ref, got_ref, tsend, trecv, load_sem, store_sem) = scratch[4 * len(every) :]
    feed_in, feed_out, crossx, crossy = plans[:4]
    selfs = plans[4:]

    loads = {}

    def load(name, src, dst):
        loads[name] = pltpu.make_async_copy(src, dst, load_sem.at[len(loads)])
        loads[name].start()

    def slot(index):
        return pool.at[index]

    load("actc", actc_hbm, slot(S_ACTC))
    load("dqc", dqc_hbm, slot(S_DQC))
    for plan, keep, got, name in (
        (feed_out, outkeep_hbm, outrecv_hbm, "out"),
        (feed_in, inkeep_hbm, inrecv_hbm, "in"),
    ):
        load(name + "keep", keep, plan.buf.at[pl.ds(0, plan.held)])
        load(name + "recv", got, plan.recv.at[pl.ds(0, plan.held)])
    spans = enc_hbm.shape[0] // LEN
    spare = (S_Q, S_K, S_V, S_DO, S_AUG, S_X)
    for n in range(spans):
        rows = pl.ds(n * LEN, LEN)
        load(("enc", n), enc_hbm.at[rows], slot(spare[3 * n]))
        load(("dk", n), dkv_hbm.at[rows, pl.ds(0, D)], slot(spare[3 * n + 1]))
        load(("dv", n), dkv_hbm.at[rows, pl.ds(D, D)], slot(spare[3 * n + 2]))
    load("part", part_hbm, enc_plan.buf)
    load("oc", oc_hbm, slot(S_OC))
    load("e2", e2_hbm, slot(S_E2))
    load("o", o_hbm, slot(S_O))
    load("dy1", dy1_hbm, dy1_ref)
    enter_barrier(n_blk, n_dp)

    def begin_feed(plan, name):
        loads[name + "keep"].wait()
        loads[name + "recv"].wait()
        plan.add(0, plan.held, False)
        plan.start(plan.first)

    def put_columns(plan, index, value):
        width = plan.cols
        count = value.shape[1] // width
        for c in range(count):
            plan.put(count * index + c, value[:, c * width : (c + 1) * width])

    begin_feed(feed_out, "out")
    begin_feed(feed_in, "in")
    loads["actc"].wait()
    loads["dqc"].wait()
    put_columns(crossx, 0, dot_tn(pool[S_ACTC], pool[S_DQC]))
    for w, name in ((1, "dk"), (2, "dv")):
        total = None
        for n in range(spans):
            if w == 1:
                loads["enc", n].wait()
            loads[name, n].wait()
            part = dot_tn(pool[spare[3 * n]], pool[spare[3 * n + w]])
            total = part if total is None else total + part
        put_columns(crossx, w, total)
    crossx.start(0)
    for name, src, index in (
        ("q", q_hbm, S_Q), ("k", k_hbm, S_K), ("v", v_hbm, S_V), ("do", do_hbm, S_DO), ("aug", aug_hbm, S_AUG), ("x", x_hbm, S_X),
    ):
        load(name, src, slot(index))
    loads["part"].wait()
    enc_plan.start(0)
    loads["oc"].wait()
    loads["e2"].wait()
    put_columns(crossy, 0, dot_tn(pool[S_OC], pool[S_E2]))
    loads["o"].wait()
    loads["dy1"].wait()
    put_columns(crossy, 1, dot_tn(pool[S_O], dy1_ref[...].astype(jnp.bfloat16)))
    crossy.start(0)
    load("act", act_hbm, slot(S_ACT))
    crossx.advance(0)
    for name in ("q", "k", "v", "do", "aug"):
        loads[name].wait()
    loads["act"].wait()
    act_t[...] = pool[S_ACT].T
    crossy.advance(0)
    enc_plan.advance(0)

    offsets = lax.broadcasted_iota(jnp.int32, (1, WIN), 1) - TILE
    chosen = bucket_vector(None, jnp.maximum(offsets, 0))
    lines, fars = bias_lines(table_ref)

    def pair_body(p):
        lanes = pl.ds(pl.multiple_of(p * LANES, LANES), LANES)
        dq, dk, dv, sums = self_pair_backward(
            pool[S_Q, :, lanes], pool[S_K, :, lanes], pool[S_V, :, lanes], pool[S_DO, :, lanes], pool[S_O, :, lanes],
            pool[S_AUG, :, lanes], ak, av, lines[2 * p : 2 * p + 2], fars[2 * p : 2 * p + 2], offsets, chosen,
            bias_ref, g_ref, gfar_ref, dqt_ref,
            lambda rows, value: pool.__setitem__((S_DK, rows, lanes), value),
            lambda rows, value: pool.__setitem__((S_DV, rows, lanes), value),
        )
        pool[S_DQ, :, lanes] = dq
        for head in range(2):
            tot_ref[3 + 2 * p + head] = jnp.concatenate(
                [sums[head], jnp.zeros((1, D - BUCKETS), jnp.float32)], axis=1
            )

    tot_ref[1] = gainc_ref[...]
    tot_ref[2] = gainf_ref[...]
    ak, av = key_marks(segment_rows(lengths_ref)), value_marks(LEN)
    rounds = {
        0: [(feed_out, 3), (feed_in, 3)],
        3: [(crossx, 1), (feed_out, 4), (feed_in, 4)],
        4: [(crossy, 1), (selfs[0], 0), (enc_plan, 1)],
        5: [(selfs[1], 0), (feed_out, 5), (feed_in, 5)],
    }
    p = 0
    for block, pairs in enumerate(BLOCK_PAIRS):
        low = p * LANES
        for _ in range(pairs):
            for plan, k in rounds.get(p, []):
                plan.advance(k)
            pair_body(p)
            p += 1
        cols = slice(low, p * LANES)
        for w, index in enumerate((S_DQ, S_DK, S_DV)):
            put_columns(selfs[block], w, dot_nn(act_t[...], pool[index, :, cols]))
        selfs[block].start(0)
    wq, wk, wv = slot(S_Q), slot(S_K), slot(S_V)
    for name, src, index in (("wq", wq_hbm, S_Q), ("wk", wk_hbm, S_K), ("wv", wv_hbm, S_V)):
        load(name, src, pool.at[index, pl.ds(0, D)])
    selfs[2].advance(0)
    for name in ("wq", "wk", "wv", "x"):
        loads[name].wait()
    pending = [
        [(selfs[3], 0), (crossx, 2), (selfs[0], 1)],
        [(crossy, 2), (selfs[1], 1), (enc_plan, 2), (selfs[2], 1)],
        [(selfs[3], 1), (crossx, 3), (selfs[0], 2)],
        [(crossy, 3), (selfs[1], 2), (enc_plan, 3), (selfs[2], 2)],
    ]
    gain_sum = jnp.zeros((1, D), jnp.float32)
    stores = []
    for i, r in enumerate(range(0, LEN, ROWS)):
        rows = slice(r, r + ROWS)
        da = (
            dot_nt(pool[S_DQ, rows], pool[S_Q, :D])
            + dot_nt(pool[S_DK, rows], pool[S_K, :D])
            + dot_nt(pool[S_DV, rows], pool[S_V, :D])
        )
        x = pool[S_X, rows].astype(jnp.float32)
        inverse = norm_parts(x)
        gain_sum = gain_sum + jnp.sum(da * x * inverse, axis=0, keepdims=True)
        dy1_ref[rows] = dy1_ref[rows] + norm_back(x, inverse, gain_ref[...].reshape(1, D), da)
        stores.append(pltpu.make_async_copy(dy1_ref.at[rows], dx_hbm.at[rows], store_sem.at[i]))
        stores[-1].start()
        for plan, k in pending[i]:
            plan.advance(k)
    tot_ref[0] = gain_sum
    links = all_links(n_blk, n_dp)

    def small_copy(j):
        axis, bit = links[j]
        return pltpu.make_async_remote_copy(
            src_ref=tot_ref,
            dst_ref=got_ref.at[j],
            send_sem=tsend.at[j],
            recv_sem=trecv.at[j],
            device_id=partner(axis, bit),
            device_id_type=pl.DeviceIdType.MESH,
        )

    small_copy(0).start()
    done = {feed_in: 5, feed_out: 5, crossx: 3, crossy: 3, enc_plan: 3}
    done.update({selfs[0]: 2, selfs[1]: 2, selfs[2]: 2, selfs[3]: 1})
    j = 0
    while True:
        for plan in (selfs[3], crossx, selfs[0], crossy, selfs[1], selfs[2], feed_out, feed_in, enc_plan):
            done[plan] += 1
            plan.advance(done[plan])
        if j < len(links):
            small_copy(j).wait()
            tot_ref[...] = tot_ref[...] + got_ref[j]
            j += 1
            if j < len(links):
                small_copy(j).start()
        if j == len(links) and all(done[plan] >= plan.steps - 1 for plan in every):
            break
    sums_ref[...] = tot_ref[...]
    for store in stores:
        store.wait()


def self_pair_backward(q_raw, k_raw, v_raw, do_raw, o_raw, aug, ak, av, line, far, offsets, chosen,
                       bias_ref, g_ref, gfar_ref, dqt_ref, put_dk, put_dv):
    for head in range(2):
        spread = jnp.broadcast_to(line[head : head + 1], (TILE, WIN))
        bias_ref[head] = pltpu.roll(spread, 0, 1, stride=1, stride_axis=0)[:, TILE:]
    g_ref[...] = jnp.zeros_like(g_ref)
    gfar_ref[...] = jnp.zeros_like(gfar_ref)
    dqt_ref[...] = jnp.zeros_like(dqt_ref)
    product = do_raw.astype(jnp.float32) * o_raw.astype(jnp.float32)
    deltas = []
    for head in range(2):
        half = in_half(LEN, head)
        deltas.append(jnp.sum(jnp.where(half, product, 0.0), axis=1, keepdims=True))
    aug_do = (-triple_lanes(deltas[0], deltas[1], LEN)).astype(jnp.bfloat16)
    q_scaled = q_raw * jnp.bfloat16(SCALE)
    k_t = k_raw.T
    accs = {}
    for head in range(2):
        half = in_half(LEN, head)
        q = jnp.where(half, q_scaled, aug)
        k = jnp.where(half, k_raw, ak)
        v = jnp.where(half, v_raw, av)
        do = jnp.where(half, do_raw, aug_do)
        for j in range(LEN // TILE):
            lo = j * TILE
            hi = min(LEN, (j + 3) * TILE)
            width = hi - lo
            near = min(2 * TILE, width)
            scores = dot_nt(k[lo : lo + TILE], q[lo:hi])
            parts = [scores[:, :near] + bias_ref[head][:, :near]]
            if width > near:
                parts.append(scores[:, near:] + far[head : head + 1])
            scores = parts[0] if len(parts) == 1 else jnp.concatenate(parts, axis=1)
            probs = jnp.exp(scores)
            grad_probs = dot_nt(v[lo : lo + TILE], do[lo:hi])
            grad_scores = probs * grad_probs
            g_ref[head, :, :near] += grad_scores[:, :near]
            if width > near:
                gfar_ref[head] += jnp.sum(grad_scores[:, near:].reshape(TILE // 8, 8, TILE), axis=0)
            ds = grad_scores.astype(jnp.bfloat16)
            accs[j, head] = (dot_nn(ds, q[lo:hi]), dot_nn(probs.astype(jnp.bfloat16), do[lo:hi]))
            dqt_ref[head * HD : (head + 1) * HD, lo:hi] += dot_nn(
                k_t[head * HD : (head + 1) * HD, lo : lo + TILE], ds
            )
            if head == 1:
                lower = in_half(TILE, 0)
                rows = slice(lo, lo + TILE)
                put_dk(rows, jnp.where(lower, accs[j, 0][0], accs[j, 1][0]).astype(jnp.bfloat16))
                put_dv(rows, jnp.where(lower, accs[j, 0][1], accs[j, 1][1]).astype(jnp.bfloat16))
    dq = (dqt_ref[...] * SCALE).T.astype(jnp.bfloat16)
    rows = []
    for head in range(2):
        total = jnp.zeros((8, WIN), jnp.float32)
        pad = jnp.zeros((8, TILE), jnp.float32)
        for a in range(TILE // 8):
            strip = jnp.concatenate([pad, g_ref[head, 8 * a : 8 * a + 8, :]], axis=1)
            if a:
                strip = pltpu.roll(strip, WIN - 8 * a, 1)
            total = total + strip
        line_sum = jnp.zeros((1, WIN), jnp.float32)
        for s in range(8):
            one = total[s : s + 1]
            line_sum = line_sum + (pltpu.roll(one, WIN - s, 1) if s else one)
        rows.append(line_sum)
    lines = jnp.concatenate(rows, axis=0)
    lines = jnp.where(offsets >= 0, lines, 0.0)
    high, mid, low = split3(lines)
    sums = sum(dot_nt(part.astype(jnp.bfloat16), chosen) for part in (high, mid, low))
    lane32 = lax.broadcasted_iota(jnp.int32, (1, BUCKETS), 1)
    tables = []
    for head in range(2):
        far_sum = jnp.sum(gfar_ref[head])
        tables.append(sums[head : head + 1] + jnp.where(lane32 == BUCKETS - 1, far_sum, 0.0))
    return dq, None, None, tables


def last_block(n_blk, n_dp, plans, enc_plan, big, little, keys):
    every = list(plans) + [enc_plan]
    links = len(all_links(n_blk, n_dp))
    scratch = [item for plan in every for item in plan.scratch()]
    scratch += [
        pltpu.VMEM((POOL, LEN, D), jnp.bfloat16),
        pltpu.VMEM((LEN, D), jnp.float32),
        pltpu.VMEM((D, LEN), jnp.bfloat16),
        pltpu.VMEM((2, TILE, 2 * TILE), jnp.float32),
        pltpu.VMEM((2, TILE, 2 * TILE), jnp.float32),
        pltpu.VMEM((2, 8, TILE), jnp.float32),
        pltpu.VMEM((LANES, LEN), jnp.float32),
        pltpu.VMEM((3 + H, 1, D), jnp.float32),
        pltpu.VMEM((links, 3 + H, 1, D), jnp.float32),
        pltpu.SemaphoreType.DMA((links,)),
        pltpu.SemaphoreType.DMA((links,)),
        pltpu.SemaphoreType.DMA((len(big) + 3 * (keys // LEN) - 2 + 1,)),
        pltpu.SemaphoreType.DMA((LEN // ROWS,)),
    ]
    return pl.pallas_call(
        partial(last_kernel, n_blk, n_dp, plans, enc_plan),
        in_specs=[any_spec()] * len(big) + [vmem_spec()] * len(little),
        out_specs=[vmem_spec()] * len(every) + [any_spec(), vmem_spec()],
        out_shape=[plan.out_shape() for plan in every]
        + [jax.ShapeDtypeStruct((LEN, D), jnp.float32), jax.ShapeDtypeStruct((3 + H, 1, D), jnp.float32)],
        scratch_shapes=scratch,
        compiler_params=pltpu.CompilerParams(
            vmem_limit_bytes=VMEM_LIMIT, collective_id=1, has_side_effects=True
        ),
        cost_estimate=pl.CostEstimate(flops=40 * LEN * D * D, bytes_accessed=80 * LEN * D, transcendentals=0),
    )(*big, *little)


def segment_rows(lengths_ref):
    rows = lax.broadcasted_iota(jnp.int32, (LEN, LANES), 0)
    end = jnp.zeros((1, 1), jnp.int32)
    seg = jnp.zeros((LEN, LANES), jnp.int32)
    for t in range(TARGETS - 1):
        end = end + lengths_ref[:, t : t + 1]
        seg = seg + (rows >= end).astype(jnp.int32)
    return seg


def query_marks(seg):
    place = lane_ids(LEN) & (HD - 1)
    return jnp.where((place >= 3) & (place - 3 == seg), 1.0, 0.0).astype(jnp.bfloat16)


def key_marks(seg):
    place = lane_ids(LEN) & (HD - 1)
    other = (place >= 3) & (place < 3 + TARGETS) & (place - 3 != seg)
    return jnp.where(place < 3, -1.0, jnp.where(other, NEG, 0.0)).astype(jnp.bfloat16)


def value_marks(rows):
    place = lane_ids(rows) & (HD - 1)
    return jnp.where(place < 3, 1.0, 0.0).astype(jnp.bfloat16)


def bias_lines(table_ref):
    offsets = lax.broadcasted_iota(jnp.int32, (1, WIN), 1) - TILE
    chosen = bucket_vector(None, jnp.maximum(offsets, 0))
    lines = dot_tn(table_ref[...], chosen)
    return jnp.where(offsets >= 0, lines, NEG), lines[:, WIN - 1 :]


def front_kernel(n_blk, n_dp, x_hbm, enc_hbm, wq_hbm, wk_hbm, wv_hbm, wo_hbm, wcq_hbm, wck_hbm, wcv_hbm,
                 lengths_ref, gain_ref, gainc_ref, table_ref,
                 q_hbm, k_hbm, v_hbm, o_hbm, aug_hbm, act_hbm, y1_hbm, actc_hbm, qc_hbm, kv_hbm, encall_hbm,
                 x_ref, w_ref, act_ref, q_ref, k_ref, v_ref, o_ref, aug_ref, y1_ref, kv_ref, enc_ref, bias_ref, ot_ref, logs_ref,
                 send_sem, recv_sem, load_sem, store_sem):
    passage = enc_hbm.shape[0]
    loads = []
    for n, (src, dst) in enumerate(
        [(enc_hbm, enc_ref.at[0]), (x_hbm, x_ref)]
        + [(w, w_ref.at[i]) for i, w in enumerate((wq_hbm, wk_hbm, wv_hbm, wo_hbm, wcq_hbm, wck_hbm, wcv_hbm))]
    ):
        loads.append(pltpu.make_async_copy(src, dst, load_sem.at[n]))
        loads[-1].start()
    stores = []

    def store(src, dst):
        stores.append(pltpu.make_async_copy(src, dst, store_sem.at[len(stores)]))
        stores[-1].start()

    bits = bits_of(n_blk)

    def gather(k):
        size = 1 << k
        return pltpu.make_async_remote_copy(
            src_ref=enc_ref.at[pl.ds(0, size)],
            dst_ref=enc_ref.at[pl.ds(size, size)],
            send_sem=send_sem.at[k],
            recv_sem=recv_sem.at[k],
            device_id=partner("blk", bits - 1 - k),
            device_id_type=pl.DeviceIdType.MESH,
        )

    barrier = pltpu.get_barrier_semaphore()
    for bit in range(bits):
        pl.semaphore_signal(barrier, inc=1, device_id=partner("blk", bit), device_id_type=pl.DeviceIdType.MESH)
    pl.semaphore_wait(barrier, bits)
    loads[0].wait()
    gather(0).start()
    loads[1].wait()
    for r in range(0, LEN, ROWS):
        rows = slice(r, r + ROWS)
        x = x_ref[rows].astype(jnp.float32)
        act_ref[rows] = (x * norm_parts(x) * gain_ref[...].reshape(1, D)).astype(jnp.bfloat16)
    for i, (ref, out) in enumerate(((q_ref, q_hbm), (k_ref, k_hbm), (v_ref, v_hbm))):
        loads[2 + i].wait()
        for r in range(0, LEN, ROWS):
            rows = slice(r, r + ROWS)
            ref[rows] = dot_nn(act_ref[rows], w_ref[i]).astype(jnp.bfloat16)
        store(ref, out)
    store(act_ref, act_hbm)
    seg = segment_rows(lengths_ref)
    aq, ak = query_marks(seg), key_marks(seg)
    lines, fars = bias_lines(table_ref)
    for p in range(PAIRS):
        lanes = slice(p * LANES, (p + 1) * LANES)
        if p % 2 == 1 and p // 2 < bits - 1:
            gather(p // 2).wait()
            gather(p // 2 + 1).start()
        self_pair_forward(q_ref[:, lanes], k_ref[:, lanes], v_ref[:, lanes], aq, ak, lines[2 * p : 2 * p + 2],
                          fars[2 * p : 2 * p + 2], bias_ref, ot_ref, logs_ref, o_ref, aug_ref, lanes)
    store(o_ref, o_hbm)
    store(aug_ref, aug_hbm)
    for k in range(min(bits - 1, PAIRS // 2), bits - 1):
        gather(k).wait()
        gather(k + 1).start()
    for n in range(5, 9):
        loads[n].wait()
    for r in range(0, LEN, ROWS):
        rows = slice(r, r + ROWS)
        y1 = x_ref[rows].astype(jnp.float32) + dot_nn(o_ref[rows], w_ref[3])
        y1_ref[rows] = y1
        store(y1_ref.at[pl.ds(r, ROWS)], y1_hbm.at[pl.ds(r, ROWS)])
        actc = (y1 * norm_parts(y1) * gainc_ref[...].reshape(1, D)).astype(jnp.bfloat16)
        x_ref[rows] = actc
        store(x_ref.at[pl.ds(r, ROWS)], actc_hbm.at[pl.ds(r, ROWS)])
    gather(bits - 1).wait()
    for s in range(0, n_blk):
        store(enc_ref.at[s], encall_hbm.at[pl.ds(s * passage, passage)])
    group = ROWS // passage
    for s in range(0, n_blk, group):
        encs = enc_ref[s : s + group].reshape(group * passage, D)
        rows = slice(s * passage, (s + group) * passage)
        kv_ref[rows, :D] = dot_nn(encs, w_ref[5]).astype(jnp.bfloat16)
        kv_ref[rows, D:] = dot_nn(encs, w_ref[6]).astype(jnp.bfloat16)
    store(kv_ref, kv_hbm)
    stores[0].wait()
    for r in range(0, LEN, ROWS):
        rows = slice(r, r + ROWS)
        q_ref[rows] = dot_nn(x_ref[rows], w_ref[4]).astype(jnp.bfloat16)
        store(q_ref.at[pl.ds(r, ROWS)], qc_hbm.at[pl.ds(r, ROWS)])
    for copy in stores[1:]:
        copy.wait()


def self_pair_forward(q_raw, k_raw, v_raw, aq, ak, line, far, bias_ref, ot_ref, logs_ref, o_ref, aug_ref, lanes):
    for head in range(2):
        spread = jnp.broadcast_to(line[head : head + 1], (TILE, WIN))
        bias_ref[head] = pltpu.roll(spread, 0, 1, stride=1, stride_axis=0)[:, TILE:]
    v_t = v_raw.T
    for head in range(2):
        half = in_half(LEN, head)
        q = jnp.where(half, q_raw * jnp.bfloat16(SCALE), aq)
        k = jnp.where(half, k_raw, ak)
        for i in range(LEN // TILE):
            cols = slice(i * TILE, (i + 1) * TILE)
            tiles = []
            for j in range(max(0, i - 2), i + 1):
                scores = dot_nt(k[j * TILE : (j + 1) * TILE], q[cols])
                if i - j < 2:
                    scores = scores + bias_ref[head, :, (i - j) * TILE : (i - j + 1) * TILE]
                else:
                    scores = scores + far[head : head + 1]
                tiles.append(scores)
            peak = tiles[0]
            for tile in tiles[1:]:
                peak = jnp.maximum(peak, tile)
            top = jnp.max(peak, axis=0, keepdims=True)
            total, mixed = None, None
            for n, j in enumerate(range(max(0, i - 2), i + 1)):
                expo = jnp.exp(tiles[n] - top)
                part = jnp.sum(expo, axis=0, keepdims=True)
                out = dot_nn(v_t[head * HD : (head + 1) * HD, j * TILE : (j + 1) * TILE], expo.astype(jnp.bfloat16))
                total = part if total is None else total + part
                mixed = out if mixed is None else mixed + out
            ot_ref[head * HD : (head + 1) * HD, cols] = mixed * (1.0 / total)
            logs_ref[head : head + 1, cols] = top + jnp.log(total)
    o_ref[:, lanes] = ot_ref[...].T.astype(jnp.bfloat16)
    first, second = split3(logs_ref[0:1]), split3(logs_ref[1:2])
    zeros = jnp.zeros((HD - 8, LEN), jnp.float32)
    pad = jnp.zeros((5, LEN), jnp.float32)
    triples = jnp.concatenate(list(second) + [pad, zeros] + list(first) + [pad, zeros], axis=0).T
    place = lane_ids(LEN) & (HD - 1)
    aug_ref[:, lanes] = jnp.where(place < 3, triples.astype(jnp.bfloat16), aq)


def front_block(n_blk, n_dp, big, little, keys, passage):
    wide = jax.ShapeDtypeStruct((LEN, D), jnp.bfloat16)
    n_store = 6 + n_blk + 3 * (LEN // ROWS) + 1
    return pl.pallas_call(
        partial(front_kernel, n_blk, n_dp),
        in_specs=[any_spec()] * len(big) + [vmem_spec()] * len(little),
        out_specs=[any_spec()] * 11,
        out_shape=[wide] * 6
        + [
            jax.ShapeDtypeStruct((LEN, D), jnp.float32),
            wide,
            wide,
            jax.ShapeDtypeStruct((keys, 2 * D), jnp.bfloat16),
            jax.ShapeDtypeStruct((keys, D), jnp.bfloat16),
        ],
        scratch_shapes=[
            pltpu.VMEM((LEN, D), jnp.bfloat16),
            pltpu.VMEM((7, D, D), jnp.bfloat16),
            pltpu.VMEM((LEN, D), jnp.bfloat16),
            pltpu.VMEM((LEN, D), jnp.bfloat16),
            pltpu.VMEM((LEN, D), jnp.bfloat16),
            pltpu.VMEM((LEN, D), jnp.bfloat16),
            pltpu.VMEM((LEN, D), jnp.bfloat16),
            pltpu.VMEM((LEN, D), jnp.bfloat16),
            pltpu.VMEM((LEN, D), jnp.float32),
            pltpu.VMEM((keys, 2 * D), jnp.bfloat16),
            pltpu.VMEM((n_blk, passage, D), jnp.bfloat16),
            pltpu.VMEM((2, TILE, 2 * TILE), jnp.float32),
            pltpu.VMEM((LANES, LEN), jnp.float32),
            pltpu.VMEM((2, LEN), jnp.float32),
            pltpu.SemaphoreType.DMA((bits_of(n_blk),)),
            pltpu.SemaphoreType.DMA((bits_of(n_blk),)),
            pltpu.SemaphoreType.DMA((len(big),)),
            pltpu.SemaphoreType.DMA((n_store,)),
        ],
        compiler_params=pltpu.CompilerParams(
            vmem_limit_bytes=VMEM_LIMIT, collective_id=2, has_side_effects=True
        ),
        cost_estimate=pl.CostEstimate(flops=20 * LEN * D * D, bytes_accessed=40 * LEN * D, transcendentals=0),
    )(*big, *little)


FF_STEPS = 4


def normal_cdf_pair(u):
    x = jnp.abs(u) * 0.7071067811865476
    gauss = jnp.exp(-0.5 * u * u)
    t = 1.0 / (1.0 + 0.3275911 * x)
    poly = ((((1.061405429 * t - 1.453152027) * t + 1.421413741) * t - 0.284496736) * t + 0.254829592) * t
    tail = 0.5 * poly * gauss
    return jnp.where(u >= 0, 1.0 - tail, tail), gauss * 0.3989422804014327


def rest_slot(owner, piece, order):
    slot = 0
    for axis, bit in order[3:]:
        mine = (lax.axis_index(axis) // (1 << bit)) % 2
        its = ((owner if axis == "blk" else piece) // (1 << bit)) % 2
        slot = 2 * slot + (its + mine) % 2
    return slot


class FeedParts:
    def __init__(self, plan, owners, units):
        self.plan, self.owners, self.units = plan, owners, units
        self.count = owners // 2 * len(units)

    def split(self, grad, even_core, put_send, put_keep):
        n = 0
        for t in range(0, self.owners, 2):
            for u in self.units:
                even, odd = grad(t, u), grad(t + 1, u)
                put_send(n, jnp.where(even_core, odd, even).astype(jnp.bfloat16))
                put_keep(n, jnp.where(even_core, even, odd).astype(jnp.bfloat16))
                n += 1

    def index(self, t, u):
        return t // 2 * len(self.units) + self.units.index(u)


def twin_units(plan, owners, units):
    axis, bit = plan.order[1]
    if axis == "dp":
        return [((t, u), (t, u + plan.mats)) for t in range(0, owners, 2) for u in units if u < plan.mats]
    return [((t, u), (t + 2, u)) for t in range(0, owners, 4) for u in units]


def feed_kernel(n_blk, n_dp, plan_in, plan_out, y1_ref, oc_ref, wco_ref, gain_ref, g_ref, w1_ref, w2_ref,
                out_ref, isend_ref, ikeep_ref, osend_ref, okeep_ref, dy2_ref, e2_ref, doc_ref, dgain_ref,
                act_ref, acc_ref, da_ref, hid_ref, du_ref, away_ref, stay_ref, got_ref,
                away2_ref, stay2_ref, got2_ref, send_sem, recv_sem):
    step = pl.program_id(0)
    even_core = lax.axis_index("blk") % 2 == 0
    group = n_blk // FF_STEPS
    parts_out = FeedParts(plan_out, group, list(range(plan_out.count)))
    parts_in = FeedParts(plan_in, n_blk, [0])
    twins_out = twin_units(plan_out, group, parts_out.units)
    twins_in = twin_units(plan_in, n_blk, parts_in.units)
    y2_ref = dy2_ref
    gain = gain_ref[...].reshape(1, D)

    def remote(src, dst, n, s, link):
        return pltpu.make_async_remote_copy(
            src_ref=src, dst_ref=dst, send_sem=send_sem.at[n, s], recv_sem=recv_sem.at[n, s],
            device_id=partner(*link), device_id_type=pl.DeviceIdType.MESH,
        )

    def exchange(s):
        return remote(away_ref.at[s], got_ref.at[s], 0, s, ("blk", 0))

    def second(s):
        first, rest = pl.ds(0, len(twins_out)), pl.ds(len(twins_out), len(twins_in))
        return (
            remote(away2_ref.at[s, first], got2_ref.at[s, first], 1, s, plan_out.order[1]),
            remote(away2_ref.at[s, rest], got2_ref.at[s, rest], 2, s, plan_in.order[1]),
        )

    def low_side(plan, k):
        axis, bit = plan.order[k]
        return (lax.axis_index(axis) // (1 << bit)) % 2 == 0

    def settle(s):
        exchange(s).wait()
        both = [(plan_out, parts_out, 0, a, b) for a, b in twins_out]
        both += [(plan_in, parts_in, parts_out.count, a, b) for a, b in twins_in]
        for n, (plan, parts, base, a, b) in enumerate(both):
            low = low_side(plan, 1)
            sums = []
            for t, u in (a, b):
                i = base + parts.index(t, u)
                sums.append((stay_ref[i].astype(jnp.float32) + got_ref[s, i].astype(jnp.float32)).astype(jnp.bfloat16))
            away2_ref[s, n] = jnp.where(low, sums[1], sums[0])
            stay2_ref[n] = jnp.where(low, sums[0], sums[1])
        for copy in second(s):
            copy.start()

    def settle2(s):
        for copy in second(s):
            copy.wait()

        def total(n):
            return (stay2_ref[n].astype(jnp.float32) + got2_ref[s, n].astype(jnp.float32)).astype(jnp.bfloat16)

        def pair_up(plan, twins, base, owner, piece, inner, send_ref, keep_ref):
            bit = plan.order[2][1]
            low = low_side(plan, 2)
            for n, ((t, u), _) in enumerate(twins):
                if (t >> bit) & 1:
                    continue
                other = [x[0] for x in twins].index((t + (1 << bit), u))
                a, b = total(base + n), total(base + other)
                slot = rest_slot(owner(t), piece(u), plan.order)
                send_ref[slot, inner(u)] = jnp.where(low, b, a)
                keep_ref[slot, inner(u)] = jnp.where(low, a, b)

        owner_out = lambda t: s * group + t
        bit_out = plan_out.order[2][1]
        if (1 << bit_out) < group:
            pair_up(plan_out, twins_out, 0, owner_out, lambda u: u // plan_out.mats, lambda u: u % plan_out.mats,
                    osend_ref, okeep_ref)
        else:
            its = (s * group // (1 << bit_out)) % 2
            mine = (lax.axis_index("blk") // (1 << bit_out)) % 2

            def put_all(ref):
                for n, ((t, u), _) in enumerate(twins_out):
                    ref[rest_slot(owner_out(t), 0, plan_out.order), u % plan_out.mats] = total(n)

            pl.when(its == mine)(lambda: put_all(okeep_ref))
            pl.when(its != mine)(lambda: put_all(osend_ref))
        pair_up(plan_in, twins_in, len(twins_out), lambda t: t, lambda u: s // plan_in.mats, lambda u: s % plan_in.mats,
                isend_ref, ikeep_ref)

    @pl.when(step == 0)
    def _():
        barrier = pltpu.get_barrier_semaphore()
        links = sorted({("blk", 0), plan_out.order[1], plan_in.order[1]})
        for link in links:
            pl.semaphore_signal(barrier, inc=1, device_id=partner(*link), device_id_type=pl.DeviceIdType.MESH)
        pl.semaphore_wait(barrier, len(links))
        for r in range(0, LEN, ROWS):
            rows = slice(r, r + ROWS)
            y2 = y1_ref[rows] + dot_nn(oc_ref[rows], wco_ref[...])
            y2_ref[rows] = y2
            act_ref[rows] = (y2 * norm_parts(y2) * gain).astype(jnp.bfloat16)
        acc_ref[...] = y2_ref[...]
        da_ref[...] = jnp.zeros_like(da_ref)

    for r in range(0, LEN, ROWS):
        rows = slice(r, r + ROWS)
        u = dot_nn(act_ref[rows], w1_ref[...])
        dh = dot_nt(g_ref[rows], w2_ref[...])
        cdf, density = normal_cdf_pair(u)
        hid = (u * cdf).astype(jnp.bfloat16)
        du = (dh * (cdf + u * density)).astype(jnp.bfloat16)
        hid_ref[rows] = hid
        du_ref[rows] = du
        acc_ref[rows] += dot_nn(hid, w2_ref[...])
        da_ref[rows] += dot_nt(du, w1_ref[...])
        if r == 0:
            pl.when(step > 0)(lambda: settle(step - 1))

    dw2 = dot_tn(hid_ref[...], g_ref[...])
    own_rows = plan_out.rows * plan_out.count
    parts_out.split(
        lambda t, m: dw2[t * own_rows + m * plan_out.rows : t * own_rows + (m + 1) * plan_out.rows],
        even_core,
        lambda n, value: away_ref.__setitem__((step, n), value),
        lambda n, value: stay_ref.__setitem__(n, value),
    )
    dw1 = dot_tn(act_ref[...], du_ref[...])
    parts_in.split(
        lambda t, m: dw1[t * plan_in.rows : (t + 1) * plan_in.rows],
        even_core,
        lambda n, value: away_ref.__setitem__((step, parts_out.count + n), value),
        lambda n, value: stay_ref.__setitem__(parts_out.count + n, value),
    )
    exchange(step).start()

    @pl.when(step > 0)
    def _():
        settle2(step - 1)

    @pl.when(step == FF_STEPS - 1)
    def _():
        gain_sum = jnp.zeros((1, D), jnp.float32)
        for r in range(0, LEN, ROWS):
            rows = slice(r, r + ROWS)
            out_ref[rows] = acc_ref[rows].astype(jnp.bfloat16)
            y2 = y2_ref[rows]
            inverse = norm_parts(y2)
            da = da_ref[rows]
            gain_sum = gain_sum + jnp.sum(da * y2 * inverse, axis=0, keepdims=True)
            if r == ROWS:
                settle(step)
            dy2 = g_ref[rows].astype(jnp.float32) + norm_back(y2, inverse, gain, da)
            dy2_ref[rows] = dy2
            e2 = dy2.astype(jnp.bfloat16)
            e2_ref[rows] = e2
            doc_ref[rows] = dot_nt(e2, wco_ref[...]).astype(jnp.bfloat16)
        dgain_ref[...] = gain_sum
        settle2(step)


def feed_block(n_blk, n_dp, y1, oc, wco, gain, g, w1, w2, plan_in, plan_out):
    ff = w1.shape[1]
    cols = ff // FF_STEPS
    fixed = vmem_spec()
    eighth = lambda plan: (plan.slots // 8, plan.mats, plan.rows, D)
    like = jax.ShapeDtypeStruct
    units = n_blk // FF_STEPS // 2 * plan_out.count + n_blk // 2
    packet = (units, D // n_blk, D)
    packet2 = (units // 2, D // n_blk, D)
    return pl.pallas_call(
        partial(feed_kernel, n_blk, n_dp, plan_in, plan_out),
        grid=(FF_STEPS,),
        in_specs=[fixed] * 5
        + [
            pl.BlockSpec((D, cols), lambda c: (0, c)),
            pl.BlockSpec((cols, D), lambda c: (c, 0)),
        ],
        out_specs=[fixed] * 9,
        out_shape=[
            like((LEN, D), jnp.bfloat16),
            like(eighth(plan_in), jnp.bfloat16),
            like(eighth(plan_in), jnp.bfloat16),
            like(eighth(plan_out), jnp.bfloat16),
            like(eighth(plan_out), jnp.bfloat16),
            like((LEN, D), jnp.float32),
            like((LEN, D), jnp.bfloat16),
            like((LEN, D), jnp.bfloat16),
            like((1, D), jnp.float32),
        ],
        scratch_shapes=[
            pltpu.VMEM((LEN, D), jnp.bfloat16),
            pltpu.VMEM((LEN, D), jnp.float32),
            pltpu.VMEM((LEN, D), jnp.float32),
            pltpu.VMEM((LEN, cols), jnp.bfloat16),
            pltpu.VMEM((LEN, cols), jnp.bfloat16),
            pltpu.VMEM((FF_STEPS,) + packet, jnp.bfloat16),
            pltpu.VMEM(packet, jnp.bfloat16),
            pltpu.VMEM((FF_STEPS,) + packet, jnp.bfloat16),
            pltpu.VMEM((FF_STEPS,) + packet2, jnp.bfloat16),
            pltpu.VMEM(packet2, jnp.bfloat16),
            pltpu.VMEM((FF_STEPS,) + packet2, jnp.bfloat16),
            pltpu.SemaphoreType.DMA((3, FF_STEPS)),
            pltpu.SemaphoreType.DMA((3, FF_STEPS)),
        ],
        compiler_params=pltpu.CompilerParams(
            vmem_limit_bytes=VMEM_LIMIT, collective_id=3, has_side_effects=True
        ),
        cost_estimate=pl.CostEstimate(flops=12 * LEN * D * ff, bytes_accessed=40 * LEN * D, transcendentals=0),
    )(y1, oc, wco, gain, g, w1, w2)


def unpack_kernel(in_ref, out_ref, crossx, crossy, *refs):
    blocks, (enc_ref, sums_ref), outs = refs[: len(BLOCK_PAIRS)], refs[len(BLOCK_PAIRS) : len(BLOCK_PAIRS) + 2], refs[len(BLOCK_PAIRS) + 2 :]
    (gq, gk, gv, go, gcq, gck, gcv, gco, gin, gout, genc, gain0, gain1, gain2, table) = outs
    for w, ref in enumerate((gq, gk, gv)):
        at = 0
        for part, pairs in zip(blocks, BLOCK_PAIRS):
            for c in range(pairs):
                ref[:, at : at + LANES] = part[pairs * w + c]
                at += LANES
    half = D // 2
    for ref, part, w in ((gcq, crossx, 0), (gck, crossx, 1), (gcv, crossx, 2), (gco, crossy, 0), (go, crossy, 1)):
        for c in range(2):
            ref[:, c * half : (c + 1) * half] = part[2 * w + c]
    rows = gq.shape[0]
    for m in range(4):
        gin[:, m * D : (m + 1) * D] = in_ref[m]
        gout[m * rows : (m + 1) * rows] = out_ref[m]
    genc[...] = enc_ref[0]
    for n, ref in enumerate((gain0, gain1, gain2)):
        ref[...] = sums_ref[n].reshape(D)
    tables = jnp.concatenate([sums_ref[3 + h][:, :LANES] for h in range(H)] + [jnp.zeros((4, LANES), jnp.float32)], axis=0)
    table[...] = tables.T[:BUCKETS, :H]


def unpack(n_blk, passage, parts):
    rows = D // n_blk
    like = lambda *shape: jax.ShapeDtypeStruct(shape, jnp.float32)
    return pl.pallas_call(
        unpack_kernel,
        in_specs=[vmem_spec()] * len(parts),
        out_specs=[vmem_spec()] * 15,
        out_shape=[like(rows, D)] * 8
        + [like(rows, 4 * D), like(4 * rows, D), like(passage, D)]
        + [like(D)] * 3
        + [like(BUCKETS, H)],
        compiler_params=pltpu.CompilerParams(vmem_limit_bytes=VMEM_LIMIT),
    )(*parts)


def swap(value, axis, bit, size):
    return lax.ppermute(value, axis, [(i, i ^ (1 << bit)) for i in range(size)])


def per_device(
    decoder_rows,
    encoder_rows,
    target_lengths,
    target_question,
    passage_question,
    self_gain,
    self_query,
    self_key,
    self_value,
    self_output,
    position_bias_matrix,
    cross_gain,
    cross_query,
    cross_key,
    cross_value,
    cross_output,
    feed_gain,
    feed_input_weight,
    feed_out,
    cotangent,
    n_dp,
    n_blk,
):
    passage = encoder_rows.shape[0]
    keys = passage * n_blk
    sizes = {"blk": n_blk, "dp": n_dp}
    (query_self, key_self, value_self, attn_self, aug_self, act_self, resid_self, act_cross, query_cross, pair_all,
     encoder_all) = front_block(
        n_blk, n_dp,
        (decoder_rows, encoder_rows, self_query, self_key, self_value, self_output, cross_query, cross_key, cross_value),
        (target_lengths, self_gain, cross_gain, position_bias_matrix), keys, passage,
    )
    layout = (target_lengths, target_question, passage_question)
    attn_cross, aug_cross = cross_forward(n_blk, passage, *layout, query_cross, pair_all)
    plan_in, plan_out = feed_plans(n_blk, n_dp)
    (block_out, in_send, in_keep, out_send, out_keep, grad_resid_cross, round_cross, grad_attn_cross, feed_sum) = feed_block(
        n_blk, n_dp, resid_self, attn_cross, cross_output, feed_gain, cotangent, feed_input_weight, feed_out,
        plan_in, plan_out,
    )
    in_got = swap(in_send, *plan_in.order[FEED_DONE - 1], sizes[plan_in.order[FEED_DONE - 1][0]])
    out_got = swap(out_send, *plan_out.order[FEED_DONE - 1], sizes[plan_out.order[FEED_DONE - 1][0]])
    dqc, dkv, grad_resid_self, grad_attn_self, encoder_part, cross_sum = cross_backward(
        n_blk, passage, *layout, query_cross, pair_all, grad_attn_cross, attn_cross, aug_cross,
        resid_self, grad_resid_cross, cross_query, cross_key, cross_value, self_output, cross_gain,
    )
    enc_plan = Exchange(1, passage, D, n_blk, n_dp, "near")
    big = (
        decoder_rows, grad_resid_self, act_self, self_query, self_key, self_value, act_cross, dqc, encoder_all, dkv,
        attn_cross, round_cross, query_self, key_self, value_self, grad_attn_self, attn_self, aug_self,
        in_keep, in_got, out_keep, out_got, encoder_part,
    )
    last = last_block(
        n_blk, n_dp, last_plans(n_blk, n_dp), enc_plan, big,
        (target_lengths, self_gain, position_bias_matrix, cross_sum, feed_sum), keys,
    )
    spot = len(last) - 2
    grad_decoder = last[spot]
    (gq, gk, gv, go, gcq, gck, gcv, gco, gin, gout, genc, gain_self, gain_cross, gain_feed, table) = unpack(
        n_blk, passage, last[:spot] + last[spot + 1 :]
    )
    return (
        block_out, grad_decoder, genc, gain_self, gq, gk, gv, go, table, gain_cross, gcq, gck, gcv, gco,
        gain_feed, gin, gout,
    )


def solution(mesh):
    split, copied, owned = P(("dp", "blk"), None), P(), P("blk", None)
    return jax.shard_map(
        partial(per_device, n_dp=mesh.shape["dp"], n_blk=mesh.shape["blk"]),
        mesh=mesh,
        in_specs=(split,) * 4 + (P("dp"),) + (copied,) * 14 + (split,),
        out_specs=(split,) * 3 + (copied,) + (owned,) * 4 + (copied,) * 2 + (owned,) * 4 + (copied,) + (owned,) * 2,
        check_vma=False,
    )
```

```python
import functools
from functools import partial

import jax
import jax.numpy as jnp
from jax import lax
from jax.experimental import pallas as pl
from jax.experimental.pallas import tpu as pltpu
from jax.sharding import PartitionSpec as P

D = 768
H = 12
HD = 64
BUCKETS = 32
LEN = 1024
TARGETS = 4
PAIRS = H // 2
LANES = 2 * HD
TILE = 256
SCALE = HD ** -0.5
NEG = -1e30
VMEM_LIMIT = 60 * 1024 * 1024

eps_norm = 1e-06
bucket_edges = (19, 21, 24, 27, 31, 35, 40, 46, 52, 59, 67, 77, 87, 99, 113)


def dot_nn(a, b):
    return jnp.dot(a, b, preferred_element_type=jnp.float32)


def dot_nt(a, b):
    return lax.dot_general(a, b, (((1,), (1,)), ((), ())), preferred_element_type=jnp.float32)


def dot_tn(a, b):
    return lax.dot_general(a, b, (((0,), (0,)), ((), ())), preferred_element_type=jnp.float32)


def lane_ids(rows):
    return lax.broadcasted_iota(jnp.int32, (rows, LANES), 1)


def in_half(rows, head):
    lane = lane_ids(rows)
    return lane < HD if head == 0 else lane >= HD


def split3(value):
    high = value.astype(jnp.bfloat16).astype(jnp.float32)
    rest = value - high
    mid = rest.astype(jnp.bfloat16).astype(jnp.float32)
    return high, mid, rest - mid


def triple_lanes(first, second, rows):
    lane = lane_ids(rows)
    out = jnp.zeros((rows, LANES), jnp.float32)
    for base, value in ((HD, first), (0, second)):
        for place, part in enumerate(split3(value)):
            out = jnp.where(lane == base + place, part, out)
    return out


def bucket_vector(table_t, offsets):
    upper = jnp.full(offsets.shape, 16, jnp.int32)
    for edge in bucket_edges:
        upper = upper + (offsets >= edge).astype(jnp.int32)
    bucket = jnp.where(offsets < 16, offsets, upper)
    rows = lax.broadcasted_iota(jnp.int32, (BUCKETS, offsets.shape[1]), 0)
    chosen = (rows == bucket).astype(jnp.float32).astype(jnp.bfloat16)
    return chosen


WIN = 3 * TILE


ROWS = 256


def norm_parts(values):
    return lax.rsqrt(jnp.mean(values * values, axis=1, keepdims=True) + eps_norm)


def norm_back(values, inverse, gain, grad):
    scaled = grad * gain
    inner = jnp.mean(scaled * values, axis=1, keepdims=True)
    return inverse * scaled - values * (inverse * inverse * inverse * inner)


CT = 256


def cross_layout(n_blk, lengths_ref, question_ref, passage_ref, order_ref, item_ref, count_ref):
    per_q = n_blk // TARGETS
    bits = bits_of(n_blk)
    me = lax.axis_index("blk")
    for t in range(TARGETS + 1):
        count_ref[t] = 0
    for s in range(n_blk):
        device = 0
        for b in range(bits):
            mine = (me // (1 << b)) % 2
            flip = (s >> (bits - 1 - b)) & 1
            device = device + (1 - mine if flip else mine) * (1 << b)
        question = passage_ref[device]
        order_ref[question * per_q + count_ref[question]] = s
        count_ref[question] = count_ref[question] + 1
    end = 0
    for t in range(TARGETS):
        start, end = end, end + lengths_ref[0, t]
        question = question_ref[0, t]

        @pl.loop(start // CT, (end + CT - 1) // CT)
        def _(tile, start=start, end=end, question=question):
            n = count_ref[TARGETS]
            item_ref[0, n] = tile
            item_ref[1, n] = question
            item_ref[2, n] = start - tile * CT
            item_ref[3, n] = end - tile * CT
            count_ref[TARGETS] = n + 1


def layout_scratch(n_blk):
    return [
        pltpu.SMEM((n_blk,), jnp.int32),
        pltpu.SMEM((4, LEN // CT + TARGETS), jnp.int32),
        pltpu.SMEM((TARGETS + 1,), jnp.int32),
    ]


def cross_forward_kernel(n_blk, passage, lengths_ref, question_ref, passage_ref, q_ref, kv_ref, o_ref, aug_ref,
                         ks_ref, vs_ref, order_ref, item_ref, count_ref):
    keys_q = n_blk // TARGETS * passage
    lower = lax.broadcasted_iota(jnp.int32, (passage, D), 1) % LANES < HD
    zero = jnp.zeros((), jnp.bfloat16)
    cross_layout(n_blk, lengths_ref, question_ref, passage_ref, order_ref, item_ref, count_ref)

    @pl.loop(0, n_blk)
    def _(s):
        src = pl.multiple_of(order_ref[s] * passage, passage)
        dst = pl.multiple_of(s * passage, passage)
        keys = kv_ref[pl.ds(src, passage), :D]
        values = kv_ref[pl.ds(src, passage), D:]
        ks_ref[0, pl.ds(dst, passage)] = jnp.where(lower, keys, zero)
        ks_ref[1, pl.ds(dst, passage)] = jnp.where(lower, zero, keys)
        vs_ref[0, pl.ds(dst, passage)] = jnp.where(lower, values, zero)
        vs_ref[1, pl.ds(dst, passage)] = jnp.where(lower, zero, values)

    o_ref[...] = jnp.zeros_like(o_ref)
    aug_ref[...] = jnp.zeros_like(aug_ref)

    @pl.loop(0, count_ref[TARGETS])
    def _(n):
        row0 = pl.multiple_of(item_ref[0, n] * CT, CT)
        key0 = pl.multiple_of(item_ref[1, n] * keys_q, keys_q)
        rows = lax.broadcasted_iota(jnp.int32, (CT, 1), 0)
        valid = (rows >= item_ref[2, n]) & (rows < item_ref[3, n])
        for pair in range(PAIRS):
            cols = slice(pair * LANES, (pair + 1) * LANES)
            q = q_ref[pl.ds(row0, CT), cols] * jnp.bfloat16(SCALE)
            outs, logs = [], []
            for head in range(2):
                scores = dot_nt(q, ks_ref[head, pl.ds(key0, keys_q), cols])
                top = jnp.max(scores, axis=1, keepdims=True)
                expo = jnp.exp(scores - top)
                total = jnp.sum(expo, axis=1, keepdims=True)
                outs.append(dot_nn(expo.astype(jnp.bfloat16), vs_ref[head, pl.ds(key0, keys_q), cols]) / total)
                logs.append(top + jnp.log(total))
            mixed = (outs[0] + outs[1]).astype(jnp.bfloat16)
            aug = triple_lanes(logs[0], logs[1], CT).astype(jnp.bfloat16)
            o_ref[pl.ds(row0, CT), cols] = jnp.where(valid, mixed, o_ref[pl.ds(row0, CT), cols])
            aug_ref[pl.ds(row0, CT), cols] = jnp.where(valid, aug, aug_ref[pl.ds(row0, CT), cols])


def smem_spec():
    return pl.BlockSpec(memory_space=pltpu.SMEM)


def vmem_spec():
    return pl.BlockSpec(memory_space=pltpu.VMEM)


def any_spec():
    return pl.BlockSpec(memory_space=pl.ANY)


def cross_forward(n_blk, passage, lengths, questions, passages, q, kv):
    keys = kv.shape[0]
    return pl.pallas_call(
        partial(cross_forward_kernel, n_blk, passage),
        in_specs=[smem_spec()] * 3 + [vmem_spec()] * 2,
        out_specs=[vmem_spec(), vmem_spec()],
        out_shape=[jax.ShapeDtypeStruct((LEN, D), jnp.bfloat16)] * 2,
        scratch_shapes=[pltpu.VMEM((2, keys, D), jnp.bfloat16)] * 2 + layout_scratch(n_blk),
        compiler_params=pltpu.CompilerParams(vmem_limit_bytes=VMEM_LIMIT),
        cost_estimate=pl.CostEstimate(flops=2 * H * LEN * LEN * HD, bytes_accessed=10 * LEN * D, transcendentals=0),
    )(lengths, questions, passages, q, kv)


def cross_backward_kernel(n_blk, passage, lengths_ref, question_ref, passage_ref, q_ref, do_ref, o_ref, aug_ref,
                          kv_hbm, y1_hbm, dy2_hbm, wcq_hbm, wck_hbm, wcv_hbm, wo_hbm, gain_ref,
                          dq_ref, dkv_ref, dy1_ref, dos_ref, part_ref, dgain_ref,
                          ks_ref, vs_ref, kt_ref, dk_ref, dv_ref, dqt_ref, y1_ref, load_sem,
                          order_ref, item_ref, count_ref):
    loads = []
    for n, (src, dst) in enumerate(
        [(kv_hbm, dkv_ref), (y1_hbm, y1_ref), (dy2_hbm, dy1_ref)]
    ):
        loads.append(pltpu.make_async_copy(src, dst, load_sem.at[n]))
        loads[-1].start()
    keys_q = n_blk // TARGETS * passage
    lane = lax.broadcasted_iota(jnp.int32, (passage, D), 1) % LANES
    lower = lane < HD
    ones = jnp.where((lane & (HD - 1)) < 3, 1.0, 0.0).astype(jnp.bfloat16)
    minus = -ones
    cross_layout(n_blk, lengths_ref, question_ref, passage_ref, order_ref, item_ref, count_ref)

    loads[0].wait()

    @pl.loop(0, n_blk)
    def _(s):
        src = pl.multiple_of(order_ref[s] * passage, passage)
        dst = pl.multiple_of(s * passage, passage)
        keys = dkv_ref[pl.ds(src, passage), :D]
        values = dkv_ref[pl.ds(src, passage), D:]
        ks_ref[0, pl.ds(dst, passage)] = jnp.where(lower, keys, minus)
        ks_ref[1, pl.ds(dst, passage)] = jnp.where(lower, minus, keys)
        vs_ref[0, pl.ds(dst, passage)] = jnp.where(lower, values, ones)
        vs_ref[1, pl.ds(dst, passage)] = jnp.where(lower, ones, values)

    lower_k = lax.broadcasted_iota(jnp.int32, (keys_q, LANES), 1) < HD
    for s in range(TARGETS):
        for pair in range(PAIRS):
            rows = slice(s * keys_q, (s + 1) * keys_q)
            cols = slice(pair * LANES, (pair + 1) * LANES)
            both = jnp.where(lower_k, ks_ref[0, rows, cols], ks_ref[1, rows, cols])
            kt_ref[cols, rows] = both.T
    dk_ref[...] = jnp.zeros_like(dk_ref)
    dv_ref[...] = jnp.zeros_like(dv_ref)
    dqt_ref[...] = jnp.zeros_like(dqt_ref)

    @pl.loop(0, count_ref[TARGETS])
    def _(n):
        row0 = pl.multiple_of(item_ref[0, n] * CT, CT)
        key0 = pl.multiple_of(item_ref[1, n] * keys_q, keys_q)
        rows = lax.broadcasted_iota(jnp.int32, (CT, 1), 0)
        valid = (rows >= item_ref[2, n]) & (rows < item_ref[3, n])
        here = pl.ds(row0, CT)
        there = pl.ds(key0, keys_q)
        for pair in range(PAIRS):
            cols = slice(pair * LANES, (pair + 1) * LANES)
            q_scaled = q_ref[here, cols] * jnp.bfloat16(SCALE)
            do_pair = jnp.where(valid, do_ref[here, cols], jnp.zeros((), jnp.bfloat16))
            product = do_pair.astype(jnp.float32) * o_ref[here, cols].astype(jnp.float32)
            deltas = []
            for head in range(2):
                deltas.append(jnp.sum(jnp.where(in_half(CT, head), product, 0.0), axis=1, keepdims=True))
            aug_do = (-triple_lanes(deltas[0], deltas[1], CT)).astype(jnp.bfloat16)
            aug = jnp.where(valid, aug_ref[here, cols], jnp.bfloat16(-NEG))
            parts = []
            for head in range(2):
                half = in_half(CT, head)
                q = jnp.where(half, q_scaled, aug)
                do = jnp.where(half, do_pair, aug_do)
                probs = jnp.exp(dot_nt(ks_ref[head, there, cols], q))
                grad_scores = probs * dot_nt(vs_ref[head, there, cols], do)
                ds = grad_scores.astype(jnp.bfloat16)
                parts.append((dot_nn(ds, q), dot_nn(probs.astype(jnp.bfloat16), do)))
                hrow = pair * LANES + head * HD
                dqt_ref[hrow : hrow + HD, here] += dot_nn(kt_ref[hrow : hrow + HD, there], ds)
            dk_ref[there, cols] += jnp.where(lower_k, parts[0][0], parts[1][0])
            dv_ref[there, cols] += jnp.where(lower_k, parts[0][1], parts[1][1])

    spots = (ks_ref.at[0], ks_ref.at[1], vs_ref.at[0], vs_ref.at[1])
    for n, w in enumerate((wcq_hbm, wck_hbm, wcv_hbm, wo_hbm)):
        loads.append(pltpu.make_async_copy(w, spots[n].at[pl.ds(0, D)], load_sem.at[3 + n]))
        loads[-1].start()
    for pair in range(PAIRS):
        cols = slice(pair * LANES, (pair + 1) * LANES)
        dq_ref[:, cols] = (dqt_ref[cols, :] * SCALE).T.astype(jnp.bfloat16)

    for copy in loads[1:]:
        copy.wait()

    @pl.loop(0, n_blk)
    def _(s):
        src = pl.multiple_of(s * passage, passage)
        spot = order_ref[s]
        dst = pl.multiple_of(spot * passage, passage)
        dk = dk_ref[pl.ds(src, passage)].astype(jnp.bfloat16)
        dv = dv_ref[pl.ds(src, passage)].astype(jnp.bfloat16)
        dkv_ref[pl.ds(dst, passage), :D] = dk
        dkv_ref[pl.ds(dst, passage), D:] = dv

    group = ROWS // passage
    for s in range(0, n_blk, group):
        rows = slice(s * passage, (s + group) * passage)
        part = dot_nt(dkv_ref[rows, :D], ks_ref[1, :D]) + dot_nt(dkv_ref[rows, D:], vs_ref[0, :D])
        part_ref[s : s + group, 0] = part.astype(jnp.bfloat16).reshape(group, passage, D)
    gain_sum = jnp.zeros((1, D), jnp.float32)
    for r in range(0, LEN, ROWS):
        rows = slice(r, r + ROWS)
        da = dot_nt(dq_ref[rows], ks_ref[0, :D])
        y1 = y1_ref[rows]
        inverse = norm_parts(y1)
        gain_sum = gain_sum + jnp.sum(da * y1 * inverse, axis=0, keepdims=True)
        dy1 = dy1_ref[rows] + norm_back(y1, inverse, gain_ref[...].reshape(1, D), da)
        dy1_ref[rows] = dy1
        dos_ref[rows] = dot_nt(dy1.astype(jnp.bfloat16), vs_ref[1, :D]).astype(jnp.bfloat16)
    dgain_ref[...] = gain_sum


def cross_backward(n_blk, passage, lengths, questions, passages, q, kv, do, o, aug, y1, dy2, wcq, wck, wcv, wo, gain):
    keys = kv.shape[0]
    like = jax.ShapeDtypeStruct
    return pl.pallas_call(
        partial(cross_backward_kernel, n_blk, passage),
        in_specs=[smem_spec()] * 3 + [vmem_spec()] * 4 + [any_spec()] * 7 + [vmem_spec()],
        out_specs=[vmem_spec()] * 6,
        out_shape=[
            like((LEN, D), jnp.bfloat16),
            like((keys, 2 * D), jnp.bfloat16),
            like((LEN, D), jnp.float32),
            like((LEN, D), jnp.bfloat16),
            like((n_blk, 1, passage, D), jnp.bfloat16),
            like((1, D), jnp.float32),
        ],
        scratch_shapes=[pltpu.VMEM((2, keys, D), jnp.bfloat16)] * 2
        + [
            pltpu.VMEM((D, keys), jnp.bfloat16),
            pltpu.VMEM((keys, D), jnp.float32),
            pltpu.VMEM((keys, D), jnp.float32),
            pltpu.VMEM((D, LEN), jnp.float32),
            pltpu.VMEM((LEN, D), jnp.float32),
            pltpu.SemaphoreType.DMA((7,)),
        ]
        + layout_scratch(n_blk),
        compiler_params=pltpu.CompilerParams(vmem_limit_bytes=VMEM_LIMIT),
        cost_estimate=pl.CostEstimate(flops=5 * H * LEN * LEN * HD, bytes_accessed=18 * LEN * D, transcendentals=0),
    )(lengths, questions, passages, q, do, o, aug, kv, y1, dy2, wcq, wck, wcv, wo, gain)


def bits_of(count):
    return count.bit_length() - 1


def place_bits(n_blk, n_dp, kind):
    blk = [("blk", bit) for bit in range(bits_of(n_blk))]
    dp = [("dp", bit) for bit in range(bits_of(n_dp))]
    if kind == "x":
        return blk[:1] + dp + blk[1:]
    if kind == "y":
        return blk[:2] + dp + blk[2:]
    return blk


def position(owner, piece, order):
    slot = 0
    for axis, bit in order:
        mine = (lax.axis_index(axis) // (1 << bit)) % 2
        static = ((owner if axis == "blk" else piece) >> bit) & 1
        slot = 2 * slot + (1 - mine if static else mine)
    return slot


def partner(axis, bit):
    me = lax.axis_index(axis)
    mine = (me // (1 << bit)) % 2
    return {axis: me + (1 - 2 * mine) * (1 << bit)}


class Exchange:
    def __init__(self, count, rows, cols, n_blk, n_dp, kind, first=0):
        if kind in "xy" and count % n_dp:
            kind = "plain"
        self.n_blk, self.n_dp, self.count, self.kind, self.first = n_blk, n_dp, count, kind, first
        self.rows, self.cols = rows, cols
        self.order = place_bits(n_blk, n_dp, kind)
        self.pieces = n_dp if kind in "xy" else 1
        self.slots = n_blk * self.pieces
        self.mats = count // self.pieces
        self.last = [("dp", bit) for bit in range(bits_of(n_dp))] if kind != "near" else []
        self.steps = len(self.order) + len(self.last)
        self.held = self.slots >> first
        self.offsets = {}
        at = self.held if first else 0
        for k in range(first, len(self.order)):
            size = self.slots >> (k + 1)
            self.offsets[k] = (at, size)
            at += size
        for j in range(len(self.last)):
            size = (1 << j) if self.pieces > 1 else 1
            self.offsets[len(self.order) + j] = (at, size)
            at += size
        self.received = at

    def scratch(self):
        shape = (self.mats, self.rows, self.cols)
        return [
            pltpu.VMEM((max(self.held, self.pieces),) + shape, jnp.bfloat16),
            pltpu.VMEM((self.received,) + shape, jnp.bfloat16),
            pltpu.SemaphoreType.DMA((self.steps,)),
            pltpu.SemaphoreType.DMA((self.steps,)),
        ]

    def out_shape(self):
        return jax.ShapeDtypeStruct((self.count, self.rows, self.cols), jnp.float32)

    def bind(self, refs, out_ref):
        self.buf, self.recv, self.send_sem, self.recv_sem = refs
        self.out = out_ref

    def put(self, index, value):
        piece, inner = index // self.mats, index % self.mats
        for owner in range(self.n_blk):
            slot = position(owner, piece, self.order)
            self.buf[slot, inner] = value[owner * self.rows : (owner + 1) * self.rows].astype(jnp.bfloat16)

    def copy(self, k):
        at, size = self.offsets[k]
        if k < len(self.order):
            axis, bit = self.order[k]
            src = self.buf.at[pl.ds(size, size)]
        else:
            axis, bit = self.last[k - len(self.order)]
            src = self.buf.at[pl.ds(0, size)]
        return pltpu.make_async_remote_copy(
            src_ref=src,
            dst_ref=self.recv.at[pl.ds(at, size)],
            send_sem=self.send_sem.at[k],
            recv_sem=self.recv_sem.at[k],
            device_id=partner(axis, bit),
            device_id_type=pl.DeviceIdType.MESH,
        )

    def start(self, k):
        self.copy(k).start()

    def add(self, at, size, final):
        for s in range(size):
            for m in range(self.mats):
                total = self.buf[s, m].astype(jnp.float32) + self.recv[at + s, m].astype(jnp.float32)
                if final:
                    self.out[m] = total
                else:
                    self.buf[s, m] = total.astype(jnp.bfloat16)

    def finish(self, k):
        self.copy(k).wait()
        at, size = self.offsets[k]
        final = k == self.steps - 1
        if k < len(self.order) or self.pieces == 1:
            self.add(at, size, final)
            return
        for s in range(size):
            for m in range(self.mats):
                self.buf[size + s, m] = self.recv[at + s, m]
        if final:
            for s in range(self.pieces):
                spot = position(0, s, self.last[::-1])
                for m in range(self.mats):
                    self.out[spot * self.mats + m] = self.buf[s, m].astype(jnp.float32)

    def advance(self, k):
        if k < self.first or k >= self.steps:
            return
        self.finish(k)
        if k + 1 < self.steps:
            self.start(k + 1)


def all_links(n_blk, n_dp):
    return [("blk", bit) for bit in range(bits_of(n_blk))] + [("dp", bit) for bit in range(bits_of(n_dp))]


def enter_barrier(n_blk, n_dp):
    barrier = pltpu.get_barrier_semaphore()
    links = all_links(n_blk, n_dp)
    for axis, bit in links:
        pl.semaphore_signal(barrier, inc=1, device_id=partner(axis, bit), device_id_type=pl.DeviceIdType.MESH)
    pl.semaphore_wait(barrier, len(links))


BLOCKS = 3
BLOCK = D // BLOCKS
BLOCK_PAIRS = (2,) * BLOCKS
FEED_DONE = 2


def last_plans(n_blk, n_dp):
    rows = D // n_blk
    halves = 2
    feed_in, feed_out = feed_plans(n_blk, n_dp, FEED_DONE)
    plans = [
        feed_in,
        feed_out,
        Exchange(3 * halves, rows, D // halves, n_blk, n_dp, "x"),
        Exchange(2 * halves, rows, D // halves, n_blk, n_dp, "y"),
    ]
    for block in range(BLOCKS):
        plans.append(Exchange(3 * halves, rows, BLOCK // halves, n_blk, n_dp, "xyx"[block]))
    return plans


def feed_plans(n_blk, n_dp, first=0):
    rows = D // n_blk
    return (
        Exchange(4, rows, D, n_blk, n_dp, "y", first),
        Exchange(4, rows, D, n_blk, n_dp, "x", first),
    )


POOL = 11
(S_ACTC, S_DQC, S_OC, S_E2, S_Q, S_K, S_V, S_DO, S_O, S_AUG, S_X) = range(POOL)
S_DQ, S_DK, S_DV, S_ACT = S_ACTC, S_DQC, S_OC, S_E2


def last_kernel(n_blk, n_dp, plans, enc_plan, *refs):
    (x_hbm, dy1_hbm, act_hbm, wq_hbm, wk_hbm, wv_hbm, actc_hbm, dqc_hbm, enc_hbm, dkv_hbm, oc_hbm, e2_hbm,
     q_hbm, k_hbm, v_hbm, do_hbm, o_hbm, aug_hbm, inkeep_hbm, inrecv_hbm, outkeep_hbm, outrecv_hbm, part_hbm,
     lengths_ref, gain_ref, table_ref, gainc_ref, gainf_ref) = refs[:28]
    every = list(plans) + [enc_plan]
    outs = refs[28 : 28 + len(every)]
    dx_hbm, sums_ref = refs[28 + len(every) : 30 + len(every)]
    scratch = refs[30 + len(every) :]
    for i, plan in enumerate(every):
        plan.bind(scratch[4 * i : 4 * i + 4], outs[i])
    (pool, dy1_ref, act_t, bias_ref, g_ref, gfar_ref, dqt_ref,
     tot_ref, got_ref, tsend, trecv, load_sem, store_sem) = scratch[4 * len(every) :]
    feed_in, feed_out, crossx, crossy, self0, self1, self2 = plans
    selfs = (self0, self1, self2)

    loads = {}

    def load(name, src, dst):
        loads[name] = pltpu.make_async_copy(src, dst, load_sem.at[len(loads)])
        loads[name].start()

    def slot(index):
        return pool.at[index]

    load("actc", actc_hbm, slot(S_ACTC))
    load("dqc", dqc_hbm, slot(S_DQC))
    for plan, keep, got, name in (
        (feed_out, outkeep_hbm, outrecv_hbm, "out"),
        (feed_in, inkeep_hbm, inrecv_hbm, "in"),
    ):
        load(name + "keep", keep, plan.buf.at[pl.ds(0, plan.held)])
        load(name + "recv", got, plan.recv.at[pl.ds(0, plan.held)])
    spans = enc_hbm.shape[0] // LEN
    spare = (S_Q, S_K, S_V, S_DO, S_AUG, S_X)
    for n in range(spans):
        rows = pl.ds(n * LEN, LEN)
        load(("enc", n), enc_hbm.at[rows], slot(spare[3 * n]))
        load(("dk", n), dkv_hbm.at[rows, pl.ds(0, D)], slot(spare[3 * n + 1]))
        load(("dv", n), dkv_hbm.at[rows, pl.ds(D, D)], slot(spare[3 * n + 2]))
    load("part", part_hbm, enc_plan.buf)
    load("oc", oc_hbm, slot(S_OC))
    load("e2", e2_hbm, slot(S_E2))
    load("o", o_hbm, slot(S_O))
    load("dy1", dy1_hbm, dy1_ref)
    enter_barrier(n_blk, n_dp)

    def begin_feed(plan, name):
        loads[name + "keep"].wait()
        loads[name + "recv"].wait()
        plan.add(0, plan.held, False)
        plan.start(plan.first)

    def put_halves(plan, index, value):
        half = plan.cols
        for c in range(2):
            plan.put(2 * index + c, value[:, c * half : (c + 1) * half])

    begin_feed(feed_out, "out")
    begin_feed(feed_in, "in")
    loads["actc"].wait()
    loads["dqc"].wait()
    put_halves(crossx, 0, dot_tn(pool[S_ACTC], pool[S_DQC]))
    for w, name in ((1, "dk"), (2, "dv")):
        total = None
        for n in range(spans):
            if w == 1:
                loads["enc", n].wait()
            loads[name, n].wait()
            part = dot_tn(pool[spare[3 * n]], pool[spare[3 * n + w]])
            total = part if total is None else total + part
        put_halves(crossx, w, total)
    crossx.start(0)
    for name, src, index in (
        ("q", q_hbm, S_Q), ("k", k_hbm, S_K), ("v", v_hbm, S_V), ("do", do_hbm, S_DO), ("aug", aug_hbm, S_AUG), ("x", x_hbm, S_X),
    ):
        load(name, src, slot(index))
    loads["part"].wait()
    enc_plan.start(0)
    loads["oc"].wait()
    loads["e2"].wait()
    put_halves(crossy, 0, dot_tn(pool[S_OC], pool[S_E2]))
    loads["o"].wait()
    loads["dy1"].wait()
    put_halves(crossy, 1, dot_tn(pool[S_O], dy1_ref[...].astype(jnp.bfloat16)))
    crossy.start(0)
    load("act", act_hbm, slot(S_ACT))
    crossx.advance(0)
    for name in ("q", "k", "v", "do", "aug"):
        loads[name].wait()
    loads["act"].wait()
    act_t[...] = pool[S_ACT].T
    crossy.advance(0)
    enc_plan.advance(0)

    offsets = lax.broadcasted_iota(jnp.int32, (1, WIN), 1) - TILE
    chosen = bucket_vector(None, jnp.maximum(offsets, 0))
    lines, fars = bias_lines(table_ref)

    def pair_body(p):
        lanes = pl.ds(pl.multiple_of(p * LANES, LANES), LANES)
        dq, dk, dv, sums = self_pair_backward(
            pool[S_Q, :, lanes], pool[S_K, :, lanes], pool[S_V, :, lanes], pool[S_DO, :, lanes], pool[S_O, :, lanes],
            pool[S_AUG, :, lanes], ak, av, lines[2 * p : 2 * p + 2], fars[2 * p : 2 * p + 2], offsets, chosen,
            bias_ref, g_ref, gfar_ref, dqt_ref,
            lambda rows, value: pool.__setitem__((S_DK, rows, lanes), value),
            lambda rows, value: pool.__setitem__((S_DV, rows, lanes), value),
        )
        pool[S_DQ, :, lanes] = dq
        for head in range(2):
            tot_ref[3 + 2 * p + head] = jnp.concatenate(
                [sums[head], jnp.zeros((1, D - BUCKETS), jnp.float32)], axis=1
            )

    tot_ref[1] = gainc_ref[...]
    tot_ref[2] = gainf_ref[...]
    ak, av = key_marks(segment_rows(lengths_ref)), value_marks(LEN)
    rounds = {
        0: [],
        1: [(feed_out, 2), (feed_in, 2)],
        2: [(crossy, 1)],
        3: [(crossx, 1), (feed_out, 3), (feed_in, 3), (enc_plan, 1)],
        4: [(crossy, 2), (self0, 0)],
        5: [(feed_out, 4), (feed_in, 4), (enc_plan, 2)],
    }
    per_block = PAIRS // BLOCKS
    for block in range(BLOCKS):
        for inner in range(per_block):
            p = block * per_block + inner
            for plan, k in rounds[p]:
                plan.advance(k)
            pair_body(p)
        cols = slice(block * BLOCK, (block + 1) * BLOCK)
        for w, index in enumerate((S_DQ, S_DK, S_DV)):
            put_halves(selfs[block], w, dot_nn(act_t[...], pool[index, :, cols]))
        selfs[block].start(0)
    wq, wk, wv = slot(S_Q), slot(S_K), slot(S_V)
    for name, src, index in (("wq", wq_hbm, S_Q), ("wk", wk_hbm, S_K), ("wv", wv_hbm, S_V)):
        load(name, src, pool.at[index, pl.ds(0, D)])
    crossx.advance(2)
    self1.advance(0)
    for name in ("wq", "wk", "wv", "x"):
        loads[name].wait()
    pending = [
        [(crossy, 3), (self0, 1), (enc_plan, 3), (self2, 0)],
        [(crossx, 3), (feed_out, 5), (feed_in, 5)],
        [(self1, 1), (crossy, 4), (self0, 2)],
        [(crossx, 4), (self2, 1)],
    ]
    gain_sum = jnp.zeros((1, D), jnp.float32)
    stores = []
    for i, r in enumerate(range(0, LEN, ROWS)):
        rows = slice(r, r + ROWS)
        da = (
            dot_nt(pool[S_DQ, rows], pool[S_Q, :D])
            + dot_nt(pool[S_DK, rows], pool[S_K, :D])
            + dot_nt(pool[S_DV, rows], pool[S_V, :D])
        )
        x = pool[S_X, rows].astype(jnp.float32)
        inverse = norm_parts(x)
        gain_sum = gain_sum + jnp.sum(da * x * inverse, axis=0, keepdims=True)
        dy1_ref[rows] = dy1_ref[rows] + norm_back(x, inverse, gain_ref[...].reshape(1, D), da)
        stores.append(pltpu.make_async_copy(dy1_ref.at[rows], dx_hbm.at[rows], store_sem.at[i]))
        stores[-1].start()
        for plan, k in pending[i]:
            plan.advance(k)
    tot_ref[0] = gain_sum
    links = all_links(n_blk, n_dp)

    def small_copy(j):
        axis, bit = links[j]
        return pltpu.make_async_remote_copy(
            src_ref=tot_ref,
            dst_ref=got_ref.at[j],
            send_sem=tsend.at[j],
            recv_sem=trecv.at[j],
            device_id=partner(axis, bit),
            device_id_type=pl.DeviceIdType.MESH,
        )

    small_copy(0).start()
    done = {feed_in: 5, feed_out: 5, crossx: 4, crossy: 4, enc_plan: 3, self0: 2, self1: 1, self2: 1}
    longest = max(plan.steps for plan in every)
    j = 0
    while True:
        for plan in (self2, self1, self0, crossx, crossy, feed_out, feed_in, enc_plan):
            done[plan] += 1
            plan.advance(done[plan])
        if j < len(links):
            small_copy(j).wait()
            tot_ref[...] = tot_ref[...] + got_ref[j]
            j += 1
            if j < len(links):
                small_copy(j).start()
        if j == len(links) and all(done[plan] >= plan.steps - 1 for plan in every):
            break
    sums_ref[...] = tot_ref[...]
    for store in stores:
        store.wait()


def self_pair_backward(q_raw, k_raw, v_raw, do_raw, o_raw, aug, ak, av, line, far, offsets, chosen,
                       bias_ref, g_ref, gfar_ref, dqt_ref, put_dk, put_dv):
    for head in range(2):
        spread = jnp.broadcast_to(line[head : head + 1], (TILE, WIN))
        bias_ref[head] = pltpu.roll(spread, 0, 1, stride=1, stride_axis=0)[:, TILE:]
    g_ref[...] = jnp.zeros_like(g_ref)
    gfar_ref[...] = jnp.zeros_like(gfar_ref)
    dqt_ref[...] = jnp.zeros_like(dqt_ref)
    product = do_raw.astype(jnp.float32) * o_raw.astype(jnp.float32)
    deltas = []
    for head in range(2):
        half = in_half(LEN, head)
        deltas.append(jnp.sum(jnp.where(half, product, 0.0), axis=1, keepdims=True))
    aug_do = (-triple_lanes(deltas[0], deltas[1], LEN)).astype(jnp.bfloat16)
    q_scaled = q_raw * jnp.bfloat16(SCALE)
    k_t = k_raw.T
    accs = {}
    for head in range(2):
        half = in_half(LEN, head)
        q = jnp.where(half, q_scaled, aug)
        k = jnp.where(half, k_raw, ak)
        v = jnp.where(half, v_raw, av)
        do = jnp.where(half, do_raw, aug_do)
        for j in range(LEN // TILE):
            lo = j * TILE
            hi = min(LEN, (j + 3) * TILE)
            width = hi - lo
            near = min(2 * TILE, width)
            scores = dot_nt(k[lo : lo + TILE], q[lo:hi])
            parts = [scores[:, :near] + bias_ref[head][:, :near]]
            if width > near:
                parts.append(scores[:, near:] + far[head : head + 1])
            scores = parts[0] if len(parts) == 1 else jnp.concatenate(parts, axis=1)
            probs = jnp.exp(scores)
            grad_probs = dot_nt(v[lo : lo + TILE], do[lo:hi])
            grad_scores = probs * grad_probs
            g_ref[head, :, :near] += grad_scores[:, :near]
            if width > near:
                gfar_ref[head] += jnp.sum(grad_scores[:, near:].reshape(TILE // 8, 8, TILE), axis=0)
            ds = grad_scores.astype(jnp.bfloat16)
            accs[j, head] = (dot_nn(ds, q[lo:hi]), dot_nn(probs.astype(jnp.bfloat16), do[lo:hi]))
            dqt_ref[head * HD : (head + 1) * HD, lo:hi] += dot_nn(
                k_t[head * HD : (head + 1) * HD, lo : lo + TILE], ds
            )
            if head == 1:
                lower = in_half(TILE, 0)
                rows = slice(lo, lo + TILE)
                put_dk(rows, jnp.where(lower, accs[j, 0][0], accs[j, 1][0]).astype(jnp.bfloat16))
                put_dv(rows, jnp.where(lower, accs[j, 0][1], accs[j, 1][1]).astype(jnp.bfloat16))
    dq = (dqt_ref[...] * SCALE).T.astype(jnp.bfloat16)
    rows = []
    for head in range(2):
        total = jnp.zeros((8, WIN), jnp.float32)
        pad = jnp.zeros((8, TILE), jnp.float32)
        for a in range(TILE // 8):
            strip = jnp.concatenate([pad, g_ref[head, 8 * a : 8 * a + 8, :]], axis=1)
            if a:
                strip = pltpu.roll(strip, WIN - 8 * a, 1)
            total = total + strip
        line_sum = jnp.zeros((1, WIN), jnp.float32)
        for s in range(8):
            one = total[s : s + 1]
            line_sum = line_sum + (pltpu.roll(one, WIN - s, 1) if s else one)
        rows.append(line_sum)
    lines = jnp.concatenate(rows, axis=0)
    lines = jnp.where(offsets >= 0, lines, 0.0)
    high, mid, low = split3(lines)
    sums = sum(dot_nt(part.astype(jnp.bfloat16), chosen) for part in (high, mid, low))
    lane32 = lax.broadcasted_iota(jnp.int32, (1, BUCKETS), 1)
    tables = []
    for head in range(2):
        far_sum = jnp.sum(gfar_ref[head])
        tables.append(sums[head : head + 1] + jnp.where(lane32 == BUCKETS - 1, far_sum, 0.0))
    return dq, None, None, tables


def last_block(n_blk, n_dp, plans, enc_plan, big, little, keys):
    every = list(plans) + [enc_plan]
    links = len(all_links(n_blk, n_dp))
    scratch = [item for plan in every for item in plan.scratch()]
    scratch += [
        pltpu.VMEM((POOL, LEN, D), jnp.bfloat16),
        pltpu.VMEM((LEN, D), jnp.float32),
        pltpu.VMEM((D, LEN), jnp.bfloat16),
        pltpu.VMEM((2, TILE, 2 * TILE), jnp.float32),
        pltpu.VMEM((2, TILE, 2 * TILE), jnp.float32),
        pltpu.VMEM((2, 8, TILE), jnp.float32),
        pltpu.VMEM((LANES, LEN), jnp.float32),
        pltpu.VMEM((3 + H, 1, D), jnp.float32),
        pltpu.VMEM((links, 3 + H, 1, D), jnp.float32),
        pltpu.SemaphoreType.DMA((links,)),
        pltpu.SemaphoreType.DMA((links,)),
        pltpu.SemaphoreType.DMA((len(big) + 3 * (keys // LEN) - 2 + 1,)),
        pltpu.SemaphoreType.DMA((LEN // ROWS,)),
    ]
    return pl.pallas_call(
        partial(last_kernel, n_blk, n_dp, plans, enc_plan),
        in_specs=[any_spec()] * len(big) + [vmem_spec()] * len(little),
        out_specs=[vmem_spec()] * len(every) + [any_spec(), vmem_spec()],
        out_shape=[plan.out_shape() for plan in every]
        + [jax.ShapeDtypeStruct((LEN, D), jnp.float32), jax.ShapeDtypeStruct((3 + H, 1, D), jnp.float32)],
        scratch_shapes=scratch,
        compiler_params=pltpu.CompilerParams(
            vmem_limit_bytes=VMEM_LIMIT, collective_id=1, has_side_effects=True
        ),
        cost_estimate=pl.CostEstimate(flops=40 * LEN * D * D, bytes_accessed=80 * LEN * D, transcendentals=0),
    )(*big, *little)


def segment_rows(lengths_ref):
    rows = lax.broadcasted_iota(jnp.int32, (LEN, LANES), 0)
    end = jnp.zeros((1, 1), jnp.int32)
    seg = jnp.zeros((LEN, LANES), jnp.int32)
    for t in range(TARGETS - 1):
        end = end + lengths_ref[:, t : t + 1]
        seg = seg + (rows >= end).astype(jnp.int32)
    return seg


def query_marks(seg):
    place = lane_ids(LEN) & (HD - 1)
    return jnp.where((place >= 3) & (place - 3 == seg), 1.0, 0.0).astype(jnp.bfloat16)


def key_marks(seg):
    place = lane_ids(LEN) & (HD - 1)
    other = (place >= 3) & (place < 3 + TARGETS) & (place - 3 != seg)
    return jnp.where(place < 3, -1.0, jnp.where(other, NEG, 0.0)).astype(jnp.bfloat16)


def value_marks(rows):
    place = lane_ids(rows) & (HD - 1)
    return jnp.where(place < 3, 1.0, 0.0).astype(jnp.bfloat16)


def bias_lines(table_ref):
    offsets = lax.broadcasted_iota(jnp.int32, (1, WIN), 1) - TILE
    chosen = bucket_vector(None, jnp.maximum(offsets, 0))
    lines = dot_tn(table_ref[...], chosen)
    return jnp.where(offsets >= 0, lines, NEG), lines[:, WIN - 1 :]


def front_kernel(n_blk, n_dp, x_hbm, enc_hbm, wq_hbm, wk_hbm, wv_hbm, wo_hbm, wcq_hbm, wck_hbm, wcv_hbm,
                 lengths_ref, gain_ref, gainc_ref, table_ref,
                 q_hbm, k_hbm, v_hbm, o_hbm, aug_hbm, act_hbm, y1_hbm, actc_hbm, qc_hbm, kv_hbm, encall_hbm,
                 x_ref, w_ref, act_ref, q_ref, k_ref, v_ref, o_ref, aug_ref, y1_ref, kv_ref, enc_ref, bias_ref, ot_ref, logs_ref,
                 send_sem, recv_sem, load_sem, store_sem):
    passage = enc_hbm.shape[0]
    loads = []
    for n, (src, dst) in enumerate(
        [(enc_hbm, enc_ref.at[0]), (x_hbm, x_ref)]
        + [(w, w_ref.at[i]) for i, w in enumerate((wq_hbm, wk_hbm, wv_hbm, wo_hbm, wcq_hbm, wck_hbm, wcv_hbm))]
    ):
        loads.append(pltpu.make_async_copy(src, dst, load_sem.at[n]))
        loads[-1].start()
    stores = []

    def store(src, dst):
        stores.append(pltpu.make_async_copy(src, dst, store_sem.at[len(stores)]))
        stores[-1].start()

    bits = bits_of(n_blk)

    def gather(k):
        size = 1 << k
        return pltpu.make_async_remote_copy(
            src_ref=enc_ref.at[pl.ds(0, size)],
            dst_ref=enc_ref.at[pl.ds(size, size)],
            send_sem=send_sem.at[k],
            recv_sem=recv_sem.at[k],
            device_id=partner("blk", bits - 1 - k),
            device_id_type=pl.DeviceIdType.MESH,
        )

    barrier = pltpu.get_barrier_semaphore()
    for bit in range(bits):
        pl.semaphore_signal(barrier, inc=1, device_id=partner("blk", bit), device_id_type=pl.DeviceIdType.MESH)
    pl.semaphore_wait(barrier, bits)
    loads[0].wait()
    gather(0).start()
    loads[1].wait()
    for r in range(0, LEN, ROWS):
        rows = slice(r, r + ROWS)
        x = x_ref[rows].astype(jnp.float32)
        act_ref[rows] = (x * norm_parts(x) * gain_ref[...].reshape(1, D)).astype(jnp.bfloat16)
    for i, (ref, out) in enumerate(((q_ref, q_hbm), (k_ref, k_hbm), (v_ref, v_hbm))):
        loads[2 + i].wait()
        for r in range(0, LEN, ROWS):
            rows = slice(r, r + ROWS)
            ref[rows] = dot_nn(act_ref[rows], w_ref[i]).astype(jnp.bfloat16)
        store(ref, out)
    store(act_ref, act_hbm)
    seg = segment_rows(lengths_ref)
    aq, ak = query_marks(seg), key_marks(seg)
    lines, fars = bias_lines(table_ref)
    for p in range(PAIRS):
        lanes = slice(p * LANES, (p + 1) * LANES)
        if p % 2 == 1 and p // 2 < bits - 1:
            gather(p // 2).wait()
            gather(p // 2 + 1).start()
        self_pair_forward(q_ref[:, lanes], k_ref[:, lanes], v_ref[:, lanes], aq, ak, lines[2 * p : 2 * p + 2],
                          fars[2 * p : 2 * p + 2], bias_ref, ot_ref, logs_ref, o_ref, aug_ref, lanes)
    store(o_ref, o_hbm)
    store(aug_ref, aug_hbm)
    for k in range(min(bits - 1, PAIRS // 2), bits - 1):
        gather(k).wait()
        gather(k + 1).start()
    for n in range(5, 9):
        loads[n].wait()
    for r in range(0, LEN, ROWS):
        rows = slice(r, r + ROWS)
        y1 = x_ref[rows].astype(jnp.float32) + dot_nn(o_ref[rows], w_ref[3])
        y1_ref[rows] = y1
        store(y1_ref.at[pl.ds(r, ROWS)], y1_hbm.at[pl.ds(r, ROWS)])
        actc = (y1 * norm_parts(y1) * gainc_ref[...].reshape(1, D)).astype(jnp.bfloat16)
        x_ref[rows] = actc
        store(x_ref.at[pl.ds(r, ROWS)], actc_hbm.at[pl.ds(r, ROWS)])
    gather(bits - 1).wait()
    for s in range(0, n_blk):
        store(enc_ref.at[s], encall_hbm.at[pl.ds(s * passage, passage)])
    group = ROWS // passage
    for s in range(0, n_blk, group):
        encs = enc_ref[s : s + group].reshape(group * passage, D)
        rows = slice(s * passage, (s + group) * passage)
        kv_ref[rows, :D] = dot_nn(encs, w_ref[5]).astype(jnp.bfloat16)
        kv_ref[rows, D:] = dot_nn(encs, w_ref[6]).astype(jnp.bfloat16)
    store(kv_ref, kv_hbm)
    stores[0].wait()
    for r in range(0, LEN, ROWS):
        rows = slice(r, r + ROWS)
        q_ref[rows] = dot_nn(x_ref[rows], w_ref[4]).astype(jnp.bfloat16)
        store(q_ref.at[pl.ds(r, ROWS)], qc_hbm.at[pl.ds(r, ROWS)])
    for copy in stores[1:]:
        copy.wait()


def self_pair_forward(q_raw, k_raw, v_raw, aq, ak, line, far, bias_ref, ot_ref, logs_ref, o_ref, aug_ref, lanes):
    for head in range(2):
        spread = jnp.broadcast_to(line[head : head + 1], (TILE, WIN))
        bias_ref[head] = pltpu.roll(spread, 0, 1, stride=1, stride_axis=0)[:, TILE:]
    v_t = v_raw.T
    for head in range(2):
        half = in_half(LEN, head)
        q = jnp.where(half, q_raw * jnp.bfloat16(SCALE), aq)
        k = jnp.where(half, k_raw, ak)
        for i in range(LEN // TILE):
            cols = slice(i * TILE, (i + 1) * TILE)
            tiles = []
            for j in range(max(0, i - 2), i + 1):
                scores = dot_nt(k[j * TILE : (j + 1) * TILE], q[cols])
                if i - j < 2:
                    scores = scores + bias_ref[head, :, (i - j) * TILE : (i - j + 1) * TILE]
                else:
                    scores = scores + far[head : head + 1]
                tiles.append(scores)
            peak = tiles[0]
            for tile in tiles[1:]:
                peak = jnp.maximum(peak, tile)
            top = jnp.max(peak, axis=0, keepdims=True)
            total, mixed = None, None
            for n, j in enumerate(range(max(0, i - 2), i + 1)):
                expo = jnp.exp(tiles[n] - top)
                part = jnp.sum(expo, axis=0, keepdims=True)
                out = dot_nn(v_t[head * HD : (head + 1) * HD, j * TILE : (j + 1) * TILE], expo.astype(jnp.bfloat16))
                total = part if total is None else total + part
                mixed = out if mixed is None else mixed + out
            ot_ref[head * HD : (head + 1) * HD, cols] = mixed * (1.0 / total)
            logs_ref[head : head + 1, cols] = top + jnp.log(total)
    o_ref[:, lanes] = ot_ref[...].T.astype(jnp.bfloat16)
    first, second = split3(logs_ref[0:1]), split3(logs_ref[1:2])
    zeros = jnp.zeros((HD - 8, LEN), jnp.float32)
    pad = jnp.zeros((5, LEN), jnp.float32)
    triples = jnp.concatenate(list(second) + [pad, zeros] + list(first) + [pad, zeros], axis=0).T
    place = lane_ids(LEN) & (HD - 1)
    aug_ref[:, lanes] = jnp.where(place < 3, triples.astype(jnp.bfloat16), aq)


def front_block(n_blk, n_dp, big, little, keys, passage):
    wide = jax.ShapeDtypeStruct((LEN, D), jnp.bfloat16)
    n_store = 6 + n_blk + 3 * (LEN // ROWS) + 1
    return pl.pallas_call(
        partial(front_kernel, n_blk, n_dp),
        in_specs=[any_spec()] * len(big) + [vmem_spec()] * len(little),
        out_specs=[any_spec()] * 11,
        out_shape=[wide] * 6
        + [
            jax.ShapeDtypeStruct((LEN, D), jnp.float32),
            wide,
            wide,
            jax.ShapeDtypeStruct((keys, 2 * D), jnp.bfloat16),
            jax.ShapeDtypeStruct((keys, D), jnp.bfloat16),
        ],
        scratch_shapes=[
            pltpu.VMEM((LEN, D), jnp.bfloat16),
            pltpu.VMEM((7, D, D), jnp.bfloat16),
            pltpu.VMEM((LEN, D), jnp.bfloat16),
            pltpu.VMEM((LEN, D), jnp.bfloat16),
            pltpu.VMEM((LEN, D), jnp.bfloat16),
            pltpu.VMEM((LEN, D), jnp.bfloat16),
            pltpu.VMEM((LEN, D), jnp.bfloat16),
            pltpu.VMEM((LEN, D), jnp.bfloat16),
            pltpu.VMEM((LEN, D), jnp.float32),
            pltpu.VMEM((keys, 2 * D), jnp.bfloat16),
            pltpu.VMEM((n_blk, passage, D), jnp.bfloat16),
            pltpu.VMEM((2, TILE, 2 * TILE), jnp.float32),
            pltpu.VMEM((LANES, LEN), jnp.float32),
            pltpu.VMEM((2, LEN), jnp.float32),
            pltpu.SemaphoreType.DMA((bits_of(n_blk),)),
            pltpu.SemaphoreType.DMA((bits_of(n_blk),)),
            pltpu.SemaphoreType.DMA((len(big),)),
            pltpu.SemaphoreType.DMA((n_store,)),
        ],
        compiler_params=pltpu.CompilerParams(
            vmem_limit_bytes=VMEM_LIMIT, collective_id=2, has_side_effects=True
        ),
        cost_estimate=pl.CostEstimate(flops=20 * LEN * D * D, bytes_accessed=40 * LEN * D, transcendentals=0),
    )(*big, *little)


FF_STEPS = 4


def normal_cdf_pair(u):
    x = jnp.abs(u) * 0.7071067811865476
    gauss = jnp.exp(-0.5 * u * u)
    t = 1.0 / (1.0 + 0.3275911 * x)
    poly = ((((1.061405429 * t - 1.453152027) * t + 1.421413741) * t - 0.284496736) * t + 0.254829592) * t
    tail = 0.5 * poly * gauss
    return jnp.where(u >= 0, 1.0 - tail, tail), gauss * 0.3989422804014327


def rest_slot(owner, piece, order):
    slot = 0
    for axis, bit in order[2:]:
        mine = (lax.axis_index(axis) // (1 << bit)) % 2
        its = ((owner if axis == "blk" else piece) // (1 << bit)) % 2
        slot = 2 * slot + (its + mine) % 2
    return slot


class FeedParts:
    def __init__(self, plan, owners, units):
        self.plan, self.owners, self.units = plan, owners, units
        self.count = owners // 2 * len(units)

    def split(self, grad, even_core, put_send, put_keep):
        n = 0
        for t in range(0, self.owners, 2):
            for u in self.units:
                even, odd = grad(t, u), grad(t + 1, u)
                put_send(n, jnp.where(even_core, odd, even).astype(jnp.bfloat16))
                put_keep(n, jnp.where(even_core, even, odd).astype(jnp.bfloat16))
                n += 1

    def index(self, t, u):
        return t // 2 * len(self.units) + self.units.index(u)


def feed_kernel(n_blk, n_dp, plan_in, plan_out, y1_ref, oc_ref, wco_ref, gain_ref, g_ref, w1_ref, w2_ref,
                out_ref, isend_ref, ikeep_ref, osend_ref, okeep_ref, dy2_ref, e2_ref, doc_ref, dgain_ref,
                y2_ref, act_ref, acc_ref, da_ref, hid_ref, du_ref, away_ref, stay_ref, got_ref, send_sem, recv_sem):
    step = pl.program_id(0)
    even_core = lax.axis_index("blk") % 2 == 0
    group = n_blk // FF_STEPS
    parts_out = FeedParts(plan_out, group, list(range(plan_out.count)))
    parts_in = FeedParts(plan_in, n_blk, [0])

    def exchange(s):
        return pltpu.make_async_remote_copy(
            src_ref=away_ref.at[s],
            dst_ref=got_ref.at[s],
            send_sem=send_sem.at[s],
            recv_sem=recv_sem.at[s],
            device_id=partner("blk", 0),
            device_id_type=pl.DeviceIdType.MESH,
        )

    def settle(s):
        exchange(s).wait()

        def total(n):
            return (stay_ref[s % 2, n].astype(jnp.float32) + got_ref[s, n].astype(jnp.float32)).astype(jnp.bfloat16)

        def place(plan, first, second, owner, piece, inner, send_ref, keep_ref):
            axis, bit = plan.order[1]
            low = (lax.axis_index(axis) // (1 << bit)) % 2 == 0
            a, b = total(first), total(second)
            slot = rest_slot(owner, piece, plan.order)
            send_ref[slot, inner] = jnp.where(low, b, a)
            keep_ref[slot, inner] = jnp.where(low, a, b)

        for t in range(0, group, 2):
            for u in parts_out.units:
                n = parts_out.index(t, u)
                owner = s * group + t
                if plan_out.order[1][0] == "dp":
                    if u // plan_out.mats == 0:
                        twin = parts_out.index(t, u + plan_out.mats)
                        place(plan_out, n, twin, owner, 0, u % plan_out.mats, osend_ref, okeep_ref)
                elif (t >> 1) & 1 == 0:
                    place(plan_out, n, parts_out.index(t + 2, u), owner, 0, u, osend_ref, okeep_ref)
        for t in range(0, n_blk, 2):
            if (t >> 1) & 1 == 0:
                n = parts_out.count + parts_in.index(t, 0)
                twin = parts_out.count + parts_in.index(t + 2, 0)
                place(plan_in, n, twin, t, s // plan_in.mats, s % plan_in.mats, isend_ref, ikeep_ref)

    @pl.when(step == 0)
    def _():
        barrier = pltpu.get_barrier_semaphore()
        pl.semaphore_signal(
            barrier, inc=1, device_id=partner("blk", 0), device_id_type=pl.DeviceIdType.MESH
        )
        pl.semaphore_wait(barrier, 1)
        for r in range(0, LEN, ROWS):
            rows = slice(r, r + ROWS)
            y2 = y1_ref[rows] + dot_nn(oc_ref[rows], wco_ref[...])
            y2_ref[rows] = y2
            act_ref[rows] = (y2 * norm_parts(y2) * gain_ref[...].reshape(1, D)).astype(jnp.bfloat16)
        acc_ref[...] = y2_ref[...]
        da_ref[...] = jnp.zeros_like(da_ref)

    for r in range(0, LEN, ROWS):
        rows = slice(r, r + ROWS)
        u = dot_nn(act_ref[rows], w1_ref[...])
        dh = dot_nt(g_ref[rows], w2_ref[...])
        cdf, density = normal_cdf_pair(u)
        hid = (u * cdf).astype(jnp.bfloat16)
        du = (dh * (cdf + u * density)).astype(jnp.bfloat16)
        hid_ref[rows] = hid
        du_ref[rows] = du
        acc_ref[rows] += dot_nn(hid, w2_ref[...])
        da_ref[rows] += dot_nt(du, w1_ref[...])
        if r == 0:
            pl.when(step > 0)(lambda: settle(step - 1))

    def put(n, value, base, ref):
        ref[base + n] = value

    dw2 = dot_tn(hid_ref[...], g_ref[...])
    own_rows = plan_out.rows * plan_out.count
    parts_out.split(
        lambda t, m: dw2[t * own_rows + m * plan_out.rows : t * own_rows + (m + 1) * plan_out.rows],
        even_core,
        lambda n, value: away_ref.__setitem__((step, n), value),
        lambda n, value: stay_ref.__setitem__((step % 2, n), value),
    )
    dw1 = dot_tn(act_ref[...], du_ref[...])
    parts_in.split(
        lambda t, m: dw1[t * plan_in.rows : (t + 1) * plan_in.rows],
        even_core,
        lambda n, value: away_ref.__setitem__((step, parts_out.count + n), value),
        lambda n, value: stay_ref.__setitem__((step % 2, parts_out.count + n), value),
    )
    exchange(step).start()

    @pl.when(step == FF_STEPS - 1)
    def _():
        gain_sum = jnp.zeros((1, D), jnp.float32)
        for r in range(0, LEN, ROWS):
            rows = slice(r, r + ROWS)
            out_ref[rows] = acc_ref[rows].astype(jnp.bfloat16)
            y2 = y2_ref[rows]
            inverse = norm_parts(y2)
            da = da_ref[rows]
            gain_sum = gain_sum + jnp.sum(da * y2 * inverse, axis=0, keepdims=True)
            dy2 = g_ref[rows].astype(jnp.float32) + norm_back(y2, inverse, gain_ref[...].reshape(1, D), da)
            dy2_ref[rows] = dy2
            e2 = dy2.astype(jnp.bfloat16)
            e2_ref[rows] = e2
            doc_ref[rows] = dot_nt(e2, wco_ref[...]).astype(jnp.bfloat16)
        dgain_ref[...] = gain_sum
        settle(step)


def feed_block(n_blk, n_dp, y1, oc, wco, gain, g, w1, w2, plan_in, plan_out):
    ff = w1.shape[1]
    cols = ff // FF_STEPS
    fixed = vmem_spec()
    quarter = lambda plan: (plan.slots // 4, plan.mats, plan.rows, D)
    like = jax.ShapeDtypeStruct
    units = n_blk // FF_STEPS // 2 * plan_out.count + n_blk // 2
    packet = (units, D // n_blk, D)
    return pl.pallas_call(
        partial(feed_kernel, n_blk, n_dp, plan_in, plan_out),
        grid=(FF_STEPS,),
        in_specs=[fixed] * 5
        + [
            pl.BlockSpec((D, cols), lambda c: (0, c)),
            pl.BlockSpec((cols, D), lambda c: (c, 0)),
        ],
        out_specs=[fixed] * 9,
        out_shape=[
            like((LEN, D), jnp.bfloat16),
            like(quarter(plan_in), jnp.bfloat16),
            like(quarter(plan_in), jnp.bfloat16),
            like(quarter(plan_out), jnp.bfloat16),
            like(quarter(plan_out), jnp.bfloat16),
            like((LEN, D), jnp.float32),
            like((LEN, D), jnp.bfloat16),
            like((LEN, D), jnp.bfloat16),
            like((1, D), jnp.float32),
        ],
        scratch_shapes=[
            pltpu.VMEM((LEN, D), jnp.float32),
            pltpu.VMEM((LEN, D), jnp.bfloat16),
            pltpu.VMEM((LEN, D), jnp.float32),
            pltpu.VMEM((LEN, D), jnp.float32),
            pltpu.VMEM((LEN, cols), jnp.bfloat16),
            pltpu.VMEM((LEN, cols), jnp.bfloat16),
            pltpu.VMEM((FF_STEPS,) + packet, jnp.bfloat16),
            pltpu.VMEM((2,) + packet, jnp.bfloat16),
            pltpu.VMEM((FF_STEPS,) + packet, jnp.bfloat16),
            pltpu.SemaphoreType.DMA((FF_STEPS,)),
            pltpu.SemaphoreType.DMA((FF_STEPS,)),
        ],
        compiler_params=pltpu.CompilerParams(
            vmem_limit_bytes=VMEM_LIMIT, collective_id=3, has_side_effects=True
        ),
        cost_estimate=pl.CostEstimate(flops=12 * LEN * D * ff, bytes_accessed=40 * LEN * D, transcendentals=0),
    )(y1, oc, wco, gain, g, w1, w2)


def unpack_kernel(in_ref, out_ref, crossx, crossy, *refs):
    blocks, (enc_ref, sums_ref), outs = refs[: len(BLOCK_PAIRS)], refs[len(BLOCK_PAIRS) : len(BLOCK_PAIRS) + 2], refs[len(BLOCK_PAIRS) + 2 :]
    (gq, gk, gv, go, gcq, gck, gcv, gco, gin, gout, genc, gain0, gain1, gain2, table) = outs
    for w, ref in enumerate((gq, gk, gv)):
        at = 0
        for part, pairs in zip(blocks, BLOCK_PAIRS):
            for c in range(pairs):
                ref[:, at : at + LANES] = part[pairs * w + c]
                at += LANES
    half = D // 2
    for ref, part, w in ((gcq, crossx, 0), (gck, crossx, 1), (gcv, crossx, 2), (gco, crossy, 0), (go, crossy, 1)):
        for c in range(2):
            ref[:, c * half : (c + 1) * half] = part[2 * w + c]
    rows = gq.shape[0]
    for m in range(4):
        gin[:, m * D : (m + 1) * D] = in_ref[m]
        gout[m * rows : (m + 1) * rows] = out_ref[m]
    genc[...] = enc_ref[0]
    for n, ref in enumerate((gain0, gain1, gain2)):
        ref[...] = sums_ref[n].reshape(D)
    tables = jnp.concatenate([sums_ref[3 + h][:, :LANES] for h in range(H)] + [jnp.zeros((4, LANES), jnp.float32)], axis=0)
    table[...] = tables.T[:BUCKETS, :H]


def unpack(n_blk, passage, parts):
    rows = D // n_blk
    like = lambda *shape: jax.ShapeDtypeStruct(shape, jnp.float32)
    return pl.pallas_call(
        unpack_kernel,
        in_specs=[vmem_spec()] * len(parts),
        out_specs=[vmem_spec()] * 15,
        out_shape=[like(rows, D)] * 8
        + [like(rows, 4 * D), like(4 * rows, D), like(passage, D)]
        + [like(D)] * 3
        + [like(BUCKETS, H)],
        compiler_params=pltpu.CompilerParams(vmem_limit_bytes=VMEM_LIMIT),
    )(*parts)


def swap(value, axis, bit, size):
    return lax.ppermute(value, axis, [(i, i ^ (1 << bit)) for i in range(size)])


def per_device(
    decoder_rows,
    encoder_rows,
    target_lengths,
    target_question,
    passage_question,
    self_gain,
    self_query,
    self_key,
    self_value,
    self_output,
    position_bias_matrix,
    cross_gain,
    cross_query,
    cross_key,
    cross_value,
    cross_output,
    feed_gain,
    feed_input_weight,
    feed_out,
    cotangent,
    n_dp,
    n_blk,
):
    passage = encoder_rows.shape[0]
    keys = passage * n_blk
    sizes = {"blk": n_blk, "dp": n_dp}
    (query_self, key_self, value_self, attn_self, aug_self, act_self, resid_self, act_cross, query_cross, pair_all,
     encoder_all) = front_block(
        n_blk, n_dp,
        (decoder_rows, encoder_rows, self_query, self_key, self_value, self_output, cross_query, cross_key, cross_value),
        (target_lengths, self_gain, cross_gain, position_bias_matrix), keys, passage,
    )
    layout = (target_lengths, target_question, passage_question)
    attn_cross, aug_cross = cross_forward(n_blk, passage, *layout, query_cross, pair_all)
    plan_in, plan_out = feed_plans(n_blk, n_dp)
    (block_out, in_send, in_keep, out_send, out_keep, grad_resid_cross, round_cross, grad_attn_cross, feed_sum) = feed_block(
        n_blk, n_dp, resid_self, attn_cross, cross_output, feed_gain, cotangent, feed_input_weight, feed_out,
        plan_in, plan_out,
    )
    in_got = swap(in_send, *plan_in.order[FEED_DONE - 1], sizes[plan_in.order[FEED_DONE - 1][0]])
    out_got = swap(out_send, *plan_out.order[FEED_DONE - 1], sizes[plan_out.order[FEED_DONE - 1][0]])
    dqc, dkv, grad_resid_self, grad_attn_self, encoder_part, cross_sum = cross_backward(
        n_blk, passage, *layout, query_cross, pair_all, grad_attn_cross, attn_cross, aug_cross,
        resid_self, grad_resid_cross, cross_query, cross_key, cross_value, self_output, cross_gain,
    )
    enc_plan = Exchange(1, passage, D, n_blk, n_dp, "near")
    big = (
        decoder_rows, grad_resid_self, act_self, self_query, self_key, self_value, act_cross, dqc, encoder_all, dkv,
        attn_cross, round_cross, query_self, key_self, value_self, grad_attn_self, attn_self, aug_self,
        in_keep, in_got, out_keep, out_got, encoder_part,
    )
    last = last_block(
        n_blk, n_dp, last_plans(n_blk, n_dp), enc_plan, big,
        (target_lengths, self_gain, position_bias_matrix, cross_sum, feed_sum), keys,
    )
    spot = len(last) - 2
    grad_decoder = last[spot]
    (gq, gk, gv, go, gcq, gck, gcv, gco, gin, gout, genc, gain_self, gain_cross, gain_feed, table) = unpack(
        n_blk, passage, last[:spot] + last[spot + 1 :]
    )
    return (
        block_out, grad_decoder, genc, gain_self, gq, gk, gv, go, table, gain_cross, gcq, gck, gcv, gco,
        gain_feed, gin, gout,
    )


def solution(mesh):
    split, copied, owned = P(("dp", "blk"), None), P(), P("blk", None)
    return jax.shard_map(
        partial(per_device, n_dp=mesh.shape["dp"], n_blk=mesh.shape["blk"]),
        mesh=mesh,
        in_specs=(split,) * 4 + (P("dp"),) + (copied,) * 14 + (split,),
        out_specs=(split,) * 3 + (copied,) + (owned,) * 4 + (copied,) * 2 + (owned,) * 4 + (copied,) + (owned,) * 2,
        check_vma=False,
    )
```

```python
import functools
from functools import partial

import jax
import jax.numpy as jnp
from jax import lax
from jax.experimental import pallas as pl
from jax.experimental.pallas import tpu as pltpu
from jax.sharding import PartitionSpec as P

D = 768
H = 12
HD = 64
BUCKETS = 32
LEN = 1024
TARGETS = 4
PAIRS = H // 2
LANES = 2 * HD
TILE = 256
SCALE = HD ** -0.5
NEG = -1e30
VMEM_LIMIT = 60 * 1024 * 1024

eps_norm = 1e-06
bucket_edges = (19, 21, 24, 27, 31, 35, 40, 46, 52, 59, 67, 77, 87, 99, 113)


def dot_nn(a, b):
    return jnp.dot(a, b, preferred_element_type=jnp.float32)


def dot_nt(a, b):
    return lax.dot_general(a, b, (((1,), (1,)), ((), ())), preferred_element_type=jnp.float32)


def dot_tn(a, b):
    return lax.dot_general(a, b, (((0,), (0,)), ((), ())), preferred_element_type=jnp.float32)


def lane_ids(rows):
    return lax.broadcasted_iota(jnp.int32, (rows, LANES), 1)


def in_half(rows, head):
    lane = lane_ids(rows)
    return lane < HD if head == 0 else lane >= HD


def split3(value):
    high = value.astype(jnp.bfloat16).astype(jnp.float32)
    rest = value - high
    mid = rest.astype(jnp.bfloat16).astype(jnp.float32)
    return high, mid, rest - mid


def triple_lanes(first, second, rows):
    lane = lane_ids(rows)
    out = jnp.zeros((rows, LANES), jnp.float32)
    for base, value in ((HD, first), (0, second)):
        for place, part in enumerate(split3(value)):
            out = jnp.where(lane == base + place, part, out)
    return out


def bucket_vector(table_t, offsets):
    upper = jnp.full(offsets.shape, 16, jnp.int32)
    for edge in bucket_edges:
        upper = upper + (offsets >= edge).astype(jnp.int32)
    bucket = jnp.where(offsets < 16, offsets, upper)
    rows = lax.broadcasted_iota(jnp.int32, (BUCKETS, offsets.shape[1]), 0)
    chosen = (rows == bucket).astype(jnp.float32).astype(jnp.bfloat16)
    return chosen


WIN = 3 * TILE


ROWS = 256


def norm_parts(values):
    return lax.rsqrt(jnp.mean(values * values, axis=1, keepdims=True) + eps_norm)


def norm_back(values, inverse, gain, grad):
    scaled = grad * gain
    inner = jnp.mean(scaled * values, axis=1, keepdims=True)
    return inverse * scaled - values * (inverse * inverse * inverse * inner)


CT = 256


def cross_layout(n_blk, lengths_ref, question_ref, passage_ref, order_ref, item_ref, count_ref):
    per_q = n_blk // TARGETS
    bits = bits_of(n_blk)
    me = lax.axis_index("blk")
    for t in range(TARGETS + 1):
        count_ref[t] = 0
    for s in range(n_blk):
        device = 0
        for b in range(bits):
            mine = (me // (1 << b)) % 2
            flip = (s >> (bits - 1 - b)) & 1
            device = device + (1 - mine if flip else mine) * (1 << b)
        question = passage_ref[device]
        order_ref[question * per_q + count_ref[question]] = s
        count_ref[question] = count_ref[question] + 1
    end = 0
    for t in range(TARGETS):
        start, end = end, end + lengths_ref[0, t]
        question = question_ref[0, t]

        @pl.loop(start // CT, (end + CT - 1) // CT)
        def _(tile, start=start, end=end, question=question):
            n = count_ref[TARGETS]
            item_ref[0, n] = tile
            item_ref[1, n] = question
            item_ref[2, n] = start - tile * CT
            item_ref[3, n] = end - tile * CT
            count_ref[TARGETS] = n + 1


def layout_scratch(n_blk):
    return [
        pltpu.SMEM((n_blk,), jnp.int32),
        pltpu.SMEM((4, LEN // CT + TARGETS), jnp.int32),
        pltpu.SMEM((TARGETS + 1,), jnp.int32),
    ]


def cross_forward_kernel(n_blk, passage, lengths_ref, question_ref, passage_ref, q_ref, kv_ref, o_ref, aug_ref,
                         ks_ref, vs_ref, order_ref, item_ref, count_ref):
    keys_q = n_blk // TARGETS * passage
    lower = lax.broadcasted_iota(jnp.int32, (passage, D), 1) % LANES < HD
    zero = jnp.zeros((), jnp.bfloat16)
    cross_layout(n_blk, lengths_ref, question_ref, passage_ref, order_ref, item_ref, count_ref)

    @pl.loop(0, n_blk)
    def _(s):
        src = pl.multiple_of(order_ref[s] * passage, passage)
        dst = pl.multiple_of(s * passage, passage)
        keys = kv_ref[pl.ds(src, passage), :D]
        values = kv_ref[pl.ds(src, passage), D:]
        ks_ref[0, pl.ds(dst, passage)] = jnp.where(lower, keys, zero)
        ks_ref[1, pl.ds(dst, passage)] = jnp.where(lower, zero, keys)
        vs_ref[0, pl.ds(dst, passage)] = jnp.where(lower, values, zero)
        vs_ref[1, pl.ds(dst, passage)] = jnp.where(lower, zero, values)

    o_ref[...] = jnp.zeros_like(o_ref)
    aug_ref[...] = jnp.zeros_like(aug_ref)

    @pl.loop(0, count_ref[TARGETS])
    def _(n):
        row0 = pl.multiple_of(item_ref[0, n] * CT, CT)
        key0 = pl.multiple_of(item_ref[1, n] * keys_q, keys_q)
        rows = lax.broadcasted_iota(jnp.int32, (CT, 1), 0)
        valid = (rows >= item_ref[2, n]) & (rows < item_ref[3, n])
        for pair in range(PAIRS):
            cols = slice(pair * LANES, (pair + 1) * LANES)
            q = q_ref[pl.ds(row0, CT), cols] * jnp.bfloat16(SCALE)
            outs, logs = [], []
            for head in range(2):
                scores = dot_nt(q, ks_ref[head, pl.ds(key0, keys_q), cols])
                top = jnp.max(scores, axis=1, keepdims=True)
                expo = jnp.exp(scores - top)
                total = jnp.sum(expo, axis=1, keepdims=True)
                outs.append(dot_nn(expo.astype(jnp.bfloat16), vs_ref[head, pl.ds(key0, keys_q), cols]) / total)
                logs.append(top + jnp.log(total))
            mixed = (outs[0] + outs[1]).astype(jnp.bfloat16)
            aug = triple_lanes(logs[0], logs[1], CT).astype(jnp.bfloat16)
            o_ref[pl.ds(row0, CT), cols] = jnp.where(valid, mixed, o_ref[pl.ds(row0, CT), cols])
            aug_ref[pl.ds(row0, CT), cols] = jnp.where(valid, aug, aug_ref[pl.ds(row0, CT), cols])


def smem_spec():
    return pl.BlockSpec(memory_space=pltpu.SMEM)


def vmem_spec():
    return pl.BlockSpec(memory_space=pltpu.VMEM)


def any_spec():
    return pl.BlockSpec(memory_space=pl.ANY)


def cross_forward(n_blk, passage, lengths, questions, passages, q, kv):
    keys = kv.shape[0]
    return pl.pallas_call(
        partial(cross_forward_kernel, n_blk, passage),
        in_specs=[smem_spec()] * 3 + [vmem_spec()] * 2,
        out_specs=[vmem_spec(), vmem_spec()],
        out_shape=[jax.ShapeDtypeStruct((LEN, D), jnp.bfloat16)] * 2,
        scratch_shapes=[pltpu.VMEM((2, keys, D), jnp.bfloat16)] * 2 + layout_scratch(n_blk),
        compiler_params=pltpu.CompilerParams(vmem_limit_bytes=VMEM_LIMIT),
        cost_estimate=pl.CostEstimate(flops=2 * H * LEN * LEN * HD, bytes_accessed=10 * LEN * D, transcendentals=0),
    )(lengths, questions, passages, q, kv)


def cross_backward_kernel(n_blk, passage, lengths_ref, question_ref, passage_ref, q_ref, do_ref, o_ref, aug_ref,
                          kv_hbm, y1_hbm, dy2_hbm, wcq_hbm, wck_hbm, wcv_hbm, wo_hbm, gain_ref,
                          dq_ref, dkv_ref, dy1_ref, dos_ref, part_ref, dgain_ref,
                          ks_ref, vs_ref, kt_ref, dk_ref, dv_ref, dqt_ref, y1_ref, load_sem,
                          order_ref, item_ref, count_ref):
    loads = []
    for n, (src, dst) in enumerate(
        [(kv_hbm, dkv_ref), (y1_hbm, y1_ref), (dy2_hbm, dy1_ref)]
    ):
        loads.append(pltpu.make_async_copy(src, dst, load_sem.at[n]))
        loads[-1].start()
    keys_q = n_blk // TARGETS * passage
    lane = lax.broadcasted_iota(jnp.int32, (passage, D), 1) % LANES
    lower = lane < HD
    ones = jnp.where((lane & (HD - 1)) < 3, 1.0, 0.0).astype(jnp.bfloat16)
    minus = -ones
    cross_layout(n_blk, lengths_ref, question_ref, passage_ref, order_ref, item_ref, count_ref)

    loads[0].wait()

    @pl.loop(0, n_blk)
    def _(s):
        src = pl.multiple_of(order_ref[s] * passage, passage)
        dst = pl.multiple_of(s * passage, passage)
        keys = dkv_ref[pl.ds(src, passage), :D]
        values = dkv_ref[pl.ds(src, passage), D:]
        ks_ref[0, pl.ds(dst, passage)] = jnp.where(lower, keys, minus)
        ks_ref[1, pl.ds(dst, passage)] = jnp.where(lower, minus, keys)
        vs_ref[0, pl.ds(dst, passage)] = jnp.where(lower, values, ones)
        vs_ref[1, pl.ds(dst, passage)] = jnp.where(lower, ones, values)

    lower_k = lax.broadcasted_iota(jnp.int32, (keys_q, LANES), 1) < HD
    for s in range(TARGETS):
        for pair in range(PAIRS):
            rows = slice(s * keys_q, (s + 1) * keys_q)
            cols = slice(pair * LANES, (pair + 1) * LANES)
            both = jnp.where(lower_k, ks_ref[0, rows, cols], ks_ref[1, rows, cols])
            kt_ref[cols, rows] = both.T
    dk_ref[...] = jnp.zeros_like(dk_ref)
    dv_ref[...] = jnp.zeros_like(dv_ref)
    dqt_ref[...] = jnp.zeros_like(dqt_ref)

    @pl.loop(0, count_ref[TARGETS])
    def _(n):
        row0 = pl.multiple_of(item_ref[0, n] * CT, CT)
        key0 = pl.multiple_of(item_ref[1, n] * keys_q, keys_q)
        rows = lax.broadcasted_iota(jnp.int32, (CT, 1), 0)
        valid = (rows >= item_ref[2, n]) & (rows < item_ref[3, n])
        here = pl.ds(row0, CT)
        there = pl.ds(key0, keys_q)
        for pair in range(PAIRS):
            cols = slice(pair * LANES, (pair + 1) * LANES)
            q_scaled = q_ref[here, cols] * jnp.bfloat16(SCALE)
            do_pair = jnp.where(valid, do_ref[here, cols], jnp.zeros((), jnp.bfloat16))
            product = do_pair.astype(jnp.float32) * o_ref[here, cols].astype(jnp.float32)
            deltas = []
            for head in range(2):
                deltas.append(jnp.sum(jnp.where(in_half(CT, head), product, 0.0), axis=1, keepdims=True))
            aug_do = (-triple_lanes(deltas[0], deltas[1], CT)).astype(jnp.bfloat16)
            aug = jnp.where(valid, aug_ref[here, cols], jnp.bfloat16(-NEG))
            parts = []
            for head in range(2):
                half = in_half(CT, head)
                q = jnp.where(half, q_scaled, aug)
                do = jnp.where(half, do_pair, aug_do)
                probs = jnp.exp(dot_nt(ks_ref[head, there, cols], q))
                grad_scores = probs * dot_nt(vs_ref[head, there, cols], do)
                ds = grad_scores.astype(jnp.bfloat16)
                parts.append((dot_nn(ds, q), dot_nn(probs.astype(jnp.bfloat16), do)))
                hrow = pair * LANES + head * HD
                dqt_ref[hrow : hrow + HD, here] += dot_nn(kt_ref[hrow : hrow + HD, there], ds)
            dk_ref[there, cols] += jnp.where(lower_k, parts[0][0], parts[1][0])
            dv_ref[there, cols] += jnp.where(lower_k, parts[0][1], parts[1][1])

    spots = (ks_ref.at[0], ks_ref.at[1], vs_ref.at[0], vs_ref.at[1])
    for n, w in enumerate((wcq_hbm, wck_hbm, wcv_hbm, wo_hbm)):
        loads.append(pltpu.make_async_copy(w, spots[n].at[pl.ds(0, D)], load_sem.at[3 + n]))
        loads[-1].start()
    for pair in range(PAIRS):
        cols = slice(pair * LANES, (pair + 1) * LANES)
        dq_ref[:, cols] = (dqt_ref[cols, :] * SCALE).T.astype(jnp.bfloat16)

    for copy in loads[1:]:
        copy.wait()

    @pl.loop(0, n_blk)
    def _(s):
        src = pl.multiple_of(s * passage, passage)
        spot = order_ref[s]
        dst = pl.multiple_of(spot * passage, passage)
        dk = dk_ref[pl.ds(src, passage)].astype(jnp.bfloat16)
        dv = dv_ref[pl.ds(src, passage)].astype(jnp.bfloat16)
        dkv_ref[pl.ds(dst, passage), :D] = dk
        dkv_ref[pl.ds(dst, passage), D:] = dv

    group = ROWS // passage
    for s in range(0, n_blk, group):
        rows = slice(s * passage, (s + group) * passage)
        part = dot_nt(dkv_ref[rows, :D], ks_ref[1, :D]) + dot_nt(dkv_ref[rows, D:], vs_ref[0, :D])
        part_ref[s : s + group, 0] = part.astype(jnp.bfloat16).reshape(group, passage, D)
    gain_sum = jnp.zeros((1, D), jnp.float32)
    for r in range(0, LEN, ROWS):
        rows = slice(r, r + ROWS)
        da = dot_nt(dq_ref[rows], ks_ref[0, :D])
        y1 = y1_ref[rows]
        inverse = norm_parts(y1)
        gain_sum = gain_sum + jnp.sum(da * y1 * inverse, axis=0, keepdims=True)
        dy1 = dy1_ref[rows] + norm_back(y1, inverse, gain_ref[...].reshape(1, D), da)
        dy1_ref[rows] = dy1
        dos_ref[rows] = dot_nt(dy1.astype(jnp.bfloat16), vs_ref[1, :D]).astype(jnp.bfloat16)
    dgain_ref[...] = gain_sum


def cross_backward(n_blk, passage, lengths, questions, passages, q, kv, do, o, aug, y1, dy2, wcq, wck, wcv, wo, gain):
    keys = kv.shape[0]
    like = jax.ShapeDtypeStruct
    return pl.pallas_call(
        partial(cross_backward_kernel, n_blk, passage),
        in_specs=[smem_spec()] * 3 + [vmem_spec()] * 4 + [any_spec()] * 7 + [vmem_spec()],
        out_specs=[vmem_spec()] * 6,
        out_shape=[
            like((LEN, D), jnp.bfloat16),
            like((keys, 2 * D), jnp.bfloat16),
            like((LEN, D), jnp.float32),
            like((LEN, D), jnp.bfloat16),
            like((n_blk, 1, passage, D), jnp.bfloat16),
            like((1, D), jnp.float32),
        ],
        scratch_shapes=[pltpu.VMEM((2, keys, D), jnp.bfloat16)] * 2
        + [
            pltpu.VMEM((D, keys), jnp.bfloat16),
            pltpu.VMEM((keys, D), jnp.float32),
            pltpu.VMEM((keys, D), jnp.float32),
            pltpu.VMEM((D, LEN), jnp.float32),
            pltpu.VMEM((LEN, D), jnp.float32),
            pltpu.SemaphoreType.DMA((7,)),
        ]
        + layout_scratch(n_blk),
        compiler_params=pltpu.CompilerParams(vmem_limit_bytes=VMEM_LIMIT),
        cost_estimate=pl.CostEstimate(flops=5 * H * LEN * LEN * HD, bytes_accessed=18 * LEN * D, transcendentals=0),
    )(lengths, questions, passages, q, do, o, aug, kv, y1, dy2, wcq, wck, wcv, wo, gain)


def bits_of(count):
    return count.bit_length() - 1


def place_bits(n_blk, n_dp, kind):
    blk = [("blk", bit) for bit in range(bits_of(n_blk))]
    dp = [("dp", bit) for bit in range(bits_of(n_dp))]
    if kind == "x":
        return blk[:1] + dp + blk[1:]
    if kind == "y":
        return blk[:2] + dp + blk[2:]
    return blk


def position(owner, piece, order):
    slot = 0
    for axis, bit in order:
        mine = (lax.axis_index(axis) // (1 << bit)) % 2
        static = ((owner if axis == "blk" else piece) >> bit) & 1
        slot = 2 * slot + (1 - mine if static else mine)
    return slot


def partner(axis, bit):
    me = lax.axis_index(axis)
    mine = (me // (1 << bit)) % 2
    return {axis: me + (1 - 2 * mine) * (1 << bit)}


class Exchange:
    def __init__(self, count, rows, cols, n_blk, n_dp, kind, first=0):
        if kind in "xy" and count % n_dp:
            kind = "plain"
        self.n_blk, self.n_dp, self.count, self.kind, self.first = n_blk, n_dp, count, kind, first
        self.rows, self.cols = rows, cols
        self.order = place_bits(n_blk, n_dp, kind)
        self.pieces = n_dp if kind in "xy" else 1
        self.slots = n_blk * self.pieces
        self.mats = count // self.pieces
        self.last = [("dp", bit) for bit in range(bits_of(n_dp))] if kind != "near" else []
        self.steps = len(self.order) + len(self.last)
        self.held = self.slots >> first
        self.offsets = {}
        at = self.held if first else 0
        for k in range(first, len(self.order)):
            size = self.slots >> (k + 1)
            self.offsets[k] = (at, size)
            at += size
        for j in range(len(self.last)):
            size = (1 << j) if self.pieces > 1 else 1
            self.offsets[len(self.order) + j] = (at, size)
            at += size
        self.received = at

    def scratch(self):
        shape = (self.mats, self.rows, self.cols)
        return [
            pltpu.VMEM((max(self.held, self.pieces),) + shape, jnp.bfloat16),
            pltpu.VMEM((self.received,) + shape, jnp.bfloat16),
            pltpu.SemaphoreType.DMA((self.steps,)),
            pltpu.SemaphoreType.DMA((self.steps,)),
        ]

    def out_shape(self):
        return jax.ShapeDtypeStruct((self.count, self.rows, self.cols), jnp.float32)

    def bind(self, refs, out_ref):
        self.buf, self.recv, self.send_sem, self.recv_sem = refs
        self.out = out_ref

    def put(self, index, value):
        piece, inner = index // self.mats, index % self.mats
        for owner in range(self.n_blk):
            slot = position(owner, piece, self.order)
            self.buf[slot, inner] = value[owner * self.rows : (owner + 1) * self.rows].astype(jnp.bfloat16)

    def copy(self, k):
        at, size = self.offsets[k]
        if k < len(self.order):
            axis, bit = self.order[k]
            src = self.buf.at[pl.ds(size, size)]
        else:
            axis, bit = self.last[k - len(self.order)]
            src = self.buf.at[pl.ds(0, size)]
        return pltpu.make_async_remote_copy(
            src_ref=src,
            dst_ref=self.recv.at[pl.ds(at, size)],
            send_sem=self.send_sem.at[k],
            recv_sem=self.recv_sem.at[k],
            device_id=partner(axis, bit),
            device_id_type=pl.DeviceIdType.MESH,
        )

    def start(self, k):
        self.copy(k).start()

    def add(self, at, size, final):
        for s in range(size):
            for m in range(self.mats):
                total = self.buf[s, m].astype(jnp.float32) + self.recv[at + s, m].astype(jnp.float32)
                if final:
                    self.out[m] = total
                else:
                    self.buf[s, m] = total.astype(jnp.bfloat16)

    def finish(self, k):
        self.copy(k).wait()
        at, size = self.offsets[k]
        final = k == self.steps - 1
        if k < len(self.order) or self.pieces == 1:
            self.add(at, size, final)
            return
        for s in range(size):
            for m in range(self.mats):
                self.buf[size + s, m] = self.recv[at + s, m]
        if final:
            for s in range(self.pieces):
                spot = position(0, s, self.last[::-1])
                for m in range(self.mats):
                    self.out[spot * self.mats + m] = self.buf[s, m].astype(jnp.float32)

    def advance(self, k):
        if k < self.first or k >= self.steps:
            return
        self.finish(k)
        if k + 1 < self.steps:
            self.start(k + 1)


def all_links(n_blk, n_dp):
    return [("blk", bit) for bit in range(bits_of(n_blk))] + [("dp", bit) for bit in range(bits_of(n_dp))]


def enter_barrier(n_blk, n_dp):
    barrier = pltpu.get_barrier_semaphore()
    links = all_links(n_blk, n_dp)
    for axis, bit in links:
        pl.semaphore_signal(barrier, inc=1, device_id=partner(axis, bit), device_id_type=pl.DeviceIdType.MESH)
    pl.semaphore_wait(barrier, len(links))


BLOCKS = 3
BLOCK = D // BLOCKS
BLOCK_PAIRS = (2,) * BLOCKS
FEED_DONE = 2


def last_plans(n_blk, n_dp):
    rows = D // n_blk
    halves = 2
    feed_in, feed_out = feed_plans(n_blk, n_dp, FEED_DONE)
    plans = [
        feed_in,
        feed_out,
        Exchange(3 * halves, rows, D // halves, n_blk, n_dp, "x"),
        Exchange(2 * halves, rows, D // halves, n_blk, n_dp, "y"),
    ]
    for block in range(BLOCKS):
        plans.append(Exchange(3 * halves, rows, BLOCK // halves, n_blk, n_dp, "xyx"[block]))
    return plans


def feed_plans(n_blk, n_dp, first=0):
    rows = D // n_blk
    return (
        Exchange(4, rows, D, n_blk, n_dp, "y", first),
        Exchange(4, rows, D, n_blk, n_dp, "x", first),
    )


POOL = 11
(S_ACTC, S_DQC, S_OC, S_E2, S_Q, S_K, S_V, S_DO, S_O, S_AUG, S_X) = range(POOL)
S_DQ, S_DK, S_DV, S_ACT = S_ACTC, S_DQC, S_OC, S_E2


def last_kernel(n_blk, n_dp, plans, enc_plan, *refs):
    (x_hbm, dy1_hbm, act_hbm, wq_hbm, wk_hbm, wv_hbm, actc_hbm, dqc_hbm, enc_hbm, dkv_hbm, oc_hbm, e2_hbm,
     q_hbm, k_hbm, v_hbm, do_hbm, o_hbm, aug_hbm, inkeep_hbm, inrecv_hbm, outkeep_hbm, outrecv_hbm, part_hbm,
     lengths_ref, gain_ref, table_ref, gainc_ref, gainf_ref) = refs[:28]
    every = list(plans) + [enc_plan]
    outs = refs[28 : 28 + len(every)]
    dx_hbm, sums_ref = refs[28 + len(every) : 30 + len(every)]
    scratch = refs[30 + len(every) :]
    for i, plan in enumerate(every):
        plan.bind(scratch[4 * i : 4 * i + 4], outs[i])
    (pool, dy1_ref, act_t, bias_ref, g_ref, gfar_ref, dqt_ref,
     tot_ref, got_ref, tsend, trecv, load_sem, store_sem) = scratch[4 * len(every) :]
    feed_in, feed_out, crossx, crossy, self0, self1, self2 = plans
    selfs = (self0, self1, self2)

    loads = {}

    def load(name, src, dst):
        loads[name] = pltpu.make_async_copy(src, dst, load_sem.at[len(loads)])
        loads[name].start()

    def slot(index):
        return pool.at[index]

    load("actc", actc_hbm, slot(S_ACTC))
    load("dqc", dqc_hbm, slot(S_DQC))
    for plan, keep, got, name in (
        (feed_out, outkeep_hbm, outrecv_hbm, "out"),
        (feed_in, inkeep_hbm, inrecv_hbm, "in"),
    ):
        load(name + "keep", keep, plan.buf.at[pl.ds(0, plan.held)])
        load(name + "recv", got, plan.recv.at[pl.ds(0, plan.held)])
    spans = enc_hbm.shape[0] // LEN
    spare = (S_Q, S_K, S_V, S_DO, S_AUG, S_X)
    for n in range(spans):
        rows = pl.ds(n * LEN, LEN)
        load(("enc", n), enc_hbm.at[rows], slot(spare[3 * n]))
        load(("dk", n), dkv_hbm.at[rows, pl.ds(0, D)], slot(spare[3 * n + 1]))
        load(("dv", n), dkv_hbm.at[rows, pl.ds(D, D)], slot(spare[3 * n + 2]))
    load("part", part_hbm, enc_plan.buf)
    load("oc", oc_hbm, slot(S_OC))
    load("e2", e2_hbm, slot(S_E2))
    load("o", o_hbm, slot(S_O))
    load("dy1", dy1_hbm, dy1_ref)
    enter_barrier(n_blk, n_dp)

    def begin_feed(plan, name):
        loads[name + "keep"].wait()
        loads[name + "recv"].wait()
        plan.add(0, plan.held, False)
        plan.start(plan.first)

    def put_halves(plan, index, value):
        half = plan.cols
        for c in range(2):
            plan.put(2 * index + c, value[:, c * half : (c + 1) * half])

    begin_feed(feed_out, "out")
    begin_feed(feed_in, "in")
    loads["actc"].wait()
    loads["dqc"].wait()
    put_halves(crossx, 0, dot_tn(pool[S_ACTC], pool[S_DQC]))
    for w, name in ((1, "dk"), (2, "dv")):
        total = None
        for n in range(spans):
            if w == 1:
                loads["enc", n].wait()
            loads[name, n].wait()
            part = dot_tn(pool[spare[3 * n]], pool[spare[3 * n + w]])
            total = part if total is None else total + part
        put_halves(crossx, w, total)
    crossx.start(0)
    for name, src, index in (
        ("q", q_hbm, S_Q), ("k", k_hbm, S_K), ("v", v_hbm, S_V), ("do", do_hbm, S_DO), ("aug", aug_hbm, S_AUG), ("x", x_hbm, S_X),
    ):
        load(name, src, slot(index))
    loads["part"].wait()
    enc_plan.start(0)
    loads["oc"].wait()
    loads["e2"].wait()
    put_halves(crossy, 0, dot_tn(pool[S_OC], pool[S_E2]))
    loads["o"].wait()
    loads["dy1"].wait()
    put_halves(crossy, 1, dot_tn(pool[S_O], dy1_ref[...].astype(jnp.bfloat16)))
    crossy.start(0)
    load("act", act_hbm, slot(S_ACT))
    crossx.advance(0)
    for name in ("q", "k", "v", "do", "aug"):
        loads[name].wait()
    loads["act"].wait()
    act_t[...] = pool[S_ACT].T
    crossy.advance(0)
    enc_plan.advance(0)

    offsets = lax.broadcasted_iota(jnp.int32, (1, WIN), 1) - TILE
    chosen = bucket_vector(None, jnp.maximum(offsets, 0))
    lines, fars = bias_lines(table_ref)

    def pair_body(p):
        lanes = pl.ds(pl.multiple_of(p * LANES, LANES), LANES)
        dq, dk, dv, sums = self_pair_backward(
            pool[S_Q, :, lanes], pool[S_K, :, lanes], pool[S_V, :, lanes], pool[S_DO, :, lanes], pool[S_O, :, lanes],
            pool[S_AUG, :, lanes], ak, av, lines[2 * p : 2 * p + 2], fars[2 * p : 2 * p + 2], offsets, chosen,
            bias_ref, g_ref, gfar_ref, dqt_ref,
            lambda rows, value: pool.__setitem__((S_DK, rows, lanes), value),
            lambda rows, value: pool.__setitem__((S_DV, rows, lanes), value),
        )
        pool[S_DQ, :, lanes] = dq
        for head in range(2):
            tot_ref[3 + 2 * p + head] = jnp.concatenate(
                [sums[head], jnp.zeros((1, D - BUCKETS), jnp.float32)], axis=1
            )

    tot_ref[1] = gainc_ref[...]
    tot_ref[2] = gainf_ref[...]
    ak, av = key_marks(segment_rows(lengths_ref)), value_marks(LEN)
    rounds = {
        0: [],
        1: [(feed_out, 2), (feed_in, 2)],
        2: [(crossy, 1)],
        3: [(crossx, 1), (feed_out, 3), (feed_in, 3), (enc_plan, 1)],
        4: [(crossy, 2), (self0, 0)],
        5: [(feed_out, 4), (feed_in, 4), (enc_plan, 2)],
    }
    per_block = PAIRS // BLOCKS
    for block in range(BLOCKS):
        for inner in range(per_block):
            p = block * per_block + inner
            for plan, k in rounds[p]:
                plan.advance(k)
            pair_body(p)
        cols = slice(block * BLOCK, (block + 1) * BLOCK)
        for w, index in enumerate((S_DQ, S_DK, S_DV)):
            put_halves(selfs[block], w, dot_nn(act_t[...], pool[index, :, cols]))
        selfs[block].start(0)
    wq, wk, wv = slot(S_Q), slot(S_K), slot(S_V)
    for name, src, index in (("wq", wq_hbm, S_Q), ("wk", wk_hbm, S_K), ("wv", wv_hbm, S_V)):
        load(name, src, pool.at[index, pl.ds(0, D)])
    crossx.advance(2)
    self1.advance(0)
    for name in ("wq", "wk", "wv", "x"):
        loads[name].wait()
    pending = [
        [(crossy, 3), (self0, 1), (enc_plan, 3), (self2, 0)],
        [(crossx, 3), (feed_out, 5), (feed_in, 5)],
        [(self1, 1), (crossy, 4), (self0, 2)],
        [(crossx, 4), (self2, 1)],
    ]
    gain_sum = jnp.zeros((1, D), jnp.float32)
    stores = []
    for i, r in enumerate(range(0, LEN, ROWS)):
        rows = slice(r, r + ROWS)
        da = (
            dot_nt(pool[S_DQ, rows], pool[S_Q, :D])
            + dot_nt(pool[S_DK, rows], pool[S_K, :D])
            + dot_nt(pool[S_DV, rows], pool[S_V, :D])
        )
        x = pool[S_X, rows].astype(jnp.float32)
        inverse = norm_parts(x)
        gain_sum = gain_sum + jnp.sum(da * x * inverse, axis=0, keepdims=True)
        dy1_ref[rows] = dy1_ref[rows] + norm_back(x, inverse, gain_ref[...].reshape(1, D), da)
        stores.append(pltpu.make_async_copy(dy1_ref.at[rows], dx_hbm.at[rows], store_sem.at[i]))
        stores[-1].start()
        for plan, k in pending[i]:
            plan.advance(k)
    tot_ref[0] = gain_sum
    links = all_links(n_blk, n_dp)

    def small_copy(j):
        axis, bit = links[j]
        return pltpu.make_async_remote_copy(
            src_ref=tot_ref,
            dst_ref=got_ref.at[j],
            send_sem=tsend.at[j],
            recv_sem=trecv.at[j],
            device_id=partner(axis, bit),
            device_id_type=pl.DeviceIdType.MESH,
        )

    small_copy(0).start()
    done = {feed_in: 5, feed_out: 5, crossx: 4, crossy: 4, enc_plan: 3, self0: 2, self1: 1, self2: 1}
    longest = max(plan.steps for plan in every)
    j = 0
    while True:
        for plan in (self2, self1, self0, crossx, crossy, feed_out, feed_in, enc_plan):
            done[plan] += 1
            plan.advance(done[plan])
        if j < len(links):
            small_copy(j).wait()
            tot_ref[...] = tot_ref[...] + got_ref[j]
            j += 1
            if j < len(links):
                small_copy(j).start()
        if j == len(links) and all(done[plan] >= plan.steps - 1 for plan in every):
            break
    sums_ref[...] = tot_ref[...]
    for store in stores:
        store.wait()


def self_pair_backward(q_raw, k_raw, v_raw, do_raw, o_raw, aug, ak, av, line, far, offsets, chosen,
                       bias_ref, g_ref, gfar_ref, dqt_ref, put_dk, put_dv):
    for head in range(2):
        spread = jnp.broadcast_to(line[head : head + 1], (TILE, WIN))
        bias_ref[head] = pltpu.roll(spread, 0, 1, stride=1, stride_axis=0)[:, TILE:]
    g_ref[...] = jnp.zeros_like(g_ref)
    gfar_ref[...] = jnp.zeros_like(gfar_ref)
    dqt_ref[...] = jnp.zeros_like(dqt_ref)
    product = do_raw.astype(jnp.float32) * o_raw.astype(jnp.float32)
    deltas = []
    for head in range(2):
        half = in_half(LEN, head)
        deltas.append(jnp.sum(jnp.where(half, product, 0.0), axis=1, keepdims=True))
    aug_do = (-triple_lanes(deltas[0], deltas[1], LEN)).astype(jnp.bfloat16)
    q_scaled = q_raw * jnp.bfloat16(SCALE)
    k_t = k_raw.T
    accs = {}
    for head in range(2):
        half = in_half(LEN, head)
        q = jnp.where(half, q_scaled, aug)
        k = jnp.where(half, k_raw, ak)
        v = jnp.where(half, v_raw, av)
        do = jnp.where(half, do_raw, aug_do)
        for j in range(LEN // TILE):
            lo = j * TILE
            hi = min(LEN, (j + 3) * TILE)
            width = hi - lo
            near = min(2 * TILE, width)
            scores = dot_nt(k[lo : lo + TILE], q[lo:hi])
            parts = [scores[:, :near] + bias_ref[head][:, :near]]
            if width > near:
                parts.append(scores[:, near:] + far[head : head + 1])
            scores = parts[0] if len(parts) == 1 else jnp.concatenate(parts, axis=1)
            probs = jnp.exp(scores)
            grad_probs = dot_nt(v[lo : lo + TILE], do[lo:hi])
            grad_scores = probs * grad_probs
            g_ref[head, :, :near] += grad_scores[:, :near]
            if width > near:
                gfar_ref[head] += jnp.sum(grad_scores[:, near:].reshape(TILE // 8, 8, TILE), axis=0)
            ds = grad_scores.astype(jnp.bfloat16)
            accs[j, head] = (dot_nn(ds, q[lo:hi]), dot_nn(probs.astype(jnp.bfloat16), do[lo:hi]))
            dqt_ref[head * HD : (head + 1) * HD, lo:hi] += dot_nn(
                k_t[head * HD : (head + 1) * HD, lo : lo + TILE], ds
            )
            if head == 1:
                lower = in_half(TILE, 0)
                rows = slice(lo, lo + TILE)
                put_dk(rows, jnp.where(lower, accs[j, 0][0], accs[j, 1][0]).astype(jnp.bfloat16))
                put_dv(rows, jnp.where(lower, accs[j, 0][1], accs[j, 1][1]).astype(jnp.bfloat16))
    dq = (dqt_ref[...] * SCALE).T.astype(jnp.bfloat16)
    rows = []
    for head in range(2):
        total = jnp.zeros((8, WIN), jnp.float32)
        pad = jnp.zeros((8, TILE), jnp.float32)
        for a in range(TILE // 8):
            strip = jnp.concatenate([pad, g_ref[head, 8 * a : 8 * a + 8, :]], axis=1)
            if a:
                strip = pltpu.roll(strip, WIN - 8 * a, 1)
            total = total + strip
        line_sum = jnp.zeros((1, WIN), jnp.float32)
        for s in range(8):
            one = total[s : s + 1]
            line_sum = line_sum + (pltpu.roll(one, WIN - s, 1) if s else one)
        rows.append(line_sum)
    lines = jnp.concatenate(rows, axis=0)
    lines = jnp.where(offsets >= 0, lines, 0.0)
    high, mid, low = split3(lines)
    sums = sum(dot_nt(part.astype(jnp.bfloat16), chosen) for part in (high, mid, low))
    lane32 = lax.broadcasted_iota(jnp.int32, (1, BUCKETS), 1)
    tables = []
    for head in range(2):
        far_sum = jnp.sum(gfar_ref[head])
        tables.append(sums[head : head + 1] + jnp.where(lane32 == BUCKETS - 1, far_sum, 0.0))
    return dq, None, None, tables


def last_block(n_blk, n_dp, plans, enc_plan, big, little, keys):
    every = list(plans) + [enc_plan]
    links = len(all_links(n_blk, n_dp))
    scratch = [item for plan in every for item in plan.scratch()]
    scratch += [
        pltpu.VMEM((POOL, LEN, D), jnp.bfloat16),
        pltpu.VMEM((LEN, D), jnp.float32),
        pltpu.VMEM((D, LEN), jnp.bfloat16),
        pltpu.VMEM((2, TILE, 2 * TILE), jnp.float32),
        pltpu.VMEM((2, TILE, 2 * TILE), jnp.float32),
        pltpu.VMEM((2, 8, TILE), jnp.float32),
        pltpu.VMEM((LANES, LEN), jnp.float32),
        pltpu.VMEM((3 + H, 1, D), jnp.float32),
        pltpu.VMEM((links, 3 + H, 1, D), jnp.float32),
        pltpu.SemaphoreType.DMA((links,)),
        pltpu.SemaphoreType.DMA((links,)),
        pltpu.SemaphoreType.DMA((len(big) + 3 * (keys // LEN) - 2 + 1,)),
        pltpu.SemaphoreType.DMA((LEN // ROWS,)),
    ]
    return pl.pallas_call(
        partial(last_kernel, n_blk, n_dp, plans, enc_plan),
        in_specs=[any_spec()] * len(big) + [vmem_spec()] * len(little),
        out_specs=[vmem_spec()] * len(every) + [any_spec(), vmem_spec()],
        out_shape=[plan.out_shape() for plan in every]
        + [jax.ShapeDtypeStruct((LEN, D), jnp.float32), jax.ShapeDtypeStruct((3 + H, 1, D), jnp.float32)],
        scratch_shapes=scratch,
        compiler_params=pltpu.CompilerParams(
            vmem_limit_bytes=VMEM_LIMIT, collective_id=1, has_side_effects=True
        ),
        cost_estimate=pl.CostEstimate(flops=40 * LEN * D * D, bytes_accessed=80 * LEN * D, transcendentals=0),
    )(*big, *little)


def segment_rows(lengths_ref):
    rows = lax.broadcasted_iota(jnp.int32, (LEN, LANES), 0)
    end = jnp.zeros((1, 1), jnp.int32)
    seg = jnp.zeros((LEN, LANES), jnp.int32)
    for t in range(TARGETS - 1):
        end = end + lengths_ref[:, t : t + 1]
        seg = seg + (rows >= end).astype(jnp.int32)
    return seg


def query_marks(seg):
    place = lane_ids(LEN) & (HD - 1)
    return jnp.where((place >= 3) & (place - 3 == seg), 1.0, 0.0).astype(jnp.bfloat16)


def key_marks(seg):
    place = lane_ids(LEN) & (HD - 1)
    other = (place >= 3) & (place < 3 + TARGETS) & (place - 3 != seg)
    return jnp.where(place < 3, -1.0, jnp.where(other, NEG, 0.0)).astype(jnp.bfloat16)


def value_marks(rows):
    place = lane_ids(rows) & (HD - 1)
    return jnp.where(place < 3, 1.0, 0.0).astype(jnp.bfloat16)


def bias_lines(table_ref):
    offsets = lax.broadcasted_iota(jnp.int32, (1, WIN), 1) - TILE
    chosen = bucket_vector(None, jnp.maximum(offsets, 0))
    lines = dot_tn(table_ref[...], chosen)
    return jnp.where(offsets >= 0, lines, NEG), lines[:, WIN - 1 :]


def front_kernel(n_blk, n_dp, x_hbm, enc_hbm, wq_hbm, wk_hbm, wv_hbm, wo_hbm, wcq_hbm, wck_hbm, wcv_hbm,
                 lengths_ref, gain_ref, gainc_ref, table_ref,
                 q_hbm, k_hbm, v_hbm, o_hbm, aug_hbm, act_hbm, y1_hbm, actc_hbm, qc_hbm, kv_hbm, encall_hbm,
                 x_ref, w_ref, act_ref, q_ref, k_ref, v_ref, o_ref, aug_ref, y1_ref, kv_ref, enc_ref, bias_ref, ot_ref, logs_ref,
                 send_sem, recv_sem, load_sem, store_sem):
    passage = enc_hbm.shape[0]
    loads = []
    for n, (src, dst) in enumerate(
        [(enc_hbm, enc_ref.at[0]), (x_hbm, x_ref)]
        + [(w, w_ref.at[i]) for i, w in enumerate((wq_hbm, wk_hbm, wv_hbm, wo_hbm, wcq_hbm, wck_hbm, wcv_hbm))]
    ):
        loads.append(pltpu.make_async_copy(src, dst, load_sem.at[n]))
        loads[-1].start()
    stores = []

    def store(src, dst):
        stores.append(pltpu.make_async_copy(src, dst, store_sem.at[len(stores)]))
        stores[-1].start()

    bits = bits_of(n_blk)

    def gather(k):
        size = 1 << k
        return pltpu.make_async_remote_copy(
            src_ref=enc_ref.at[pl.ds(0, size)],
            dst_ref=enc_ref.at[pl.ds(size, size)],
            send_sem=send_sem.at[k],
            recv_sem=recv_sem.at[k],
            device_id=partner("blk", bits - 1 - k),
            device_id_type=pl.DeviceIdType.MESH,
        )

    barrier = pltpu.get_barrier_semaphore()
    for bit in range(bits):
        pl.semaphore_signal(barrier, inc=1, device_id=partner("blk", bit), device_id_type=pl.DeviceIdType.MESH)
    pl.semaphore_wait(barrier, bits)
    loads[0].wait()
    gather(0).start()
    loads[1].wait()
    for r in range(0, LEN, ROWS):
        rows = slice(r, r + ROWS)
        x = x_ref[rows].astype(jnp.float32)
        act_ref[rows] = (x * norm_parts(x) * gain_ref[...].reshape(1, D)).astype(jnp.bfloat16)
    for i, (ref, out) in enumerate(((q_ref, q_hbm), (k_ref, k_hbm), (v_ref, v_hbm))):
        loads[2 + i].wait()
        for r in range(0, LEN, ROWS):
            rows = slice(r, r + ROWS)
            ref[rows] = dot_nn(act_ref[rows], w_ref[i]).astype(jnp.bfloat16)
        store(ref, out)
    store(act_ref, act_hbm)
    seg = segment_rows(lengths_ref)
    aq, ak = query_marks(seg), key_marks(seg)
    lines, fars = bias_lines(table_ref)
    for p in range(PAIRS):
        lanes = slice(p * LANES, (p + 1) * LANES)
        if p % 2 == 1 and p // 2 < bits - 1:
            gather(p // 2).wait()
            gather(p // 2 + 1).start()
        self_pair_forward(q_ref[:, lanes], k_ref[:, lanes], v_ref[:, lanes], aq, ak, lines[2 * p : 2 * p + 2],
                          fars[2 * p : 2 * p + 2], bias_ref, ot_ref, logs_ref, o_ref, aug_ref, lanes)
    store(o_ref, o_hbm)
    store(aug_ref, aug_hbm)
    for k in range(min(bits - 1, PAIRS // 2), bits - 1):
        gather(k).wait()
        gather(k + 1).start()
    for n in range(5, 9):
        loads[n].wait()
    for r in range(0, LEN, ROWS):
        rows = slice(r, r + ROWS)
        y1 = x_ref[rows].astype(jnp.float32) + dot_nn(o_ref[rows], w_ref[3])
        y1_ref[rows] = y1
        store(y1_ref.at[pl.ds(r, ROWS)], y1_hbm.at[pl.ds(r, ROWS)])
        actc = (y1 * norm_parts(y1) * gainc_ref[...].reshape(1, D)).astype(jnp.bfloat16)
        x_ref[rows] = actc
        store(x_ref.at[pl.ds(r, ROWS)], actc_hbm.at[pl.ds(r, ROWS)])
    gather(bits - 1).wait()
    for s in range(0, n_blk):
        store(enc_ref.at[s], encall_hbm.at[pl.ds(s * passage, passage)])
    group = ROWS // passage
    for s in range(0, n_blk, group):
        encs = enc_ref[s : s + group].reshape(group * passage, D)
        rows = slice(s * passage, (s + group) * passage)
        kv_ref[rows, :D] = dot_nn(encs, w_ref[5]).astype(jnp.bfloat16)
        kv_ref[rows, D:] = dot_nn(encs, w_ref[6]).astype(jnp.bfloat16)
    store(kv_ref, kv_hbm)
    stores[0].wait()
    for r in range(0, LEN, ROWS):
        rows = slice(r, r + ROWS)
        q_ref[rows] = dot_nn(x_ref[rows], w_ref[4]).astype(jnp.bfloat16)
        store(q_ref.at[pl.ds(r, ROWS)], qc_hbm.at[pl.ds(r, ROWS)])
    for copy in stores[1:]:
        copy.wait()


def self_pair_forward(q_raw, k_raw, v_raw, aq, ak, line, far, bias_ref, ot_ref, logs_ref, o_ref, aug_ref, lanes):
    for head in range(2):
        spread = jnp.broadcast_to(line[head : head + 1], (TILE, WIN))
        bias_ref[head] = pltpu.roll(spread, 0, 1, stride=1, stride_axis=0)[:, TILE:]
    v_t = v_raw.T
    for head in range(2):
        half = in_half(LEN, head)
        q = jnp.where(half, q_raw * jnp.bfloat16(SCALE), aq)
        k = jnp.where(half, k_raw, ak)
        for i in range(LEN // TILE):
            cols = slice(i * TILE, (i + 1) * TILE)
            tiles = []
            for j in range(max(0, i - 2), i + 1):
                scores = dot_nt(k[j * TILE : (j + 1) * TILE], q[cols])
                if i - j < 2:
                    scores = scores + bias_ref[head, :, (i - j) * TILE : (i - j + 1) * TILE]
                else:
                    scores = scores + far[head : head + 1]
                tiles.append(scores)
            peak = tiles[0]
            for tile in tiles[1:]:
                peak = jnp.maximum(peak, tile)
            top = jnp.max(peak, axis=0, keepdims=True)
            total, mixed = None, None
            for n, j in enumerate(range(max(0, i - 2), i + 1)):
                expo = jnp.exp(tiles[n] - top)
                part = jnp.sum(expo, axis=0, keepdims=True)
                out = dot_nn(v_t[head * HD : (head + 1) * HD, j * TILE : (j + 1) * TILE], expo.astype(jnp.bfloat16))
                total = part if total is None else total + part
                mixed = out if mixed is None else mixed + out
            ot_ref[head * HD : (head + 1) * HD, cols] = mixed * (1.0 / total)
            logs_ref[head : head + 1, cols] = top + jnp.log(total)
    o_ref[:, lanes] = ot_ref[...].T.astype(jnp.bfloat16)
    first, second = split3(logs_ref[0:1]), split3(logs_ref[1:2])
    zeros = jnp.zeros((HD - 8, LEN), jnp.float32)
    pad = jnp.zeros((5, LEN), jnp.float32)
    triples = jnp.concatenate(list(second) + [pad, zeros] + list(first) + [pad, zeros], axis=0).T
    place = lane_ids(LEN) & (HD - 1)
    aug_ref[:, lanes] = jnp.where(place < 3, triples.astype(jnp.bfloat16), aq)


def front_block(n_blk, n_dp, big, little, keys, passage):
    wide = jax.ShapeDtypeStruct((LEN, D), jnp.bfloat16)
    n_store = 6 + n_blk + 3 * (LEN // ROWS) + 1
    return pl.pallas_call(
        partial(front_kernel, n_blk, n_dp),
        in_specs=[any_spec()] * len(big) + [vmem_spec()] * len(little),
        out_specs=[any_spec()] * 11,
        out_shape=[wide] * 6
        + [
            jax.ShapeDtypeStruct((LEN, D), jnp.float32),
            wide,
            wide,
            jax.ShapeDtypeStruct((keys, 2 * D), jnp.bfloat16),
            jax.ShapeDtypeStruct((keys, D), jnp.bfloat16),
        ],
        scratch_shapes=[
            pltpu.VMEM((LEN, D), jnp.bfloat16),
            pltpu.VMEM((7, D, D), jnp.bfloat16),
            pltpu.VMEM((LEN, D), jnp.bfloat16),
            pltpu.VMEM((LEN, D), jnp.bfloat16),
            pltpu.VMEM((LEN, D), jnp.bfloat16),
            pltpu.VMEM((LEN, D), jnp.bfloat16),
            pltpu.VMEM((LEN, D), jnp.bfloat16),
            pltpu.VMEM((LEN, D), jnp.bfloat16),
            pltpu.VMEM((LEN, D), jnp.float32),
            pltpu.VMEM((keys, 2 * D), jnp.bfloat16),
            pltpu.VMEM((n_blk, passage, D), jnp.bfloat16),
            pltpu.VMEM((2, TILE, 2 * TILE), jnp.float32),
            pltpu.VMEM((LANES, LEN), jnp.float32),
            pltpu.VMEM((2, LEN), jnp.float32),
            pltpu.SemaphoreType.DMA((bits_of(n_blk),)),
            pltpu.SemaphoreType.DMA((bits_of(n_blk),)),
            pltpu.SemaphoreType.DMA((len(big),)),
            pltpu.SemaphoreType.DMA((n_store,)),
        ],
        compiler_params=pltpu.CompilerParams(
            vmem_limit_bytes=VMEM_LIMIT, collective_id=2, has_side_effects=True
        ),
        cost_estimate=pl.CostEstimate(flops=20 * LEN * D * D, bytes_accessed=40 * LEN * D, transcendentals=0),
    )(*big, *little)


FF_STEPS = 4


def normal_cdf_pair(u):
    x = jnp.abs(u) * 0.7071067811865476
    gauss = jnp.exp(-0.5 * u * u)
    t = 1.0 / (1.0 + 0.3275911 * x)
    poly = ((((1.061405429 * t - 1.453152027) * t + 1.421413741) * t - 0.284496736) * t + 0.254829592) * t
    tail = 0.5 * poly * gauss
    return jnp.where(u >= 0, 1.0 - tail, tail), gauss * 0.3989422804014327


def rest_slot(owner, piece, order):
    slot = 0
    for axis, bit in order[2:]:
        mine = (lax.axis_index(axis) // (1 << bit)) % 2
        its = ((owner if axis == "blk" else piece) // (1 << bit)) % 2
        slot = 2 * slot + (its + mine) % 2
    return slot


class FeedParts:
    def __init__(self, plan, owners, units):
        self.plan, self.owners, self.units = plan, owners, units
        self.count = owners // 2 * len(units)

    def split(self, grad, even_core, put_send, put_keep):
        n = 0
        for t in range(0, self.owners, 2):
            for u in self.units:
                even, odd = grad(t, u), grad(t + 1, u)
                put_send(n, jnp.where(even_core, odd, even).astype(jnp.bfloat16))
                put_keep(n, jnp.where(even_core, even, odd).astype(jnp.bfloat16))
                n += 1

    def index(self, t, u):
        return t // 2 * len(self.units) + self.units.index(u)


def feed_kernel(n_blk, n_dp, plan_in, plan_out, y1_ref, oc_ref, wco_ref, gain_ref, g_ref, w1_ref, w2_ref,
                out_ref, isend_ref, ikeep_ref, osend_ref, okeep_ref, dy2_ref, e2_ref, doc_ref, dgain_ref,
                y2_ref, act_ref, acc_ref, da_ref, hid_ref, du_ref, away_ref, stay_ref, got_ref, send_sem, recv_sem):
    step = pl.program_id(0)
    even_core = lax.axis_index("blk") % 2 == 0
    group = n_blk // FF_STEPS
    parts_out = FeedParts(plan_out, group, list(range(plan_out.count)))
    parts_in = FeedParts(plan_in, n_blk, [0])

    def exchange(s):
        return pltpu.make_async_remote_copy(
            src_ref=away_ref.at[s],
            dst_ref=got_ref.at[s],
            send_sem=send_sem.at[s],
            recv_sem=recv_sem.at[s],
            device_id=partner("blk", 0),
            device_id_type=pl.DeviceIdType.MESH,
        )

    def settle(s):
        exchange(s).wait()

        def total(n):
            return (stay_ref[s % 2, n].astype(jnp.float32) + got_ref[s, n].astype(jnp.float32)).astype(jnp.bfloat16)

        def place(plan, first, second, owner, piece, inner, send_ref, keep_ref):
            axis, bit = plan.order[1]
            low = (lax.axis_index(axis) // (1 << bit)) % 2 == 0
            a, b = total(first), total(second)
            slot = rest_slot(owner, piece, plan.order)
            send_ref[slot, inner] = jnp.where(low, b, a)
            keep_ref[slot, inner] = jnp.where(low, a, b)

        for t in range(0, group, 2):
            for u in parts_out.units:
                n = parts_out.index(t, u)
                owner = s * group + t
                if plan_out.order[1][0] == "dp":
                    if u // plan_out.mats == 0:
                        twin = parts_out.index(t, u + plan_out.mats)
                        place(plan_out, n, twin, owner, 0, u % plan_out.mats, osend_ref, okeep_ref)
                elif (t >> 1) & 1 == 0:
                    place(plan_out, n, parts_out.index(t + 2, u), owner, 0, u, osend_ref, okeep_ref)
        for t in range(0, n_blk, 2):
            if (t >> 1) & 1 == 0:
                n = parts_out.count + parts_in.index(t, 0)
                twin = parts_out.count + parts_in.index(t + 2, 0)
                place(plan_in, n, twin, t, s // plan_in.mats, s % plan_in.mats, isend_ref, ikeep_ref)

    @pl.when(step == 0)
    def _():
        barrier = pltpu.get_barrier_semaphore()
        pl.semaphore_signal(
            barrier, inc=1, device_id=partner("blk", 0), device_id_type=pl.DeviceIdType.MESH
        )
        pl.semaphore_wait(barrier, 1)
        for r in range(0, LEN, ROWS):
            rows = slice(r, r + ROWS)
            y2 = y1_ref[rows] + dot_nn(oc_ref[rows], wco_ref[...])
            y2_ref[rows] = y2
            act_ref[rows] = (y2 * norm_parts(y2) * gain_ref[...].reshape(1, D)).astype(jnp.bfloat16)
        acc_ref[...] = y2_ref[...]
        da_ref[...] = jnp.zeros_like(da_ref)

    for r in range(0, LEN, ROWS):
        rows = slice(r, r + ROWS)
        u = dot_nn(act_ref[rows], w1_ref[...])
        dh = dot_nt(g_ref[rows], w2_ref[...])
        cdf, density = normal_cdf_pair(u)
        hid = (u * cdf).astype(jnp.bfloat16)
        du = (dh * (cdf + u * density)).astype(jnp.bfloat16)
        hid_ref[rows] = hid
        du_ref[rows] = du
        acc_ref[rows] += dot_nn(hid, w2_ref[...])
        da_ref[rows] += dot_nt(du, w1_ref[...])

    def put(n, value, base, ref):
        ref[base + n] = value

    dw2 = dot_tn(hid_ref[...], g_ref[...])
    own_rows = plan_out.rows * plan_out.count
    parts_out.split(
        lambda t, m: dw2[t * own_rows + m * plan_out.rows : t * own_rows + (m + 1) * plan_out.rows],
        even_core,
        lambda n, value: away_ref.__setitem__((step, n), value),
        lambda n, value: stay_ref.__setitem__((step % 2, n), value),
    )
    dw1 = dot_tn(act_ref[...], du_ref[...])
    parts_in.split(
        lambda t, m: dw1[t * plan_in.rows : (t + 1) * plan_in.rows],
        even_core,
        lambda n, value: away_ref.__setitem__((step, parts_out.count + n), value),
        lambda n, value: stay_ref.__setitem__((step % 2, parts_out.count + n), value),
    )
    exchange(step).start()

    @pl.when(step > 0)
    def _():
        settle(step - 1)

    @pl.when(step == FF_STEPS - 1)
    def _():
        gain_sum = jnp.zeros((1, D), jnp.float32)
        for r in range(0, LEN, ROWS):
            rows = slice(r, r + ROWS)
            out_ref[rows] = acc_ref[rows].astype(jnp.bfloat16)
            y2 = y2_ref[rows]
            inverse = norm_parts(y2)
            da = da_ref[rows]
            gain_sum = gain_sum + jnp.sum(da * y2 * inverse, axis=0, keepdims=True)
            dy2 = g_ref[rows].astype(jnp.float32) + norm_back(y2, inverse, gain_ref[...].reshape(1, D), da)
            dy2_ref[rows] = dy2
            e2 = dy2.astype(jnp.bfloat16)
            e2_ref[rows] = e2
            doc_ref[rows] = dot_nt(e2, wco_ref[...]).astype(jnp.bfloat16)
        dgain_ref[...] = gain_sum
        settle(step)


def feed_block(n_blk, n_dp, y1, oc, wco, gain, g, w1, w2, plan_in, plan_out):
    ff = w1.shape[1]
    cols = ff // FF_STEPS
    fixed = vmem_spec()
    quarter = lambda plan: (plan.slots // 4, plan.mats, plan.rows, D)
    like = jax.ShapeDtypeStruct
    units = n_blk // FF_STEPS // 2 * plan_out.count + n_blk // 2
    packet = (units, D // n_blk, D)
    return pl.pallas_call(
        partial(feed_kernel, n_blk, n_dp, plan_in, plan_out),
        grid=(FF_STEPS,),
        in_specs=[fixed] * 5
        + [
            pl.BlockSpec((D, cols), lambda c: (0, c)),
            pl.BlockSpec((cols, D), lambda c: (c, 0)),
        ],
        out_specs=[fixed] * 9,
        out_shape=[
            like((LEN, D), jnp.bfloat16),
            like(quarter(plan_in), jnp.bfloat16),
            like(quarter(plan_in), jnp.bfloat16),
            like(quarter(plan_out), jnp.bfloat16),
            like(quarter(plan_out), jnp.bfloat16),
            like((LEN, D), jnp.float32),
            like((LEN, D), jnp.bfloat16),
            like((LEN, D), jnp.bfloat16),
            like((1, D), jnp.float32),
        ],
        scratch_shapes=[
            pltpu.VMEM((LEN, D), jnp.float32),
            pltpu.VMEM((LEN, D), jnp.bfloat16),
            pltpu.VMEM((LEN, D), jnp.float32),
            pltpu.VMEM((LEN, D), jnp.float32),
            pltpu.VMEM((LEN, cols), jnp.bfloat16),
            pltpu.VMEM((LEN, cols), jnp.bfloat16),
            pltpu.VMEM((FF_STEPS,) + packet, jnp.bfloat16),
            pltpu.VMEM((2,) + packet, jnp.bfloat16),
            pltpu.VMEM((FF_STEPS,) + packet, jnp.bfloat16),
            pltpu.SemaphoreType.DMA((FF_STEPS,)),
            pltpu.SemaphoreType.DMA((FF_STEPS,)),
        ],
        compiler_params=pltpu.CompilerParams(
            vmem_limit_bytes=VMEM_LIMIT, collective_id=3, has_side_effects=True
        ),
        cost_estimate=pl.CostEstimate(flops=12 * LEN * D * ff, bytes_accessed=40 * LEN * D, transcendentals=0),
    )(y1, oc, wco, gain, g, w1, w2)


def unpack_kernel(in_ref, out_ref, crossx, crossy, *refs):
    blocks, (enc_ref, sums_ref), outs = refs[: len(BLOCK_PAIRS)], refs[len(BLOCK_PAIRS) : len(BLOCK_PAIRS) + 2], refs[len(BLOCK_PAIRS) + 2 :]
    (gq, gk, gv, go, gcq, gck, gcv, gco, gin, gout, genc, gain0, gain1, gain2, table) = outs
    for w, ref in enumerate((gq, gk, gv)):
        at = 0
        for part, pairs in zip(blocks, BLOCK_PAIRS):
            for c in range(pairs):
                ref[:, at : at + LANES] = part[pairs * w + c]
                at += LANES
    half = D // 2
    for ref, part, w in ((gcq, crossx, 0), (gck, crossx, 1), (gcv, crossx, 2), (gco, crossy, 0), (go, crossy, 1)):
        for c in range(2):
            ref[:, c * half : (c + 1) * half] = part[2 * w + c]
    rows = gq.shape[0]
    for m in range(4):
        gin[:, m * D : (m + 1) * D] = in_ref[m]
        gout[m * rows : (m + 1) * rows] = out_ref[m]
    genc[...] = enc_ref[0]
    for n, ref in enumerate((gain0, gain1, gain2)):
        ref[...] = sums_ref[n].reshape(D)
    tables = jnp.concatenate([sums_ref[3 + h][:, :LANES] for h in range(H)] + [jnp.zeros((4, LANES), jnp.float32)], axis=0)
    table[...] = tables.T[:BUCKETS, :H]


def unpack(n_blk, passage, parts):
    rows = D // n_blk
    like = lambda *shape: jax.ShapeDtypeStruct(shape, jnp.float32)
    return pl.pallas_call(
        unpack_kernel,
        in_specs=[vmem_spec()] * len(parts),
        out_specs=[vmem_spec()] * 15,
        out_shape=[like(rows, D)] * 8
        + [like(rows, 4 * D), like(4 * rows, D), like(passage, D)]
        + [like(D)] * 3
        + [like(BUCKETS, H)],
        compiler_params=pltpu.CompilerParams(vmem_limit_bytes=VMEM_LIMIT),
    )(*parts)


def swap(value, axis, bit, size):
    return lax.ppermute(value, axis, [(i, i ^ (1 << bit)) for i in range(size)])


def per_device(
    decoder_rows,
    encoder_rows,
    target_lengths,
    target_question,
    passage_question,
    self_gain,
    self_query,
    self_key,
    self_value,
    self_output,
    position_bias_matrix,
    cross_gain,
    cross_query,
    cross_key,
    cross_value,
    cross_output,
    feed_gain,
    feed_input_weight,
    feed_out,
    cotangent,
    n_dp,
    n_blk,
):
    passage = encoder_rows.shape[0]
    keys = passage * n_blk
    sizes = {"blk": n_blk, "dp": n_dp}
    (query_self, key_self, value_self, attn_self, aug_self, act_self, resid_self, act_cross, query_cross, pair_all,
     encoder_all) = front_block(
        n_blk, n_dp,
        (decoder_rows, encoder_rows, self_query, self_key, self_value, self_output, cross_query, cross_key, cross_value),
        (target_lengths, self_gain, cross_gain, position_bias_matrix), keys, passage,
    )
    layout = (target_lengths, target_question, passage_question)
    attn_cross, aug_cross = cross_forward(n_blk, passage, *layout, query_cross, pair_all)
    plan_in, plan_out = feed_plans(n_blk, n_dp)
    (block_out, in_send, in_keep, out_send, out_keep, grad_resid_cross, round_cross, grad_attn_cross, feed_sum) = feed_block(
        n_blk, n_dp, resid_self, attn_cross, cross_output, feed_gain, cotangent, feed_input_weight, feed_out,
        plan_in, plan_out,
    )
    in_got = swap(in_send, *plan_in.order[FEED_DONE - 1], sizes[plan_in.order[FEED_DONE - 1][0]])
    out_got = swap(out_send, *plan_out.order[FEED_DONE - 1], sizes[plan_out.order[FEED_DONE - 1][0]])
    dqc, dkv, grad_resid_self, grad_attn_self, encoder_part, cross_sum = cross_backward(
        n_blk, passage, *layout, query_cross, pair_all, grad_attn_cross, attn_cross, aug_cross,
        resid_self, grad_resid_cross, cross_query, cross_key, cross_value, self_output, cross_gain,
    )
    enc_plan = Exchange(1, passage, D, n_blk, n_dp, "near")
    big = (
        decoder_rows, grad_resid_self, act_self, self_query, self_key, self_value, act_cross, dqc, encoder_all, dkv,
        attn_cross, round_cross, query_self, key_self, value_self, grad_attn_self, attn_self, aug_self,
        in_keep, in_got, out_keep, out_got, encoder_part,
    )
    last = last_block(
        n_blk, n_dp, last_plans(n_blk, n_dp), enc_plan, big,
        (target_lengths, self_gain, position_bias_matrix, cross_sum, feed_sum), keys,
    )
    spot = len(last) - 2
    grad_decoder = last[spot]
    (gq, gk, gv, go, gcq, gck, gcv, gco, gin, gout, genc, gain_self, gain_cross, gain_feed, table) = unpack(
        n_blk, passage, last[:spot] + last[spot + 1 :]
    )
    return (
        block_out, grad_decoder, genc, gain_self, gq, gk, gv, go, table, gain_cross, gcq, gck, gcv, gco,
        gain_feed, gin, gout,
    )


def solution(mesh):
    split, copied, owned = P(("dp", "blk"), None), P(), P("blk", None)
    return jax.shard_map(
        partial(per_device, n_dp=mesh.shape["dp"], n_blk=mesh.shape["blk"]),
        mesh=mesh,
        in_specs=(split,) * 4 + (P("dp"),) + (copied,) * 14 + (split,),
        out_specs=(split,) * 3 + (copied,) + (owned,) * 4 + (copied,) * 2 + (owned,) * 4 + (copied,) + (owned,) * 2,
        check_vma=False,
    )
```

```python
import functools
from functools import partial

import jax
import jax.numpy as jnp
from jax import lax
from jax.experimental import pallas as pl
from jax.experimental.pallas import tpu as pltpu
from jax.sharding import PartitionSpec as P

D = 768
H = 12
HD = 64
BUCKETS = 32
LEN = 1024
TARGETS = 4
PAIRS = H // 2
LANES = 2 * HD
TILE = 256
SCALE = HD ** -0.5
NEG = -1e30
VMEM_LIMIT = 60 * 1024 * 1024

eps_norm = 1e-06
bucket_edges = (19, 21, 24, 27, 31, 35, 40, 46, 52, 59, 67, 77, 87, 99, 113)


def dot_nn(a, b):
    return jnp.dot(a, b, preferred_element_type=jnp.float32)


def dot_nt(a, b):
    return lax.dot_general(a, b, (((1,), (1,)), ((), ())), preferred_element_type=jnp.float32)


def dot_tn(a, b):
    return lax.dot_general(a, b, (((0,), (0,)), ((), ())), preferred_element_type=jnp.float32)


def lane_ids(rows):
    return lax.broadcasted_iota(jnp.int32, (rows, LANES), 1)


def in_half(rows, head):
    lane = lane_ids(rows)
    return lane < HD if head == 0 else lane >= HD


def split3(value):
    high = value.astype(jnp.bfloat16).astype(jnp.float32)
    rest = value - high
    mid = rest.astype(jnp.bfloat16).astype(jnp.float32)
    return high, mid, rest - mid


def triple_lanes(first, second, rows):
    lane = lane_ids(rows)
    out = jnp.zeros((rows, LANES), jnp.float32)
    for base, value in ((HD, first), (0, second)):
        for place, part in enumerate(split3(value)):
            out = jnp.where(lane == base + place, part, out)
    return out


def bucket_vector(table_t, offsets):
    upper = jnp.full(offsets.shape, 16, jnp.int32)
    for edge in bucket_edges:
        upper = upper + (offsets >= edge).astype(jnp.int32)
    bucket = jnp.where(offsets < 16, offsets, upper)
    rows = lax.broadcasted_iota(jnp.int32, (BUCKETS, offsets.shape[1]), 0)
    chosen = (rows == bucket).astype(jnp.float32).astype(jnp.bfloat16)
    return chosen


WIN = 3 * TILE


ROWS = 256


def norm_parts(values):
    return lax.rsqrt(jnp.mean(values * values, axis=1, keepdims=True) + eps_norm)


def norm_back(values, inverse, gain, grad):
    scaled = grad * gain
    inner = jnp.mean(scaled * values, axis=1, keepdims=True)
    return inverse * scaled - values * (inverse * inverse * inverse * inner)


CT = 256


def cross_layout(n_blk, lengths_ref, question_ref, passage_ref, order_ref, item_ref, count_ref):
    per_q = n_blk // TARGETS
    bits = bits_of(n_blk)
    me = lax.axis_index("blk")
    for t in range(TARGETS + 1):
        count_ref[t] = 0
    for s in range(n_blk):
        device = 0
        for b in range(bits):
            mine = (me // (1 << b)) % 2
            flip = (s >> (bits - 1 - b)) & 1
            device = device + (1 - mine if flip else mine) * (1 << b)
        question = passage_ref[device]
        order_ref[question * per_q + count_ref[question]] = s
        count_ref[question] = count_ref[question] + 1
    end = 0
    for t in range(TARGETS):
        start, end = end, end + lengths_ref[0, t]
        question = question_ref[0, t]

        @pl.loop(start // CT, (end + CT - 1) // CT)
        def _(tile, start=start, end=end, question=question):
            n = count_ref[TARGETS]
            item_ref[0, n] = tile
            item_ref[1, n] = question
            item_ref[2, n] = start - tile * CT
            item_ref[3, n] = end - tile * CT
            count_ref[TARGETS] = n + 1


def layout_scratch(n_blk):
    return [
        pltpu.SMEM((n_blk,), jnp.int32),
        pltpu.SMEM((4, LEN // CT + TARGETS), jnp.int32),
        pltpu.SMEM((TARGETS + 1,), jnp.int32),
    ]


def cross_forward_kernel(n_blk, passage, lengths_ref, question_ref, passage_ref, q_ref, kv_ref, o_ref, aug_ref,
                         ks_ref, vs_ref, order_ref, item_ref, count_ref):
    keys_q = n_blk // TARGETS * passage
    lower = lax.broadcasted_iota(jnp.int32, (passage, D), 1) % LANES < HD
    zero = jnp.zeros((), jnp.bfloat16)
    cross_layout(n_blk, lengths_ref, question_ref, passage_ref, order_ref, item_ref, count_ref)

    @pl.loop(0, n_blk)
    def _(s):
        src = pl.multiple_of(order_ref[s] * passage, passage)
        dst = pl.multiple_of(s * passage, passage)
        keys = kv_ref[pl.ds(src, passage), :D]
        values = kv_ref[pl.ds(src, passage), D:]
        ks_ref[0, pl.ds(dst, passage)] = jnp.where(lower, keys, zero)
        ks_ref[1, pl.ds(dst, passage)] = jnp.where(lower, zero, keys)
        vs_ref[0, pl.ds(dst, passage)] = jnp.where(lower, values, zero)
        vs_ref[1, pl.ds(dst, passage)] = jnp.where(lower, zero, values)

    o_ref[...] = jnp.zeros_like(o_ref)
    aug_ref[...] = jnp.zeros_like(aug_ref)

    @pl.loop(0, count_ref[TARGETS])
    def _(n):
        row0 = pl.multiple_of(item_ref[0, n] * CT, CT)
        key0 = pl.multiple_of(item_ref[1, n] * keys_q, keys_q)
        rows = lax.broadcasted_iota(jnp.int32, (CT, 1), 0)
        valid = (rows >= item_ref[2, n]) & (rows < item_ref[3, n])
        for pair in range(PAIRS):
            cols = slice(pair * LANES, (pair + 1) * LANES)
            q = q_ref[pl.ds(row0, CT), cols] * jnp.bfloat16(SCALE)
            outs, logs = [], []
            for head in range(2):
                scores = dot_nt(q, ks_ref[head, pl.ds(key0, keys_q), cols])
                top = jnp.max(scores, axis=1, keepdims=True)
                expo = jnp.exp(scores - top)
                total = jnp.sum(expo, axis=1, keepdims=True)
                outs.append(dot_nn(expo.astype(jnp.bfloat16), vs_ref[head, pl.ds(key0, keys_q), cols]) / total)
                logs.append(top + jnp.log(total))
            mixed = (outs[0] + outs[1]).astype(jnp.bfloat16)
            aug = triple_lanes(logs[0], logs[1], CT).astype(jnp.bfloat16)
            o_ref[pl.ds(row0, CT), cols] = jnp.where(valid, mixed, o_ref[pl.ds(row0, CT), cols])
            aug_ref[pl.ds(row0, CT), cols] = jnp.where(valid, aug, aug_ref[pl.ds(row0, CT), cols])


def smem_spec():
    return pl.BlockSpec(memory_space=pltpu.SMEM)


def vmem_spec():
    return pl.BlockSpec(memory_space=pltpu.VMEM)


def any_spec():
    return pl.BlockSpec(memory_space=pl.ANY)


def cross_forward(n_blk, passage, lengths, questions, passages, q, kv):
    keys = kv.shape[0]
    return pl.pallas_call(
        partial(cross_forward_kernel, n_blk, passage),
        in_specs=[smem_spec()] * 3 + [vmem_spec()] * 2,
        out_specs=[vmem_spec(), vmem_spec()],
        out_shape=[jax.ShapeDtypeStruct((LEN, D), jnp.bfloat16)] * 2,
        scratch_shapes=[pltpu.VMEM((2, keys, D), jnp.bfloat16)] * 2 + layout_scratch(n_blk),
        compiler_params=pltpu.CompilerParams(vmem_limit_bytes=VMEM_LIMIT),
        cost_estimate=pl.CostEstimate(flops=2 * H * LEN * LEN * HD, bytes_accessed=10 * LEN * D, transcendentals=0),
    )(lengths, questions, passages, q, kv)


def cross_backward_kernel(n_blk, passage, lengths_ref, question_ref, passage_ref, q_ref, do_ref, o_ref, aug_ref,
                          kv_hbm, y1_hbm, dy2_hbm, wcq_hbm, wck_hbm, wcv_hbm, wo_hbm, gain_ref,
                          dq_ref, dkv_ref, dy1_ref, dos_ref, part_ref, dgain_ref,
                          ks_ref, vs_ref, kt_ref, dk_ref, dv_ref, dqt_ref, y1_ref, load_sem,
                          order_ref, item_ref, count_ref):
    loads = []
    for n, (src, dst) in enumerate(
        [(kv_hbm, dkv_ref), (y1_hbm, y1_ref), (dy2_hbm, dy1_ref)]
    ):
        loads.append(pltpu.make_async_copy(src, dst, load_sem.at[n]))
        loads[-1].start()
    keys_q = n_blk // TARGETS * passage
    lane = lax.broadcasted_iota(jnp.int32, (passage, D), 1) % LANES
    lower = lane < HD
    ones = jnp.where((lane & (HD - 1)) < 3, 1.0, 0.0).astype(jnp.bfloat16)
    minus = -ones
    cross_layout(n_blk, lengths_ref, question_ref, passage_ref, order_ref, item_ref, count_ref)

    loads[0].wait()

    @pl.loop(0, n_blk)
    def _(s):
        src = pl.multiple_of(order_ref[s] * passage, passage)
        dst = pl.multiple_of(s * passage, passage)
        keys = dkv_ref[pl.ds(src, passage), :D]
        values = dkv_ref[pl.ds(src, passage), D:]
        ks_ref[0, pl.ds(dst, passage)] = jnp.where(lower, keys, minus)
        ks_ref[1, pl.ds(dst, passage)] = jnp.where(lower, minus, keys)
        vs_ref[0, pl.ds(dst, passage)] = jnp.where(lower, values, ones)
        vs_ref[1, pl.ds(dst, passage)] = jnp.where(lower, ones, values)

    lower_k = lax.broadcasted_iota(jnp.int32, (keys_q, LANES), 1) < HD
    for s in range(TARGETS):
        for pair in range(PAIRS):
            rows = slice(s * keys_q, (s + 1) * keys_q)
            cols = slice(pair * LANES, (pair + 1) * LANES)
            both = jnp.where(lower_k, ks_ref[0, rows, cols], ks_ref[1, rows, cols])
            kt_ref[cols, rows] = both.T
    dk_ref[...] = jnp.zeros_like(dk_ref)
    dv_ref[...] = jnp.zeros_like(dv_ref)
    dqt_ref[...] = jnp.zeros_like(dqt_ref)

    @pl.loop(0, count_ref[TARGETS])
    def _(n):
        row0 = pl.multiple_of(item_ref[0, n] * CT, CT)
        key0 = pl.multiple_of(item_ref[1, n] * keys_q, keys_q)
        rows = lax.broadcasted_iota(jnp.int32, (CT, 1), 0)
        valid = (rows >= item_ref[2, n]) & (rows < item_ref[3, n])
        here = pl.ds(row0, CT)
        there = pl.ds(key0, keys_q)
        for pair in range(PAIRS):
            cols = slice(pair * LANES, (pair + 1) * LANES)
            q_scaled = q_ref[here, cols] * jnp.bfloat16(SCALE)
            do_pair = jnp.where(valid, do_ref[here, cols], jnp.zeros((), jnp.bfloat16))
            product = do_pair.astype(jnp.float32) * o_ref[here, cols].astype(jnp.float32)
            deltas = []
            for head in range(2):
                deltas.append(jnp.sum(jnp.where(in_half(CT, head), product, 0.0), axis=1, keepdims=True))
            aug_do = (-triple_lanes(deltas[0], deltas[1], CT)).astype(jnp.bfloat16)
            aug = jnp.where(valid, aug_ref[here, cols], jnp.bfloat16(-NEG))
            parts = []
            for head in range(2):
                half = in_half(CT, head)
                q = jnp.where(half, q_scaled, aug)
                do = jnp.where(half, do_pair, aug_do)
                probs = jnp.exp(dot_nt(ks_ref[head, there, cols], q))
                grad_scores = probs * dot_nt(vs_ref[head, there, cols], do)
                ds = grad_scores.astype(jnp.bfloat16)
                parts.append((dot_nn(ds, q), dot_nn(probs.astype(jnp.bfloat16), do)))
                hrow = pair * LANES + head * HD
                dqt_ref[hrow : hrow + HD, here] += dot_nn(kt_ref[hrow : hrow + HD, there], ds)
            dk_ref[there, cols] += jnp.where(lower_k, parts[0][0], parts[1][0])
            dv_ref[there, cols] += jnp.where(lower_k, parts[0][1], parts[1][1])

    spots = (ks_ref.at[0], ks_ref.at[1], vs_ref.at[0], vs_ref.at[1])
    for n, w in enumerate((wcq_hbm, wck_hbm, wcv_hbm, wo_hbm)):
        loads.append(pltpu.make_async_copy(w, spots[n].at[pl.ds(0, D)], load_sem.at[3 + n]))
        loads[-1].start()
    for pair in range(PAIRS):
        cols = slice(pair * LANES, (pair + 1) * LANES)
        dq_ref[:, cols] = (dqt_ref[cols, :] * SCALE).T.astype(jnp.bfloat16)

    for copy in loads[1:]:
        copy.wait()

    @pl.loop(0, n_blk)
    def _(s):
        src = pl.multiple_of(s * passage, passage)
        spot = order_ref[s]
        dst = pl.multiple_of(spot * passage, passage)
        dk = dk_ref[pl.ds(src, passage)].astype(jnp.bfloat16)
        dv = dv_ref[pl.ds(src, passage)].astype(jnp.bfloat16)
        dkv_ref[pl.ds(dst, passage), :D] = dk
        dkv_ref[pl.ds(dst, passage), D:] = dv

    group = ROWS // passage
    for s in range(0, n_blk, group):
        rows = slice(s * passage, (s + group) * passage)
        part = dot_nt(dkv_ref[rows, :D], ks_ref[1, :D]) + dot_nt(dkv_ref[rows, D:], vs_ref[0, :D])
        part_ref[s : s + group, 0] = part.astype(jnp.bfloat16).reshape(group, passage, D)
    gain_sum = jnp.zeros((1, D), jnp.float32)
    for r in range(0, LEN, ROWS):
        rows = slice(r, r + ROWS)
        da = dot_nt(dq_ref[rows], ks_ref[0, :D])
        y1 = y1_ref[rows]
        inverse = norm_parts(y1)
        gain_sum = gain_sum + jnp.sum(da * y1 * inverse, axis=0, keepdims=True)
        dy1 = dy1_ref[rows] + norm_back(y1, inverse, gain_ref[1:2], da)
        dy1_ref[rows] = dy1
        dos_ref[rows] = dot_nt(dy1.astype(jnp.bfloat16), vs_ref[1, :D]).astype(jnp.bfloat16)
    dgain_ref[...] = gain_sum


def cross_backward(n_blk, passage, lengths, questions, passages, q, kv, do, o, aug, y1, dy2, wcq, wck, wcv, wo, gain):
    keys = kv.shape[0]
    like = jax.ShapeDtypeStruct
    return pl.pallas_call(
        partial(cross_backward_kernel, n_blk, passage),
        in_specs=[smem_spec()] * 3 + [vmem_spec()] * 4 + [any_spec()] * 7 + [vmem_spec()],
        out_specs=[vmem_spec()] * 6,
        out_shape=[
            like((LEN, D), jnp.bfloat16),
            like((keys, 2 * D), jnp.bfloat16),
            like((LEN, D), jnp.float32),
            like((LEN, D), jnp.bfloat16),
            like((n_blk, 1, passage, D), jnp.bfloat16),
            like((1, D), jnp.float32),
        ],
        scratch_shapes=[pltpu.VMEM((2, keys, D), jnp.bfloat16)] * 2
        + [
            pltpu.VMEM((D, keys), jnp.bfloat16),
            pltpu.VMEM((keys, D), jnp.float32),
            pltpu.VMEM((keys, D), jnp.float32),
            pltpu.VMEM((D, LEN), jnp.float32),
            pltpu.VMEM((LEN, D), jnp.float32),
            pltpu.SemaphoreType.DMA((7,)),
        ]
        + layout_scratch(n_blk),
        compiler_params=pltpu.CompilerParams(vmem_limit_bytes=VMEM_LIMIT),
        cost_estimate=pl.CostEstimate(flops=5 * H * LEN * LEN * HD, bytes_accessed=18 * LEN * D, transcendentals=0),
    )(lengths, questions, passages, q, do, o, aug, kv, y1, dy2, wcq, wck, wcv, wo, gain)


def bits_of(count):
    return count.bit_length() - 1


def place_bits(n_blk, n_dp, kind):
    blk = [("blk", bit) for bit in range(bits_of(n_blk))]
    dp = [("dp", bit) for bit in range(bits_of(n_dp))]
    if kind == "x":
        return blk[:1] + dp + blk[1:]
    if kind == "y":
        return blk[:2] + dp + blk[2:]
    return blk


def position(owner, piece, order):
    slot = 0
    for axis, bit in order:
        mine = (lax.axis_index(axis) // (1 << bit)) % 2
        static = ((owner if axis == "blk" else piece) >> bit) & 1
        slot = 2 * slot + (1 - mine if static else mine)
    return slot


def partner(axis, bit):
    me = lax.axis_index(axis)
    mine = (me // (1 << bit)) % 2
    return {axis: me + (1 - 2 * mine) * (1 << bit)}


class Exchange:
    def __init__(self, count, rows, cols, n_blk, n_dp, kind, first=0):
        if kind in "xy" and count % n_dp:
            kind = "plain"
        self.n_blk, self.n_dp, self.count, self.kind, self.first = n_blk, n_dp, count, kind, first
        self.rows, self.cols = rows, cols
        self.order = place_bits(n_blk, n_dp, kind)
        self.pieces = n_dp if kind in "xy" else 1
        self.slots = n_blk * self.pieces
        self.mats = count // self.pieces
        self.last = [("dp", bit) for bit in range(bits_of(n_dp))] if kind != "near" else []
        self.steps = len(self.order) + len(self.last)
        self.held = self.slots >> first
        self.offsets = {}
        at = self.held if first else 0
        for k in range(first, len(self.order)):
            size = self.slots >> (k + 1)
            self.offsets[k] = (at, size)
            at += size
        for j in range(len(self.last)):
            size = (1 << j) if self.pieces > 1 else 1
            self.offsets[len(self.order) + j] = (at, size)
            at += size
        self.received = at

    def scratch(self):
        shape = (self.mats, self.rows, self.cols)
        return [
            pltpu.VMEM((max(self.held, self.pieces),) + shape, jnp.bfloat16),
            pltpu.VMEM((self.received,) + shape, jnp.bfloat16),
            pltpu.SemaphoreType.DMA((self.steps,)),
            pltpu.SemaphoreType.DMA((self.steps,)),
        ]

    def out_shape(self):
        return jax.ShapeDtypeStruct((self.count, self.rows, self.cols), jnp.float32)

    def bind(self, refs, out_ref):
        self.buf, self.recv, self.send_sem, self.recv_sem = refs
        self.out = out_ref

    def put(self, index, value):
        piece, inner = index // self.mats, index % self.mats
        for owner in range(self.n_blk):
            slot = position(owner, piece, self.order)
            self.buf[slot, inner] = value[owner * self.rows : (owner + 1) * self.rows].astype(jnp.bfloat16)

    def copy(self, k):
        at, size = self.offsets[k]
        if k < len(self.order):
            axis, bit = self.order[k]
            src = self.buf.at[pl.ds(size, size)]
        else:
            axis, bit = self.last[k - len(self.order)]
            src = self.buf.at[pl.ds(0, size)]
        return pltpu.make_async_remote_copy(
            src_ref=src,
            dst_ref=self.recv.at[pl.ds(at, size)],
            send_sem=self.send_sem.at[k],
            recv_sem=self.recv_sem.at[k],
            device_id=partner(axis, bit),
            device_id_type=pl.DeviceIdType.MESH,
        )

    def start(self, k):
        self.copy(k).start()

    def add(self, at, size, final):
        for s in range(size):
            for m in range(self.mats):
                total = self.buf[s, m].astype(jnp.float32) + self.recv[at + s, m].astype(jnp.float32)
                if final:
                    self.out[m] = total
                else:
                    self.buf[s, m] = total.astype(jnp.bfloat16)

    def finish(self, k):
        self.copy(k).wait()
        at, size = self.offsets[k]
        final = k == self.steps - 1
        if k < len(self.order) or self.pieces == 1:
            self.add(at, size, final)
            return
        for s in range(size):
            for m in range(self.mats):
                self.buf[size + s, m] = self.recv[at + s, m]
        if final:
            for s in range(self.pieces):
                spot = position(0, s, self.last[::-1])
                for m in range(self.mats):
                    self.out[spot * self.mats + m] = self.buf[s, m].astype(jnp.float32)

    def advance(self, k):
        if k < self.first or k >= self.steps:
            return
        self.finish(k)
        if k + 1 < self.steps:
            self.start(k + 1)


def all_links(n_blk, n_dp):
    return [("blk", bit) for bit in range(bits_of(n_blk))] + [("dp", bit) for bit in range(bits_of(n_dp))]


def enter_barrier(n_blk, n_dp):
    barrier = pltpu.get_barrier_semaphore()
    links = all_links(n_blk, n_dp)
    for axis, bit in links:
        pl.semaphore_signal(barrier, inc=1, device_id=partner(axis, bit), device_id_type=pl.DeviceIdType.MESH)
    pl.semaphore_wait(barrier, len(links))


BLOCKS = 3
BLOCK = D // BLOCKS
BLOCK_PAIRS = (2,) * BLOCKS
FEED_DONE = 2


def last_plans(n_blk, n_dp):
    rows = D // n_blk
    halves = 2
    feed_in, feed_out = feed_plans(n_blk, n_dp, FEED_DONE)
    plans = [
        feed_in,
        feed_out,
        Exchange(3 * halves, rows, D // halves, n_blk, n_dp, "x"),
        Exchange(2 * halves, rows, D // halves, n_blk, n_dp, "y"),
    ]
    for block in range(BLOCKS):
        plans.append(Exchange(3 * halves, rows, BLOCK // halves, n_blk, n_dp, "xyx"[block]))
    return plans


def feed_plans(n_blk, n_dp, first=0):
    rows = D // n_blk
    return (
        Exchange(4, rows, D, n_blk, n_dp, "y", first),
        Exchange(4, rows, D, n_blk, n_dp, "x", first),
    )


POOL = 11
(S_ACTC, S_DQC, S_OC, S_E2, S_Q, S_K, S_V, S_DO, S_O, S_AUG, S_X) = range(POOL)
S_DQ, S_DK, S_DV, S_ACT = S_ACTC, S_DQC, S_OC, S_E2


def last_kernel(n_blk, n_dp, plans, enc_plan, *refs):
    (x_hbm, dy1_hbm, act_hbm, wq_hbm, wk_hbm, wv_hbm, actc_hbm, dqc_hbm, enc_hbm, dkv_hbm, oc_hbm, e2_hbm,
     q_hbm, k_hbm, v_hbm, do_hbm, o_hbm, aug_hbm, inkeep_hbm, inrecv_hbm, outkeep_hbm, outrecv_hbm, part_hbm,
     lengths_ref, gain_ref, table_ref, gainc_ref, gainf_ref) = refs[:28]
    every = list(plans) + [enc_plan]
    outs = refs[28 : 28 + len(every)]
    dx_hbm, sums_ref = refs[28 + len(every) : 30 + len(every)]
    scratch = refs[30 + len(every) :]
    for i, plan in enumerate(every):
        plan.bind(scratch[4 * i : 4 * i + 4], outs[i])
    (pool, dy1_ref, act_t, bias_ref, g_ref, gfar_ref, dqt_ref,
     tot_ref, got_ref, tsend, trecv, load_sem, store_sem) = scratch[4 * len(every) :]
    feed_in, feed_out, crossx, crossy, self0, self1, self2 = plans
    selfs = (self0, self1, self2)

    loads = {}

    def load(name, src, dst):
        loads[name] = pltpu.make_async_copy(src, dst, load_sem.at[len(loads)])
        loads[name].start()

    def slot(index):
        return pool.at[index]

    load("actc", actc_hbm, slot(S_ACTC))
    load("dqc", dqc_hbm, slot(S_DQC))
    for plan, keep, got, name in (
        (feed_out, outkeep_hbm, outrecv_hbm, "out"),
        (feed_in, inkeep_hbm, inrecv_hbm, "in"),
    ):
        load(name + "keep", keep, plan.buf.at[pl.ds(0, plan.held)])
        load(name + "recv", got, plan.recv.at[pl.ds(0, plan.held)])
    spans = enc_hbm.shape[0] // LEN
    spare = (S_Q, S_K, S_V, S_DO, S_AUG, S_X)
    for n in range(spans):
        rows = pl.ds(n * LEN, LEN)
        load(("enc", n), enc_hbm.at[rows], slot(spare[3 * n]))
        load(("dk", n), dkv_hbm.at[rows, pl.ds(0, D)], slot(spare[3 * n + 1]))
        load(("dv", n), dkv_hbm.at[rows, pl.ds(D, D)], slot(spare[3 * n + 2]))
    load("part", part_hbm, enc_plan.buf)
    load("oc", oc_hbm, slot(S_OC))
    load("e2", e2_hbm, slot(S_E2))
    load("o", o_hbm, slot(S_O))
    load("dy1", dy1_hbm, dy1_ref)
    enter_barrier(n_blk, n_dp)

    def begin_feed(plan, name):
        loads[name + "keep"].wait()
        loads[name + "recv"].wait()
        plan.add(0, plan.held, False)
        plan.start(plan.first)

    def put_halves(plan, index, value):
        half = plan.cols
        for c in range(2):
            plan.put(2 * index + c, value[:, c * half : (c + 1) * half])

    begin_feed(feed_out, "out")
    begin_feed(feed_in, "in")
    loads["actc"].wait()
    loads["dqc"].wait()
    put_halves(crossx, 0, dot_tn(pool[S_ACTC], pool[S_DQC]))
    for w, name in ((1, "dk"), (2, "dv")):
        total = None
        for n in range(spans):
            if w == 1:
                loads["enc", n].wait()
            loads[name, n].wait()
            part = dot_tn(pool[spare[3 * n]], pool[spare[3 * n + w]])
            total = part if total is None else total + part
        put_halves(crossx, w, total)
    crossx.start(0)
    for name, src, index in (
        ("q", q_hbm, S_Q), ("k", k_hbm, S_K), ("v", v_hbm, S_V), ("do", do_hbm, S_DO), ("aug", aug_hbm, S_AUG), ("x", x_hbm, S_X),
    ):
        load(name, src, slot(index))
    loads["part"].wait()
    enc_plan.start(0)
    loads["oc"].wait()
    loads["e2"].wait()
    put_halves(crossy, 0, dot_tn(pool[S_OC], pool[S_E2]))
    loads["o"].wait()
    loads["dy1"].wait()
    put_halves(crossy, 1, dot_tn(pool[S_O], dy1_ref[...].astype(jnp.bfloat16)))
    crossy.start(0)
    load("act", act_hbm, slot(S_ACT))
    crossx.advance(0)
    for name in ("q", "k", "v", "do", "aug"):
        loads[name].wait()
    loads["act"].wait()
    act_t[...] = pool[S_ACT].T
    crossy.advance(0)
    enc_plan.advance(0)

    offsets = lax.broadcasted_iota(jnp.int32, (1, WIN), 1) - TILE
    chosen = bucket_vector(None, jnp.maximum(offsets, 0))
    lines, fars = bias_lines(table_ref)

    def pair_body(p):
        lanes = pl.ds(pl.multiple_of(p * LANES, LANES), LANES)
        dq, dk, dv, sums = self_pair_backward(
            pool[S_Q, :, lanes], pool[S_K, :, lanes], pool[S_V, :, lanes], pool[S_DO, :, lanes], pool[S_O, :, lanes],
            pool[S_AUG, :, lanes], ak, av, lines[2 * p : 2 * p + 2], fars[2 * p : 2 * p + 2], offsets, chosen,
            bias_ref, g_ref, gfar_ref, dqt_ref,
            lambda rows, value: pool.__setitem__((S_DK, rows, lanes), value),
            lambda rows, value: pool.__setitem__((S_DV, rows, lanes), value),
        )
        pool[S_DQ, :, lanes] = dq
        for head in range(2):
            tot_ref[3 + 2 * p + head] = jnp.concatenate(
                [sums[head], jnp.zeros((1, D - BUCKETS), jnp.float32)], axis=1
            )

    tot_ref[1] = gainc_ref[...]
    tot_ref[2] = gainf_ref[...]
    ak, av = key_marks(segment_rows(lengths_ref)), value_marks(LEN)
    rounds = {
        0: [],
        1: [(feed_out, 2), (feed_in, 2)],
        2: [(crossy, 1)],
        3: [(crossx, 1), (feed_out, 3), (feed_in, 3), (enc_plan, 1)],
        4: [(crossy, 2), (self0, 0)],
        5: [(feed_out, 4), (feed_in, 4), (enc_plan, 2)],
    }
    per_block = PAIRS // BLOCKS
    for block in range(BLOCKS):
        for inner in range(per_block):
            p = block * per_block + inner
            for plan, k in rounds[p]:
                plan.advance(k)
            pair_body(p)
        cols = slice(block * BLOCK, (block + 1) * BLOCK)
        for w, index in enumerate((S_DQ, S_DK, S_DV)):
            put_halves(selfs[block], w, dot_nn(act_t[...], pool[index, :, cols]))
        selfs[block].start(0)
    wq, wk, wv = slot(S_Q), slot(S_K), slot(S_V)
    for name, src, index in (("wq", wq_hbm, S_Q), ("wk", wk_hbm, S_K), ("wv", wv_hbm, S_V)):
        load(name, src, pool.at[index, pl.ds(0, D)])
    crossx.advance(2)
    self1.advance(0)
    for name in ("wq", "wk", "wv", "x"):
        loads[name].wait()
    pending = [
        [(crossy, 3), (self0, 1), (enc_plan, 3), (self2, 0)],
        [(crossx, 3), (feed_out, 5), (feed_in, 5)],
        [(self1, 1), (crossy, 4), (self0, 2)],
        [(crossx, 4), (self2, 1)],
    ]
    gain_sum = jnp.zeros((1, D), jnp.float32)
    stores = []
    for i, r in enumerate(range(0, LEN, ROWS)):
        rows = slice(r, r + ROWS)
        da = (
            dot_nt(pool[S_DQ, rows], pool[S_Q, :D])
            + dot_nt(pool[S_DK, rows], pool[S_K, :D])
            + dot_nt(pool[S_DV, rows], pool[S_V, :D])
        )
        x = pool[S_X, rows].astype(jnp.float32)
        inverse = norm_parts(x)
        gain_sum = gain_sum + jnp.sum(da * x * inverse, axis=0, keepdims=True)
        dy1_ref[rows] = dy1_ref[rows] + norm_back(x, inverse, gain_ref[0:1], da)
        stores.append(pltpu.make_async_copy(dy1_ref.at[rows], dx_hbm.at[rows], store_sem.at[i]))
        stores[-1].start()
        for plan, k in pending[i]:
            plan.advance(k)
    tot_ref[0] = gain_sum
    links = all_links(n_blk, n_dp)

    def small_copy(j):
        axis, bit = links[j]
        return pltpu.make_async_remote_copy(
            src_ref=tot_ref,
            dst_ref=got_ref.at[j],
            send_sem=tsend.at[j],
            recv_sem=trecv.at[j],
            device_id=partner(axis, bit),
            device_id_type=pl.DeviceIdType.MESH,
        )

    small_copy(0).start()
    done = {feed_in: 5, feed_out: 5, crossx: 4, crossy: 4, enc_plan: 3, self0: 2, self1: 1, self2: 1}
    longest = max(plan.steps for plan in every)
    j = 0
    while True:
        for plan in (self2, self1, self0, crossx, crossy, feed_out, feed_in, enc_plan):
            done[plan] += 1
            plan.advance(done[plan])
        if j < len(links):
            small_copy(j).wait()
            tot_ref[...] = tot_ref[...] + got_ref[j]
            j += 1
            if j < len(links):
                small_copy(j).start()
        if j == len(links) and all(done[plan] >= plan.steps - 1 for plan in every):
            break
    sums_ref[...] = tot_ref[...]
    for store in stores:
        store.wait()


def self_pair_backward(q_raw, k_raw, v_raw, do_raw, o_raw, aug, ak, av, line, far, offsets, chosen,
                       bias_ref, g_ref, gfar_ref, dqt_ref, put_dk, put_dv):
    for head in range(2):
        spread = jnp.broadcast_to(line[head : head + 1], (TILE, WIN))
        bias_ref[head] = pltpu.roll(spread, 0, 1, stride=1, stride_axis=0)[:, TILE:]
    g_ref[...] = jnp.zeros_like(g_ref)
    gfar_ref[...] = jnp.zeros_like(gfar_ref)
    dqt_ref[...] = jnp.zeros_like(dqt_ref)
    product = do_raw.astype(jnp.float32) * o_raw.astype(jnp.float32)
    deltas = []
    for head in range(2):
        half = in_half(LEN, head)
        deltas.append(jnp.sum(jnp.where(half, product, 0.0), axis=1, keepdims=True))
    aug_do = (-triple_lanes(deltas[0], deltas[1], LEN)).astype(jnp.bfloat16)
    q_scaled = q_raw * jnp.bfloat16(SCALE)
    k_t = k_raw.T
    accs = {}
    for head in range(2):
        half = in_half(LEN, head)
        q = jnp.where(half, q_scaled, aug)
        k = jnp.where(half, k_raw, ak)
        v = jnp.where(half, v_raw, av)
        do = jnp.where(half, do_raw, aug_do)
        for j in range(LEN // TILE):
            lo = j * TILE
            hi = min(LEN, (j + 3) * TILE)
            width = hi - lo
            near = min(2 * TILE, width)
            scores = dot_nt(k[lo : lo + TILE], q[lo:hi])
            parts = [scores[:, :near] + bias_ref[head][:, :near]]
            if width > near:
                parts.append(scores[:, near:] + far[head : head + 1])
            scores = parts[0] if len(parts) == 1 else jnp.concatenate(parts, axis=1)
            probs = jnp.exp(scores)
            grad_probs = dot_nt(v[lo : lo + TILE], do[lo:hi])
            grad_scores = probs * grad_probs
            g_ref[head, :, :near] += grad_scores[:, :near]
            if width > near:
                gfar_ref[head] += jnp.sum(grad_scores[:, near:].reshape(TILE // 8, 8, TILE), axis=0)
            ds = grad_scores.astype(jnp.bfloat16)
            accs[j, head] = (dot_nn(ds, q[lo:hi]), dot_nn(probs.astype(jnp.bfloat16), do[lo:hi]))
            dqt_ref[head * HD : (head + 1) * HD, lo:hi] += dot_nn(
                k_t[head * HD : (head + 1) * HD, lo : lo + TILE], ds
            )
            if head == 1:
                lower = in_half(TILE, 0)
                rows = slice(lo, lo + TILE)
                put_dk(rows, jnp.where(lower, accs[j, 0][0], accs[j, 1][0]).astype(jnp.bfloat16))
                put_dv(rows, jnp.where(lower, accs[j, 0][1], accs[j, 1][1]).astype(jnp.bfloat16))
    dq = (dqt_ref[...] * SCALE).T.astype(jnp.bfloat16)
    rows = []
    for head in range(2):
        total = jnp.zeros((8, WIN), jnp.float32)
        pad = jnp.zeros((8, TILE), jnp.float32)
        for a in range(TILE // 8):
            strip = jnp.concatenate([pad, g_ref[head, 8 * a : 8 * a + 8, :]], axis=1)
            if a:
                strip = pltpu.roll(strip, WIN - 8 * a, 1)
            total = total + strip
        line_sum = jnp.zeros((1, WIN), jnp.float32)
        for s in range(8):
            one = total[s : s + 1]
            line_sum = line_sum + (pltpu.roll(one, WIN - s, 1) if s else one)
        rows.append(line_sum)
    lines = jnp.concatenate(rows, axis=0)
    lines = jnp.where(offsets >= 0, lines, 0.0)
    high, mid, low = split3(lines)
    sums = sum(dot_nt(part.astype(jnp.bfloat16), chosen) for part in (high, mid, low))
    lane32 = lax.broadcasted_iota(jnp.int32, (1, BUCKETS), 1)
    tables = []
    for head in range(2):
        far_sum = jnp.sum(gfar_ref[head])
        tables.append(sums[head : head + 1] + jnp.where(lane32 == BUCKETS - 1, far_sum, 0.0))
    return dq, None, None, tables


def last_block(n_blk, n_dp, plans, enc_plan, big, little, keys):
    every = list(plans) + [enc_plan]
    links = len(all_links(n_blk, n_dp))
    scratch = [item for plan in every for item in plan.scratch()]
    scratch += [
        pltpu.VMEM((POOL, LEN, D), jnp.bfloat16),
        pltpu.VMEM((LEN, D), jnp.float32),
        pltpu.VMEM((D, LEN), jnp.bfloat16),
        pltpu.VMEM((2, TILE, 2 * TILE), jnp.float32),
        pltpu.VMEM((2, TILE, 2 * TILE), jnp.float32),
        pltpu.VMEM((2, 8, TILE), jnp.float32),
        pltpu.VMEM((LANES, LEN), jnp.float32),
        pltpu.VMEM((3 + H, 1, D), jnp.float32),
        pltpu.VMEM((links, 3 + H, 1, D), jnp.float32),
        pltpu.SemaphoreType.DMA((links,)),
        pltpu.SemaphoreType.DMA((links,)),
        pltpu.SemaphoreType.DMA((len(big) + 3 * (keys // LEN) - 2 + 1,)),
        pltpu.SemaphoreType.DMA((LEN // ROWS,)),
    ]
    return pl.pallas_call(
        partial(last_kernel, n_blk, n_dp, plans, enc_plan),
        in_specs=[any_spec()] * len(big) + [vmem_spec()] * len(little),
        out_specs=[vmem_spec()] * len(every) + [any_spec(), vmem_spec()],
        out_shape=[plan.out_shape() for plan in every]
        + [jax.ShapeDtypeStruct((LEN, D), jnp.float32), jax.ShapeDtypeStruct((3 + H, 1, D), jnp.float32)],
        scratch_shapes=scratch,
        compiler_params=pltpu.CompilerParams(
            vmem_limit_bytes=VMEM_LIMIT, collective_id=1, has_side_effects=True
        ),
        cost_estimate=pl.CostEstimate(flops=40 * LEN * D * D, bytes_accessed=80 * LEN * D, transcendentals=0),
    )(*big, *little)


def segment_rows(lengths_ref):
    rows = lax.broadcasted_iota(jnp.int32, (LEN, LANES), 0)
    end = jnp.zeros((1, 1), jnp.int32)
    seg = jnp.zeros((LEN, LANES), jnp.int32)
    for t in range(TARGETS - 1):
        end = end + lengths_ref[:, t : t + 1]
        seg = seg + (rows >= end).astype(jnp.int32)
    return seg


def query_marks(seg):
    place = lane_ids(LEN) & (HD - 1)
    return jnp.where((place >= 3) & (place - 3 == seg), 1.0, 0.0).astype(jnp.bfloat16)


def key_marks(seg):
    place = lane_ids(LEN) & (HD - 1)
    other = (place >= 3) & (place < 3 + TARGETS) & (place - 3 != seg)
    return jnp.where(place < 3, -1.0, jnp.where(other, NEG, 0.0)).astype(jnp.bfloat16)


def value_marks(rows):
    place = lane_ids(rows) & (HD - 1)
    return jnp.where(place < 3, 1.0, 0.0).astype(jnp.bfloat16)


def bias_lines(table_ref):
    offsets = lax.broadcasted_iota(jnp.int32, (1, WIN), 1) - TILE
    chosen = bucket_vector(None, jnp.maximum(offsets, 0))
    lines = dot_tn(table_ref[...], chosen)
    return jnp.where(offsets >= 0, lines, NEG), lines[:, WIN - 1 :]


def front_kernel(n_blk, n_dp, x_hbm, enc_hbm, wq_hbm, wk_hbm, wv_hbm, wo_hbm, wcq_hbm, wck_hbm, wcv_hbm,
                 lengths_ref, gain_ref, gainc_ref, table_ref,
                 q_hbm, k_hbm, v_hbm, o_hbm, aug_hbm, act_hbm, y1_hbm, actc_hbm, qc_hbm, kv_hbm, encall_hbm,
                 x_ref, w_ref, act_ref, q_ref, k_ref, v_ref, o_ref, aug_ref, y1_ref, kv_ref, enc_ref, bias_ref, ot_ref, logs_ref,
                 send_sem, recv_sem, load_sem, store_sem):
    passage = enc_hbm.shape[0]
    loads = []
    for n, (src, dst) in enumerate(
        [(enc_hbm, enc_ref.at[0]), (x_hbm, x_ref)]
        + [(w, w_ref.at[i]) for i, w in enumerate((wq_hbm, wk_hbm, wv_hbm, wo_hbm, wcq_hbm, wck_hbm, wcv_hbm))]
    ):
        loads.append(pltpu.make_async_copy(src, dst, load_sem.at[n]))
        loads[-1].start()
    stores = []

    def store(src, dst):
        stores.append(pltpu.make_async_copy(src, dst, store_sem.at[len(stores)]))
        stores[-1].start()

    bits = bits_of(n_blk)

    def gather(k):
        size = 1 << k
        return pltpu.make_async_remote_copy(
            src_ref=enc_ref.at[pl.ds(0, size)],
            dst_ref=enc_ref.at[pl.ds(size, size)],
            send_sem=send_sem.at[k],
            recv_sem=recv_sem.at[k],
            device_id=partner("blk", bits - 1 - k),
            device_id_type=pl.DeviceIdType.MESH,
        )

    barrier = pltpu.get_barrier_semaphore()
    for bit in range(bits):
        pl.semaphore_signal(barrier, inc=1, device_id=partner("blk", bit), device_id_type=pl.DeviceIdType.MESH)
    pl.semaphore_wait(barrier, bits)
    loads[0].wait()
    gather(0).start()
    loads[1].wait()
    for r in range(0, LEN, ROWS):
        rows = slice(r, r + ROWS)
        x = x_ref[rows].astype(jnp.float32)
        act_ref[rows] = (x * norm_parts(x) * gain_ref[0:1]).astype(jnp.bfloat16)
    for i, (ref, out) in enumerate(((q_ref, q_hbm), (k_ref, k_hbm), (v_ref, v_hbm))):
        loads[2 + i].wait()
        for r in range(0, LEN, ROWS):
            rows = slice(r, r + ROWS)
            ref[rows] = dot_nn(act_ref[rows], w_ref[i]).astype(jnp.bfloat16)
        store(ref, out)
    store(act_ref, act_hbm)
    seg = segment_rows(lengths_ref)
    aq, ak = query_marks(seg), key_marks(seg)
    lines, fars = bias_lines(table_ref)
    for p in range(PAIRS):
        lanes = slice(p * LANES, (p + 1) * LANES)
        if p % 2 == 1 and p // 2 < bits - 1:
            gather(p // 2).wait()
            gather(p // 2 + 1).start()
        self_pair_forward(q_ref[:, lanes], k_ref[:, lanes], v_ref[:, lanes], aq, ak, lines[2 * p : 2 * p + 2],
                          fars[2 * p : 2 * p + 2], bias_ref, ot_ref, logs_ref, o_ref, aug_ref, lanes)
    store(o_ref, o_hbm)
    store(aug_ref, aug_hbm)
    for k in range(min(bits - 1, PAIRS // 2), bits - 1):
        gather(k).wait()
        gather(k + 1).start()
    for n in range(5, 9):
        loads[n].wait()
    for r in range(0, LEN, ROWS):
        rows = slice(r, r + ROWS)
        y1 = x_ref[rows].astype(jnp.float32) + dot_nn(o_ref[rows], w_ref[3])
        y1_ref[rows] = y1
        store(y1_ref.at[pl.ds(r, ROWS)], y1_hbm.at[pl.ds(r, ROWS)])
        actc = (y1 * norm_parts(y1) * gainc_ref[1:2]).astype(jnp.bfloat16)
        x_ref[rows] = actc
        store(x_ref.at[pl.ds(r, ROWS)], actc_hbm.at[pl.ds(r, ROWS)])
    gather(bits - 1).wait()
    for s in range(0, n_blk):
        store(enc_ref.at[s], encall_hbm.at[pl.ds(s * passage, passage)])
    group = ROWS // passage
    for s in range(0, n_blk, group):
        encs = enc_ref[s : s + group].reshape(group * passage, D)
        rows = slice(s * passage, (s + group) * passage)
        kv_ref[rows, :D] = dot_nn(encs, w_ref[5]).astype(jnp.bfloat16)
        kv_ref[rows, D:] = dot_nn(encs, w_ref[6]).astype(jnp.bfloat16)
    store(kv_ref, kv_hbm)
    stores[0].wait()
    for r in range(0, LEN, ROWS):
        rows = slice(r, r + ROWS)
        q_ref[rows] = dot_nn(x_ref[rows], w_ref[4]).astype(jnp.bfloat16)
        store(q_ref.at[pl.ds(r, ROWS)], qc_hbm.at[pl.ds(r, ROWS)])
    for copy in stores[1:]:
        copy.wait()


def self_pair_forward(q_raw, k_raw, v_raw, aq, ak, line, far, bias_ref, ot_ref, logs_ref, o_ref, aug_ref, lanes):
    for head in range(2):
        spread = jnp.broadcast_to(line[head : head + 1], (TILE, WIN))
        bias_ref[head] = pltpu.roll(spread, 0, 1, stride=1, stride_axis=0)[:, TILE:]
    v_t = v_raw.T
    for head in range(2):
        half = in_half(LEN, head)
        q = jnp.where(half, q_raw * jnp.bfloat16(SCALE), aq)
        k = jnp.where(half, k_raw, ak)
        for i in range(LEN // TILE):
            cols = slice(i * TILE, (i + 1) * TILE)
            tiles = []
            for j in range(max(0, i - 2), i + 1):
                scores = dot_nt(k[j * TILE : (j + 1) * TILE], q[cols])
                if i - j < 2:
                    scores = scores + bias_ref[head, :, (i - j) * TILE : (i - j + 1) * TILE]
                else:
                    scores = scores + far[head : head + 1]
                tiles.append(scores)
            peak = tiles[0]
            for tile in tiles[1:]:
                peak = jnp.maximum(peak, tile)
            top = jnp.max(peak, axis=0, keepdims=True)
            total, mixed = None, None
            for n, j in enumerate(range(max(0, i - 2), i + 1)):
                expo = jnp.exp(tiles[n] - top)
                part = jnp.sum(expo, axis=0, keepdims=True)
                out = dot_nn(v_t[head * HD : (head + 1) * HD, j * TILE : (j + 1) * TILE], expo.astype(jnp.bfloat16))
                total = part if total is None else total + part
                mixed = out if mixed is None else mixed + out
            ot_ref[head * HD : (head + 1) * HD, cols] = mixed * (1.0 / total)
            logs_ref[head : head + 1, cols] = top + jnp.log(total)
    o_ref[:, lanes] = ot_ref[...].T.astype(jnp.bfloat16)
    first, second = split3(logs_ref[0:1]), split3(logs_ref[1:2])
    zeros = jnp.zeros((HD - 8, LEN), jnp.float32)
    pad = jnp.zeros((5, LEN), jnp.float32)
    triples = jnp.concatenate(list(second) + [pad, zeros] + list(first) + [pad, zeros], axis=0).T
    place = lane_ids(LEN) & (HD - 1)
    aug_ref[:, lanes] = jnp.where(place < 3, triples.astype(jnp.bfloat16), aq)


def front_block(n_blk, n_dp, big, little, keys, passage):
    wide = jax.ShapeDtypeStruct((LEN, D), jnp.bfloat16)
    n_store = 6 + n_blk + 3 * (LEN // ROWS) + 1
    return pl.pallas_call(
        partial(front_kernel, n_blk, n_dp),
        in_specs=[any_spec()] * len(big) + [vmem_spec()] * len(little),
        out_specs=[any_spec()] * 11,
        out_shape=[wide] * 6
        + [
            jax.ShapeDtypeStruct((LEN, D), jnp.float32),
            wide,
            wide,
            jax.ShapeDtypeStruct((keys, 2 * D), jnp.bfloat16),
            jax.ShapeDtypeStruct((keys, D), jnp.bfloat16),
        ],
        scratch_shapes=[
            pltpu.VMEM((LEN, D), jnp.bfloat16),
            pltpu.VMEM((7, D, D), jnp.bfloat16),
            pltpu.VMEM((LEN, D), jnp.bfloat16),
            pltpu.VMEM((LEN, D), jnp.bfloat16),
            pltpu.VMEM((LEN, D), jnp.bfloat16),
            pltpu.VMEM((LEN, D), jnp.bfloat16),
            pltpu.VMEM((LEN, D), jnp.bfloat16),
            pltpu.VMEM((LEN, D), jnp.bfloat16),
            pltpu.VMEM((LEN, D), jnp.float32),
            pltpu.VMEM((keys, 2 * D), jnp.bfloat16),
            pltpu.VMEM((n_blk, passage, D), jnp.bfloat16),
            pltpu.VMEM((2, TILE, 2 * TILE), jnp.float32),
            pltpu.VMEM((LANES, LEN), jnp.float32),
            pltpu.VMEM((2, LEN), jnp.float32),
            pltpu.SemaphoreType.DMA((bits_of(n_blk),)),
            pltpu.SemaphoreType.DMA((bits_of(n_blk),)),
            pltpu.SemaphoreType.DMA((len(big),)),
            pltpu.SemaphoreType.DMA((n_store,)),
        ],
        compiler_params=pltpu.CompilerParams(
            vmem_limit_bytes=VMEM_LIMIT, collective_id=2, has_side_effects=True
        ),
        cost_estimate=pl.CostEstimate(flops=20 * LEN * D * D, bytes_accessed=40 * LEN * D, transcendentals=0),
    )(*big, *little)


FF_STEPS = 4


def normal_cdf_pair(u):
    x = jnp.abs(u) * 0.7071067811865476
    gauss = jnp.exp(-0.5 * u * u)
    t = 1.0 / (1.0 + 0.3275911 * x)
    poly = ((((1.061405429 * t - 1.453152027) * t + 1.421413741) * t - 0.284496736) * t + 0.254829592) * t
    tail = 0.5 * poly * gauss
    return jnp.where(u >= 0, 1.0 - tail, tail), gauss * 0.3989422804014327


def rest_slot(owner, piece, order):
    slot = 0
    for axis, bit in order[2:]:
        mine = (lax.axis_index(axis) // (1 << bit)) % 2
        its = ((owner if axis == "blk" else piece) // (1 << bit)) % 2
        slot = 2 * slot + (its + mine) % 2
    return slot


class FeedParts:
    def __init__(self, plan, owners, units):
        self.plan, self.owners, self.units = plan, owners, units
        self.count = owners // 2 * len(units)

    def split(self, grad, even_core, put_send, put_keep):
        n = 0
        for t in range(0, self.owners, 2):
            for u in self.units:
                even, odd = grad(t, u), grad(t + 1, u)
                put_send(n, jnp.where(even_core, odd, even).astype(jnp.bfloat16))
                put_keep(n, jnp.where(even_core, even, odd).astype(jnp.bfloat16))
                n += 1

    def index(self, t, u):
        return t // 2 * len(self.units) + self.units.index(u)


def feed_kernel(n_blk, n_dp, plan_in, plan_out, y1_ref, oc_ref, wco_ref, gain_ref, g_ref, w1_ref, w2_ref,
                out_ref, isend_ref, ikeep_ref, osend_ref, okeep_ref, dy2_ref, e2_ref, doc_ref, dgain_ref,
                y2_ref, act_ref, acc_ref, da_ref, hid_ref, du_ref, away_ref, stay_ref, got_ref, send_sem, recv_sem):
    step = pl.program_id(0)
    even_core = lax.axis_index("blk") % 2 == 0
    group = n_blk // FF_STEPS
    parts_out = FeedParts(plan_out, group, list(range(plan_out.count)))
    parts_in = FeedParts(plan_in, n_blk, [0])

    def exchange(s):
        return pltpu.make_async_remote_copy(
            src_ref=away_ref.at[s],
            dst_ref=got_ref.at[s],
            send_sem=send_sem.at[s],
            recv_sem=recv_sem.at[s],
            device_id=partner("blk", 0),
            device_id_type=pl.DeviceIdType.MESH,
        )

    def settle(s):
        exchange(s).wait()

        def total(n):
            return (stay_ref[s % 2, n].astype(jnp.float32) + got_ref[s, n].astype(jnp.float32)).astype(jnp.bfloat16)

        def place(plan, first, second, owner, piece, inner, send_ref, keep_ref):
            axis, bit = plan.order[1]
            low = (lax.axis_index(axis) // (1 << bit)) % 2 == 0
            a, b = total(first), total(second)
            slot = rest_slot(owner, piece, plan.order)
            send_ref[slot, inner] = jnp.where(low, b, a)
            keep_ref[slot, inner] = jnp.where(low, a, b)

        for t in range(0, group, 2):
            for u in parts_out.units:
                n = parts_out.index(t, u)
                owner = s * group + t
                if plan_out.order[1][0] == "dp":
                    if u // plan_out.mats == 0:
                        twin = parts_out.index(t, u + plan_out.mats)
                        place(plan_out, n, twin, owner, 0, u % plan_out.mats, osend_ref, okeep_ref)
                elif (t >> 1) & 1 == 0:
                    place(plan_out, n, parts_out.index(t + 2, u), owner, 0, u, osend_ref, okeep_ref)
        for t in range(0, n_blk, 2):
            if (t >> 1) & 1 == 0:
                n = parts_out.count + parts_in.index(t, 0)
                twin = parts_out.count + parts_in.index(t + 2, 0)
                place(plan_in, n, twin, t, s // plan_in.mats, s % plan_in.mats, isend_ref, ikeep_ref)

    @pl.when(step == 0)
    def _():
        barrier = pltpu.get_barrier_semaphore()
        pl.semaphore_signal(
            barrier, inc=1, device_id=partner("blk", 0), device_id_type=pl.DeviceIdType.MESH
        )
        pl.semaphore_wait(barrier, 1)
        for r in range(0, LEN, ROWS):
            rows = slice(r, r + ROWS)
            y2 = y1_ref[rows] + dot_nn(oc_ref[rows], wco_ref[...])
            y2_ref[rows] = y2
            act_ref[rows] = (y2 * norm_parts(y2) * gain_ref[2:3]).astype(jnp.bfloat16)
        acc_ref[...] = y2_ref[...]
        da_ref[...] = jnp.zeros_like(da_ref)

    for r in range(0, LEN, ROWS):
        rows = slice(r, r + ROWS)
        u = dot_nn(act_ref[rows], w1_ref[...])
        dh = dot_nt(g_ref[rows], w2_ref[...])
        cdf, density = normal_cdf_pair(u)
        hid = (u * cdf).astype(jnp.bfloat16)
        du = (dh * (cdf + u * density)).astype(jnp.bfloat16)
        hid_ref[rows] = hid
        du_ref[rows] = du
        acc_ref[rows] += dot_nn(hid, w2_ref[...])
        da_ref[rows] += dot_nt(du, w1_ref[...])

    def put(n, value, base, ref):
        ref[base + n] = value

    dw2 = dot_tn(hid_ref[...], g_ref[...])
    own_rows = plan_out.rows * plan_out.count
    parts_out.split(
        lambda t, m: dw2[t * own_rows + m * plan_out.rows : t * own_rows + (m + 1) * plan_out.rows],
        even_core,
        lambda n, value: away_ref.__setitem__((step, n), value),
        lambda n, value: stay_ref.__setitem__((step % 2, n), value),
    )
    dw1 = dot_tn(act_ref[...], du_ref[...])
    parts_in.split(
        lambda t, m: dw1[t * plan_in.rows : (t + 1) * plan_in.rows],
        even_core,
        lambda n, value: away_ref.__setitem__((step, parts_out.count + n), value),
        lambda n, value: stay_ref.__setitem__((step % 2, parts_out.count + n), value),
    )
    exchange(step).start()

    @pl.when(step > 0)
    def _():
        settle(step - 1)

    @pl.when(step == FF_STEPS - 1)
    def _():
        gain_sum = jnp.zeros((1, D), jnp.float32)
        for r in range(0, LEN, ROWS):
            rows = slice(r, r + ROWS)
            out_ref[rows] = acc_ref[rows].astype(jnp.bfloat16)
            y2 = y2_ref[rows]
            inverse = norm_parts(y2)
            da = da_ref[rows]
            gain_sum = gain_sum + jnp.sum(da * y2 * inverse, axis=0, keepdims=True)
            dy2 = g_ref[rows].astype(jnp.float32) + norm_back(y2, inverse, gain_ref[2:3], da)
            dy2_ref[rows] = dy2
            e2 = dy2.astype(jnp.bfloat16)
            e2_ref[rows] = e2
            doc_ref[rows] = dot_nt(e2, wco_ref[...]).astype(jnp.bfloat16)
        dgain_ref[...] = gain_sum
        settle(step)


def feed_block(n_blk, n_dp, y1, oc, wco, gain, g, w1, w2, plan_in, plan_out):
    ff = w1.shape[1]
    cols = ff // FF_STEPS
    fixed = vmem_spec()
    quarter = lambda plan: (plan.slots // 4, plan.mats, plan.rows, D)
    like = jax.ShapeDtypeStruct
    units = n_blk // FF_STEPS // 2 * plan_out.count + n_blk // 2
    packet = (units, D // n_blk, D)
    return pl.pallas_call(
        partial(feed_kernel, n_blk, n_dp, plan_in, plan_out),
        grid=(FF_STEPS,),
        in_specs=[fixed] * 5
        + [
            pl.BlockSpec((D, cols), lambda c: (0, c)),
            pl.BlockSpec((cols, D), lambda c: (c, 0)),
        ],
        out_specs=[fixed] * 9,
        out_shape=[
            like((LEN, D), jnp.bfloat16),
            like(quarter(plan_in), jnp.bfloat16),
            like(quarter(plan_in), jnp.bfloat16),
            like(quarter(plan_out), jnp.bfloat16),
            like(quarter(plan_out), jnp.bfloat16),
            like((LEN, D), jnp.float32),
            like((LEN, D), jnp.bfloat16),
            like((LEN, D), jnp.bfloat16),
            like((1, D), jnp.float32),
        ],
        scratch_shapes=[
            pltpu.VMEM((LEN, D), jnp.float32),
            pltpu.VMEM((LEN, D), jnp.bfloat16),
            pltpu.VMEM((LEN, D), jnp.float32),
            pltpu.VMEM((LEN, D), jnp.float32),
            pltpu.VMEM((LEN, cols), jnp.bfloat16),
            pltpu.VMEM((LEN, cols), jnp.bfloat16),
            pltpu.VMEM((FF_STEPS,) + packet, jnp.bfloat16),
            pltpu.VMEM((2,) + packet, jnp.bfloat16),
            pltpu.VMEM((FF_STEPS,) + packet, jnp.bfloat16),
            pltpu.SemaphoreType.DMA((FF_STEPS,)),
            pltpu.SemaphoreType.DMA((FF_STEPS,)),
        ],
        compiler_params=pltpu.CompilerParams(
            vmem_limit_bytes=VMEM_LIMIT, collective_id=3, has_side_effects=True
        ),
        cost_estimate=pl.CostEstimate(flops=12 * LEN * D * ff, bytes_accessed=40 * LEN * D, transcendentals=0),
    )(y1, oc, wco, gain, g, w1, w2)


def unpack_kernel(in_ref, out_ref, crossx, crossy, *refs):
    blocks, (enc_ref, sums_ref), outs = refs[: len(BLOCK_PAIRS)], refs[len(BLOCK_PAIRS) : len(BLOCK_PAIRS) + 2], refs[len(BLOCK_PAIRS) + 2 :]
    (gq, gk, gv, go, gcq, gck, gcv, gco, gin, gout, genc, gain0, gain1, gain2, table) = outs
    for w, ref in enumerate((gq, gk, gv)):
        at = 0
        for part, pairs in zip(blocks, BLOCK_PAIRS):
            for c in range(pairs):
                ref[:, at : at + LANES] = part[pairs * w + c]
                at += LANES
    half = D // 2
    for ref, part, w in ((gcq, crossx, 0), (gck, crossx, 1), (gcv, crossx, 2), (gco, crossy, 0), (go, crossy, 1)):
        for c in range(2):
            ref[:, c * half : (c + 1) * half] = part[2 * w + c]
    rows = gq.shape[0]
    for m in range(4):
        gin[:, m * D : (m + 1) * D] = in_ref[m]
        gout[m * rows : (m + 1) * rows] = out_ref[m]
    genc[...] = enc_ref[0]
    for n, ref in enumerate((gain0, gain1, gain2)):
        ref[...] = sums_ref[n].reshape(D)
    tables = jnp.concatenate([sums_ref[3 + h][:, :LANES] for h in range(H)] + [jnp.zeros((4, LANES), jnp.float32)], axis=0)
    table[...] = tables.T[:BUCKETS, :H]


def unpack(n_blk, passage, parts):
    rows = D // n_blk
    like = lambda *shape: jax.ShapeDtypeStruct(shape, jnp.float32)
    return pl.pallas_call(
        unpack_kernel,
        in_specs=[vmem_spec()] * len(parts),
        out_specs=[vmem_spec()] * 15,
        out_shape=[like(rows, D)] * 8
        + [like(rows, 4 * D), like(4 * rows, D), like(passage, D)]
        + [like(D)] * 3
        + [like(BUCKETS, H)],
        compiler_params=pltpu.CompilerParams(vmem_limit_bytes=VMEM_LIMIT),
    )(*parts)


def swap(value, axis, bit, size):
    return lax.ppermute(value, axis, [(i, i ^ (1 << bit)) for i in range(size)])


def per_device(
    decoder_rows,
    encoder_rows,
    target_lengths,
    target_question,
    passage_question,
    self_gain,
    self_query,
    self_key,
    self_value,
    self_output,
    position_bias_matrix,
    cross_gain,
    cross_query,
    cross_key,
    cross_value,
    cross_output,
    feed_gain,
    feed_input_weight,
    feed_out,
    cotangent,
    n_dp,
    n_blk,
):
    passage = encoder_rows.shape[0]
    keys = passage * n_blk
    sizes = {"blk": n_blk, "dp": n_dp}
    self_gain = cross_gain = feed_gain = jnp.stack([self_gain, cross_gain, feed_gain])
    (query_self, key_self, value_self, attn_self, aug_self, act_self, resid_self, act_cross, query_cross, pair_all,
     encoder_all) = front_block(
        n_blk, n_dp,
        (decoder_rows, encoder_rows, self_query, self_key, self_value, self_output, cross_query, cross_key, cross_value),
        (target_lengths, self_gain, cross_gain, position_bias_matrix), keys, passage,
    )
    layout = (target_lengths, target_question, passage_question)
    attn_cross, aug_cross = cross_forward(n_blk, passage, *layout, query_cross, pair_all)
    plan_in, plan_out = feed_plans(n_blk, n_dp)
    (block_out, in_send, in_keep, out_send, out_keep, grad_resid_cross, round_cross, grad_attn_cross, feed_sum) = feed_block(
        n_blk, n_dp, resid_self, attn_cross, cross_output, feed_gain, cotangent, feed_input_weight, feed_out,
        plan_in, plan_out,
    )
    in_got = swap(in_send, *plan_in.order[FEED_DONE - 1], sizes[plan_in.order[FEED_DONE - 1][0]])
    out_got = swap(out_send, *plan_out.order[FEED_DONE - 1], sizes[plan_out.order[FEED_DONE - 1][0]])
    dqc, dkv, grad_resid_self, grad_attn_self, encoder_part, cross_sum = cross_backward(
        n_blk, passage, *layout, query_cross, pair_all, grad_attn_cross, attn_cross, aug_cross,
        resid_self, grad_resid_cross, cross_query, cross_key, cross_value, self_output, cross_gain,
    )
    enc_plan = Exchange(1, passage, D, n_blk, n_dp, "near")
    big = (
        decoder_rows, grad_resid_self, act_self, self_query, self_key, self_value, act_cross, dqc, encoder_all, dkv,
        attn_cross, round_cross, query_self, key_self, value_self, grad_attn_self, attn_self, aug_self,
        in_keep, in_got, out_keep, out_got, encoder_part,
    )
    last = last_block(
        n_blk, n_dp, last_plans(n_blk, n_dp), enc_plan, big,
        (target_lengths, self_gain, position_bias_matrix, cross_sum, feed_sum), keys,
    )
    spot = len(last) - 2
    grad_decoder = last[spot]
    (gq, gk, gv, go, gcq, gck, gcv, gco, gin, gout, genc, gain_self, gain_cross, gain_feed, table) = unpack(
        n_blk, passage, last[:spot] + last[spot + 1 :]
    )
    return (
        block_out, grad_decoder, genc, gain_self, gq, gk, gv, go, table, gain_cross, gcq, gck, gcv, gco,
        gain_feed, gin, gout,
    )


def solution(mesh):
    split, copied, owned = P(("dp", "blk"), None), P(), P("blk", None)
    return jax.shard_map(
        partial(per_device, n_dp=mesh.shape["dp"], n_blk=mesh.shape["blk"]),
        mesh=mesh,
        in_specs=(split,) * 4 + (P("dp"),) + (copied,) * 14 + (split,),
        out_specs=(split,) * 3 + (copied,) + (owned,) * 4 + (copied,) * 2 + (owned,) * 4 + (copied,) + (owned,) * 2,
        check_vma=False,
    )
```
